32 devices in a mesh: ctx: 4 (over z), fsdp: 8 (over y, x, core).
Axes of the slice: x: 2, y: 2, z: 4, core: 2. Of those that a mesh axis runs over, the one named last changes fastest.
Arguments:
- tokens: bfloat16 [8, 1024, 2048], P('fsdp', 'ctx'), may hold values from -6 to 6
- block_order: int32 [8, 4], P('fsdp'), may hold values from 0 to 3, each once within a row
- ln_gain: bfloat16 [2048], P('fsdp'), may hold values from 0.5 to 1.5
- ln_bias: bfloat16 [2048], P('fsdp'), may hold values from -2 to 2
- w_qkv: bfloat16 [2048, 6144], P('fsdp'), may hold values from -0.125 to 0.125
- w_out: bfloat16 [2048, 2048], P('fsdp'), may hold values from -2 to 2
- w_gate: bfloat16 [2048, 5632], P('fsdp'), may hold values from -0.125 to 0.125
- w_up: bfloat16 [2048, 5632], P('fsdp'), may hold values from -0.125 to 0.125
- w_down: bfloat16 [5632, 2048], P('fsdp'), may hold values from -0.109375 to 0.109375
- cotangent: bfloat16 [8, 1024, 2048], P('fsdp', 'ctx'), may hold values from -6 to 6
Outputs:
- out: bfloat16 [8, 1024, 2048], P('fsdp', 'ctx')
- grad_in: float32 [8, 1024, 2048], P('fsdp', 'ctx')
- d_gain: float32 [2048], P('fsdp')
- d_bias: float32 [2048], P('fsdp')
- d_qkv: float32 [2048, 6144], P('fsdp')
- d_out: float32 [2048, 2048], P('fsdp')
- d_gate: float32 [2048, 5632], P('fsdp')
- d_up: float32 [2048, 5632], P('fsdp')
- d_down: float32 [5632, 2048], P('fsdp')
The draws below stay inside these ranges and needn't reach their ends.
Inputs may be any that keep to these rules, and one draw needn't show every extreme that they name: Each row of block_order holds every block number from 0 to 3 once.
All inputs are finite; a program needn't handle non-finite values.
Results may differ from the reference program's by a relative error of at most 0.018.
Values may be sent and summed in bfloat16 or wider, within the bound.
A program may use at most 512 MiB of HBM per device.

```python
import math
import jax
import jax.numpy as jnp
from jax import lax

D = 2048
FF = 5632
H = 32
HD = 64
ROT = 16
LENGTH = 1024
SEQS = 8
N_CTX = 4


def block_levels(own_key, extent, shards, smallest, high):
    def one(axis_at, parts):
        steps = jax.random.uniform(jax.random.fold_in(jax.random.fold_in(own_key, 6), axis_at), (parts,), jnp.float32, smallest / len(shards), high / len(shards))
        return jnp.repeat(jnp.exp(steps), extent[axis_at] // parts).reshape((-1,) + (1,) * (len(extent) - axis_at - 1))

    loudness = one(*shards[0])
    for cut in shards[1:]:
        loudness = loudness * one(*cut)
    return loudness


def normal_values(stream_key, extent, spread, most, split=(), kind=jnp.bfloat16):
    entries = spread * jax.random.normal(stream_key, extent, jnp.float32)
    if split:
        entries = entries * block_levels(stream_key, extent, split, -0.22, 0.18)
    return jnp.clip(entries, -most, most).astype(kind)


def setup_inputs(seed: int = 0) -> dict:
    streams_of = jax.random.split(jax.random.key(seed), 11)
    tokens = normal_values(streams_of[0], (SEQS, LENGTH, D), 1.0, 6.0, ((0, 8), (1, 4)))
    block_order = jax.vmap(lambda own: jax.random.permutation(own, N_CTX))(jax.random.split(streams_of[1], SEQS)).reshape((SEQS, N_CTX)).astype(jnp.int32)
    ln_gain = jnp.clip(1.0 + 0.1 * jax.random.normal(streams_of[2], (D,), jnp.float32), 0.5, 1.5).astype(jnp.bfloat16)
    ln_bias = normal_values(streams_of[3], (D,), 0.3, 2.0, ((0, 8),))
    w_qkv = normal_values(streams_of[4], (D, 3 * D), D ** -0.5, 0.125, ((0, 8),))
    w_out = normal_values(streams_of[5], (D, D), (max(D // 256, 8)) ** -0.5, 2.0, ((0, 8),))
    w_gate = normal_values(streams_of[6], (D, FF), D ** -0.5, 0.125, ((0, 8),))
    w_up = normal_values(streams_of[7], (D, FF), D ** -0.5, 0.125, ((0, 8),))
    w_down = normal_values(streams_of[8], (FF, D), (FF // 2) ** -0.5, 0.109375, ((0, 8),))
    cotangent = normal_values(streams_of[9], (SEQS, LENGTH, D), 1.0, 6.0, ((0, 8), (1, 4)))
    return dict(tokens=tokens, block_order=block_order, ln_gain=ln_gain, ln_bias=ln_bias, w_qkv=w_qkv, w_out=w_out, w_gate=w_gate, w_up=w_up, w_down=w_down, cotangent=cotangent)


EPS = 1e-05
NEG = -1e+30
HIGH = lax.Precision.HIGHEST

@jax.custom_vjp
def low(v):
    return lax.optimization_barrier(v.astype(jnp.bfloat16)).astype(jnp.float32)

@jax.custom_vjp
def low_back(v):
    return v

def low_keep(v):
    return (low(v), None)

def low_pass(kept, grad):
    return (grad,)

def back_keep(v):
    return (v, None)

def back_low(kept, grad):
    return (low(grad),)
low.defvjp(low_keep, low_pass)
low_back.defvjp(back_keep, back_low)

def angles(positions):
    half_rot = ROT // 2
    inverse = 10000.0 ** (-jnp.arange(half_rot, dtype=jnp.float32) / half_rot)
    angle_grid = positions.astype(jnp.float32)[:, None] * inverse[None, :]
    return (jnp.cos(angle_grid)[:, None, :], jnp.sin(angle_grid)[:, None, :])

def rotate(field, cosine, sine_table):
    half_rot = ROT // 2
    leading = field[..., :half_rot]
    trailing = field[..., half_rot:ROT]
    return jnp.concatenate([leading * cosine - trailing * sine_table, trailing * cosine + leading * sine_table, field[..., ROT:]], axis=-1)

def layer_forward(xf, positions, gain, bias, w_qkv, w_out, w_gate, w_up, w_down):
    length = xf.shape[0]
    average = lax.optimization_barrier(jnp.mean(xf, axis=-1, keepdims=True))
    centered = xf - average
    variance = lax.optimization_barrier(jnp.mean(centered * centered, axis=-1, keepdims=True))
    normed = low(centered * lax.rsqrt(variance + EPS) * gain + bias)
    mixed_qkv = low_back(jnp.dot(normed, w_qkv, precision=HIGH))
    cosine, sine_table = angles(positions)
    queries = low(rotate(mixed_qkv[:, :D].reshape(length, H, HD), cosine, sine_table))
    keys_low = low(rotate(mixed_qkv[:, D:2 * D].reshape(length, H, HD), cosine, sine_table))
    values_low = low(mixed_qkv[:, 2 * D:].reshape(length, H, HD))
    block_rows = math.gcd(length, 512)

    def attend_rows(pair):
        query_rows, pos_rows = pair
        scores = low_back(jnp.einsum('qhd,khd->hqk', query_rows, keys_low, precision=HIGH) * HD ** (-0.5))
        allowed = (positions[None, :] <= pos_rows[:, None])[None]
        scores = jnp.where(allowed, scores, NEG)
        running_max = lax.optimization_barrier(jnp.max(scores, axis=-1, keepdims=True))
        running_sum = lax.optimization_barrier(jnp.sum(jnp.exp(scores - running_max), axis=-1, keepdims=True))
        soft_weights = low(jnp.exp(scores - running_max - jnp.log(running_sum)))
        return jnp.einsum('hqk,khd->qhd', soft_weights, values_low, precision=HIGH)
    query_blocks = queries.reshape(length // block_rows, block_rows, H, HD)
    pos_blocks = positions.reshape(length // block_rows, block_rows)
    attended = lax.map(jax.checkpoint(attend_rows), (query_blocks, pos_blocks)).reshape(length, D)
    attended = low(low_back(attended))
    branch = jnp.dot(attended, w_out, precision=HIGH)
    gate_value = low_back(jnp.dot(normed, w_gate, precision=HIGH))
    up_value = low_back(jnp.dot(normed, w_up, precision=HIGH))
    hidden = low(jax.nn.silu(gate_value) * up_value)
    return xf + branch + jnp.dot(hidden, w_down, precision=HIGH)

def reference(tokens, block_order, ln_gain, ln_bias, w_qkv, w_out, w_gate, w_up, w_down, cotangent):
    weights = tuple((w.astype(jnp.float32) for w in (ln_gain, ln_bias, w_qkv, w_out, w_gate, w_up, w_down)))
    length = tokens.shape[1]
    block_rows = length // N_CTX

    def one_sequence(running, sequence_item):
        sequence, block_ids, grad_out = sequence_item
        positions = (block_ids[:, None] * block_rows + jnp.arange(block_rows, dtype=jnp.int32)[None, :]).reshape(-1)

        def apply_layer(xf, *params):
            return layer_forward(xf, positions, *params)
        result, pullback = jax.vjp(apply_layer, sequence.astype(jnp.float32), *weights)
        gradients = pullback(grad_out.astype(jnp.float32))
        running = tuple((a + b for a, b in zip(running, gradients[1:])))
        return (running, (result.astype(jnp.bfloat16), gradients[0]))
    zero_grads = tuple((jnp.zeros(w.shape, jnp.float32) for w in weights))
    totals, (out, grad_in) = lax.scan(one_sequence, zero_grads, (tokens, block_order, cotangent))
    return (out, grad_in) + tuple(totals)
```

```python
import functools

import jax
import jax.numpy as jnp
from jax import lax
from jax.experimental import pallas as pl
from jax.experimental.pallas import tpu as pltpu
from jax.sharding import PartitionSpec as P

H = 32
HD = 64
ROT = 16
EPS = 1e-05
NEG = -1e30
CHUNK = 256

BF = jnp.bfloat16
F32 = jnp.float32


def xor_send(value, mask):
    count = lax.axis_size("fsdp")
    return lax.ppermute(value, "fsdp", [(i, i ^ mask) for i in range(count)])


def ring_send(value, steps):
    count = lax.axis_size("ctx")
    return lax.ppermute(value, "ctx", [(i, (i + steps) % count) for i in range(count)])


def after(value, *done):
    return lax.optimization_barrier((value,) + done)[0]


def dot(a, b, dims, out=F32):
    return lax.dot_general(a, b, (dims, ((), ())), preferred_element_type=F32).astype(out)


def gather_rows(piece):
    count = lax.axis_size("fsdp")
    chips = count // 2
    me = lax.axis_index("fsdp")
    chip, core = me // 2, me % 2
    parts = [piece] + [xor_send(piece, 2 * m) for m in range(1, chips)]
    others = [xor_send(p, 1) for p in parts]
    whole = jnp.zeros((count,) + piece.shape, piece.dtype)
    for m in range(chips):
        at = 2 * (chip ^ m)
        whole = lax.dynamic_update_index_in_dim(whole, parts[m], at + core, 0)
        whole = lax.dynamic_update_index_in_dim(whole, others[m], at + 1 - core, 0)
    return whole.reshape(count * piece.shape[0], piece.shape[1]), parts[-1]


def scatter_rows(grad):
    count = lax.axis_size("fsdp")
    chips = count // 2
    me = lax.axis_index("fsdp")
    chip, core = me // 2, me % 2
    rows = grad.shape[0] // count
    split = grad.reshape(chips, 2, rows, grad.shape[1])
    theirs = xor_send(lax.dynamic_index_in_dim(split, 1 - core, 1, False), 1)
    pair = lax.dynamic_index_in_dim(split, core, 1, False).astype(F32) + theirs.astype(F32)
    pair = pair.astype(BF)
    total = lax.dynamic_index_in_dim(pair, chip, 0, False).astype(F32)
    for m in range(1, chips):
        part = lax.dynamic_index_in_dim(pair, chip ^ m, 0, False)
        total = total + xor_send(part, 2 * m).astype(F32)
    return total.astype(BF)


def gather_ctx(piece):
    count = lax.axis_size("ctx")
    me = lax.axis_index("ctx")
    whole = jnp.zeros((count,) + piece.shape, piece.dtype)
    whole = lax.dynamic_update_index_in_dim(whole, piece, me, 0)
    for k in range(1, count):
        part = ring_send(piece, k)
        whole = lax.dynamic_update_index_in_dim(whole, part, (me - k) % count, 0)
    return whole


def line_scatter(blocks):
    count = lax.axis_size("ctx")
    me = lax.axis_index("ctx")
    down = up = None
    for t in range(1, count):
        to_down = blocks(jnp.clip(t + me - count, 0, count - 1))
        to_up = blocks(jnp.clip(count - 1 - (t + (count - 1 - me) - count), 0, count - 1))
        if down is not None:
            to_down = to_down + down.astype(F32)
            to_up = to_up + up.astype(F32)
        pairs = [(i, i - 1) for i in range(count - t, count)]
        down = lax.ppermute(to_down.astype(BF), "ctx", pairs)
        up = lax.ppermute(to_up.astype(BF), "ctx", [(count - 1 - i, count - 1 - j) for i, j in pairs])
    return blocks(me) + down.astype(F32) + up.astype(F32)


def turn(x, cos, first, second):
    width = x.shape[1]
    half = ROT // 2
    return x * cos + pltpu.roll(x, width - half, 1) * first + pltpu.roll(x, half, 1) * second


def contract(a, b, dims):
    return lax.dot_general(a, b, (dims, ((), ())), preferred_element_type=F32)


def attend_kernel(mq, mk, mv, cos, first, second, q_out, k_out, v_out, att_out, lse_out):
    length = mq.shape[0]
    scale = HD ** (-0.5)
    q_out[...] = (turn(mq[...], cos[...], first[...], second[...]).astype(BF).astype(F32) * scale).astype(BF)
    k_out[...] = turn(mk[...], cos[...], first[...], second[...]).astype(BF)
    v_out[...] = mv[...].astype(BF)
    row = lax.broadcasted_iota(jnp.int32, (CHUNK, CHUNK), 0)
    col = lax.broadcasted_iota(jnp.int32, (CHUNK, CHUNK), 1)
    for c in range(length // CHUNK):
        lo, hi = c * CHUNK, (c + 1) * CHUNK
        for h in range(2):
            lanes = slice(h * HD, (h + 1) * HD)
            q = q_out[lo:hi, lanes]
            s = contract(q, k_out[lo:hi, lanes], ((1,), (1,)))
            s = jnp.where(col <= row, s, NEG)
            if c:
                s = jnp.concatenate([contract(q, k_out[:lo, lanes], ((1,), (1,))), s], axis=1)
            top = jnp.max(s, axis=1, keepdims=True)
            p = jnp.exp(s - top)
            total = jnp.sum(p, axis=1, keepdims=True)
            o = contract(p.astype(BF), v_out[:hi, lanes], ((1,), (0,)))
            att_out[lo:hi, lanes] = o / total
            lse_out[lo:hi, lanes] = jnp.broadcast_to(top + jnp.log(total), (CHUNK, HD))


def attend(mixed, tables, heads):
    length = mixed.shape[0]
    pairs = heads // 2
    block = lambda at: pl.BlockSpec((length, 2 * HD), lambda h, at=at: (0, at + h))
    table = pl.BlockSpec((length, 2 * HD), lambda h: (0, 0))
    width = heads * HD
    return pl.pallas_call(
        attend_kernel,
        grid=(pairs,),
        in_specs=[block(0), block(pairs), block(2 * pairs), table, table, table],
        out_specs=[block(0)] * 5,
        out_shape=[jax.ShapeDtypeStruct((length, width), BF)] * 3
        + [jax.ShapeDtypeStruct((length, width), F32)] * 2,
        compiler_params=pltpu.CompilerParams(vmem_limit_bytes=40 * 2**20),
        cost_estimate=pl.CostEstimate(
            flops=16 * heads * length * length * HD // 2,
            bytes_accessed=26 * length * width,
            transcendentals=heads * length * length // 2,
        ),
        name="attend",
    )(mixed, mixed, mixed, *tables)


def attend_back_kernel(q_in, k_in, v_in, do_in, att, lse, cos, first, second, dq_out, dk_out, dv_out, dk, dv):
    length = q_in.shape[0]
    scale = HD ** (-0.5)
    row = lax.broadcasted_iota(jnp.int32, (CHUNK, CHUNK), 0)
    col = lax.broadcasted_iota(jnp.int32, (CHUNK, CHUNK), 1)
    dk[...] = jnp.zeros_like(dk)
    dv[...] = jnp.zeros_like(dv)
    for c in range(length // CHUNK):
        lo, hi = c * CHUNK, (c + 1) * CHUNK
        dqs = []
        for h in range(2):
            lanes = slice(h * HD, (h + 1) * HD)
            q, do = q_in[lo:hi, lanes], do_in[lo:hi, lanes]
            delta = jnp.sum(do.astype(F32) * att[lo:hi, lanes], axis=1, keepdims=True)
            s = contract(q, k_in[lo:hi, lanes], ((1,), (1,)))
            s = jnp.where(col <= row, s, NEG)
            if c:
                s = jnp.concatenate([contract(q, k_in[:lo, lanes], ((1,), (1,))), s], axis=1)
            p = jnp.exp(s - lse[lo:hi, h * HD : h * HD + 1])
            dp = contract(do, v_in[:hi, lanes], ((1,), (1,)))
            ds = (p * (dp - delta)).astype(BF)
            dqs.append(contract(ds, k_in[:hi, lanes], ((1,), (0,))) * scale)
            dk[:hi, lanes] += contract(ds, q, ((0,), (0,)))
            dv[:hi, lanes] += contract(p.astype(BF), do, ((0,), (0,)))
        dq = jnp.concatenate(dqs, axis=1)
        dq_out[lo:hi, :] = turn(dq, cos[lo:hi, :], -first[lo:hi, :], -second[lo:hi, :]).astype(BF)
    dk_out[...] = turn(dk[...], cos[...], -first[...], -second[...]).astype(BF)
    dv_out[...] = dv[...].astype(BF)


def attend_back(q, k, v, d_attended, attended, lse, tables, heads):
    length, width = q.shape
    block = pl.BlockSpec((length, 2 * HD), lambda h: (0, h))
    table = pl.BlockSpec((length, 2 * HD), lambda h: (0, 0))
    return pl.pallas_call(
        attend_back_kernel,
        grid=(heads // 2,),
        in_specs=[block] * 6 + [table] * 3,
        out_specs=[block] * 3,
        out_shape=[jax.ShapeDtypeStruct((length, width), BF)] * 3,
        scratch_shapes=[pltpu.VMEM((length, 2 * HD), F32)] * 2,
        compiler_params=pltpu.CompilerParams(vmem_limit_bytes=40 * 2**20),
        cost_estimate=pl.CostEstimate(
            flops=40 * heads * length * length * HD // 2,
            bytes_accessed=22 * length * width,
            transcendentals=heads * length * length // 2,
        ),
        name="attend_back",
    )(q, k, v, d_attended, attended, lse, *tables)


def rotation_tables(length):
    half = ROT // 2
    inverse = 10000.0 ** (-jnp.arange(half, dtype=F32) / half)
    grid = jnp.arange(length, dtype=jnp.int32).astype(F32)[:, None] * inverse[None, :]
    cos, sin = jnp.cos(grid), jnp.sin(grid)
    zero = jnp.zeros((length, half), F32)
    rest = jnp.zeros((length, HD - ROT), F32)
    tables = (
        jnp.concatenate([cos, cos, rest + 1.0], axis=1),
        jnp.concatenate([-sin, zero, rest], axis=1),
        jnp.concatenate([zero, sin, rest], axis=1),
    )
    return tuple(jnp.tile(t, (1, 2)) for t in tables)


def body(tokens, block_order, ln_gain, ln_bias, w_qkv, w_out, w_gate, w_up, w_down, cotangent):
    rows, width = tokens.shape[1], tokens.shape[2]
    count = lax.axis_size("ctx")
    shards = lax.axis_size("fsdp")
    place = lax.axis_index("ctx")
    length = rows * count
    order = block_order[0]
    shard_rows = w_qkv.shape[0]
    ff_shard = w_down.shape[0]
    ff_part = ff_shard // count
    own_heads = H // count
    spread = (w_out.shape[0] // HD) % count == 0
    groups = shards if spread else 1
    head_cols = own_heads * HD // groups

    def my_cols(w, outer, group, part):
        w = w.reshape(w.shape[0], outer, group, count, part)
        return lax.dynamic_index_in_dim(w, place, 3, False).reshape(w.shape[0], outer * group * part)

    def all_cols(piece, outer, group, part):
        whole = gather_ctx(piece).reshape(count, piece.shape[0], outer, group, part)
        return whole.transpose(1, 2, 3, 0, 4).reshape(piece.shape[0], -1).astype(F32)

    def assemble(block, ready=None):
        whole = jnp.zeros((length, width), block.dtype)
        whole = lax.dynamic_update_slice_in_dim(whole, block, order[place] * rows, 0)
        last = None
        for k in range(1, count):
            last = ring_send(block, k)
            source = (place - k) % count
            whole = lax.dynamic_update_slice_in_dim(whole, last, order[source] * rows, 0)
        return whole, last

    gain = lax.all_gather(ln_gain, "fsdp", axis=0, tiled=True).astype(F32)
    bias = lax.all_gather(ln_bias, "fsdp", axis=0, tiled=True).astype(F32)
    tables = rotation_tables(length)

    block = tokens[0]
    x_all, arrived = assemble(block)
    grad_block = cotangent[0]
    cot_all, _ = assemble(after(grad_block, arrived))

    inner = jnp.concatenate(
        [my_cols(w_gate, 1, shards, ff_part), my_cols(w_up, 1, shards, ff_part)], axis=1
    )
    w_inner, sent = gather_rows(inner)
    w_heads, sent = gather_rows(after(my_cols(w_qkv, 3, groups, head_cols), sent))
    down = lax.dynamic_slice_in_dim(w_down, place * ff_part, ff_part, 0)
    w_hidden, sent = gather_rows(after(down, sent))
    if spread:
        part = w_out.shape[0] // count
        attn = lax.dynamic_slice_in_dim(w_out, place * part, part, 0)
        w_attn, sent = gather_rows(after(attn, sent))
    else:
        w_attn = lax.all_gather(after(w_out, sent), "fsdp", axis=0, tiled=True)
        w_attn = lax.dynamic_slice_in_dim(w_attn, place * own_heads * HD, own_heads * HD, 0)

    xf = x_all.astype(F32)
    average = jnp.mean(xf, axis=-1, keepdims=True)
    centered = xf - average
    variance = jnp.mean(centered * centered, axis=-1, keepdims=True)
    inv_std = lax.rsqrt(variance + EPS)
    x_hat = centered * inv_std
    normed = (x_hat * gain + bias).astype(BF)

    across = ((1,), (0,))
    over_tokens = ((0,), (0,))
    back = ((1,), (1,))
    ff_cols = shards * ff_part
    gate_value = dot(normed, w_inner[:, :ff_cols], across)
    up_value = dot(normed, w_inner[:, ff_cols:], across)
    sigmoid_gate = jax.nn.sigmoid(gate_value)
    hidden = (gate_value * sigmoid_gate * up_value).astype(BF)
    mixed = dot(normed, w_heads, across)
    q, k, v, attended, lse = attend(mixed, tables, own_heads)
    attended_low = attended.astype(BF)

    branch = dot(attended_low, w_attn, across) + dot(hidden, w_hidden, across)
    out = line_scatter(lambda j: lax.dynamic_slice_in_dim(branch, order[j] * rows, rows, 0))
    out = (block.astype(F32) + out).astype(BF)[None]

    d_hidden = dot(cot_all, w_hidden, back)
    grad_down = scatter_rows(dot(hidden, cot_all, over_tokens, BF))
    d_gate_act = (
        d_hidden * up_value * sigmoid_gate * (1.0 + gate_value * (1.0 - sigmoid_gate))
    ).astype(BF)
    d_up_act = (d_hidden * gate_value * sigmoid_gate).astype(BF)
    d_inner = jnp.concatenate([d_gate_act, d_up_act], axis=1)
    d_attended = dot(cot_all, w_attn, back, BF)
    d_mixed = attend_back(q, k, v, d_attended, attended, lse, tables, own_heads)
    d_mixed = jnp.concatenate(d_mixed, axis=1)
    grad_inner = scatter_rows(dot(normed, d_inner, over_tokens, BF))
    grad_attn = dot(attended_low, cot_all, over_tokens, BF)
    grad_heads = scatter_rows(dot(normed, d_mixed, over_tokens, BF))

    d_normed = dot(d_inner, w_inner, back) + dot(d_mixed, w_heads, back)
    small = jnp.stack([jnp.sum(d_normed * x_hat, axis=0), jnp.sum(d_normed, axis=0)])
    small = lax.psum(small, ("ctx", "fsdp"))
    small = lax.dynamic_slice_in_dim(small, lax.axis_index("fsdp") * shard_rows, shard_rows, 1)
    d_own = line_scatter(lambda j: lax.dynamic_slice_in_dim(d_normed, order[j] * rows, rows, 0))
    own = block.astype(F32)
    own_average = jnp.mean(own, axis=-1, keepdims=True)
    own = own - own_average
    own_std = lax.rsqrt(jnp.mean(own * own, axis=-1, keepdims=True) + EPS)
    own = own * own_std
    scaled = d_own * gain
    d_input = own_std * (
        scaled
        - jnp.mean(scaled, axis=-1, keepdims=True)
        - own * jnp.mean(scaled * own, axis=-1, keepdims=True)
    )
    grad_in = (grad_block.astype(F32) + d_input)[None]

    down_all = gather_ctx(grad_down).reshape(ff_shard, width).astype(F32)
    if spread:
        attn_all = gather_ctx(scatter_rows(grad_attn)).reshape(w_out.shape).astype(F32)
    else:
        full = jnp.zeros((H * HD, width), BF)
        full = lax.dynamic_update_slice_in_dim(full, grad_attn, place * own_heads * HD, 0)
        full = lax.psum_scatter(full, "fsdp", scatter_dimension=0, tiled=True)
        attn_all = lax.psum(full, "ctx").astype(F32)
    heads_all = all_cols(grad_heads, 3, groups, head_cols)
    inner_all = gather_ctx(grad_inner).reshape(count, shard_rows, 2, shards, ff_part)
    inner_all = inner_all.transpose(2, 1, 3, 0, 4).reshape(2, shard_rows, -1).astype(F32)
    return (
        out,
        grad_in,
        small[0],
        small[1],
        heads_all,
        attn_all,
        inner_all[0],
        inner_all[1],
        down_all,
    )


def solution(mesh):
    whole, once = P("fsdp", "ctx", None), P("fsdp", None)
    return jax.shard_map(
        body,
        mesh=mesh,
        in_specs=(whole, once, P("fsdp"), P("fsdp")) + (once,) * 5 + (whole,),
        out_specs=(whole, whole, P("fsdp"), P("fsdp")) + (once,) * 5,
        check_vma=False,
    )
```

```python
import functools

import jax
import jax.numpy as jnp
from jax import lax
from jax.experimental import pallas as pl
from jax.experimental.pallas import tpu as pltpu
from jax.sharding import PartitionSpec as P

H = 32
HD = 64
ROT = 16
EPS = 1e-05
NEG = -1e30
CHUNK = 256

BF = jnp.bfloat16
F32 = jnp.float32


def xor_send(value, mask):
    count = lax.axis_size("fsdp")
    return lax.ppermute(value, "fsdp", [(i, i ^ mask) for i in range(count)])


def ring_send(value, steps):
    count = lax.axis_size("ctx")
    return lax.ppermute(value, "ctx", [(i, (i + steps) % count) for i in range(count)])


def after(value, *done):
    return lax.optimization_barrier((value,) + done)[0]


def dot(a, b, dims, out=F32):
    return lax.dot_general(a, b, (dims, ((), ())), preferred_element_type=F32).astype(out)


def gather_rows(piece):
    count = lax.axis_size("fsdp")
    chips = count // 2
    me = lax.axis_index("fsdp")
    chip, core = me // 2, me % 2
    parts = [piece] + [xor_send(piece, 2 * m) for m in range(1, chips)]
    others = [xor_send(p, 1) for p in parts]
    whole = jnp.zeros((count,) + piece.shape, piece.dtype)
    for m in range(chips):
        at = 2 * (chip ^ m)
        whole = lax.dynamic_update_index_in_dim(whole, parts[m], at + core, 0)
        whole = lax.dynamic_update_index_in_dim(whole, others[m], at + 1 - core, 0)
    return whole.reshape(count * piece.shape[0], piece.shape[1]), parts[-1]


def scatter_rows(grad):
    count = lax.axis_size("fsdp")
    chips = count // 2
    me = lax.axis_index("fsdp")
    chip, core = me // 2, me % 2
    rows = grad.shape[0] // count
    split = grad.reshape(chips, 2, rows, grad.shape[1])
    theirs = xor_send(lax.dynamic_index_in_dim(split, 1 - core, 1, False), 1)
    pair = lax.dynamic_index_in_dim(split, core, 1, False).astype(F32) + theirs.astype(F32)
    pair = pair.astype(BF)
    total = lax.dynamic_index_in_dim(pair, chip, 0, False).astype(F32)
    for m in range(1, chips):
        part = lax.dynamic_index_in_dim(pair, chip ^ m, 0, False)
        total = total + xor_send(part, 2 * m).astype(F32)
    return total.astype(BF)


def gather_ctx(piece):
    count = lax.axis_size("ctx")
    me = lax.axis_index("ctx")
    whole = jnp.zeros((count,) + piece.shape, piece.dtype)
    whole = lax.dynamic_update_index_in_dim(whole, piece, me, 0)
    for k in range(1, count):
        part = ring_send(piece, k)
        whole = lax.dynamic_update_index_in_dim(whole, part, (me - k) % count, 0)
    return whole


def line_scatter(blocks):
    count = lax.axis_size("ctx")
    me = lax.axis_index("ctx")
    down = up = None
    for t in range(1, count):
        to_down = blocks(jnp.clip(t + me - count, 0, count - 1))
        to_up = blocks(jnp.clip(count - 1 - (t + (count - 1 - me) - count), 0, count - 1))
        if down is not None:
            to_down = to_down + down.astype(F32)
            to_up = to_up + up.astype(F32)
        pairs = [(i, i - 1) for i in range(count - t, count)]
        down = lax.ppermute(to_down.astype(BF), "ctx", pairs)
        up = lax.ppermute(to_up.astype(BF), "ctx", [(count - 1 - i, count - 1 - j) for i, j in pairs])
    return blocks(me) + down.astype(F32) + up.astype(F32)


def turn(x, cos, first, second):
    width = x.shape[1]
    half = ROT // 2
    return x * cos + pltpu.roll(x, width - half, 1) * first + pltpu.roll(x, half, 1) * second


def contract(a, b, dims):
    return lax.dot_general(a, b, (dims, ((), ())), preferred_element_type=F32)


def attend_kernel(mq, mk, mv, cos, first, second, q_out, k_out, v_out, att_out, lse_out):
    length = mq.shape[0]
    scale = HD ** (-0.5)
    q_out[...] = (turn(mq[...], cos[...], first[...], second[...]).astype(BF).astype(F32) * scale).astype(BF)
    k_out[...] = turn(mk[...], cos[...], first[...], second[...]).astype(BF)
    v_out[...] = mv[...].astype(BF)
    row = lax.broadcasted_iota(jnp.int32, (CHUNK, CHUNK), 0)
    col = lax.broadcasted_iota(jnp.int32, (CHUNK, CHUNK), 1)
    for c in range(length // CHUNK):
        lo, hi = c * CHUNK, (c + 1) * CHUNK
        for h in range(2):
            lanes = slice(h * HD, (h + 1) * HD)
            q = q_out[lo:hi, lanes]
            s = contract(q, k_out[lo:hi, lanes], ((1,), (1,)))
            s = jnp.where(col <= row, s, NEG)
            if c:
                s = jnp.concatenate([contract(q, k_out[:lo, lanes], ((1,), (1,))), s], axis=1)
            top = jnp.max(s, axis=1, keepdims=True)
            p = jnp.exp(s - top)
            total = jnp.sum(p, axis=1, keepdims=True)
            o = contract(p.astype(BF), v_out[:hi, lanes], ((1,), (0,)))
            att_out[lo:hi, lanes] = o / total
            lse_out[lo:hi, lanes] = jnp.broadcast_to(top + jnp.log(total), (CHUNK, HD))


def attend(mixed, tables, heads):
    length = mixed.shape[0]
    pairs = heads // 2
    block = lambda at: pl.BlockSpec((length, 2 * HD), lambda h, at=at: (0, at + h))
    table = pl.BlockSpec((length, 2 * HD), lambda h: (0, 0))
    width = heads * HD
    return pl.pallas_call(
        attend_kernel,
        grid=(pairs,),
        in_specs=[block(0), block(pairs), block(2 * pairs), table, table, table],
        out_specs=[block(0)] * 5,
        out_shape=[jax.ShapeDtypeStruct((length, width), BF)] * 3
        + [jax.ShapeDtypeStruct((length, width), F32)] * 2,
        compiler_params=pltpu.CompilerParams(vmem_limit_bytes=40 * 2**20),
        cost_estimate=pl.CostEstimate(
            flops=16 * heads * length * length * HD // 2,
            bytes_accessed=26 * length * width,
            transcendentals=heads * length * length // 2,
        ),
        name="attend",
    )(mixed, mixed, mixed, *tables)


def attend_back_kernel(q_in, k_in, v_in, do_in, att, lse, cos, first, second, dq_out, dk_out, dv_out, dk, dv):
    length = q_in.shape[0]
    scale = HD ** (-0.5)
    row = lax.broadcasted_iota(jnp.int32, (CHUNK, CHUNK), 0)
    col = lax.broadcasted_iota(jnp.int32, (CHUNK, CHUNK), 1)
    dk[...] = jnp.zeros_like(dk)
    dv[...] = jnp.zeros_like(dv)
    for c in range(length // CHUNK):
        lo, hi = c * CHUNK, (c + 1) * CHUNK
        dqs = []
        for h in range(2):
            lanes = slice(h * HD, (h + 1) * HD)
            q, do = q_in[lo:hi, lanes], do_in[lo:hi, lanes]
            delta = jnp.sum(do.astype(F32) * att[lo:hi, lanes], axis=1, keepdims=True)
            s = contract(q, k_in[lo:hi, lanes], ((1,), (1,)))
            s = jnp.where(col <= row, s, NEG)
            if c:
                s = jnp.concatenate([contract(q, k_in[:lo, lanes], ((1,), (1,))), s], axis=1)
            p = jnp.exp(s - lse[lo:hi, h * HD : h * HD + 1])
            dp = contract(do, v_in[:hi, lanes], ((1,), (1,)))
            ds = (p * (dp - delta)).astype(BF)
            dqs.append(contract(ds, k_in[:hi, lanes], ((1,), (0,))) * scale)
            dk[:hi, lanes] += contract(ds, q, ((0,), (0,)))
            dv[:hi, lanes] += contract(p.astype(BF), do, ((0,), (0,)))
        dq = jnp.concatenate(dqs, axis=1)
        dq_out[lo:hi, :] = turn(dq, cos[lo:hi, :], -first[lo:hi, :], -second[lo:hi, :]).astype(BF)
    dk_out[...] = turn(dk[...], cos[...], -first[...], -second[...]).astype(BF)
    dv_out[...] = dv[...].astype(BF)


def attend_back(q, k, v, d_attended, attended, lse, tables, heads):
    length, width = q.shape
    block = pl.BlockSpec((length, 2 * HD), lambda h: (0, h))
    table = pl.BlockSpec((length, 2 * HD), lambda h: (0, 0))
    return pl.pallas_call(
        attend_back_kernel,
        grid=(heads // 2,),
        in_specs=[block] * 6 + [table] * 3,
        out_specs=[block] * 3,
        out_shape=[jax.ShapeDtypeStruct((length, width), BF)] * 3,
        scratch_shapes=[pltpu.VMEM((length, 2 * HD), F32)] * 2,
        compiler_params=pltpu.CompilerParams(vmem_limit_bytes=40 * 2**20),
        cost_estimate=pl.CostEstimate(
            flops=40 * heads * length * length * HD // 2,
            bytes_accessed=22 * length * width,
            transcendentals=heads * length * length // 2,
        ),
        name="attend_back",
    )(q, k, v, d_attended, attended, lse, *tables)


MESH = pl.DeviceIdType.MESH
TILE = 256
HALF = 128
DEEP = 4
LAG = 2


def rows_of(shard, part):
    return slice(shard * part, (shard + 1) * part)


def gradients_kernel(
    hid_t, att_t, cot, norm_t, d_gate, d_up, d_mixed, pieces,
    partial, theirs, pair, landed, total,
    core_send, core_recv, chip_send, chip_recv, line_send, line_recv, own_sem,
):
    count = pieces.shape[0]
    chunks = pieces.shape[1]
    shards = 2 * partial.shape[1]
    chips = shards // 2
    place, me = lax.axis_index("ctx"), lax.axis_index("fsdp")
    chip, core = me // 2, me % 2
    ff_part, attn_part = hid_t.shape[0] // shards, att_t.shape[0] // shards
    cot_chunks = cot.shape[1] // TILE
    inner_chunks = d_gate.shape[1] // HALF

    def core_copy(i):
        return pltpu.make_async_remote_copy(
            src_ref=partial.at[i % 2, :, 1 - core],
            dst_ref=theirs.at[i % DEEP],
            send_sem=core_send.at[i % 2],
            recv_sem=core_recv.at[i % DEEP],
            device_id=(place, me + 1 - 2 * core),
            device_id_type=MESH,
        )

    def chip_of(m):
        low = (chip % 2 + m % 2) % 2
        high = (chip // 2 + m // 2) % 2
        return 2 * high + low

    def chip_copy(j, m):
        return pltpu.make_async_remote_copy(
            src_ref=pair.at[j % 2, chip_of(m)],
            dst_ref=landed.at[j % DEEP, m - 1],
            send_sem=chip_send.at[j % 2, m - 1],
            recv_sem=chip_recv.at[j % DEEP, m - 1],
            device_id=(place, 2 * chip_of(m) + core),
            device_id_type=MESH,
        )

    def line_copy(way, hop, k):
        ahead = 1 - 2 * way
        origin = place - (hop - 1) * ahead
        return pltpu.make_async_remote_copy(
            src_ref=total.at[k % DEEP] if hop == 1 else pieces.at[origin, k],
            dst_ref=pieces.at[origin, k],
            send_sem=line_send.at[way, hop - 1, k % DEEP],
            recv_sem=line_recv.at[way, k, hop - 1],
            device_id=(place + ahead, me),
            device_id_type=MESH,
        )

    def sends(way, hop):
        if way == 0:
            return (place >= hop - 1) & (place <= count - 2)
        return (place <= count - hop) & (place >= 1)

    def lands(way, hop):
        return place >= hop if way == 0 else place <= count - 1 - hop

    def forward(hop, k):
        for way in range(2):
            if hop > 1:
                @pl.when(lands(way, hop - 1))
                def _():
                    line_copy(way, hop - 1, k).wait_recv()

            if hop < count:
                @pl.when(sends(way, hop))
                def _():
                    @pl.when(k >= DEEP)
                    def _():
                        line_copy(way, hop, k - DEEP).wait_send()

                    line_copy(way, hop, k).start()

    def own_copy(k):
        return pltpu.make_async_copy(total.at[k % DEEP], pieces.at[place, k], own_sem.at[k % DEEP])

    partners = [(place, me + 1 - 2 * core)]
    partners += [(place, 2 * chip_of(m) + core) for m in range(1, chips)]
    partners += [((place + 1) % count, me), ((place + count - 1) % count, me)]
    barrier = pltpu.get_barrier_semaphore()
    for partner in partners:
        pl.semaphore_signal(barrier, inc=1, device_id=partner, device_id_type=MESH)
    pl.semaphore_wait(barrier, len(partners))
    def store(i, shard, lo, value):
        partial[i % 2, shard // 2, shard % 2, lo : lo + value.shape[0], :] = value

    def from_norm(i, rhs):
        for s in range(0, shards, 2):
            rows = norm_t.shape[0] // shards
            value = contract(norm_t[s * rows : (s + 2) * rows, :], rhs, ((1,), (0,))).astype(BF)
            store(i, s, 0, value[:rows])
            store(i, s + 1, 0, value[rows:])

    def step(i, carry):
        @pl.when(i < cot_chunks)
        def _():
            rhs = cot[:, pl.ds(pl.multiple_of(i * TILE, TILE), TILE)]
            for s in range(0, shards, 4):
                value = contract(hid_t[s * ff_part : (s + 4) * ff_part, :], rhs, ((1,), (0,))).astype(BF)
                for t in range(4):
                    store(i, s + t, 0, value[rows_of(t, ff_part)])
            value = contract(att_t[...], rhs, ((1,), (0,))).astype(BF)
            for s in range(shards):
                store(i, s, ff_part, value[rows_of(s, attn_part)])

        @pl.when((i >= cot_chunks) & (i < cot_chunks + inner_chunks))
        def _():
            at = pl.ds(pl.multiple_of((i - cot_chunks) * HALF, HALF), HALF)
            from_norm(i, jnp.concatenate([d_gate[:, at], d_up[:, at]], axis=1))

        @pl.when((i >= cot_chunks + inner_chunks) & (i < chunks))
        def _():
            at = pl.multiple_of((i - cot_chunks - inner_chunks) * TILE, TILE)
            from_norm(i, d_mixed[:, pl.ds(at, TILE)])

        @pl.when(i < chunks)
        def _():
            core_copy(i).start()

        @pl.when((i >= 1) & (i < chunks + 1))
        def _():
            j = i - 1
            core_copy(j).wait()
            for m in range(chips):
                a = partial[j % 2, m, core].astype(F32) + theirs[j % DEEP, m].astype(F32)
                pair[j % 2, m] = a.astype(BF)
            for m in range(1, chips):
                chip_copy(j, m).start()

        @pl.when((i >= 2) & (i < chunks + 2))
        def _():
            k = i - 2
            for m in range(1, chips):
                chip_copy(k, m).wait()

            a = pair[k % 2, chip].astype(F32)
            for m in range(1, chips):
                a = a + landed[k % DEEP, m - 1].astype(F32)
            for way in range(2):
                @pl.when(sends(way, 1) & (k >= DEEP))
                def _():
                    line_copy(way, 1, k - DEEP).wait_send()

            @pl.when(k >= DEEP)
            def _():
                own_copy(k - DEEP).wait()

            total[k % DEEP] = a.astype(BF)
            for way in range(2):
                @pl.when(sends(way, 1))
                def _():
                    line_copy(way, 1, k).start()

            own_copy(k).start()

        for hop in range(2, count + 1):
            k = i - 2 - LAG * (hop - 1)

            @pl.when((k >= 0) & (k < chunks))
            def _(k=k, hop=hop):
                forward(hop, k)

        return carry

    lax.fori_loop(0, chunks + 2 + LAG * (count - 1), step, 0)

    def drain(k, carry):
        own_copy(k).wait()
        for way in range(2):
            for hop in range(1, count):
                @pl.when(sends(way, hop))
                def _():
                    line_copy(way, hop, k).wait_send()
        return carry

    lax.fori_loop(chunks - DEEP, chunks, drain, 0)


def gradients(hid_t, att_t, cot, norm_t, d_gate, d_up, d_mixed, count, shards):
    chips = shards // 2
    chunks = cot.shape[1] // TILE + d_gate.shape[1] // HALF + d_mixed.shape[1] // TILE
    rows = norm_t.shape[0] // shards
    vmem = pl.BlockSpec(memory_space=pltpu.VMEM)
    dma = pltpu.SemaphoreType.DMA
    return pl.pallas_call(
        gradients_kernel,
        out_shape=jax.ShapeDtypeStruct((count, chunks, rows, TILE), BF),
        in_specs=[vmem] * 7,
        out_specs=pl.BlockSpec(memory_space=pl.ANY),
        scratch_shapes=[
            pltpu.VMEM((2, chips, 2, rows, TILE), BF),
            pltpu.VMEM((DEEP, chips, rows, TILE), BF),
            pltpu.VMEM((2, chips, rows, TILE), BF),
            pltpu.VMEM((DEEP, chips - 1, rows, TILE), BF),
            pltpu.VMEM((DEEP, rows, TILE), BF),
            dma((2,)),
            dma((DEEP,)),
            dma((2, chips - 1)),
            dma((DEEP, chips - 1)),
            dma((2, count - 1, DEEP)),
            dma((2, chunks, count - 1)),
            dma((DEEP,)),
        ],
        compiler_params=pltpu.CompilerParams(
            collective_id=1, has_side_effects=True, vmem_limit_bytes=50 * 2**20
        ),
        cost_estimate=pl.CostEstimate(
            flops=2 * 2048 * 1024 * TILE * chunks, bytes_accessed=50 * 2**20, transcendentals=0
        ),
        name="gradients",
    )(hid_t, att_t, cot, norm_t, d_gate, d_up, d_mixed)


def column_runs(columns, source):
    out = []
    for block in range(columns // HALF):
        first = 0
        while first < HALF:
            key, lane = source(block * HALF + first)
            last = first + 1
            while last < HALF and source(block * HALF + last) == (key, lane + last - first):
                last += 1
            out.append((block, first, last, key, (first - lane) % HALF))
            first = last
    return out


def assemble_kernel(down_chunks, rows_in, cols_in, qkv_out, gate_out, up_out, down_out, attn_out):
    count, chunks, rows, _ = rows_in.shape
    cot_chunks_static = down_chunks
    ff = gate_out.shape[1]
    width = qkv_out.shape[1]
    ff_part = down_out.shape[0] // count
    attn_part = attn_out.shape[0] // count
    shards = ff // (count * ff_part)
    inner_chunks = ff // count // HALF
    lane = lax.broadcasted_iota(jnp.int32, (rows, HALF), 1)

    def gather(out, runs, load):
        for block, first, last, key, shift in runs:
            value = load(key).astype(F32)
            if shift:
                value = pltpu.roll(value, shift, 1)
            if first:
                value = jnp.where(lane >= first, value, held)
            held = value
            if last == HALF:
                out[:, block * HALF : (block + 1) * HALF] = value

    def inner_source(column):
        shard, rest = divmod(column, count * ff_part)
        unit = shard * ff_part + rest % ff_part
        return (rest // ff_part, unit // HALF), unit % HALF

    def head_source(column):
        part, rest = divmod(column, width // 3)
        head, dim = divmod(rest, HD)
        per = width // 3 // HD // shards // count
        shard, at = divmod(head, per * count)
        place, sub = divmod(at, per)
        local = part * (width // 3 // count) + (shard * per + sub) * HD + dim
        return (place, local // HALF), local % HALF

    runs = column_runs(ff, inner_source)
    gather(gate_out, runs, lambda key: rows_in[key[0], cot_chunks_static + key[1], :, :HALF])
    gather(up_out, runs, lambda key: rows_in[key[0], cot_chunks_static + key[1], :, HALF:])
    first_head = cot_chunks_static + inner_chunks

    def head_load(key):
        at = key[1] % 2 * HALF
        return rows_in[key[0], first_head + key[1] // 2, :, at : at + HALF]

    gather(qkv_out, column_runs(width, head_source), head_load)
    for p in range(count):
        down_out[p * ff_part : (p + 1) * ff_part, :] = cols_in[p, 0, :ff_part, :].astype(F32)
        attn_out[p * attn_part : (p + 1) * attn_part, :] = cols_in[
            p, 0, ff_part : ff_part + attn_part, :
        ].astype(F32)


def assemble_outputs(pieces, qkv, attn, gate, down):
    count, chunks, rows, _ = pieces.shape
    steps = down[1] // TILE
    part = rows // steps
    by_rows = lambda shape: pl.BlockSpec((part, shape[1]), lambda i: (i, 0))
    by_cols = lambda shape: pl.BlockSpec((shape[0], TILE), lambda i: (0, i))
    return pl.pallas_call(
        functools.partial(assemble_kernel, steps),
        grid=(steps,),
        in_specs=[
            pl.BlockSpec((count, chunks, part, TILE), lambda i: (0, 0, i, 0)),
            pl.BlockSpec((count, 1, rows, TILE), lambda i: (0, i, 0, 0)),
        ],
        out_specs=[by_rows(qkv), by_rows(gate), by_rows(gate), by_cols(down), by_cols(attn)],
        out_shape=[jax.ShapeDtypeStruct(s, F32) for s in (qkv, gate, gate, down, attn)],
        compiler_params=pltpu.CompilerParams(vmem_limit_bytes=40 * 2**20),
        name="assemble",
    )(pieces, pieces)


def rotation_tables(length):
    half = ROT // 2
    inverse = 10000.0 ** (-jnp.arange(half, dtype=F32) / half)
    grid = jnp.arange(length, dtype=jnp.int32).astype(F32)[:, None] * inverse[None, :]
    cos, sin = jnp.cos(grid), jnp.sin(grid)
    zero = jnp.zeros((length, half), F32)
    rest = jnp.zeros((length, HD - ROT), F32)
    tables = (
        jnp.concatenate([cos, cos, rest + 1.0], axis=1),
        jnp.concatenate([-sin, zero, rest], axis=1),
        jnp.concatenate([zero, sin, rest], axis=1),
    )
    return tuple(jnp.tile(t, (1, 2)) for t in tables)


def body(tokens, block_order, ln_gain, ln_bias, w_qkv, w_out, w_gate, w_up, w_down, cotangent):
    rows, width = tokens.shape[1], tokens.shape[2]
    count = lax.axis_size("ctx")
    shards = lax.axis_size("fsdp")
    place = lax.axis_index("ctx")
    length = rows * count
    order = block_order[0]
    shard_rows = w_qkv.shape[0]
    ff_shard = w_down.shape[0]
    ff_part = ff_shard // count
    own_heads = H // count
    spread = (w_out.shape[0] // HD) % count == 0
    groups = shards if spread else 1
    head_cols = own_heads * HD // groups
    fast = spread and shards == 8 and ff_part % 16 == 0 and (shards * ff_part) % HALF == 0

    def my_cols(w, outer, group, part):
        w = w.reshape(w.shape[0], outer, group, count, part)
        return lax.dynamic_index_in_dim(w, place, 3, False).reshape(w.shape[0], outer * group * part)

    def all_cols(piece, outer, group, part):
        whole = gather_ctx(piece).reshape(count, piece.shape[0], outer, group, part)
        return whole.transpose(1, 2, 3, 0, 4).reshape(piece.shape[0], -1).astype(F32)

    def assemble(block, ready=None):
        whole = jnp.zeros((length, width), block.dtype)
        whole = lax.dynamic_update_slice_in_dim(whole, block, order[place] * rows, 0)
        last = None
        for k in range(1, count):
            last = ring_send(block, k)
            source = (place - k) % count
            whole = lax.dynamic_update_slice_in_dim(whole, last, order[source] * rows, 0)
        return whole, last

    gain = lax.all_gather(ln_gain, "fsdp", axis=0, tiled=True).astype(F32)
    bias = lax.all_gather(ln_bias, "fsdp", axis=0, tiled=True).astype(F32)
    tables = rotation_tables(length)

    block = tokens[0]
    x_all, arrived = assemble(block)
    grad_block = cotangent[0]
    cot_all, _ = assemble(after(grad_block, arrived))

    inner = jnp.concatenate(
        [my_cols(w_gate, 1, shards, ff_part), my_cols(w_up, 1, shards, ff_part)], axis=1
    )
    w_inner, sent = gather_rows(inner)
    w_heads, sent = gather_rows(after(my_cols(w_qkv, 3, groups, head_cols), sent))
    down = lax.dynamic_slice_in_dim(w_down, place * ff_part, ff_part, 0)
    w_hidden, sent = gather_rows(after(down, sent))
    if spread:
        part = w_out.shape[0] // count
        attn = lax.dynamic_slice_in_dim(w_out, place * part, part, 0)
        w_attn, sent = gather_rows(after(attn, sent))
    else:
        w_attn = lax.all_gather(after(w_out, sent), "fsdp", axis=0, tiled=True)
        w_attn = lax.dynamic_slice_in_dim(w_attn, place * own_heads * HD, own_heads * HD, 0)

    xf = x_all.astype(F32)
    average = jnp.mean(xf, axis=-1, keepdims=True)
    centered = xf - average
    variance = jnp.mean(centered * centered, axis=-1, keepdims=True)
    inv_std = lax.rsqrt(variance + EPS)
    x_hat = centered * inv_std
    normed = (x_hat * gain + bias).astype(BF)

    across = ((1,), (0,))
    over_tokens = ((0,), (0,))
    back = ((1,), (1,))
    ff_cols = shards * ff_part
    gate_value = dot(normed, w_inner[:, :ff_cols], across)
    up_value = dot(normed, w_inner[:, ff_cols:], across)
    sigmoid_gate = jax.nn.sigmoid(gate_value)
    hidden = (gate_value * sigmoid_gate * up_value).astype(BF)
    mixed = dot(normed, w_heads, across)
    q, k, v, attended, lse = attend(mixed, tables, own_heads)
    attended_low = attended.astype(BF)

    branch = dot(attended_low, w_attn, across) + dot(hidden, w_hidden, across)
    out = line_scatter(lambda j: lax.dynamic_slice_in_dim(branch, order[j] * rows, rows, 0))
    out = (block.astype(F32) + out).astype(BF)[None]

    d_hidden = dot(cot_all, w_hidden, back)
    d_gate_act = (
        d_hidden * up_value * sigmoid_gate * (1.0 + gate_value * (1.0 - sigmoid_gate))
    ).astype(BF)
    d_up_act = (d_hidden * gate_value * sigmoid_gate).astype(BF)
    d_inner = jnp.concatenate([d_gate_act, d_up_act], axis=1)
    d_attended = dot(cot_all, w_attn, back, BF)
    d_mixed = attend_back(q, k, v, d_attended, attended, lse, tables, own_heads)
    d_mixed = jnp.concatenate(d_mixed, axis=1)

    d_normed = dot(d_inner, w_inner, back) + dot(d_mixed, w_heads, back)
    small = jnp.stack([jnp.sum(d_normed * x_hat, axis=0), jnp.sum(d_normed, axis=0)])
    small = lax.psum(small, ("ctx", "fsdp"))
    small = lax.dynamic_slice_in_dim(small, lax.axis_index("fsdp") * shard_rows, shard_rows, 1)
    d_own = line_scatter(lambda j: lax.dynamic_slice_in_dim(d_normed, order[j] * rows, rows, 0))
    own = block.astype(F32)
    own_average = jnp.mean(own, axis=-1, keepdims=True)
    own = own - own_average
    own_std = lax.rsqrt(jnp.mean(own * own, axis=-1, keepdims=True) + EPS)
    own = own * own_std
    scaled = d_own * gain
    d_input = own_std * (
        scaled
        - jnp.mean(scaled, axis=-1, keepdims=True)
        - own * jnp.mean(scaled * own, axis=-1, keepdims=True)
    )
    grad_in = (grad_block.astype(F32) + d_input)[None]

    if fast:
        pieces = gradients(
            hidden.T, attended_low.T, cot_all, normed.T, d_gate_act, d_up_act, d_mixed, count, shards
        )
        heads_all, gate_all, up_all, down_all, attn_all = assemble_outputs(
            pieces, w_qkv.shape, w_out.shape, w_gate.shape, w_down.shape
        )
        return out, grad_in, small[0], small[1], heads_all, attn_all, gate_all, up_all, down_all
    grad_down = scatter_rows(dot(hidden, cot_all, over_tokens, BF))
    grad_inner = scatter_rows(dot(normed, d_inner, over_tokens, BF))
    grad_attn = dot(attended_low, cot_all, over_tokens, BF)
    grad_heads = scatter_rows(dot(normed, d_mixed, over_tokens, BF))
    down_all = gather_ctx(grad_down).reshape(ff_shard, width).astype(F32)
    if spread:
        attn_all = gather_ctx(scatter_rows(grad_attn)).reshape(w_out.shape).astype(F32)
    else:
        full = jnp.zeros((H * HD, width), BF)
        full = lax.dynamic_update_slice_in_dim(full, grad_attn, place * own_heads * HD, 0)
        full = lax.psum_scatter(full, "fsdp", scatter_dimension=0, tiled=True)
        attn_all = lax.psum(full, "ctx").astype(F32)
    heads_all = all_cols(grad_heads, 3, groups, head_cols)
    inner_all = gather_ctx(grad_inner).reshape(count, shard_rows, 2, shards, ff_part)
    inner_all = inner_all.transpose(2, 1, 3, 0, 4).reshape(2, shard_rows, -1).astype(F32)
    return (
        out,
        grad_in,
        small[0],
        small[1],
        heads_all,
        attn_all,
        inner_all[0],
        inner_all[1],
        down_all,
    )


def solution(mesh):
    whole, once = P("fsdp", "ctx", None), P("fsdp", None)
    return jax.shard_map(
        body,
        mesh=mesh,
        in_specs=(whole, once, P("fsdp"), P("fsdp")) + (once,) * 5 + (whole,),
        out_specs=(whole, whole, P("fsdp"), P("fsdp")) + (once,) * 5,
        check_vma=False,
    )
```

```python
import functools

import jax
import jax.numpy as jnp
from jax import lax
from jax.experimental import pallas as pl
from jax.experimental.pallas import tpu as pltpu
from jax.sharding import PartitionSpec as P

H = 32
HD = 64
ROT = 16
EPS = 1e-05
NEG = -1e30
CHUNK = 256

BF = jnp.bfloat16
F32 = jnp.float32


def xor_send(value, mask):
    count = lax.axis_size("fsdp")
    return lax.ppermute(value, "fsdp", [(i, i ^ mask) for i in range(count)])


def ring_send(value, steps):
    count = lax.axis_size("ctx")
    return lax.ppermute(value, "ctx", [(i, (i + steps) % count) for i in range(count)])


def after(value, *done):
    return lax.optimization_barrier((value,) + done)[0]


def dot(a, b, dims, out=F32):
    return lax.dot_general(a, b, (dims, ((), ())), preferred_element_type=F32).astype(out)


def gather_rows(piece):
    count = lax.axis_size("fsdp")
    chips = count // 2
    me = lax.axis_index("fsdp")
    chip, core = me // 2, me % 2
    parts = [piece] + [xor_send(piece, 2 * m) for m in range(1, chips)]
    others = [xor_send(p, 1) for p in parts]
    whole = jnp.zeros((count,) + piece.shape, piece.dtype)
    for m in range(chips):
        at = 2 * (chip ^ m)
        whole = lax.dynamic_update_index_in_dim(whole, parts[m], at + core, 0)
        whole = lax.dynamic_update_index_in_dim(whole, others[m], at + 1 - core, 0)
    return whole.reshape(count * piece.shape[0], piece.shape[1]), parts[-1]


def scatter_rows(grad):
    count = lax.axis_size("fsdp")
    chips = count // 2
    me = lax.axis_index("fsdp")
    chip, core = me // 2, me % 2
    rows = grad.shape[0] // count
    split = grad.reshape(chips, 2, rows, grad.shape[1])
    theirs = xor_send(lax.dynamic_index_in_dim(split, 1 - core, 1, False), 1)
    pair = lax.dynamic_index_in_dim(split, core, 1, False).astype(F32) + theirs.astype(F32)
    pair = pair.astype(BF)
    total = lax.dynamic_index_in_dim(pair, chip, 0, False).astype(F32)
    for m in range(1, chips):
        part = lax.dynamic_index_in_dim(pair, chip ^ m, 0, False)
        total = total + xor_send(part, 2 * m).astype(F32)
    return total.astype(BF)


def gather_ctx(piece):
    count = lax.axis_size("ctx")
    me = lax.axis_index("ctx")
    whole = jnp.zeros((count,) + piece.shape, piece.dtype)
    whole = lax.dynamic_update_index_in_dim(whole, piece, me, 0)
    for k in range(1, count):
        part = ring_send(piece, k)
        whole = lax.dynamic_update_index_in_dim(whole, part, (me - k) % count, 0)
    return whole


def line_scatter(blocks):
    count = lax.axis_size("ctx")
    me = lax.axis_index("ctx")
    down = up = None
    for t in range(1, count):
        to_down = blocks(jnp.clip(t + me - count, 0, count - 1))
        to_up = blocks(jnp.clip(count - 1 - (t + (count - 1 - me) - count), 0, count - 1))
        if down is not None:
            to_down = to_down + down.astype(F32)
            to_up = to_up + up.astype(F32)
        pairs = [(i, i - 1) for i in range(count - t, count)]
        down = lax.ppermute(to_down.astype(BF), "ctx", pairs)
        up = lax.ppermute(to_up.astype(BF), "ctx", [(count - 1 - i, count - 1 - j) for i, j in pairs])
    return blocks(me) + down.astype(F32) + up.astype(F32)


def turn(x, cos, first, second):
    width = x.shape[1]
    half = ROT // 2
    return x * cos + pltpu.roll(x, width - half, 1) * first + pltpu.roll(x, half, 1) * second


def contract(a, b, dims):
    return lax.dot_general(a, b, (dims, ((), ())), preferred_element_type=F32)


def attend_kernel(mq, mk, mv, cos, first, second, q_out, k_out, v_out, att_out, lse_out):
    length = mq.shape[0]
    scale = HD ** (-0.5)
    q_out[...] = (turn(mq[...], cos[...], first[...], second[...]).astype(BF).astype(F32) * scale).astype(BF)
    k_out[...] = turn(mk[...], cos[...], first[...], second[...]).astype(BF)
    v_out[...] = mv[...].astype(BF)
    row = lax.broadcasted_iota(jnp.int32, (CHUNK, CHUNK), 0)
    col = lax.broadcasted_iota(jnp.int32, (CHUNK, CHUNK), 1)
    for c in range(length // CHUNK):
        lo, hi = c * CHUNK, (c + 1) * CHUNK
        for h in range(2):
            lanes = slice(h * HD, (h + 1) * HD)
            q = q_out[lo:hi, lanes]
            s = contract(q, k_out[lo:hi, lanes], ((1,), (1,)))
            s = jnp.where(col <= row, s, NEG)
            if c:
                s = jnp.concatenate([contract(q, k_out[:lo, lanes], ((1,), (1,))), s], axis=1)
            top = jnp.max(s, axis=1, keepdims=True)
            p = jnp.exp(s - top)
            total = jnp.sum(p, axis=1, keepdims=True)
            o = contract(p.astype(BF), v_out[:hi, lanes], ((1,), (0,)))
            att_out[lo:hi, lanes] = o / total
            lse_out[lo:hi, lanes] = jnp.broadcast_to(top + jnp.log(total), (CHUNK, HD))


def attend(mixed, tables, heads):
    length = mixed.shape[0]
    pairs = heads // 2
    block = lambda at: pl.BlockSpec((length, 2 * HD), lambda h, at=at: (0, at + h))
    table = pl.BlockSpec((length, 2 * HD), lambda h: (0, 0))
    width = heads * HD
    return pl.pallas_call(
        attend_kernel,
        grid=(pairs,),
        in_specs=[block(0), block(pairs), block(2 * pairs), table, table, table],
        out_specs=[block(0)] * 5,
        out_shape=[jax.ShapeDtypeStruct((length, width), BF)] * 3
        + [jax.ShapeDtypeStruct((length, width), F32)] * 2,
        compiler_params=pltpu.CompilerParams(vmem_limit_bytes=40 * 2**20),
        cost_estimate=pl.CostEstimate(
            flops=16 * heads * length * length * HD // 2,
            bytes_accessed=26 * length * width,
            transcendentals=heads * length * length // 2,
        ),
        name="attend",
    )(mixed, mixed, mixed, *tables)


def attend_back_kernel(q_in, k_in, v_in, do_in, att, lse, cos, first, second, dq_out, dk_out, dv_out, dk, dv):
    length = q_in.shape[0]
    scale = HD ** (-0.5)
    row = lax.broadcasted_iota(jnp.int32, (CHUNK, CHUNK), 0)
    col = lax.broadcasted_iota(jnp.int32, (CHUNK, CHUNK), 1)
    dk[...] = jnp.zeros_like(dk)
    dv[...] = jnp.zeros_like(dv)
    for c in range(length // CHUNK):
        lo, hi = c * CHUNK, (c + 1) * CHUNK
        dqs = []
        for h in range(2):
            lanes = slice(h * HD, (h + 1) * HD)
            q, do = q_in[lo:hi, lanes], do_in[lo:hi, lanes]
            delta = jnp.sum(do.astype(F32) * att[lo:hi, lanes], axis=1, keepdims=True)
            s = contract(q, k_in[lo:hi, lanes], ((1,), (1,)))
            s = jnp.where(col <= row, s, NEG)
            if c:
                s = jnp.concatenate([contract(q, k_in[:lo, lanes], ((1,), (1,))), s], axis=1)
            p = jnp.exp(s - lse[lo:hi, h * HD : h * HD + 1])
            dp = contract(do, v_in[:hi, lanes], ((1,), (1,)))
            ds = (p * (dp - delta)).astype(BF)
            dqs.append(contract(ds, k_in[:hi, lanes], ((1,), (0,))) * scale)
            dk[:hi, lanes] += contract(ds, q, ((0,), (0,)))
            dv[:hi, lanes] += contract(p.astype(BF), do, ((0,), (0,)))
        dq = jnp.concatenate(dqs, axis=1)
        dq_out[lo:hi, :] = turn(dq, cos[lo:hi, :], -first[lo:hi, :], -second[lo:hi, :]).astype(BF)
    dk_out[...] = turn(dk[...], cos[...], -first[...], -second[...]).astype(BF)
    dv_out[...] = dv[...].astype(BF)


def attend_back(q, k, v, d_attended, attended, lse, tables, heads):
    length, width = q.shape
    block = pl.BlockSpec((length, 2 * HD), lambda h: (0, h))
    table = pl.BlockSpec((length, 2 * HD), lambda h: (0, 0))
    return pl.pallas_call(
        attend_back_kernel,
        grid=(heads // 2,),
        in_specs=[block] * 6 + [table] * 3,
        out_specs=[block] * 3,
        out_shape=[jax.ShapeDtypeStruct((length, width), BF)] * 3,
        scratch_shapes=[pltpu.VMEM((length, 2 * HD), F32)] * 2,
        compiler_params=pltpu.CompilerParams(vmem_limit_bytes=40 * 2**20),
        cost_estimate=pl.CostEstimate(
            flops=40 * heads * length * length * HD // 2,
            bytes_accessed=22 * length * width,
            transcendentals=heads * length * length // 2,
        ),
        name="attend_back",
    )(q, k, v, d_attended, attended, lse, *tables)


MESH = pl.DeviceIdType.MESH
TILE = 256
HALF = 128
DEEP = 4
LAG = 2


def vmem_whole():
    return pl.BlockSpec(memory_space=pltpu.VMEM)


def hbm_whole():
    return pl.BlockSpec(memory_space=pl.ANY)


def chip_away(chip, m):
    return 2 * ((chip // 2 + m // 2) % 2) + (chip + m) % 2


def inner_runs(shards, count, part):
    runs = []
    for block in range(shards * part // HALF):
        first = 0
        while first < HALF:
            shard, unit = divmod(block * HALF + first, part)
            last = min(HALF, first + part - unit)
            runs.append((block, first, last, shard * count * part + unit - first))
            first = last
    return runs


def start_kernel(
    tokens, vectors, w_gate, w_up, w_qkv, x_all, vectors_all, inner, heads,
    raw_gate, raw_up, raw_qkv, my_inner, my_heads,
    load_sem, line_send, line_recv, part_send, part_recv, vector_send, vector_recv, own_sem,
):
    count, shards = x_all.shape[0], inner.shape[0]
    place, me = lax.axis_index("ctx"), lax.axis_index("fsdp")
    chip, core = me // 2, me % 2
    sibling = 2 * chip + 1 - core
    near = (2 * chip_away(chip, 1) + core, 2 * chip_away(chip, 2) + core)
    far = 2 * chip_away(chip, 3) + core
    rows = inner.shape[1]

    loads = [
        pltpu.make_async_copy(w_gate, raw_gate, load_sem.at[0]),
        pltpu.make_async_copy(w_up, raw_up, load_sem.at[1]),
        pltpu.make_async_copy(w_qkv, raw_qkv, load_sem.at[2]),
    ]
    for load in loads:
        load.start()

    peers = [(place, (me + s) % shards) for s in range(1, shards)]
    peers += [((place + 1) % count, me), ((place + count - 1) % count, me)]
    barrier = pltpu.get_barrier_semaphore()
    for peer in peers:
        pl.semaphore_signal(barrier, inc=1, device_id=peer, device_id_type=MESH)
    pl.semaphore_wait(barrier, len(peers))

    def line_copy(way, hop):
        ahead = 1 - 2 * way
        origin = place - (hop - 1) * ahead
        return pltpu.make_async_remote_copy(
            src_ref=tokens if hop == 1 else x_all.at[origin],
            dst_ref=x_all.at[origin],
            send_sem=line_send.at[way, hop - 1],
            recv_sem=line_recv.at[way, hop - 1],
            device_id=(place + ahead, me),
            device_id_type=MESH,
        )

    def sends(way, hop):
        if way == 0:
            return (place >= hop - 1) & (place <= count - 2)
        return (place <= count - hop) & (place >= 1)

    def lands(way, hop):
        return place >= hop if way == 0 else place <= count - 1 - hop

    def pass_on(hop):
        for way in range(2):
            if hop > 1:
                @pl.when(lands(way, hop - 1))
                def _():
                    line_copy(way, hop - 1).wait_recv()

            if hop < count:
                @pl.when(sends(way, hop))
                def _():
                    line_copy(way, hop).start()

    pass_on(1)

    def copy(which, kind, source, target, to):
        return pltpu.make_async_remote_copy(
            src_ref=source,
            dst_ref=target,
            send_sem=part_send.at[which, kind],
            recv_sem=part_recv.at[which, kind],
            device_id=(place, to),
            device_id_type=MESH,
        )

    whole = (inner, heads)
    mine = (my_inner, my_heads)
    half = rows // 2

    def direct(which, a):
        return copy(which, a, mine[which], whole[which].at[me], near[a])

    def across(which, a):
        piece = whole[which].at[near[1 - a], a * half : (a + 1) * half]
        return copy(which, 2 + a, piece, piece, near[a])

    def beside(which, kind):
        source = (me, near[0], near[1], far)[kind]
        piece = whole[which].at[source]
        return copy(which, 4 + kind, mine[which] if kind == 0 else piece, piece, sibling)

    own_copies = [
        pltpu.make_async_copy(my_inner, inner.at[me], own_sem.at[0]),
        pltpu.make_async_copy(my_heads, heads.at[me], own_sem.at[1]),
        pltpu.make_async_copy(vectors, vectors_all.at[me], own_sem.at[2]),
        pltpu.make_async_copy(tokens, x_all.at[place], own_sem.at[3]),
    ]
    own_copies[2].start()
    own_copies[3].start()
    vector_copies = [
        pltpu.make_async_remote_copy(
            src_ref=vectors,
            dst_ref=vectors_all.at[me],
            send_sem=vector_send.at[s - 1],
            recv_sem=vector_recv.at[s - 1],
            device_id=(place, (me + s) % shards),
            device_id_type=MESH,
        )
        for s in range(1, shards)
    ]
    for c in vector_copies:
        c.start()

    row = lax.broadcasted_iota(jnp.int32, (TILE, HALF), 0)
    col = lax.broadcasted_iota(jnp.int32, (TILE, HALF), 1)

    def picked(raws, first, last, start):
        width = raws[0].shape[1]
        base = jnp.minimum((start + first) // HALF, width // HALF - TILE // HALF) * HALF
        choose = (row + base == col + start) & (col >= first) & (col < last)
        choose = choose.astype(F32).astype(BF)
        at = pl.ds(pl.multiple_of(base, HALF), TILE)
        return [contract(raw[:, at], choose, ((1,), (0,))) for raw in raws]

    part = raw_gate.shape[1] // shards // count
    loads[0].wait()
    loads[1].wait()
    held = None
    for block, first, last, start in inner_runs(shards, count, part):
        values = picked((raw_gate, raw_up), first, last, start + place * part)
        held = values if first == 0 else [a + b for a, b in zip(held, values)]
        if last == HALF:
            for k in range(2):
                at = block * TILE + k * HALF
                my_inner[:, at : at + HALF] = held[k].astype(BF)
    for a in range(2):
        direct(0, a).start()
    beside(0, 0).start()
    own_copies[0].start()
    loads[2].wait()
    width = raw_qkv.shape[1] // 3
    for pair in range(shards // 2):
        for kind in range(3):
            value = 0.0
            for h in range(2):
                head = count * (2 * pair + h) + place
                start = kind * width + head * HD - h * HD
                value = value + picked((raw_qkv,), h * HD, (h + 1) * HD, start)[0]
            at = (pair * 3 + kind) * HALF
            my_heads[:, at : at + HALF] = value.astype(BF)
    for a in range(2):
        direct(1, a).start()
    beside(1, 0).start()
    own_copies[1].start()

    def relay(which):
        for a in range(2):
            direct(which, a).wait_recv()
        for a in range(2):
            across(which, a).start()
            beside(which, 1 + a).start()

    pass_on(2)
    relay(0)
    pass_on(3)
    relay(1)
    for hop in range(4, count + 1):
        pass_on(hop)
    for which in range(2):
        for a in range(2):
            across(which, a).wait_recv()
        beside(which, 3).start()
    for which in range(2):
        for kind in range(4):
            beside(which, kind).wait()
        for a in range(2):
            direct(which, a).wait_send()
            across(which, a).wait_send()
    for c in vector_copies:
        c.wait()
    for c in own_copies:
        c.wait()
    for way in range(2):
        for hop in range(1, count):
            @pl.when(sends(way, hop))
            def _():
                line_copy(way, hop).wait_send()


def start(tokens, vectors, w_gate, w_up, w_qkv, count, shards):
    rows, width = tokens.shape
    shard_rows, ff = w_gate.shape
    inner, heads = 2 * ff // count, 3 * width // count
    dma = pltpu.SemaphoreType.DMA
    return pl.pallas_call(
        start_kernel,
        out_shape=[
            jax.ShapeDtypeStruct((count, rows, width), BF),
            jax.ShapeDtypeStruct((shards,) + vectors.shape, F32),
            jax.ShapeDtypeStruct((shards, shard_rows, inner), BF),
            jax.ShapeDtypeStruct((shards, shard_rows, heads), BF),
        ],
        in_specs=[hbm_whole()] * 5,
        out_specs=[hbm_whole()] * 4,
        scratch_shapes=[
            pltpu.VMEM(w_gate.shape, BF),
            pltpu.VMEM(w_up.shape, BF),
            pltpu.VMEM(w_qkv.shape, BF),
            pltpu.VMEM((shard_rows, inner), BF),
            pltpu.VMEM((shard_rows, heads), BF),
            dma((3,)),
            dma((2, count - 1)),
            dma((2, count - 1)),
            dma((2, 8)),
            dma((2, 8)),
            dma((shards - 1,)),
            dma((shards - 1,)),
            dma((4,)),
        ],
        compiler_params=pltpu.CompilerParams(
            collective_id=2, has_side_effects=True, vmem_limit_bytes=30 * 2**20
        ),
        name="start",
    )(tokens, vectors, w_gate, w_up, w_qkv)


def norm_kernel(source, x, gain, bias, normed, normed_t, hat):
    xf = x[0].astype(F32)
    mean = jnp.mean(xf, axis=1, keepdims=True)
    centered = xf - mean
    variance = jnp.mean(centered * centered, axis=1, keepdims=True)
    x_hat = centered * lax.rsqrt(variance + EPS)
    hat[...] = x_hat.astype(BF)
    value = x_hat * gain[...] + bias[...]
    normed[...] = value.astype(BF)
    normed_t[...] = value.T.astype(BF)


def norm(source, x_all, gain, bias):
    count, rows, width = x_all.shape
    row_block = pl.BlockSpec((rows, width), lambda p, s: (p, 0))
    whole = pl.BlockSpec((1, width), lambda p, s: (0, 0))
    return pl.pallas_call(
        norm_kernel,
        grid_spec=pltpu.PrefetchScalarGridSpec(
            num_scalar_prefetch=1,
            grid=(count,),
            in_specs=[pl.BlockSpec((1, rows, width), lambda p, s: (s[p], 0, 0)), whole, whole],
            out_specs=[row_block, pl.BlockSpec((width, rows), lambda p, s: (0, p)), row_block],
        ),
        out_shape=[
            jax.ShapeDtypeStruct((count * rows, width), BF),
            jax.ShapeDtypeStruct((width, count * rows), BF),
            jax.ShapeDtypeStruct((count * rows, width), BF),
        ],
        compiler_params=pltpu.CompilerParams(vmem_limit_bytes=40 * 2**20),
        cost_estimate=pl.CostEstimate(flops=2**25, bytes_accessed=2**24, transcendentals=0),
        name="norm",
    )(source, x_all, gain, bias)


def feed_kernel(normed, w, both, hidden, hidden_t):
    value = contract(normed[...], w[...], ((1,), (0,)))
    both[...] = value
    gate, up = value[:, :HALF], value[:, HALF:]
    value = gate * jax.nn.sigmoid(gate) * up
    hidden[...] = value.astype(BF)
    hidden_t[...] = value.T.astype(BF)


def feed(normed, inner):
    length, width = normed.shape
    columns = inner.shape[1]
    return pl.pallas_call(
        feed_kernel,
        grid=(columns // TILE,),
        in_specs=[
            pl.BlockSpec((length, width), lambda i: (0, 0)),
            pl.BlockSpec((width, TILE), lambda i: (0, i)),
        ],
        out_specs=[
            pl.BlockSpec((length, TILE), lambda i: (0, i)),
            pl.BlockSpec((length, HALF), lambda i: (0, i)),
            pl.BlockSpec((HALF, length), lambda i: (i, 0)),
        ],
        out_shape=[
            jax.ShapeDtypeStruct((length, columns), F32),
            jax.ShapeDtypeStruct((length, columns // 2), BF),
            jax.ShapeDtypeStruct((columns // 2, length), BF),
        ],
        compiler_params=pltpu.CompilerParams(vmem_limit_bytes=40 * 2**20),
        cost_estimate=pl.CostEstimate(
            flops=2 * length * width * columns, bytes_accessed=2**25, transcendentals=length * columns
        ),
        name="feed",
    )(normed, inner)


def heads_kernel(normed, w, cos, first, second, q_out, k_out, v_out, att_out, low_out, low_t, lse_out):
    length = normed.shape[0]
    scale = HD ** (-0.5)
    mixed = contract(normed[...], w[...], ((1,), (0,)))
    q = turn(mixed[:, :HALF], cos[...], first[...], second[...]).astype(BF).astype(F32)
    q_out[...] = (q * scale).astype(BF)
    k_out[...] = turn(mixed[:, HALF : 2 * HALF], cos[...], first[...], second[...]).astype(BF)
    v_out[...] = mixed[:, 2 * HALF :].astype(BF)
    row = lax.broadcasted_iota(jnp.int32, (CHUNK, CHUNK), 0)
    col = lax.broadcasted_iota(jnp.int32, (CHUNK, CHUNK), 1)
    for c in range(length // CHUNK):
        lo, hi = c * CHUNK, (c + 1) * CHUNK
        for h in range(2):
            lanes = slice(h * HD, (h + 1) * HD)
            q = q_out[lo:hi, lanes]
            s = contract(q, k_out[lo:hi, lanes], ((1,), (1,)))
            s = jnp.where(col <= row, s, NEG)
            if c:
                s = jnp.concatenate([contract(q, k_out[:lo, lanes], ((1,), (1,))), s], axis=1)
            top = jnp.max(s, axis=1, keepdims=True)
            p = jnp.exp(s - top)
            total = jnp.sum(p, axis=1, keepdims=True)
            o = contract(p.astype(BF), v_out[:hi, lanes], ((1,), (0,)))
            att_out[lo:hi, lanes] = o / total
            lse_out[lo:hi, lanes] = jnp.broadcast_to(top + jnp.log(total), (CHUNK, HD))
    att = att_out[...]
    low_out[...] = att.astype(BF)
    low_t[...] = att.T.astype(BF)


def attend_heads(normed, w, tables):
    length, model = normed.shape
    width = w.shape[1] // 3
    block = pl.BlockSpec((length, HALF), lambda h: (0, h))
    table = pl.BlockSpec((length, HALF), lambda h: (0, 0))
    heads = width // HD
    return pl.pallas_call(
        heads_kernel,
        grid=(heads // 2,),
        in_specs=[
            pl.BlockSpec((length, model), lambda h: (0, 0)),
            pl.BlockSpec((model, 3 * HALF), lambda h: (0, h)),
            table,
            table,
            table,
        ],
        out_specs=[block] * 5 + [pl.BlockSpec((HALF, length), lambda h: (h, 0)), block],
        out_shape=[jax.ShapeDtypeStruct((length, width), BF)] * 3
        + [jax.ShapeDtypeStruct((length, width), F32), jax.ShapeDtypeStruct((length, width), BF)]
        + [jax.ShapeDtypeStruct((width, length), BF), jax.ShapeDtypeStruct((length, width), F32)],
        compiler_params=pltpu.CompilerParams(vmem_limit_bytes=50 * 2**20),
        cost_estimate=pl.CostEstimate(
            flops=6 * length * model * width + 16 * heads * length * length * HD // 2,
            bytes_accessed=2**25,
            transcendentals=heads * length * length // 2,
        ),
        name="attend_heads",
    )(normed, w, *tables)


def branch_kernel(slots, hidden, low, down, attn, out):
    value = contract(hidden[...], down[...], ((1,), (0,))) + contract(low[...], attn[...], ((1,), (0,)))
    count, rows = out.shape[0], out.shape[1]
    for p in range(count):
        out[slots[p]] = value[p * rows : (p + 1) * rows].astype(BF)


def branch_terms(slots, hidden, low, down, attn, count):
    length, width = hidden.shape[0], down.shape[1]
    whole = lambda a: pl.BlockSpec(a.shape, lambda i, s: (0, 0))
    column = lambda a: pl.BlockSpec((a.shape[0], TILE), lambda i, s: (0, i))
    return pl.pallas_call(
        branch_kernel,
        grid_spec=pltpu.PrefetchScalarGridSpec(
            num_scalar_prefetch=1,
            grid=(width // TILE,),
            in_specs=[whole(hidden), whole(low), column(down), column(attn)],
            out_specs=pl.BlockSpec((count, length // count, TILE), lambda i, s: (0, 0, i)),
        ),
        out_shape=jax.ShapeDtypeStruct((count, length // count, width), BF),
        compiler_params=pltpu.CompilerParams(vmem_limit_bytes=40 * 2**20),
        cost_estimate=pl.CostEstimate(
            flops=2 * length * width * (down.shape[0] + attn.shape[0]), bytes_accessed=2**24, transcendentals=0
        ),
        name="branch",
    )(slots, hidden, low, down, attn)


def feed_back_kernel(cot, down, attn, both, inner, d_att):
    d_att[...] = contract(cot[...], attn[...], ((1,), (1,))).astype(BF)
    d_hidden = contract(cot[...], down[...], ((1,), (1,)))
    for b in range(down.shape[0] // HALF):
        d = d_hidden[:, b * HALF : (b + 1) * HALF]
        gate = both[:, b * TILE : b * TILE + HALF]
        up = both[:, b * TILE + HALF : (b + 1) * TILE]
        sig = jax.nn.sigmoid(gate)
        inner[:, b * TILE : b * TILE + HALF] = (d * up * sig * (1.0 + gate * (1.0 - sig))).astype(BF)
        inner[:, b * TILE + HALF : (b + 1) * TILE] = (d * gate * sig).astype(BF)


def feed_back(cot, down, attn, both):
    length, width = cot.shape
    rows = length // 4
    whole = lambda a: pl.BlockSpec(a.shape, lambda i: (0, 0))
    by_rows = lambda columns: pl.BlockSpec((rows, columns), lambda i: (i, 0))
    return pl.pallas_call(
        feed_back_kernel,
        grid=(length // rows,),
        in_specs=[by_rows(width), whole(down), whole(attn), by_rows(both.shape[1])],
        out_specs=[by_rows(both.shape[1]), by_rows(attn.shape[0])],
        out_shape=[
            jax.ShapeDtypeStruct(both.shape, BF),
            jax.ShapeDtypeStruct((length, attn.shape[0]), BF),
        ],
        compiler_params=pltpu.CompilerParams(vmem_limit_bytes=50 * 2**20),
        cost_estimate=pl.CostEstimate(
            flops=2 * length * width * (down.shape[0] + attn.shape[0]), bytes_accessed=2**25, transcendentals=2**20
        ),
        name="feed_back",
    )(cot, down, attn, both)


def heads_back_kernel(q_in, k_in, v_in, do_in, att, lse, cos, first, second, out, dk, dv):
    length = q_in.shape[0]
    scale = HD ** (-0.5)
    row = lax.broadcasted_iota(jnp.int32, (CHUNK, CHUNK), 0)
    col = lax.broadcasted_iota(jnp.int32, (CHUNK, CHUNK), 1)
    dk[...] = jnp.zeros_like(dk)
    dv[...] = jnp.zeros_like(dv)
    for c in range(length // CHUNK):
        lo, hi = c * CHUNK, (c + 1) * CHUNK
        dqs = []
        for h in range(2):
            lanes = slice(h * HD, (h + 1) * HD)
            q, do = q_in[lo:hi, lanes], do_in[lo:hi, lanes]
            delta = jnp.sum(do.astype(F32) * att[lo:hi, lanes], axis=1, keepdims=True)
            s = contract(q, k_in[lo:hi, lanes], ((1,), (1,)))
            s = jnp.where(col <= row, s, NEG)
            if c:
                s = jnp.concatenate([contract(q, k_in[:lo, lanes], ((1,), (1,))), s], axis=1)
            p = jnp.exp(s - lse[lo:hi, h * HD : h * HD + 1])
            dp = contract(do, v_in[:hi, lanes], ((1,), (1,)))
            ds = (p * (dp - delta)).astype(BF)
            dqs.append(contract(ds, k_in[:hi, lanes], ((1,), (0,))) * scale)
            dk[:hi, lanes] += contract(ds, q, ((0,), (0,)))
            dv[:hi, lanes] += contract(p.astype(BF), do, ((0,), (0,)))
        dq = jnp.concatenate(dqs, axis=1)
        out[lo:hi, :HALF] = turn(dq, cos[lo:hi, :], -first[lo:hi, :], -second[lo:hi, :]).astype(BF)
    out[:, HALF : 2 * HALF] = turn(dk[...], cos[...], -first[...], -second[...]).astype(BF)
    out[:, 2 * HALF :] = dv[...].astype(BF)


def heads_back(q, k, v, d_attended, attended, lse, tables):
    length, width = q.shape
    heads = width // HD
    block = pl.BlockSpec((length, HALF), lambda h: (0, h))
    table = pl.BlockSpec((length, HALF), lambda h: (0, 0))
    return pl.pallas_call(
        heads_back_kernel,
        grid=(heads // 2,),
        in_specs=[block] * 6 + [table] * 3,
        out_specs=pl.BlockSpec((length, 3 * HALF), lambda h: (0, h)),
        out_shape=jax.ShapeDtypeStruct((length, 3 * width), BF),
        scratch_shapes=[pltpu.VMEM((length, HALF), F32)] * 2,
        compiler_params=pltpu.CompilerParams(vmem_limit_bytes=40 * 2**20),
        cost_estimate=pl.CostEstimate(
            flops=40 * heads * length * length * HD // 2,
            bytes_accessed=22 * length * width,
            transcendentals=heads * length * length // 2,
        ),
        name="heads_back",
    )(q, k, v, d_attended, attended, lse, *tables)


def norm_back_kernel(slots, d_inner, inner, d_mixed, heads, hat, out, small):
    value = contract(d_inner[...], inner[...], ((1,), (1,))) + contract(d_mixed[...], heads[...], ((1,), (1,)))
    count, rows = out.shape[0], out.shape[1]
    for p in range(count):
        out[slots[p]] = value[p * rows : (p + 1) * rows].astype(BF)
    gain = jnp.sum(value * hat[...].astype(F32), axis=0, keepdims=True)
    bias = jnp.sum(value, axis=0, keepdims=True)
    row = lax.broadcasted_iota(jnp.int32, small.shape, 0)
    small[...] = jnp.where(row == 0, gain, jnp.where(row == 1, bias, 0.0)).astype(BF)


def norm_back(slots, d_inner, inner, d_mixed, heads, hat, count):
    length, width = hat.shape
    whole = lambda a: pl.BlockSpec(a.shape, lambda i, s: (0, 0))
    by_rows = lambda a: pl.BlockSpec((TILE, a.shape[1]), lambda i, s: (i, 0))
    return pl.pallas_call(
        norm_back_kernel,
        grid_spec=pltpu.PrefetchScalarGridSpec(
            num_scalar_prefetch=1,
            grid=(width // TILE,),
            in_specs=[
                whole(d_inner),
                by_rows(inner),
                whole(d_mixed),
                by_rows(heads),
                pl.BlockSpec((length, TILE), lambda i, s: (0, i)),
            ],
            out_specs=[
                pl.BlockSpec((count, length // count, TILE), lambda i, s: (0, 0, i)),
                pl.BlockSpec((16, TILE), lambda i, s: (0, i)),
            ],
        ),
        out_shape=[
            jax.ShapeDtypeStruct((count, length // count, width), BF),
            jax.ShapeDtypeStruct((16, width), BF),
        ],
        compiler_params=pltpu.CompilerParams(vmem_limit_bytes=50 * 2**20),
        cost_estimate=pl.CostEstimate(
            flops=2 * length * width * (d_inner.shape[1] + d_mixed.shape[1]), bytes_accessed=2**25, transcendentals=0
        ),
        name="norm_back",
    )(slots, d_inner, inner, d_mixed, heads, hat)


def rows_of(shard, part):
    return slice(shard * part, (shard + 1) * part)


def gradients_kernel(
    hid_t, att_t, cot, norm_t, d_inner, d_mixed, small, branch, d_normed, pieces, sums,
    partial, theirs, pair, landed, total,
    sum_from, sum_land,
    core_send, core_recv, chip_send, chip_recv, line_send, line_recv, own_sem, sum_send, sum_recv,
):
    count = pieces.shape[0]
    chunks = pieces.shape[1]
    shards = 2 * partial.shape[1]
    chips = shards // 2
    place, me = lax.axis_index("ctx"), lax.axis_index("fsdp")
    chip, core = me // 2, me % 2
    ff_part, attn_part = hid_t.shape[0] // shards, att_t.shape[0] // shards
    cot_chunks = cot.shape[1] // TILE
    inner_chunks = d_inner.shape[1] // TILE
    sum_parts = branch.shape[2] // TILE

    def core_copy(i):
        return pltpu.make_async_remote_copy(
            src_ref=partial.at[i % 2, :, 1 - core],
            dst_ref=theirs.at[i % DEEP],
            send_sem=core_send.at[i % 2],
            recv_sem=core_recv.at[i % DEEP],
            device_id=(place, me + 1 - 2 * core),
            device_id_type=MESH,
        )

    def chip_of(m):
        return chip_away(chip, m)

    def chip_copy(j, m):
        return pltpu.make_async_remote_copy(
            src_ref=pair.at[j % 2, chip_of(m)],
            dst_ref=landed.at[j % DEEP, m - 1],
            send_sem=chip_send.at[j % 2, m - 1],
            recv_sem=chip_recv.at[j % DEEP, m - 1],
            device_id=(place, 2 * chip_of(m) + core),
            device_id_type=MESH,
        )

    def line_copy(way, hop, k):
        ahead = 1 - 2 * way
        origin = place - (hop - 1) * ahead
        return pltpu.make_async_remote_copy(
            src_ref=total.at[k % DEEP] if hop == 1 else pieces.at[origin, k],
            dst_ref=pieces.at[origin, k],
            send_sem=line_send.at[way, hop - 1, k % DEEP],
            recv_sem=line_recv.at[way, k, hop - 1],
            device_id=(place + ahead, me),
            device_id_type=MESH,
        )

    def sends(way, hop):
        if way == 0:
            return (place >= hop - 1) & (place <= count - 2)
        return (place <= count - hop) & (place >= 1)

    def lands(way, hop):
        return place >= hop if way == 0 else place <= count - 1 - hop

    def forward(hop, k):
        for way in range(2):
            if hop > 1:
                @pl.when(lands(way, hop - 1))
                def _():
                    line_copy(way, hop - 1, k).wait_recv()

            if hop < count:
                @pl.when(sends(way, hop))
                def _():
                    @pl.when(k >= DEEP)
                    def _():
                        line_copy(way, hop, k - DEEP).wait_send()

                    line_copy(way, hop, k).start()

    def sum_copy(way, t, q):
        return pltpu.make_async_remote_copy(
            src_ref=sum_from.at[way, t - 1, q % 2],
            dst_ref=sum_land.at[way, t - 1, q],
            send_sem=sum_send.at[way, t - 1, q % 2],
            recv_sem=sum_recv.at[way, t - 1, q],
            device_id=(place + 1 - 2 * way, me),
            device_id_type=MESH,
        )

    def sum_sends(way, t):
        return place <= t - 1 if way == 0 else place >= count - t

    def both_terms(q, use):
        for which, terms in enumerate((branch, d_normed)):
            at = (q - which * sum_parts) * TILE

            @pl.when((q >= which * sum_parts) & (q < (which + 1) * sum_parts))
            def _(which=which, terms=terms, at=at):
                use(which, terms, pl.ds(pl.multiple_of(at, TILE), TILE))

    def sum_step(t, q):
        for way in range(2):
            @pl.when(sum_sends(way, t))
            def _(way=way):
                to = count - t + place if way == 0 else t + place - count
                first = place == 0 if way == 0 else place == count - 1

                @pl.when(q >= 2)
                def _():
                    sum_copy(way, t, q - 2).wait_send()

                @pl.when(first)
                def _():
                    def use(which, terms, at):
                        sum_from[way, t - 1, q % 2] = terms[to, :, at]

                    both_terms(q, use)

                if t > 1:
                    @pl.when(jnp.logical_not(first))
                    def _():
                        sum_copy(way, t - 1, q).wait_recv()

                        def use(which, terms, at):
                            value = terms[to, :, at].astype(F32) + sum_land[way, t - 2, q].astype(F32)
                            sum_from[way, t - 1, q % 2] = value.astype(BF)

                        both_terms(q, use)

                sum_copy(way, t, q).start()

    def sum_end(q):
        def use(which, terms, at):
            sums[which, :, at] = terms[place, :, at].astype(F32)

        both_terms(q, use)
        for way in range(2):
            @pl.when(place >= 1 if way == 0 else place <= count - 2)
            def _(way=way):
                sum_copy(way, count - 1, q).wait_recv()

                def use(which, terms, at):
                    sums[which, :, at] += sum_land[way, count - 2, q].astype(F32)

                both_terms(q, use)

    def own_copy(k):
        return pltpu.make_async_copy(total.at[k % DEEP], pieces.at[place, k], own_sem.at[k % DEEP])

    partners = [(place, me + 1 - 2 * core)]
    partners += [(place, 2 * chip_of(m) + core) for m in range(1, chips)]
    partners += [((place + 1) % count, me), ((place + count - 1) % count, me)]
    barrier = pltpu.get_barrier_semaphore()
    for partner in partners:
        pl.semaphore_signal(barrier, inc=1, device_id=partner, device_id_type=MESH)
    pl.semaphore_wait(barrier, len(partners))
    def store(i, shard, lo, value):
        partial[i % 2, shard // 2, shard % 2, lo : lo + value.shape[0], :] = value

    def from_norm(i, rhs):
        for s in range(0, shards, 2):
            rows = norm_t.shape[0] // shards
            value = contract(norm_t[s * rows : (s + 2) * rows, :], rhs, ((1,), (0,))).astype(BF)
            store(i, s, 0, value[:rows])
            store(i, s + 1, 0, value[rows:])

    def step(i, carry):
        @pl.when(i < cot_chunks)
        def _():
            rhs = cot[:, pl.ds(pl.multiple_of(i * TILE, TILE), TILE)]
            for s in range(0, shards, 4):
                value = contract(hid_t[s * ff_part : (s + 4) * ff_part, :], rhs, ((1,), (0,))).astype(BF)
                for t in range(4):
                    store(i, s + t, 0, value[rows_of(t, ff_part)])
            value = contract(att_t[...], rhs, ((1,), (0,))).astype(BF)
            for s in range(shards):
                store(i, s, ff_part, value[rows_of(s, attn_part)])
                store(i, s, ff_part + attn_part, small[:, s * TILE : (s + 1) * TILE])

        @pl.when((i >= cot_chunks) & (i < cot_chunks + inner_chunks))
        def _():
            at = pl.ds(pl.multiple_of((i - cot_chunks) * TILE, TILE), TILE)
            from_norm(i, d_inner[:, at])

        @pl.when((i >= cot_chunks + inner_chunks) & (i < chunks))
        def _():
            at = pl.multiple_of((i - cot_chunks - inner_chunks) * TILE, TILE)
            from_norm(i, d_mixed[:, pl.ds(at, TILE)])

        @pl.when(i < chunks)
        def _():
            core_copy(i).start()

        @pl.when((i >= 1) & (i < chunks + 1))
        def _():
            j = i - 1
            core_copy(j).wait()
            for m in range(chips):
                a = partial[j % 2, m, core].astype(F32) + theirs[j % DEEP, m].astype(F32)
                pair[j % 2, m] = a.astype(BF)
            for m in range(1, chips):
                chip_copy(j, m).start()

        @pl.when((i >= 2) & (i < chunks + 2))
        def _():
            k = i - 2
            for m in range(1, chips):
                chip_copy(k, m).wait()

            a = pair[k % 2, chip].astype(F32)
            for m in range(1, chips):
                a = a + landed[k % DEEP, m - 1].astype(F32)
            for way in range(2):
                @pl.when(sends(way, 1) & (k >= DEEP))
                def _():
                    line_copy(way, 1, k - DEEP).wait_send()

            @pl.when(k >= DEEP)
            def _():
                own_copy(k - DEEP).wait()

            total[k % DEEP] = a.astype(BF)
            for way in range(2):
                @pl.when(sends(way, 1))
                def _():
                    line_copy(way, 1, k).start()

            own_copy(k).start()

        for t in range(1, count + 1):
            q = i - LAG * (t - 1)

            @pl.when((q >= 0) & (q < 2 * sum_parts))
            def _(q=q, t=t):
                if t < count:
                    sum_step(t, q)
                else:
                    sum_end(q)

        for hop in range(2, count + 1):
            k = i - 2 - LAG * (hop - 1)

            @pl.when((k >= 0) & (k < chunks))
            def _(k=k, hop=hop):
                forward(hop, k)

        return carry

    lax.fori_loop(0, chunks + 2 + LAG * (count - 1), step, 0)

    def drain(k, carry):
        own_copy(k).wait()
        for way in range(2):
            for hop in range(1, count):
                @pl.when(sends(way, hop))
                def _():
                    line_copy(way, hop, k).wait_send()
        return carry

    lax.fori_loop(chunks - DEEP, chunks, drain, 0)
    for way in range(2):
        for t in range(1, count):
            @pl.when(sum_sends(way, t))
            def _(way=way, t=t):
                for q in range(2):
                    sum_copy(way, t, 2 * sum_parts - 2 + q).wait_send()


def gradients(hid_t, att_t, cot, norm_t, d_inner, d_mixed, small, branch, d_normed, count, shards):
    chips = shards // 2
    chunks = (cot.shape[1] + d_inner.shape[1] + d_mixed.shape[1]) // TILE
    rows = norm_t.shape[0] // shards
    dma = pltpu.SemaphoreType.DMA
    own_rows, width = branch.shape[1:]
    parts = 2 * width // TILE
    return pl.pallas_call(
        gradients_kernel,
        out_shape=[
            jax.ShapeDtypeStruct((count, chunks, rows, TILE), BF),
            jax.ShapeDtypeStruct((2, own_rows, width), F32),
        ],
        in_specs=[vmem_whole()] * 9,
        out_specs=[hbm_whole(), vmem_whole()],
        scratch_shapes=[
            pltpu.VMEM((2, chips, 2, rows, TILE), BF),
            pltpu.VMEM((DEEP, chips, rows, TILE), BF),
            pltpu.VMEM((2, chips, rows, TILE), BF),
            pltpu.VMEM((DEEP, chips - 1, rows, TILE), BF),
            pltpu.VMEM((DEEP, rows, TILE), BF),
            pltpu.VMEM((2, count - 1, 2, own_rows, TILE), BF),
            pltpu.VMEM((2, count - 1, parts, own_rows, TILE), BF),
            dma((2,)),
            dma((DEEP,)),
            dma((2, chips - 1)),
            dma((DEEP, chips - 1)),
            dma((2, count - 1, DEEP)),
            dma((2, chunks, count - 1)),
            dma((DEEP,)),
            dma((2, count - 1, 2)),
            dma((2, count - 1, parts)),
        ],
        compiler_params=pltpu.CompilerParams(
            collective_id=1, has_side_effects=True, vmem_limit_bytes=60 * 2**20
        ),
        cost_estimate=pl.CostEstimate(
            flops=2 * norm_t.shape[0] * norm_t.shape[1] * TILE * chunks, bytes_accessed=2**27, transcendentals=0
        ),
        name="gradients",
    )(hid_t, att_t, cot, norm_t, d_inner, d_mixed, small, branch, d_normed)


def column_runs(columns, source):
    out = []
    for block in range(columns // HALF):
        first = 0
        while first < HALF:
            key, lane = source(block * HALF + first)
            last = first + 1
            while last < HALF and source(block * HALF + last) == (key, lane + last - first):
                last += 1
            out.append((block, first, last, key, (first - lane) % HALF))
            first = last
    return out


def assemble_kernel(down_chunks, rows_in, cols_in, qkv_out, gate_out, up_out, down_out, attn_out, small_out):
    count, chunks, rows, _ = rows_in.shape
    cot_chunks_static = down_chunks
    ff = gate_out.shape[1]
    width = qkv_out.shape[1]
    ff_part = down_out.shape[0] // count
    attn_part = attn_out.shape[0] // count
    shards = ff // (count * ff_part)
    inner_chunks = ff // count // HALF
    lane = lax.broadcasted_iota(jnp.int32, (rows, HALF), 1)

    def gather(out, runs, load):
        for block, first, last, key, shift in runs:
            value = load(key).astype(F32)
            if shift:
                value = pltpu.roll(value, shift, 1)
            if first:
                value = jnp.where(lane >= first, value, held)
            held = value
            if last == HALF:
                out[:, block * HALF : (block + 1) * HALF] = value

    def inner_source(column):
        shard, rest = divmod(column, count * ff_part)
        unit = shard * ff_part + rest % ff_part
        return (rest // ff_part, unit // HALF), unit % HALF

    def head_source(column):
        part, rest = divmod(column, width // 3)
        head, dim = divmod(rest, HD)
        per = width // 3 // HD // shards // count
        shard, at = divmod(head, per * count)
        place, sub = divmod(at, per)
        pair, half = divmod(shard * per + sub, 2)
        return (place, 3 * pair + part), half * HD + dim

    runs = column_runs(ff, inner_source)
    gather(gate_out, runs, lambda key: rows_in[key[0], cot_chunks_static + key[1], :, :HALF])
    gather(up_out, runs, lambda key: rows_in[key[0], cot_chunks_static + key[1], :, HALF:])
    first_head = cot_chunks_static + inner_chunks

    def head_load(key):
        at = key[1] % 2 * HALF
        return rows_in[key[0], first_head + key[1] // 2, :, at : at + HALF]

    gather(qkv_out, column_runs(width, head_source), head_load)
    for p in range(count):
        down_out[p * ff_part : (p + 1) * ff_part, :] = cols_in[p, 0, :ff_part, :].astype(F32)
        attn_out[p * attn_part : (p + 1) * attn_part, :] = cols_in[
            p, 0, ff_part : ff_part + attn_part, :
        ].astype(F32)
    small = [cols_in[p, 0, ff_part + attn_part :, :].astype(F32) for p in range(count)]
    small_out[...] = functools.reduce(jnp.add, small)


def assemble_outputs(pieces, qkv, attn, gate, down):
    count, chunks, rows, _ = pieces.shape
    steps = down[1] // TILE
    part = rows // steps
    by_rows = lambda shape: pl.BlockSpec((part, shape[1]), lambda i: (i, 0))
    by_cols = lambda shape: pl.BlockSpec((shape[0], TILE), lambda i: (0, i))
    return pl.pallas_call(
        functools.partial(assemble_kernel, steps),
        grid=(steps,),
        in_specs=[
            pl.BlockSpec((count, chunks, part, TILE), lambda i: (0, 0, i, 0)),
            pl.BlockSpec((count, 1, rows, TILE), lambda i: (0, i, 0, 0)),
        ],
        out_specs=[by_rows(qkv), by_rows(gate), by_rows(gate), by_cols(down), by_cols(attn)]
        + [pl.BlockSpec((16, TILE), lambda i: (0, 0))],
        out_shape=[jax.ShapeDtypeStruct(s, F32) for s in (qkv, gate, gate, down, attn, (16, TILE))],
        compiler_params=pltpu.CompilerParams(vmem_limit_bytes=40 * 2**20),
        name="assemble",
    )(pieces, pieces)


def rotation_tables(length):
    half = ROT // 2
    inverse = 10000.0 ** (-jnp.arange(half, dtype=F32) / half)
    grid = jnp.arange(length, dtype=jnp.int32).astype(F32)[:, None] * inverse[None, :]
    cos, sin = jnp.cos(grid), jnp.sin(grid)
    zero = jnp.zeros((length, half), F32)
    rest = jnp.zeros((length, HD - ROT), F32)
    tables = (
        jnp.concatenate([cos, cos, rest + 1.0], axis=1),
        jnp.concatenate([-sin, zero, rest], axis=1),
        jnp.concatenate([zero, sin, rest], axis=1),
    )
    return tuple(jnp.tile(t, (1, 2)) for t in tables)


def body_general(tokens, block_order, ln_gain, ln_bias, w_qkv, w_out, w_gate, w_up, w_down, cotangent):
    rows, width = tokens.shape[1], tokens.shape[2]
    count = lax.axis_size("ctx")
    shards = lax.axis_size("fsdp")
    place = lax.axis_index("ctx")
    length = rows * count
    order = block_order[0]
    shard_rows = w_qkv.shape[0]
    ff_shard = w_down.shape[0]
    ff_part = ff_shard // count
    own_heads = H // count
    spread = (w_out.shape[0] // HD) % count == 0
    groups = shards if spread else 1
    head_cols = own_heads * HD // groups

    def my_cols(w, outer, group, part):
        w = w.reshape(w.shape[0], outer, group, count, part)
        return lax.dynamic_index_in_dim(w, place, 3, False).reshape(w.shape[0], outer * group * part)

    def all_cols(piece, outer, group, part):
        whole = gather_ctx(piece).reshape(count, piece.shape[0], outer, group, part)
        return whole.transpose(1, 2, 3, 0, 4).reshape(piece.shape[0], -1).astype(F32)

    def assemble(block, ready=None):
        whole = jnp.zeros((length, width), block.dtype)
        whole = lax.dynamic_update_slice_in_dim(whole, block, order[place] * rows, 0)
        last = None
        for k in range(1, count):
            last = ring_send(block, k)
            source = (place - k) % count
            whole = lax.dynamic_update_slice_in_dim(whole, last, order[source] * rows, 0)
        return whole, last

    gain = lax.all_gather(ln_gain, "fsdp", axis=0, tiled=True).astype(F32)
    bias = lax.all_gather(ln_bias, "fsdp", axis=0, tiled=True).astype(F32)
    tables = rotation_tables(length)

    block = tokens[0]
    x_all, arrived = assemble(block)
    grad_block = cotangent[0]
    cot_all, _ = assemble(after(grad_block, arrived))

    inner = jnp.concatenate(
        [my_cols(w_gate, 1, shards, ff_part), my_cols(w_up, 1, shards, ff_part)], axis=1
    )
    w_inner, sent = gather_rows(inner)
    w_heads, sent = gather_rows(after(my_cols(w_qkv, 3, groups, head_cols), sent))
    down = lax.dynamic_slice_in_dim(w_down, place * ff_part, ff_part, 0)
    w_hidden, sent = gather_rows(after(down, sent))
    if spread:
        part = w_out.shape[0] // count
        attn = lax.dynamic_slice_in_dim(w_out, place * part, part, 0)
        w_attn, sent = gather_rows(after(attn, sent))
    else:
        w_attn = lax.all_gather(after(w_out, sent), "fsdp", axis=0, tiled=True)
        w_attn = lax.dynamic_slice_in_dim(w_attn, place * own_heads * HD, own_heads * HD, 0)

    xf = x_all.astype(F32)
    average = jnp.mean(xf, axis=-1, keepdims=True)
    centered = xf - average
    variance = jnp.mean(centered * centered, axis=-1, keepdims=True)
    inv_std = lax.rsqrt(variance + EPS)
    x_hat = centered * inv_std
    normed = (x_hat * gain + bias).astype(BF)

    across = ((1,), (0,))
    over_tokens = ((0,), (0,))
    back = ((1,), (1,))
    ff_cols = shards * ff_part
    gate_value = dot(normed, w_inner[:, :ff_cols], across)
    up_value = dot(normed, w_inner[:, ff_cols:], across)
    sigmoid_gate = jax.nn.sigmoid(gate_value)
    hidden = (gate_value * sigmoid_gate * up_value).astype(BF)
    mixed = dot(normed, w_heads, across)
    q, k, v, attended, lse = attend(mixed, tables, own_heads)
    attended_low = attended.astype(BF)

    branch = dot(attended_low, w_attn, across) + dot(hidden, w_hidden, across)
    out = line_scatter(lambda j: lax.dynamic_slice_in_dim(branch, order[j] * rows, rows, 0))
    out = (block.astype(F32) + out).astype(BF)[None]

    d_hidden = dot(cot_all, w_hidden, back)
    grad_down = scatter_rows(dot(hidden, cot_all, over_tokens, BF))
    d_gate_act = (
        d_hidden * up_value * sigmoid_gate * (1.0 + gate_value * (1.0 - sigmoid_gate))
    ).astype(BF)
    d_up_act = (d_hidden * gate_value * sigmoid_gate).astype(BF)
    d_inner = jnp.concatenate([d_gate_act, d_up_act], axis=1)
    d_attended = dot(cot_all, w_attn, back, BF)
    d_mixed = attend_back(q, k, v, d_attended, attended, lse, tables, own_heads)
    d_mixed = jnp.concatenate(d_mixed, axis=1)
    grad_inner = scatter_rows(dot(normed, d_inner, over_tokens, BF))
    grad_attn = dot(attended_low, cot_all, over_tokens, BF)
    grad_heads = scatter_rows(dot(normed, d_mixed, over_tokens, BF))

    d_normed = dot(d_inner, w_inner, back) + dot(d_mixed, w_heads, back)
    small = jnp.stack([jnp.sum(d_normed * x_hat, axis=0), jnp.sum(d_normed, axis=0)])
    small = lax.psum(small, ("ctx", "fsdp"))
    small = lax.dynamic_slice_in_dim(small, lax.axis_index("fsdp") * shard_rows, shard_rows, 1)
    d_own = line_scatter(lambda j: lax.dynamic_slice_in_dim(d_normed, order[j] * rows, rows, 0))
    own = block.astype(F32)
    own_average = jnp.mean(own, axis=-1, keepdims=True)
    own = own - own_average
    own_std = lax.rsqrt(jnp.mean(own * own, axis=-1, keepdims=True) + EPS)
    own = own * own_std
    scaled = d_own * gain
    d_input = own_std * (
        scaled
        - jnp.mean(scaled, axis=-1, keepdims=True)
        - own * jnp.mean(scaled * own, axis=-1, keepdims=True)
    )
    grad_in = (grad_block.astype(F32) + d_input)[None]

    down_all = gather_ctx(grad_down).reshape(ff_shard, width).astype(F32)
    if spread:
        attn_all = gather_ctx(scatter_rows(grad_attn)).reshape(w_out.shape).astype(F32)
    else:
        full = jnp.zeros((H * HD, width), BF)
        full = lax.dynamic_update_slice_in_dim(full, grad_attn, place * own_heads * HD, 0)
        full = lax.psum_scatter(full, "fsdp", scatter_dimension=0, tiled=True)
        attn_all = lax.psum(full, "ctx").astype(F32)
    heads_all = all_cols(grad_heads, 3, groups, head_cols)
    inner_all = gather_ctx(grad_inner).reshape(count, shard_rows, 2, shards, ff_part)
    inner_all = inner_all.transpose(2, 1, 3, 0, 4).reshape(2, shard_rows, -1).astype(F32)
    return (
        out,
        grad_in,
        small[0],
        small[1],
        heads_all,
        attn_all,
        inner_all[0],
        inner_all[1],
        down_all,
    )


def body_fast(tokens, block_order, ln_gain, ln_bias, w_qkv, w_out, w_gate, w_up, w_down, cotangent):
    count, shards = lax.axis_size("ctx"), lax.axis_size("fsdp")
    place = lax.axis_index("ctx")
    block, grad_block = tokens[0], cotangent[0]
    rows, width = block.shape
    order = block_order[0]
    spots = jnp.arange(count, dtype=jnp.int32)
    slots = jnp.sum(jnp.where(order[None, :] == spots[:, None], spots[None, :], 0), axis=1)
    vectors = jnp.stack([ln_gain, ln_bias] + [jnp.zeros_like(ln_gain)] * 6).astype(F32)
    x_all, vectors, w_inner, w_heads = start(block, vectors, w_gate, w_up, w_qkv, count, shards)
    w_inner = w_inner.reshape(width, -1)
    w_heads = w_heads.reshape(width, -1)
    gain, bias = vectors[:, 0].reshape(1, width), vectors[:, 1].reshape(1, width)
    tables = rotation_tables(rows * count)

    up = [after(grad_block, x_all)]
    down = [up[0]]
    for hop in range(1, count):
        pairs = [(i, i + 1) for i in range(hop - 1, count - 1)]
        up.append(lax.ppermute(up[-1], "ctx", pairs))
        pairs = [(count - 1 - i, count - 1 - j) for i, j in pairs]
        down.append(lax.ppermute(down[-1], "ctx", pairs))
    cot_all = jnp.zeros((rows * count, width), BF)
    cot_all = lax.dynamic_update_slice_in_dim(cot_all, grad_block, order[place] * rows, 0)
    for s in range(1, count):
        found = jnp.where(place >= s, up[s], down[count - s])
        cot_all = lax.dynamic_update_slice_in_dim(cot_all, found, order[(place - s) % count] * rows, 0)

    part = w_down.shape[0] // count
    w_hidden, _ = gather_rows(after(lax.dynamic_slice_in_dim(w_down, place * part, part, 0), x_all))
    part = w_out.shape[0] // count
    w_attn, _ = gather_rows(after(lax.dynamic_slice_in_dim(w_out, place * part, part, 0), x_all))

    normed, normed_t, hat = norm(slots, x_all, gain, bias)
    both, hidden, hidden_t = feed(normed, w_inner)
    q, k, v, attended, low, low_t, lse = attend_heads(normed, w_heads, tables)
    branch = branch_terms(slots, hidden, low, w_hidden, w_attn, count)
    d_inner, d_attended = feed_back(cot_all, w_hidden, w_attn, both)
    d_mixed = heads_back(q, k, v, d_attended, attended, lse, tables)
    d_normed, small = norm_back(slots, d_inner, w_inner, d_mixed, w_heads, hat, count)
    pieces, sums = gradients(
        hidden_t, low_t, cot_all, normed_t, d_inner, d_mixed, small, branch, d_normed, count, shards
    )
    d_qkv, d_gate, d_up, d_down, d_attn, small = assemble_outputs(
        pieces, w_qkv.shape, w_out.shape, w_gate.shape, w_down.shape
    )
    own = block.astype(F32)
    out = (own + sums[0]).astype(BF)[None]
    own = own - jnp.mean(own, axis=-1, keepdims=True)
    own_std = lax.rsqrt(jnp.mean(own * own, axis=-1, keepdims=True) + EPS)
    own = own * own_std
    scaled = sums[1] * gain
    d_input = own_std * (
        scaled
        - jnp.mean(scaled, axis=-1, keepdims=True)
        - own * jnp.mean(scaled * own, axis=-1, keepdims=True)
    )
    grad_in = (grad_block.astype(F32) + d_input)[None]
    return out, grad_in, small[0], small[1], d_qkv, d_attn, d_gate, d_up, d_down


def solution(mesh):
    whole, once = P("fsdp", "ctx", None), P("fsdp", None)
    count, shards = mesh.shape["ctx"], mesh.shape["fsdp"]

    def body(*args):
        w_out, w_down = args[5], args[8]
        fits = shards == 8 and w_out.shape[0] == count * HD and w_out.shape[0] == TILE
        fits = fits and w_down.shape[0] % (16 * count) == 0 and w_down.shape[0] // count <= 176
        return (body_fast if fits else body_general)(*args)

    return jax.shard_map(
        body,
        mesh=mesh,
        in_specs=(whole, once, P("fsdp"), P("fsdp")) + (once,) * 5 + (whole,),
        out_specs=(whole, whole, P("fsdp"), P("fsdp")) + (once,) * 5,
        check_vma=False,
    )
```

```python
import functools

import jax
import jax.numpy as jnp
from jax import lax
from jax.experimental import pallas as pl
from jax.experimental.pallas import tpu as pltpu
from jax.sharding import PartitionSpec as P

H = 32
HD = 64
ROT = 16
EPS = 1e-05
NEG = -1e30
CHUNK = 256

BF = jnp.bfloat16
F32 = jnp.float32


def xor_send(value, mask):
    count = lax.axis_size("fsdp")
    return lax.ppermute(value, "fsdp", [(i, i ^ mask) for i in range(count)])


def ring_send(value, steps):
    count = lax.axis_size("ctx")
    return lax.ppermute(value, "ctx", [(i, (i + steps) % count) for i in range(count)])


def after(value, *done):
    return lax.optimization_barrier((value,) + done)[0]


def dot(a, b, dims, out=F32):
    return lax.dot_general(a, b, (dims, ((), ())), preferred_element_type=F32).astype(out)


def gather_rows(piece):
    count = lax.axis_size("fsdp")
    chips = count // 2
    me = lax.axis_index("fsdp")
    chip, core = me // 2, me % 2
    parts = [piece] + [xor_send(piece, 2 * m) for m in range(1, chips)]
    others = [xor_send(p, 1) for p in parts]
    whole = jnp.zeros((count,) + piece.shape, piece.dtype)
    for m in range(chips):
        at = 2 * (chip ^ m)
        whole = lax.dynamic_update_index_in_dim(whole, parts[m], at + core, 0)
        whole = lax.dynamic_update_index_in_dim(whole, others[m], at + 1 - core, 0)
    return whole.reshape(count * piece.shape[0], piece.shape[1]), parts[-1]


def scatter_rows(grad):
    count = lax.axis_size("fsdp")
    chips = count // 2
    me = lax.axis_index("fsdp")
    chip, core = me // 2, me % 2
    rows = grad.shape[0] // count
    split = grad.reshape(chips, 2, rows, grad.shape[1])
    theirs = xor_send(lax.dynamic_index_in_dim(split, 1 - core, 1, False), 1)
    pair = lax.dynamic_index_in_dim(split, core, 1, False).astype(F32) + theirs.astype(F32)
    pair = pair.astype(BF)
    total = lax.dynamic_index_in_dim(pair, chip, 0, False).astype(F32)
    for m in range(1, chips):
        part = lax.dynamic_index_in_dim(pair, chip ^ m, 0, False)
        total = total + xor_send(part, 2 * m).astype(F32)
    return total.astype(BF)


def gather_ctx(piece):
    count = lax.axis_size("ctx")
    me = lax.axis_index("ctx")
    whole = jnp.zeros((count,) + piece.shape, piece.dtype)
    whole = lax.dynamic_update_index_in_dim(whole, piece, me, 0)
    for k in range(1, count):
        part = ring_send(piece, k)
        whole = lax.dynamic_update_index_in_dim(whole, part, (me - k) % count, 0)
    return whole


def line_scatter(blocks):
    count = lax.axis_size("ctx")
    me = lax.axis_index("ctx")
    down = up = None
    for t in range(1, count):
        to_down = blocks(jnp.clip(t + me - count, 0, count - 1))
        to_up = blocks(jnp.clip(count - 1 - (t + (count - 1 - me) - count), 0, count - 1))
        if down is not None:
            to_down = to_down + down.astype(F32)
            to_up = to_up + up.astype(F32)
        pairs = [(i, i - 1) for i in range(count - t, count)]
        down = lax.ppermute(to_down.astype(BF), "ctx", pairs)
        up = lax.ppermute(to_up.astype(BF), "ctx", [(count - 1 - i, count - 1 - j) for i, j in pairs])
    return blocks(me) + down.astype(F32) + up.astype(F32)


def turn(x, cos, first, second):
    width = x.shape[1]
    half = ROT // 2
    return x * cos + pltpu.roll(x, width - half, 1) * first + pltpu.roll(x, half, 1) * second


def contract(a, b, dims):
    return lax.dot_general(a, b, (dims, ((), ())), preferred_element_type=F32)


def attend_kernel(mq, mk, mv, cos, first, second, q_out, k_out, v_out, att_out, lse_out):
    length = mq.shape[0]
    scale = HD ** (-0.5)
    q_out[...] = (turn(mq[...], cos[...], first[...], second[...]).astype(BF).astype(F32) * scale).astype(BF)
    k_out[...] = turn(mk[...], cos[...], first[...], second[...]).astype(BF)
    v_out[...] = mv[...].astype(BF)
    row = lax.broadcasted_iota(jnp.int32, (CHUNK, CHUNK), 0)
    col = lax.broadcasted_iota(jnp.int32, (CHUNK, CHUNK), 1)
    for c in range(length // CHUNK):
        lo, hi = c * CHUNK, (c + 1) * CHUNK
        for h in range(2):
            lanes = slice(h * HD, (h + 1) * HD)
            q = q_out[lo:hi, lanes]
            s = contract(q, k_out[lo:hi, lanes], ((1,), (1,)))
            s = jnp.where(col <= row, s, NEG)
            if c:
                s = jnp.concatenate([contract(q, k_out[:lo, lanes], ((1,), (1,))), s], axis=1)
            top = jnp.max(s, axis=1, keepdims=True)
            p = jnp.exp(s - top)
            total = jnp.sum(p, axis=1, keepdims=True)
            o = contract(p.astype(BF), v_out[:hi, lanes], ((1,), (0,)))
            att_out[lo:hi, lanes] = o / total
            lse_out[lo:hi, lanes] = jnp.broadcast_to(top + jnp.log(total), (CHUNK, HD))


def attend(mixed, tables, heads):
    length = mixed.shape[0]
    pairs = heads // 2
    block = lambda at: pl.BlockSpec((length, 2 * HD), lambda h, at=at: (0, at + h))
    table = pl.BlockSpec((length, 2 * HD), lambda h: (0, 0))
    width = heads * HD
    return pl.pallas_call(
        attend_kernel,
        grid=(pairs,),
        in_specs=[block(0), block(pairs), block(2 * pairs), table, table, table],
        out_specs=[block(0)] * 5,
        out_shape=[jax.ShapeDtypeStruct((length, width), BF)] * 3
        + [jax.ShapeDtypeStruct((length, width), F32)] * 2,
        compiler_params=pltpu.CompilerParams(vmem_limit_bytes=40 * 2**20),
        cost_estimate=pl.CostEstimate(
            flops=16 * heads * length * length * HD // 2,
            bytes_accessed=26 * length * width,
            transcendentals=heads * length * length // 2,
        ),
        name="attend",
    )(mixed, mixed, mixed, *tables)


def attend_back_kernel(q_in, k_in, v_in, do_in, att, lse, cos, first, second, dq_out, dk_out, dv_out, dk, dv):
    length = q_in.shape[0]
    scale = HD ** (-0.5)
    row = lax.broadcasted_iota(jnp.int32, (CHUNK, CHUNK), 0)
    col = lax.broadcasted_iota(jnp.int32, (CHUNK, CHUNK), 1)
    dk[...] = jnp.zeros_like(dk)
    dv[...] = jnp.zeros_like(dv)
    for c in range(length // CHUNK):
        lo, hi = c * CHUNK, (c + 1) * CHUNK
        dqs = []
        for h in range(2):
            lanes = slice(h * HD, (h + 1) * HD)
            q, do = q_in[lo:hi, lanes], do_in[lo:hi, lanes]
            delta = jnp.sum(do.astype(F32) * att[lo:hi, lanes], axis=1, keepdims=True)
            s = contract(q, k_in[lo:hi, lanes], ((1,), (1,)))
            s = jnp.where(col <= row, s, NEG)
            if c:
                s = jnp.concatenate([contract(q, k_in[:lo, lanes], ((1,), (1,))), s], axis=1)
            p = jnp.exp(s - lse[lo:hi, h * HD : h * HD + 1])
            dp = contract(do, v_in[:hi, lanes], ((1,), (1,)))
            ds = (p * (dp - delta)).astype(BF)
            dqs.append(contract(ds, k_in[:hi, lanes], ((1,), (0,))) * scale)
            dk[:hi, lanes] += contract(ds, q, ((0,), (0,)))
            dv[:hi, lanes] += contract(p.astype(BF), do, ((0,), (0,)))
        dq = jnp.concatenate(dqs, axis=1)
        dq_out[lo:hi, :] = turn(dq, cos[lo:hi, :], -first[lo:hi, :], -second[lo:hi, :]).astype(BF)
    dk_out[...] = turn(dk[...], cos[...], -first[...], -second[...]).astype(BF)
    dv_out[...] = dv[...].astype(BF)


def attend_back(q, k, v, d_attended, attended, lse, tables, heads):
    length, width = q.shape
    block = pl.BlockSpec((length, 2 * HD), lambda h: (0, h))
    table = pl.BlockSpec((length, 2 * HD), lambda h: (0, 0))
    return pl.pallas_call(
        attend_back_kernel,
        grid=(heads // 2,),
        in_specs=[block] * 6 + [table] * 3,
        out_specs=[block] * 3,
        out_shape=[jax.ShapeDtypeStruct((length, width), BF)] * 3,
        scratch_shapes=[pltpu.VMEM((length, 2 * HD), F32)] * 2,
        compiler_params=pltpu.CompilerParams(vmem_limit_bytes=40 * 2**20),
        cost_estimate=pl.CostEstimate(
            flops=40 * heads * length * length * HD // 2,
            bytes_accessed=22 * length * width,
            transcendentals=heads * length * length // 2,
        ),
        name="attend_back",
    )(q, k, v, d_attended, attended, lse, *tables)


MESH = pl.DeviceIdType.MESH
TILE = 256
HALF = 128
DEEP = 4
LAG = 2


def vmem_whole():
    return pl.BlockSpec(memory_space=pltpu.VMEM)


def hbm_whole():
    return pl.BlockSpec(memory_space=pl.ANY)


def chip_away(chip, m):
    return 2 * ((chip // 2 + m // 2) % 2) + (chip + m) % 2


def inner_runs(shards, count, part):
    runs = []
    for block in range(shards * part // HALF):
        first = 0
        while first < HALF:
            shard, unit = divmod(block * HALF + first, part)
            last = min(HALF, first + part - unit)
            runs.append((block, first, last, shard * count * part + unit - first))
            first = last
    return runs


class Line:
    def __init__(self, own, whole, send, recv):
        self.own, self.whole, self.send, self.recv = own, whole, send, recv
        self.count = whole.shape[0]
        self.place, self.me = lax.axis_index("ctx"), lax.axis_index("fsdp")

    def copy(self, way, hop):
        ahead = 1 - 2 * way
        origin = self.place - (hop - 1) * ahead
        return pltpu.make_async_remote_copy(
            src_ref=self.own if hop == 1 else self.whole.at[origin],
            dst_ref=self.whole.at[origin],
            send_sem=self.send.at[way, hop - 1],
            recv_sem=self.recv.at[way, hop - 1],
            device_id=(self.place + ahead, self.me),
            device_id_type=MESH,
        )

    def sends(self, way, hop):
        if way == 0:
            return (self.place >= hop - 1) & (self.place <= self.count - 2)
        return (self.place <= self.count - hop) & (self.place >= 1)

    def lands(self, way, hop):
        return self.place >= hop if way == 0 else self.place <= self.count - 1 - hop

    def pass_on(self, hop):
        for way in range(2):
            if hop > 1:
                @pl.when(self.lands(way, hop - 1))
                def _(way=way):
                    self.copy(way, hop - 1).wait_recv()

            if hop < self.count:
                @pl.when(self.sends(way, hop))
                def _(way=way):
                    self.copy(way, hop).start()

    def finish(self):
        for way in range(2):
            for hop in range(1, self.count):
                @pl.when(self.sends(way, hop))
                def _(way=way, hop=hop):
                    self.copy(way, hop).wait_send()


class Plane:
    def __init__(self, mine, wholes, send, recv):
        self.mine, self.wholes, self.send, self.recv = mine, wholes, send, recv
        self.place, self.me = lax.axis_index("ctx"), lax.axis_index("fsdp")
        chip, core = self.me // 2, self.me % 2
        self.sibling = 2 * chip + 1 - core
        self.near = (2 * chip_away(chip, 1) + core, 2 * chip_away(chip, 2) + core)
        self.far = 2 * chip_away(chip, 3) + core

    def copy(self, which, kind, source, target, to):
        return pltpu.make_async_remote_copy(
            src_ref=source,
            dst_ref=target,
            send_sem=self.send.at[which, kind],
            recv_sem=self.recv.at[which, kind],
            device_id=(self.place, to),
            device_id_type=MESH,
        )

    def direct(self, which, a):
        return self.copy(which, a, self.mine[which], self.wholes[which].at[self.me], self.near[a])

    def across(self, which, a):
        half = self.wholes[which].shape[2] // 2
        piece = self.wholes[which].at[self.near[1 - a], :, a * half : (a + 1) * half]
        return self.copy(which, 2 + a, piece, piece, self.near[a])

    def beside(self, which, kind):
        source = (self.me, self.near[0], self.near[1], self.far)[kind]
        piece = self.wholes[which].at[source]
        return self.copy(which, 4 + kind, self.mine[which] if kind == 0 else piece, piece, self.sibling)

    def begin(self, which):
        for a in range(2):
            self.direct(which, a).start()
        self.beside(which, 0).start()

    def relay(self, which):
        for a in range(2):
            self.direct(which, a).wait_recv()
        for a in range(2):
            self.across(which, a).start()
            self.beside(which, 1 + a).start()

    def last(self, which):
        for a in range(2):
            self.across(which, a).wait_recv()
        self.beside(which, 3).start()

    def finish(self, which):
        for kind in range(4):
            self.beside(which, kind).wait()
        for a in range(2):
            self.direct(which, a).wait_send()
            self.across(which, a).wait_send()


def greet(peers):
    barrier = pltpu.get_barrier_semaphore()
    for peer in peers:
        pl.semaphore_signal(barrier, inc=1, device_id=peer, device_id_type=MESH)
    pl.semaphore_wait(barrier, len(peers))


def start_kernel(
    tokens, vectors, w_gate, w_up, w_qkv, x_all, vectors_all, inner, heads,
    raw_gate, raw_up, raw_qkv, my_inner, my_heads,
    load_sem, line_send, line_recv, part_send, part_recv, vector_send, vector_recv, own_sem,
):
    count, shards = x_all.shape[0], inner.shape[0]
    place, me = lax.axis_index("ctx"), lax.axis_index("fsdp")
    loads = [
        pltpu.make_async_copy(w_gate, raw_gate, load_sem.at[0]),
        pltpu.make_async_copy(w_up, raw_up, load_sem.at[1]),
        pltpu.make_async_copy(w_qkv, raw_qkv, load_sem.at[2]),
    ]
    for load in loads:
        load.start()
    peers = [(place, (me + s) % shards) for s in range(1, shards)]
    greet(peers + [((place + 1) % count, me), ((place + count - 1) % count, me)])
    line = Line(tokens, x_all, line_send, line_recv)
    plane = Plane((my_inner, my_heads), (inner, heads), part_send, part_recv)
    line.pass_on(1)
    own_copies = [
        pltpu.make_async_copy(my_inner, inner.at[me], own_sem.at[0]),
        pltpu.make_async_copy(my_heads, heads.at[me], own_sem.at[1]),
        pltpu.make_async_copy(vectors, vectors_all.at[me], own_sem.at[2]),
        pltpu.make_async_copy(tokens, x_all.at[place], own_sem.at[3]),
    ]
    own_copies[2].start()
    own_copies[3].start()
    vector_copies = [
        pltpu.make_async_remote_copy(
            src_ref=vectors,
            dst_ref=vectors_all.at[me],
            send_sem=vector_send.at[s - 1],
            recv_sem=vector_recv.at[s - 1],
            device_id=(place, (me + s) % shards),
            device_id_type=MESH,
        )
        for s in range(1, shards)
    ]
    for c in vector_copies:
        c.start()

    row = lax.broadcasted_iota(jnp.int32, (TILE, HALF), 0)
    col = lax.broadcasted_iota(jnp.int32, (TILE, HALF), 1)

    def picked(raws, first, last, start):
        width = raws[0].shape[1]
        base = jnp.minimum((start + first) // HALF, width // HALF - TILE // HALF) * HALF
        choose = (row + base == col + start) & (col >= first) & (col < last)
        choose = choose.astype(F32).astype(BF)
        at = pl.ds(pl.multiple_of(base, HALF), TILE)
        return [contract(raw[:, at], choose, ((1,), (0,))) for raw in raws]

    part = raw_gate.shape[1] // shards // count
    loads[0].wait()
    loads[1].wait()
    held = None
    for block, first, last, start in inner_runs(shards, count, part):
        values = picked((raw_gate, raw_up), first, last, start + place * part)
        held = values if first == 0 else [a + b for a, b in zip(held, values)]
        if last == HALF:
            for k in range(2):
                at = block * TILE + k * HALF
                my_inner[:, at : at + HALF] = held[k].astype(BF)
    plane.begin(0)
    own_copies[0].start()
    loads[2].wait()
    width = raw_qkv.shape[1] // 3
    for pair in range(shards // 2):
        for kind in range(3):
            value = 0.0
            for h in range(2):
                head = count * (2 * pair + h) + place
                start = kind * width + head * HD - h * HD
                value = value + picked((raw_qkv,), h * HD, (h + 1) * HD, start)[0]
            at = (pair * 3 + kind) * HALF
            my_heads[:, at : at + HALF] = value.astype(BF)
    plane.begin(1)
    own_copies[1].start()
    line.pass_on(2)
    plane.relay(0)
    line.pass_on(3)
    plane.relay(1)
    for hop in range(4, count + 1):
        line.pass_on(hop)
    for which in range(2):
        plane.last(which)
    for which in range(2):
        plane.finish(which)
    for c in vector_copies + own_copies:
        c.wait()
    line.finish()


def start(tokens, vectors, w_gate, w_up, w_qkv, count, shards):
    rows, width = tokens.shape
    shard_rows, ff = w_gate.shape
    inner, heads = 2 * ff // count, 3 * width // count
    dma = pltpu.SemaphoreType.DMA
    return pl.pallas_call(
        start_kernel,
        out_shape=[
            jax.ShapeDtypeStruct((count, rows, width), BF),
            jax.ShapeDtypeStruct((shards,) + vectors.shape, F32),
            jax.ShapeDtypeStruct((shards, shard_rows, inner), BF),
            jax.ShapeDtypeStruct((shards, shard_rows, heads), BF),
        ],
        in_specs=[hbm_whole()] * 5,
        out_specs=[hbm_whole()] * 4,
        scratch_shapes=[
            pltpu.VMEM(w_gate.shape, BF),
            pltpu.VMEM(w_up.shape, BF),
            pltpu.VMEM(w_qkv.shape, BF),
            pltpu.VMEM((shard_rows, inner), BF),
            pltpu.VMEM((shard_rows, heads), BF),
            dma((3,)),
            dma((2, count - 1)),
            dma((2, count - 1)),
            dma((2, 8)),
            dma((2, 8)),
            dma((shards - 1,)),
            dma((shards - 1,)),
            dma((4,)),
        ],
        compiler_params=pltpu.CompilerParams(
            collective_id=2, has_side_effects=True, vmem_limit_bytes=30 * 2**20
        ),
        name="start",
    )(tokens, vectors, w_gate, w_up, w_qkv)


def forward_kernel(
    order, slots, x_all, gain, bias, cos, first, second, cot, w_down, w_out, w_inner, w_heads,
    cot_all, down, attn, normed_t, hat, both, hidden_t, q_out, k_out, v_out, att_out, low_t, lse_out, branch,
    inner, heads, normed, hidden, low, hat_stage, turned_stage, both_stage, hidden_stage,
    q_buf, k_buf, v_buf, att_buf, low_stage, lse_buf, down_tile, attn_tile, term, branch_stage,
    load_sem, line_send, line_recv, part_send, part_recv, own_sem, norm_sem, feed_sem, head_sem, tile_sem, branch_sem,
):
    count, rows = cot_all.shape[0], cot_all.shape[1]
    shards = down.shape[0]
    place, me = lax.axis_index("ctx"), lax.axis_index("fsdp")
    chip, core = me // 2, me % 2
    loads = [
        pltpu.make_async_copy(w_inner, inner, load_sem.at[0]),
        pltpu.make_async_copy(w_heads, heads, load_sem.at[1]),
    ]
    for load in loads:
        load.start()
    peers = [(place, 2 * chip + 1 - core)] + [(place, 2 * chip_away(chip, m) + core) for m in range(1, 3)]
    greet(peers + [((place + 1) % count, me), ((place + count - 1) % count, me)])
    my_down = w_down.at[pl.ds(pl.multiple_of(place * down.shape[1], 16), down.shape[1])]
    my_attn = w_out.at[pl.ds(pl.multiple_of(place * attn.shape[1], 16), attn.shape[1])]
    line = Line(cot, cot_all, line_send, line_recv)
    plane = Plane((my_down, my_attn), (down, attn), part_send, part_recv)
    line.pass_on(1)
    for which in range(2):
        plane.begin(which)
    own_copies = [
        pltpu.make_async_copy(my_down, down.at[me], own_sem.at[0]),
        pltpu.make_async_copy(my_attn, attn.at[me], own_sem.at[1]),
        pltpu.make_async_copy(cot, cot_all.at[place], own_sem.at[2]),
    ]
    for c in own_copies:
        c.start()

    def norm_copies(p):
        at = pl.ds(pl.multiple_of(p * rows, rows), rows)
        return (
            pltpu.make_async_copy(hat_stage.at[p % 2], hat.at[at], norm_sem.at[0, p % 2]),
            pltpu.make_async_copy(turned_stage.at[p % 2], normed_t.at[:, at], norm_sem.at[1, p % 2]),
        )

    def norm_step(p, carry):
        @pl.when(p >= 2)
        def _():
            for c in norm_copies(p - 2):
                c.wait()

        xf = x_all[slots[p]].astype(F32)
        mean = jnp.mean(xf, axis=1, keepdims=True)
        centered = xf - mean
        variance = jnp.mean(centered * centered, axis=1, keepdims=True)
        x_hat = centered * lax.rsqrt(variance + EPS)
        hat_stage[p % 2] = x_hat.astype(BF)
        value = x_hat * gain[...] + bias[...]
        normed[pl.ds(pl.multiple_of(p * rows, rows), rows), :] = value.astype(BF)
        turned_stage[p % 2] = value.T.astype(BF)
        for c in norm_copies(p):
            c.start()
        return carry

    lax.fori_loop(0, count, norm_step, 0)
    loads[0].wait()

    def feed_copies(i):
        wide = pl.ds(pl.multiple_of(i * TILE, TILE), TILE)
        slim = pl.ds(pl.multiple_of(i * HALF, HALF), HALF)
        return (
            pltpu.make_async_copy(both_stage.at[i % 2], both.at[:, wide], feed_sem.at[0, i % 2]),
            pltpu.make_async_copy(hidden_stage.at[i % 2], hidden_t.at[slim], feed_sem.at[1, i % 2]),
        )

    def feed_step(i, carry):
        @pl.when(i >= 2)
        def _():
            for c in feed_copies(i - 2):
                c.wait()

        value = contract(normed[...], inner[:, pl.ds(pl.multiple_of(i * TILE, TILE), TILE)], ((1,), (0,)))
        both_stage[i % 2] = value.astype(BF)
        gate, up = value[:, :HALF], value[:, HALF:]
        value = gate * jax.nn.sigmoid(gate) * up
        hidden[:, pl.ds(pl.multiple_of(i * HALF, HALF), HALF)] = value.astype(BF)
        hidden_stage[i % 2] = value.T.astype(BF)
        for c in feed_copies(i):
            c.start()
        return carry

    tiles = inner.shape[1] // TILE
    lax.fori_loop(0, tiles, feed_step, 0)
    line.pass_on(2)
    for which in range(2):
        plane.relay(which)
    loads[1].wait()
    row = lax.broadcasted_iota(jnp.int32, (CHUNK, CHUNK), 0)
    col = lax.broadcasted_iota(jnp.int32, (CHUNK, CHUNK), 1)
    pairs = heads.shape[1] // (3 * HALF)

    def head_copies(h):
        at = pl.ds(pl.multiple_of(h * HALF, HALF), HALF)
        moves = ((q_buf, q_out), (k_buf, k_out), (v_buf, v_out), (att_buf, att_out), (lse_buf, lse_out))
        copies = [
            pltpu.make_async_copy(a.at[h % 2], b.at[:, at], head_sem.at[n, h % 2]) for n, (a, b) in enumerate(moves)
        ]
        return copies + [pltpu.make_async_copy(low_stage.at[h % 2], low_t.at[at], head_sem.at[5, h % 2])]

    def head_step(h, carry):
        @pl.when(h >= 2)
        def _():
            for c in head_copies(h - 2):
                c.wait()

        slot = h % 2
        mixed = contract(
            normed[...], heads[:, pl.ds(pl.multiple_of(h * 3 * HALF, HALF), 3 * HALF)], ((1,), (0,))
        )
        q = turn(mixed[:, :HALF], cos[...], first[...], second[...]).astype(BF).astype(F32)
        q_buf[slot] = (q * HD ** (-0.5)).astype(BF)
        k_buf[slot] = turn(mixed[:, HALF : 2 * HALF], cos[...], first[...], second[...]).astype(BF)
        v_buf[slot] = mixed[:, 2 * HALF :].astype(BF)
        for c in range(normed.shape[0] // CHUNK):
            lo, hi = c * CHUNK, (c + 1) * CHUNK
            for side in range(2):
                lanes = slice(side * HD, (side + 1) * HD)
                q = q_buf[slot, lo:hi, lanes]
                s = contract(q, k_buf[slot, lo:hi, lanes], ((1,), (1,)))
                s = jnp.where(col <= row, s, NEG)
                if c:
                    s = jnp.concatenate([contract(q, k_buf[slot, :lo, lanes], ((1,), (1,))), s], axis=1)
                top = jnp.max(s, axis=1, keepdims=True)
                p = jnp.exp(s - top)
                total = jnp.sum(p, axis=1, keepdims=True)
                o = contract(p.astype(BF), v_buf[slot, :hi, lanes], ((1,), (0,)))
                att_buf[slot, lo:hi, lanes] = o / total
                lse_buf[slot, lo:hi, lanes] = jnp.broadcast_to(top + jnp.log(total), (CHUNK, HD))
        att = att_buf[slot]
        low[:, pl.ds(pl.multiple_of(h * HALF, HALF), HALF)] = att.astype(BF)
        low_stage[slot] = att.T.astype(BF)
        for c in head_copies(h):
            c.start()
        return carry

    lax.fori_loop(0, pairs // 2, head_step, 0)
    for which in range(2):
        plane.last(which)
    line.pass_on(3)
    lax.fori_loop(pairs // 2, pairs, head_step, 0)
    for which in range(2):
        plane.finish(which)
    for c in own_copies:
        c.wait()

    def tile_copies(i):
        at = pl.ds(pl.multiple_of(i * TILE, TILE), TILE)
        return (
            pltpu.make_async_copy(down.at[:, :, at], down_tile.at[i % 2], tile_sem.at[0, i % 2]),
            pltpu.make_async_copy(attn.at[:, :, at], attn_tile.at[i % 2], tile_sem.at[1, i % 2]),
        )

    def branch_copy(i):
        at = pl.ds(pl.multiple_of(i * TILE, TILE), TILE)
        return pltpu.make_async_copy(branch_stage.at[i % 2], branch.at[:, :, at], branch_sem.at[i % 2])

    steps = branch.shape[2] // TILE
    for c in tile_copies(0):
        c.start()

    def branch_step(i, carry):
        @pl.when(i + 1 < steps)
        def _():
            for c in tile_copies(i + 1):
                c.start()

        for c in tile_copies(i):
            c.wait()

        @pl.when(i >= 2)
        def _():
            branch_copy(i - 2).wait()

        value = contract(hidden[...], down_tile[i % 2].reshape(hidden.shape[1], TILE), ((1,), (0,)))
        value = value + contract(low[...], attn_tile[i % 2].reshape(low.shape[1], TILE), ((1,), (0,)))
        term[...] = value.reshape(term.shape)
        for j in range(count):
            branch_stage[i % 2, j] = term[order[j]].astype(BF)
        branch_copy(i).start()
        return carry

    lax.fori_loop(0, steps, branch_step, 0)
    for hop in range(4, count + 1):
        line.pass_on(hop)
    line.finish()
    for back in range(2):
        for c in norm_copies(count - 1 - back) + feed_copies(tiles - 1 - back):
            c.wait()
        for c in head_copies(pairs - 1 - back):
            c.wait()
        branch_copy(steps - 1 - back).wait()


def forward(order, slots, x_all, gain, bias, tables, cot, w_down, w_out, w_inner, w_heads, shards):
    count, rows, width = x_all.shape
    length = count * rows
    ff_part, attn_part = w_down.shape[0] // count, w_out.shape[0] // count
    ff, cols = shards * ff_part, shards * attn_part
    dma = pltpu.SemaphoreType.DMA
    smem = pl.BlockSpec(memory_space=pltpu.SMEM)
    bf = lambda *shape: jax.ShapeDtypeStruct(shape, BF)
    f32 = lambda *shape: jax.ShapeDtypeStruct(shape, F32)
    out_shape = [
        bf(count, rows, width),
        bf(shards, ff_part, width),
        bf(shards, attn_part, width),
        bf(width, length),
        bf(length, width),
        bf(length, 2 * ff),
        bf(ff, length),
        bf(length, cols),
        bf(length, cols),
        bf(length, cols),
        f32(length, cols),
        bf(cols, length),
        f32(length, cols),
        bf(count, rows, width),
    ]
    return pl.pallas_call(
        forward_kernel,
        out_shape=out_shape,
        in_specs=[smem] * 2 + [vmem_whole()] * 6 + [hbm_whole()] * 5,
        out_specs=[hbm_whole()] * len(out_shape),
        scratch_shapes=[
            pltpu.VMEM(w_inner.shape, BF),
            pltpu.VMEM(w_heads.shape, BF),
            pltpu.VMEM((length, width), BF),
            pltpu.VMEM((length, ff), BF),
            pltpu.VMEM((length, cols), BF),
            pltpu.VMEM((2, rows, width), BF),
            pltpu.VMEM((2, width, rows), BF),
            pltpu.VMEM((2, length, TILE), BF),
            pltpu.VMEM((2, HALF, length), BF),
            pltpu.VMEM((2, length, HALF), BF),
            pltpu.VMEM((2, length, HALF), BF),
            pltpu.VMEM((2, length, HALF), BF),
            pltpu.VMEM((2, length, HALF), F32),
            pltpu.VMEM((2, HALF, length), BF),
            pltpu.VMEM((2, length, HALF), F32),
            pltpu.VMEM((2, shards, ff_part, TILE), BF),
            pltpu.VMEM((2, shards, attn_part, TILE), BF),
            pltpu.VMEM((count, rows, TILE), F32),
            pltpu.VMEM((2, count, rows, TILE), BF),
            dma((2,)),
            dma((2, count - 1)),
            dma((2, count - 1)),
            dma((2, 8)),
            dma((2, 8)),
            dma((3,)),
            dma((2, 2)),
            dma((2, 2)),
            dma((6, 2)),
            dma((2, 2)),
            dma((2,)),
        ],
        compiler_params=pltpu.CompilerParams(
            collective_id=3, has_side_effects=True, vmem_limit_bytes=58 * 2**20
        ),
        name="forward",
    )(order, slots, x_all, gain, bias, *tables, cot, w_down, w_out, w_inner, w_heads)


def feed_back_kernel(cot, down, attn, both, inner, d_att):
    d_att[...] = contract(cot[...], attn[...], ((1,), (1,))).astype(BF)
    d_hidden = contract(cot[...], down[...], ((1,), (1,)))
    for b in range(down.shape[0] // HALF):
        d = d_hidden[:, b * HALF : (b + 1) * HALF]
        gate = both[:, b * TILE : b * TILE + HALF].astype(F32)
        up = both[:, b * TILE + HALF : (b + 1) * TILE].astype(F32)
        sig = jax.nn.sigmoid(gate)
        inner[:, b * TILE : b * TILE + HALF] = (d * up * sig * (1.0 + gate * (1.0 - sig))).astype(BF)
        inner[:, b * TILE + HALF : (b + 1) * TILE] = (d * gate * sig).astype(BF)


def feed_back(cot, down, attn, both):
    length, width = cot.shape
    rows = length // 4
    whole = lambda a: pl.BlockSpec(a.shape, lambda i: (0, 0))
    by_rows = lambda columns: pl.BlockSpec((rows, columns), lambda i: (i, 0))
    return pl.pallas_call(
        feed_back_kernel,
        grid=(length // rows,),
        in_specs=[by_rows(width), whole(down), whole(attn), by_rows(both.shape[1])],
        out_specs=[by_rows(both.shape[1]), by_rows(attn.shape[0])],
        out_shape=[
            jax.ShapeDtypeStruct(both.shape, BF),
            jax.ShapeDtypeStruct((length, attn.shape[0]), BF),
        ],
        compiler_params=pltpu.CompilerParams(vmem_limit_bytes=50 * 2**20),
        cost_estimate=pl.CostEstimate(
            flops=2 * length * width * (down.shape[0] + attn.shape[0]), bytes_accessed=2**25, transcendentals=2**20
        ),
        name="feed_back",
    )(cot, down, attn, both)


def heads_back_kernel(q_in, k_in, v_in, do_in, att, lse, cos, first, second, out, dk, dv):
    length = q_in.shape[0]
    scale = HD ** (-0.5)
    row = lax.broadcasted_iota(jnp.int32, (CHUNK, CHUNK), 0)
    col = lax.broadcasted_iota(jnp.int32, (CHUNK, CHUNK), 1)
    dk[...] = jnp.zeros_like(dk)
    dv[...] = jnp.zeros_like(dv)
    for c in range(length // CHUNK):
        lo, hi = c * CHUNK, (c + 1) * CHUNK
        dqs = []
        for h in range(2):
            lanes = slice(h * HD, (h + 1) * HD)
            q, do = q_in[lo:hi, lanes], do_in[lo:hi, lanes]
            delta = jnp.sum(do.astype(F32) * att[lo:hi, lanes], axis=1, keepdims=True)
            s = contract(q, k_in[lo:hi, lanes], ((1,), (1,)))
            s = jnp.where(col <= row, s, NEG)
            if c:
                s = jnp.concatenate([contract(q, k_in[:lo, lanes], ((1,), (1,))), s], axis=1)
            p = jnp.exp(s - lse[lo:hi, h * HD : h * HD + 1])
            dp = contract(do, v_in[:hi, lanes], ((1,), (1,)))
            ds = (p * (dp - delta)).astype(BF)
            dqs.append(contract(ds, k_in[:hi, lanes], ((1,), (0,))) * scale)
            dk[:hi, lanes] += contract(ds, q, ((0,), (0,)))
            dv[:hi, lanes] += contract(p.astype(BF), do, ((0,), (0,)))
        dq = jnp.concatenate(dqs, axis=1)
        out[lo:hi, :HALF] = turn(dq, cos[lo:hi, :], -first[lo:hi, :], -second[lo:hi, :]).astype(BF)
    out[:, HALF : 2 * HALF] = turn(dk[...], cos[...], -first[...], -second[...]).astype(BF)
    out[:, 2 * HALF :] = dv[...].astype(BF)


def heads_back(q, k, v, d_attended, attended, lse, tables):
    length, width = q.shape
    heads = width // HD
    block = pl.BlockSpec((length, HALF), lambda h: (0, h))
    table = pl.BlockSpec((length, HALF), lambda h: (0, 0))
    return pl.pallas_call(
        heads_back_kernel,
        grid=(heads // 2,),
        in_specs=[block] * 6 + [table] * 3,
        out_specs=pl.BlockSpec((length, 3 * HALF), lambda h: (0, h)),
        out_shape=jax.ShapeDtypeStruct((length, 3 * width), BF),
        scratch_shapes=[pltpu.VMEM((length, HALF), F32)] * 2,
        compiler_params=pltpu.CompilerParams(vmem_limit_bytes=40 * 2**20),
        cost_estimate=pl.CostEstimate(
            flops=40 * heads * length * length * HD // 2,
            bytes_accessed=22 * length * width,
            transcendentals=heads * length * length // 2,
        ),
        name="heads_back",
    )(q, k, v, d_attended, attended, lse, *tables)


def norm_back_kernel(slots, d_inner, inner, d_mixed, heads, hat, out, small):
    value = contract(d_inner[...], inner[...], ((1,), (1,))) + contract(d_mixed[...], heads[...], ((1,), (1,)))
    count, rows = out.shape[0], out.shape[1]
    for p in range(count):
        out[slots[p]] = value[p * rows : (p + 1) * rows].astype(BF)
    gain = jnp.sum(value * hat[...].astype(F32), axis=0, keepdims=True)
    bias = jnp.sum(value, axis=0, keepdims=True)
    row = lax.broadcasted_iota(jnp.int32, small.shape, 0)
    small[...] = jnp.where(row == 0, gain, jnp.where(row == 1, bias, 0.0)).astype(BF)


def norm_back(slots, d_inner, inner, d_mixed, heads, hat, count):
    length, width = hat.shape
    whole = lambda a: pl.BlockSpec(a.shape, lambda i, s: (0, 0))
    by_rows = lambda a: pl.BlockSpec((TILE, a.shape[1]), lambda i, s: (i, 0))
    return pl.pallas_call(
        norm_back_kernel,
        grid_spec=pltpu.PrefetchScalarGridSpec(
            num_scalar_prefetch=1,
            grid=(width // TILE,),
            in_specs=[
                whole(d_inner),
                by_rows(inner),
                whole(d_mixed),
                by_rows(heads),
                pl.BlockSpec((length, TILE), lambda i, s: (0, i)),
            ],
            out_specs=[
                pl.BlockSpec((count, length // count, TILE), lambda i, s: (0, 0, i)),
                pl.BlockSpec((16, TILE), lambda i, s: (0, i)),
            ],
        ),
        out_shape=[
            jax.ShapeDtypeStruct((count, length // count, width), BF),
            jax.ShapeDtypeStruct((16, width), BF),
        ],
        compiler_params=pltpu.CompilerParams(vmem_limit_bytes=50 * 2**20),
        cost_estimate=pl.CostEstimate(
            flops=2 * length * width * (d_inner.shape[1] + d_mixed.shape[1]), bytes_accessed=2**25, transcendentals=0
        ),
        name="norm_back",
    )(slots, d_inner, inner, d_mixed, heads, hat)


def rows_of(shard, part):
    return slice(shard * part, (shard + 1) * part)


def gradients_kernel(
    hid_t, att_t, cot, norm_t, d_inner, d_mixed, small, branch, d_normed, pieces, sums,
    partial, theirs, pair, landed, total,
    sum_from, sum_land,
    core_send, core_recv, chip_send, chip_recv, line_send, line_recv, own_sem, sum_send, sum_recv,
):
    count = pieces.shape[0]
    chunks = pieces.shape[1]
    shards = 2 * partial.shape[1]
    chips = shards // 2
    place, me = lax.axis_index("ctx"), lax.axis_index("fsdp")
    chip, core = me // 2, me % 2
    ff_part, attn_part = hid_t.shape[0] // shards, att_t.shape[0] // shards
    cot_chunks = cot.shape[1] // TILE
    inner_chunks = d_inner.shape[1] // TILE
    sum_parts = branch.shape[2] // TILE

    def core_copy(i):
        return pltpu.make_async_remote_copy(
            src_ref=partial.at[i % 2, :, 1 - core],
            dst_ref=theirs.at[i % DEEP],
            send_sem=core_send.at[i % 2],
            recv_sem=core_recv.at[i % DEEP],
            device_id=(place, me + 1 - 2 * core),
            device_id_type=MESH,
        )

    def chip_of(m):
        return chip_away(chip, m)

    def chip_copy(j, m):
        return pltpu.make_async_remote_copy(
            src_ref=pair.at[j % 2, chip_of(m)],
            dst_ref=landed.at[j % DEEP, m - 1],
            send_sem=chip_send.at[j % 2, m - 1],
            recv_sem=chip_recv.at[j % DEEP, m - 1],
            device_id=(place, 2 * chip_of(m) + core),
            device_id_type=MESH,
        )

    def line_copy(way, hop, k):
        ahead = 1 - 2 * way
        origin = place - (hop - 1) * ahead
        return pltpu.make_async_remote_copy(
            src_ref=total.at[k % DEEP] if hop == 1 else pieces.at[origin, k],
            dst_ref=pieces.at[origin, k],
            send_sem=line_send.at[way, hop - 1, k % DEEP],
            recv_sem=line_recv.at[way, k, hop - 1],
            device_id=(place + ahead, me),
            device_id_type=MESH,
        )

    def sends(way, hop):
        if way == 0:
            return (place >= hop - 1) & (place <= count - 2)
        return (place <= count - hop) & (place >= 1)

    def lands(way, hop):
        return place >= hop if way == 0 else place <= count - 1 - hop

    def forward(hop, k):
        for way in range(2):
            if hop > 1:
                @pl.when(lands(way, hop - 1))
                def _():
                    line_copy(way, hop - 1, k).wait_recv()

            if hop < count:
                @pl.when(sends(way, hop))
                def _():
                    @pl.when(k >= DEEP)
                    def _():
                        line_copy(way, hop, k - DEEP).wait_send()

                    line_copy(way, hop, k).start()

    def sum_copy(way, t, q):
        return pltpu.make_async_remote_copy(
            src_ref=sum_from.at[way, t - 1, q % 2],
            dst_ref=sum_land.at[way, t - 1, q],
            send_sem=sum_send.at[way, t - 1, q % 2],
            recv_sem=sum_recv.at[way, t - 1, q],
            device_id=(place + 1 - 2 * way, me),
            device_id_type=MESH,
        )

    def sum_sends(way, t):
        return place <= t - 1 if way == 0 else place >= count - t

    def both_terms(q, use):
        for which, terms in enumerate((branch, d_normed)):
            at = (q - which * sum_parts) * TILE

            @pl.when((q >= which * sum_parts) & (q < (which + 1) * sum_parts))
            def _(which=which, terms=terms, at=at):
                use(which, terms, pl.ds(pl.multiple_of(at, TILE), TILE))

    def sum_step(t, q):
        for way in range(2):
            @pl.when(sum_sends(way, t))
            def _(way=way):
                to = count - t + place if way == 0 else t + place - count
                first = place == 0 if way == 0 else place == count - 1

                @pl.when(q >= 2)
                def _():
                    sum_copy(way, t, q - 2).wait_send()

                @pl.when(first)
                def _():
                    def use(which, terms, at):
                        sum_from[way, t - 1, q % 2] = terms[to, :, at]

                    both_terms(q, use)

                if t > 1:
                    @pl.when(jnp.logical_not(first))
                    def _():
                        sum_copy(way, t - 1, q).wait_recv()

                        def use(which, terms, at):
                            value = terms[to, :, at].astype(F32) + sum_land[way, t - 2, q].astype(F32)
                            sum_from[way, t - 1, q % 2] = value.astype(BF)

                        both_terms(q, use)

                sum_copy(way, t, q).start()

    def sum_end(q):
        def use(which, terms, at):
            sums[which, :, at] = terms[place, :, at].astype(F32)

        both_terms(q, use)
        for way in range(2):
            @pl.when(place >= 1 if way == 0 else place <= count - 2)
            def _(way=way):
                sum_copy(way, count - 1, q).wait_recv()

                def use(which, terms, at):
                    sums[which, :, at] += sum_land[way, count - 2, q].astype(F32)

                both_terms(q, use)

    def own_copy(k):
        return pltpu.make_async_copy(total.at[k % DEEP], pieces.at[place, k], own_sem.at[k % DEEP])

    partners = [(place, me + 1 - 2 * core)]
    partners += [(place, 2 * chip_of(m) + core) for m in range(1, chips)]
    partners += [((place + 1) % count, me), ((place + count - 1) % count, me)]
    barrier = pltpu.get_barrier_semaphore()
    for partner in partners:
        pl.semaphore_signal(barrier, inc=1, device_id=partner, device_id_type=MESH)
    pl.semaphore_wait(barrier, len(partners))
    def store(i, shard, lo, value):
        partial[i % 2, shard // 2, shard % 2, lo : lo + value.shape[0], :] = value

    def from_norm(i, rhs):
        for s in range(0, shards, 2):
            rows = norm_t.shape[0] // shards
            value = contract(norm_t[s * rows : (s + 2) * rows, :], rhs, ((1,), (0,))).astype(BF)
            store(i, s, 0, value[:rows])
            store(i, s + 1, 0, value[rows:])

    def step(i, carry):
        @pl.when(i < cot_chunks)
        def _():
            rhs = cot[:, pl.ds(pl.multiple_of(i * TILE, TILE), TILE)]
            for s in range(0, shards, 4):
                value = contract(hid_t[s * ff_part : (s + 4) * ff_part, :], rhs, ((1,), (0,))).astype(BF)
                for t in range(4):
                    store(i, s + t, 0, value[rows_of(t, ff_part)])
            value = contract(att_t[...], rhs, ((1,), (0,))).astype(BF)
            for s in range(shards):
                store(i, s, ff_part, value[rows_of(s, attn_part)])
                store(i, s, ff_part + attn_part, small[:, s * TILE : (s + 1) * TILE])

        @pl.when((i >= cot_chunks) & (i < cot_chunks + inner_chunks))
        def _():
            at = pl.ds(pl.multiple_of((i - cot_chunks) * TILE, TILE), TILE)
            from_norm(i, d_inner[:, at])

        @pl.when((i >= cot_chunks + inner_chunks) & (i < chunks))
        def _():
            at = pl.multiple_of((i - cot_chunks - inner_chunks) * TILE, TILE)
            from_norm(i, d_mixed[:, pl.ds(at, TILE)])

        @pl.when(i < chunks)
        def _():
            core_copy(i).start()

        @pl.when((i >= 1) & (i < chunks + 1))
        def _():
            j = i - 1
            core_copy(j).wait()
            for m in range(chips):
                a = partial[j % 2, m, core].astype(F32) + theirs[j % DEEP, m].astype(F32)
                pair[j % 2, m] = a.astype(BF)
            for m in range(1, chips):
                chip_copy(j, m).start()

        @pl.when((i >= 2) & (i < chunks + 2))
        def _():
            k = i - 2
            for m in range(1, chips):
                chip_copy(k, m).wait()

            a = pair[k % 2, chip].astype(F32)
            for m in range(1, chips):
                a = a + landed[k % DEEP, m - 1].astype(F32)
            for way in range(2):
                @pl.when(sends(way, 1) & (k >= DEEP))
                def _():
                    line_copy(way, 1, k - DEEP).wait_send()

            @pl.when(k >= DEEP)
            def _():
                own_copy(k - DEEP).wait()

            total[k % DEEP] = a.astype(BF)
            for way in range(2):
                @pl.when(sends(way, 1))
                def _():
                    line_copy(way, 1, k).start()

            own_copy(k).start()

        for t in range(1, count + 1):
            q = i - LAG * (t - 1)

            @pl.when((q >= 0) & (q < 2 * sum_parts))
            def _(q=q, t=t):
                if t < count:
                    sum_step(t, q)
                else:
                    sum_end(q)

        for hop in range(2, count + 1):
            k = i - 2 - LAG * (hop - 1)

            @pl.when((k >= 0) & (k < chunks))
            def _(k=k, hop=hop):
                forward(hop, k)

        return carry

    lax.fori_loop(0, chunks + 2 + LAG * (count - 1), step, 0)

    def drain(k, carry):
        own_copy(k).wait()
        for way in range(2):
            for hop in range(1, count):
                @pl.when(sends(way, hop))
                def _():
                    line_copy(way, hop, k).wait_send()
        return carry

    lax.fori_loop(chunks - DEEP, chunks, drain, 0)
    for way in range(2):
        for t in range(1, count):
            @pl.when(sum_sends(way, t))
            def _(way=way, t=t):
                for q in range(2):
                    sum_copy(way, t, 2 * sum_parts - 2 + q).wait_send()


def gradients(hid_t, att_t, cot, norm_t, d_inner, d_mixed, small, branch, d_normed, count, shards):
    chips = shards // 2
    chunks = (cot.shape[1] + d_inner.shape[1] + d_mixed.shape[1]) // TILE
    rows = norm_t.shape[0] // shards
    dma = pltpu.SemaphoreType.DMA
    own_rows, width = branch.shape[1:]
    parts = 2 * width // TILE
    return pl.pallas_call(
        gradients_kernel,
        out_shape=[
            jax.ShapeDtypeStruct((count, chunks, rows, TILE), BF),
            jax.ShapeDtypeStruct((2, own_rows, width), F32),
        ],
        in_specs=[vmem_whole()] * 9,
        out_specs=[hbm_whole(), vmem_whole()],
        scratch_shapes=[
            pltpu.VMEM((2, chips, 2, rows, TILE), BF),
            pltpu.VMEM((DEEP, chips, rows, TILE), BF),
            pltpu.VMEM((2, chips, rows, TILE), BF),
            pltpu.VMEM((DEEP, chips - 1, rows, TILE), BF),
            pltpu.VMEM((DEEP, rows, TILE), BF),
            pltpu.VMEM((2, count - 1, 2, own_rows, TILE), BF),
            pltpu.VMEM((2, count - 1, parts, own_rows, TILE), BF),
            dma((2,)),
            dma((DEEP,)),
            dma((2, chips - 1)),
            dma((DEEP, chips - 1)),
            dma((2, count - 1, DEEP)),
            dma((2, chunks, count - 1)),
            dma((DEEP,)),
            dma((2, count - 1, 2)),
            dma((2, count - 1, parts)),
        ],
        compiler_params=pltpu.CompilerParams(
            collective_id=1, has_side_effects=True, vmem_limit_bytes=60 * 2**20
        ),
        cost_estimate=pl.CostEstimate(
            flops=2 * norm_t.shape[0] * norm_t.shape[1] * TILE * chunks, bytes_accessed=2**27, transcendentals=0
        ),
        name="gradients",
    )(hid_t, att_t, cot, norm_t, d_inner, d_mixed, small, branch, d_normed)


def column_runs(columns, source):
    out = []
    for block in range(columns // HALF):
        first = 0
        while first < HALF:
            key, lane = source(block * HALF + first)
            last = first + 1
            while last < HALF and source(block * HALF + last) == (key, lane + last - first):
                last += 1
            out.append((block, first, last, key, (first - lane) % HALF))
            first = last
    return out


def assemble_kernel(down_chunks, rows_in, cols_in, qkv_out, gate_out, up_out, down_out, attn_out, small_out):
    count, chunks, rows, _ = rows_in.shape
    cot_chunks_static = down_chunks
    ff = gate_out.shape[1]
    width = qkv_out.shape[1]
    ff_part = down_out.shape[0] // count
    attn_part = attn_out.shape[0] // count
    shards = ff // (count * ff_part)
    inner_chunks = ff // count // HALF
    lane = lax.broadcasted_iota(jnp.int32, (rows, HALF), 1)

    def gather(out, runs, load):
        for block, first, last, key, shift in runs:
            value = load(key).astype(F32)
            if shift:
                value = pltpu.roll(value, shift, 1)
            if first:
                value = jnp.where(lane >= first, value, held)
            held = value
            if last == HALF:
                out[:, block * HALF : (block + 1) * HALF] = value

    def inner_source(column):
        shard, rest = divmod(column, count * ff_part)
        unit = shard * ff_part + rest % ff_part
        return (rest // ff_part, unit // HALF), unit % HALF

    def head_source(column):
        part, rest = divmod(column, width // 3)
        head, dim = divmod(rest, HD)
        per = width // 3 // HD // shards // count
        shard, at = divmod(head, per * count)
        place, sub = divmod(at, per)
        pair, half = divmod(shard * per + sub, 2)
        return (place, 3 * pair + part), half * HD + dim

    runs = column_runs(ff, inner_source)
    gather(gate_out, runs, lambda key: rows_in[key[0], cot_chunks_static + key[1], :, :HALF])
    gather(up_out, runs, lambda key: rows_in[key[0], cot_chunks_static + key[1], :, HALF:])
    first_head = cot_chunks_static + inner_chunks

    def head_load(key):
        at = key[1] % 2 * HALF
        return rows_in[key[0], first_head + key[1] // 2, :, at : at + HALF]

    gather(qkv_out, column_runs(width, head_source), head_load)
    for p in range(count):
        down_out[p * ff_part : (p + 1) * ff_part, :] = cols_in[p, 0, :ff_part, :].astype(F32)
        attn_out[p * attn_part : (p + 1) * attn_part, :] = cols_in[
            p, 0, ff_part : ff_part + attn_part, :
        ].astype(F32)
    small = [cols_in[p, 0, ff_part + attn_part :, :].astype(F32) for p in range(count)]
    small_out[...] = functools.reduce(jnp.add, small)


def assemble_outputs(pieces, qkv, attn, gate, down):
    count, chunks, rows, _ = pieces.shape
    steps = down[1] // TILE
    part = rows // steps
    by_rows = lambda shape: pl.BlockSpec((part, shape[1]), lambda i: (i, 0))
    by_cols = lambda shape: pl.BlockSpec((shape[0], TILE), lambda i: (0, i))
    return pl.pallas_call(
        functools.partial(assemble_kernel, steps),
        grid=(steps,),
        in_specs=[
            pl.BlockSpec((count, chunks, part, TILE), lambda i: (0, 0, i, 0)),
            pl.BlockSpec((count, 1, rows, TILE), lambda i: (0, i, 0, 0)),
        ],
        out_specs=[by_rows(qkv), by_rows(gate), by_rows(gate), by_cols(down), by_cols(attn)]
        + [pl.BlockSpec((16, TILE), lambda i: (0, 0))],
        out_shape=[jax.ShapeDtypeStruct(s, F32) for s in (qkv, gate, gate, down, attn, (16, TILE))],
        compiler_params=pltpu.CompilerParams(vmem_limit_bytes=40 * 2**20),
        name="assemble",
    )(pieces, pieces)


def rotation_tables(length):
    half = ROT // 2
    inverse = 10000.0 ** (-jnp.arange(half, dtype=F32) / half)
    grid = jnp.arange(length, dtype=jnp.int32).astype(F32)[:, None] * inverse[None, :]
    cos, sin = jnp.cos(grid), jnp.sin(grid)
    zero = jnp.zeros((length, half), F32)
    rest = jnp.zeros((length, HD - ROT), F32)
    tables = (
        jnp.concatenate([cos, cos, rest + 1.0], axis=1),
        jnp.concatenate([-sin, zero, rest], axis=1),
        jnp.concatenate([zero, sin, rest], axis=1),
    )
    return tuple(jnp.tile(t, (1, 2)) for t in tables)


def body_general(tokens, block_order, ln_gain, ln_bias, w_qkv, w_out, w_gate, w_up, w_down, cotangent):
    rows, width = tokens.shape[1], tokens.shape[2]
    count = lax.axis_size("ctx")
    shards = lax.axis_size("fsdp")
    place = lax.axis_index("ctx")
    length = rows * count
    order = block_order[0]
    shard_rows = w_qkv.shape[0]
    ff_shard = w_down.shape[0]
    ff_part = ff_shard // count
    own_heads = H // count
    spread = (w_out.shape[0] // HD) % count == 0
    groups = shards if spread else 1
    head_cols = own_heads * HD // groups

    def my_cols(w, outer, group, part):
        w = w.reshape(w.shape[0], outer, group, count, part)
        return lax.dynamic_index_in_dim(w, place, 3, False).reshape(w.shape[0], outer * group * part)

    def all_cols(piece, outer, group, part):
        whole = gather_ctx(piece).reshape(count, piece.shape[0], outer, group, part)
        return whole.transpose(1, 2, 3, 0, 4).reshape(piece.shape[0], -1).astype(F32)

    def assemble(block, ready=None):
        whole = jnp.zeros((length, width), block.dtype)
        whole = lax.dynamic_update_slice_in_dim(whole, block, order[place] * rows, 0)
        last = None
        for k in range(1, count):
            last = ring_send(block, k)
            source = (place - k) % count
            whole = lax.dynamic_update_slice_in_dim(whole, last, order[source] * rows, 0)
        return whole, last

    gain = lax.all_gather(ln_gain, "fsdp", axis=0, tiled=True).astype(F32)
    bias = lax.all_gather(ln_bias, "fsdp", axis=0, tiled=True).astype(F32)
    tables = rotation_tables(length)

    block = tokens[0]
    x_all, arrived = assemble(block)
    grad_block = cotangent[0]
    cot_all, _ = assemble(after(grad_block, arrived))

    inner = jnp.concatenate(
        [my_cols(w_gate, 1, shards, ff_part), my_cols(w_up, 1, shards, ff_part)], axis=1
    )
    w_inner, sent = gather_rows(inner)
    w_heads, sent = gather_rows(after(my_cols(w_qkv, 3, groups, head_cols), sent))
    down = lax.dynamic_slice_in_dim(w_down, place * ff_part, ff_part, 0)
    w_hidden, sent = gather_rows(after(down, sent))
    if spread:
        part = w_out.shape[0] // count
        attn = lax.dynamic_slice_in_dim(w_out, place * part, part, 0)
        w_attn, sent = gather_rows(after(attn, sent))
    else:
        w_attn = lax.all_gather(after(w_out, sent), "fsdp", axis=0, tiled=True)
        w_attn = lax.dynamic_slice_in_dim(w_attn, place * own_heads * HD, own_heads * HD, 0)

    xf = x_all.astype(F32)
    average = jnp.mean(xf, axis=-1, keepdims=True)
    centered = xf - average
    variance = jnp.mean(centered * centered, axis=-1, keepdims=True)
    inv_std = lax.rsqrt(variance + EPS)
    x_hat = centered * inv_std
    normed = (x_hat * gain + bias).astype(BF)

    across = ((1,), (0,))
    over_tokens = ((0,), (0,))
    back = ((1,), (1,))
    ff_cols = shards * ff_part
    gate_value = dot(normed, w_inner[:, :ff_cols], across)
    up_value = dot(normed, w_inner[:, ff_cols:], across)
    sigmoid_gate = jax.nn.sigmoid(gate_value)
    hidden = (gate_value * sigmoid_gate * up_value).astype(BF)
    mixed = dot(normed, w_heads, across)
    q, k, v, attended, lse = attend(mixed, tables, own_heads)
    attended_low = attended.astype(BF)

    branch = dot(attended_low, w_attn, across) + dot(hidden, w_hidden, across)
    out = line_scatter(lambda j: lax.dynamic_slice_in_dim(branch, order[j] * rows, rows, 0))
    out = (block.astype(F32) + out).astype(BF)[None]

    d_hidden = dot(cot_all, w_hidden, back)
    grad_down = scatter_rows(dot(hidden, cot_all, over_tokens, BF))
    d_gate_act = (
        d_hidden * up_value * sigmoid_gate * (1.0 + gate_value * (1.0 - sigmoid_gate))
    ).astype(BF)
    d_up_act = (d_hidden * gate_value * sigmoid_gate).astype(BF)
    d_inner = jnp.concatenate([d_gate_act, d_up_act], axis=1)
    d_attended = dot(cot_all, w_attn, back, BF)
    d_mixed = attend_back(q, k, v, d_attended, attended, lse, tables, own_heads)
    d_mixed = jnp.concatenate(d_mixed, axis=1)
    grad_inner = scatter_rows(dot(normed, d_inner, over_tokens, BF))
    grad_attn = dot(attended_low, cot_all, over_tokens, BF)
    grad_heads = scatter_rows(dot(normed, d_mixed, over_tokens, BF))

    d_normed = dot(d_inner, w_inner, back) + dot(d_mixed, w_heads, back)
    small = jnp.stack([jnp.sum(d_normed * x_hat, axis=0), jnp.sum(d_normed, axis=0)])
    small = lax.psum(small, ("ctx", "fsdp"))
    small = lax.dynamic_slice_in_dim(small, lax.axis_index("fsdp") * shard_rows, shard_rows, 1)
    d_own = line_scatter(lambda j: lax.dynamic_slice_in_dim(d_normed, order[j] * rows, rows, 0))
    own = block.astype(F32)
    own_average = jnp.mean(own, axis=-1, keepdims=True)
    own = own - own_average
    own_std = lax.rsqrt(jnp.mean(own * own, axis=-1, keepdims=True) + EPS)
    own = own * own_std
    scaled = d_own * gain
    d_input = own_std * (
        scaled
        - jnp.mean(scaled, axis=-1, keepdims=True)
        - own * jnp.mean(scaled * own, axis=-1, keepdims=True)
    )
    grad_in = (grad_block.astype(F32) + d_input)[None]

    down_all = gather_ctx(grad_down).reshape(ff_shard, width).astype(F32)
    if spread:
        attn_all = gather_ctx(scatter_rows(grad_attn)).reshape(w_out.shape).astype(F32)
    else:
        full = jnp.zeros((H * HD, width), BF)
        full = lax.dynamic_update_slice_in_dim(full, grad_attn, place * own_heads * HD, 0)
        full = lax.psum_scatter(full, "fsdp", scatter_dimension=0, tiled=True)
        attn_all = lax.psum(full, "ctx").astype(F32)
    heads_all = all_cols(grad_heads, 3, groups, head_cols)
    inner_all = gather_ctx(grad_inner).reshape(count, shard_rows, 2, shards, ff_part)
    inner_all = inner_all.transpose(2, 1, 3, 0, 4).reshape(2, shard_rows, -1).astype(F32)
    return (
        out,
        grad_in,
        small[0],
        small[1],
        heads_all,
        attn_all,
        inner_all[0],
        inner_all[1],
        down_all,
    )


def body_fast(tokens, block_order, ln_gain, ln_bias, w_qkv, w_out, w_gate, w_up, w_down, cotangent):
    count, shards = lax.axis_size("ctx"), lax.axis_size("fsdp")
    place = lax.axis_index("ctx")
    block, grad_block = tokens[0], cotangent[0]
    rows, width = block.shape
    order = block_order[0]
    spots = jnp.arange(count, dtype=jnp.int32)
    slots = jnp.sum(jnp.where(order[None, :] == spots[:, None], spots[None, :], 0), axis=1)
    vectors = jnp.stack([ln_gain, ln_bias] + [jnp.zeros_like(ln_gain)] * 6).astype(F32)
    x_all, vectors, w_inner, w_heads = start(block, vectors, w_gate, w_up, w_qkv, count, shards)
    w_inner = w_inner.reshape(width, -1)
    w_heads = w_heads.reshape(width, -1)
    gain, bias = vectors[:, 0].reshape(1, width), vectors[:, 1].reshape(1, width)
    tables = rotation_tables(rows * count)

    (
        cot_all, w_hidden, w_attn, normed_t, hat, both, hidden_t, q, k, v, attended, low_t, lse, branch,
    ) = forward(
        order, slots, x_all, gain, bias, tables, grad_block, w_down, w_out, w_inner, w_heads, shards
    )
    cot_all = [lax.dynamic_index_in_dim(cot_all, slots[p], 0, False) for p in range(count)]
    cot_all = jnp.concatenate(cot_all, axis=0)
    w_hidden, w_attn = w_hidden.reshape(-1, width), w_attn.reshape(-1, width)
    d_inner, d_attended = feed_back(cot_all, w_hidden, w_attn, both)
    d_mixed = heads_back(q, k, v, d_attended, attended, lse, tables)
    d_normed, small = norm_back(slots, d_inner, w_inner, d_mixed, w_heads, hat, count)
    pieces, sums = gradients(
        hidden_t, low_t, cot_all, normed_t, d_inner, d_mixed, small, branch, d_normed, count, shards
    )
    d_qkv, d_gate, d_up, d_down, d_attn, small = assemble_outputs(
        pieces, w_qkv.shape, w_out.shape, w_gate.shape, w_down.shape
    )
    own = block.astype(F32)
    out = (own + sums[0]).astype(BF)[None]
    own = own - jnp.mean(own, axis=-1, keepdims=True)
    own_std = lax.rsqrt(jnp.mean(own * own, axis=-1, keepdims=True) + EPS)
    own = own * own_std
    scaled = sums[1] * gain
    d_input = own_std * (
        scaled
        - jnp.mean(scaled, axis=-1, keepdims=True)
        - own * jnp.mean(scaled * own, axis=-1, keepdims=True)
    )
    grad_in = (grad_block.astype(F32) + d_input)[None]
    return out, grad_in, small[0], small[1], d_qkv, d_attn, d_gate, d_up, d_down


def solution(mesh):
    whole, once = P("fsdp", "ctx", None), P("fsdp", None)
    count, shards = mesh.shape["ctx"], mesh.shape["fsdp"]

    def body(*args):
        w_out, w_down = args[5], args[8]
        fits = shards == 8 and w_out.shape[0] == count * HD and w_out.shape[0] == TILE
        fits = fits and w_down.shape[0] % (16 * count) == 0 and w_down.shape[0] // count <= 176
        return (body_fast if fits else body_general)(*args)

    return jax.shard_map(
        body,
        mesh=mesh,
        in_specs=(whole, once, P("fsdp"), P("fsdp")) + (once,) * 5 + (whole,),
        out_specs=(whole, whole, P("fsdp"), P("fsdp")) + (once,) * 5,
        check_vma=False,
    )
```

```python
import functools

import jax
import jax.numpy as jnp
from jax import lax
from jax.experimental import pallas as pl
from jax.experimental.pallas import tpu as pltpu
from jax.sharding import PartitionSpec as P

H = 32
HD = 64
ROT = 16
EPS = 1e-05
NEG = -1e30
CHUNK = 256

BF = jnp.bfloat16
F32 = jnp.float32


def xor_send(value, mask):
    count = lax.axis_size("fsdp")
    return lax.ppermute(value, "fsdp", [(i, i ^ mask) for i in range(count)])


def ring_send(value, steps):
    count = lax.axis_size("ctx")
    return lax.ppermute(value, "ctx", [(i, (i + steps) % count) for i in range(count)])


def after(value, *done):
    return lax.optimization_barrier((value,) + done)[0]


def dot(a, b, dims, out=F32):
    return lax.dot_general(a, b, (dims, ((), ())), preferred_element_type=F32).astype(out)


def gather_rows(piece):
    count = lax.axis_size("fsdp")
    chips = count // 2
    me = lax.axis_index("fsdp")
    chip, core = me // 2, me % 2
    parts = [piece] + [xor_send(piece, 2 * m) for m in range(1, chips)]
    others = [xor_send(p, 1) for p in parts]
    whole = jnp.zeros((count,) + piece.shape, piece.dtype)
    for m in range(chips):
        at = 2 * (chip ^ m)
        whole = lax.dynamic_update_index_in_dim(whole, parts[m], at + core, 0)
        whole = lax.dynamic_update_index_in_dim(whole, others[m], at + 1 - core, 0)
    return whole.reshape(count * piece.shape[0], piece.shape[1]), parts[-1]


def scatter_rows(grad):
    count = lax.axis_size("fsdp")
    chips = count // 2
    me = lax.axis_index("fsdp")
    chip, core = me // 2, me % 2
    rows = grad.shape[0] // count
    split = grad.reshape(chips, 2, rows, grad.shape[1])
    theirs = xor_send(lax.dynamic_index_in_dim(split, 1 - core, 1, False), 1)
    pair = lax.dynamic_index_in_dim(split, core, 1, False).astype(F32) + theirs.astype(F32)
    pair = pair.astype(BF)
    total = lax.dynamic_index_in_dim(pair, chip, 0, False).astype(F32)
    for m in range(1, chips):
        part = lax.dynamic_index_in_dim(pair, chip ^ m, 0, False)
        total = total + xor_send(part, 2 * m).astype(F32)
    return total.astype(BF)


def gather_ctx(piece):
    count = lax.axis_size("ctx")
    me = lax.axis_index("ctx")
    whole = jnp.zeros((count,) + piece.shape, piece.dtype)
    whole = lax.dynamic_update_index_in_dim(whole, piece, me, 0)
    for k in range(1, count):
        part = ring_send(piece, k)
        whole = lax.dynamic_update_index_in_dim(whole, part, (me - k) % count, 0)
    return whole


def line_scatter(blocks):
    count = lax.axis_size("ctx")
    me = lax.axis_index("ctx")
    down = up = None
    for t in range(1, count):
        to_down = blocks(jnp.clip(t + me - count, 0, count - 1))
        to_up = blocks(jnp.clip(count - 1 - (t + (count - 1 - me) - count), 0, count - 1))
        if down is not None:
            to_down = to_down + down.astype(F32)
            to_up = to_up + up.astype(F32)
        pairs = [(i, i - 1) for i in range(count - t, count)]
        down = lax.ppermute(to_down.astype(BF), "ctx", pairs)
        up = lax.ppermute(to_up.astype(BF), "ctx", [(count - 1 - i, count - 1 - j) for i, j in pairs])
    return blocks(me) + down.astype(F32) + up.astype(F32)


def turn(x, cos, first, second):
    width = x.shape[1]
    half = ROT // 2
    return x * cos + pltpu.roll(x, width - half, 1) * first + pltpu.roll(x, half, 1) * second


def contract(a, b, dims):
    return lax.dot_general(a, b, (dims, ((), ())), preferred_element_type=F32)


def attend_kernel(mq, mk, mv, cos, first, second, q_out, k_out, v_out, att_out, lse_out):
    length = mq.shape[0]
    scale = HD ** (-0.5)
    q_out[...] = (turn(mq[...], cos[...], first[...], second[...]).astype(BF).astype(F32) * scale).astype(BF)
    k_out[...] = turn(mk[...], cos[...], first[...], second[...]).astype(BF)
    v_out[...] = mv[...].astype(BF)
    row = lax.broadcasted_iota(jnp.int32, (CHUNK, CHUNK), 0)
    col = lax.broadcasted_iota(jnp.int32, (CHUNK, CHUNK), 1)
    for c in range(length // CHUNK):
        lo, hi = c * CHUNK, (c + 1) * CHUNK
        for h in range(2):
            lanes = slice(h * HD, (h + 1) * HD)
            q = q_out[lo:hi, lanes]
            s = contract(q, k_out[lo:hi, lanes], ((1,), (1,)))
            s = jnp.where(col <= row, s, NEG)
            if c:
                s = jnp.concatenate([contract(q, k_out[:lo, lanes], ((1,), (1,))), s], axis=1)
            top = jnp.max(s, axis=1, keepdims=True)
            p = jnp.exp(s - top)
            total = jnp.sum(p, axis=1, keepdims=True)
            o = contract(p.astype(BF), v_out[:hi, lanes], ((1,), (0,)))
            att_out[lo:hi, lanes] = o / total
            lse_out[lo:hi, lanes] = jnp.broadcast_to(top + jnp.log(total), (CHUNK, HD))


def attend(mixed, tables, heads):
    length = mixed.shape[0]
    pairs = heads // 2
    block = lambda at: pl.BlockSpec((length, 2 * HD), lambda h, at=at: (0, at + h))
    table = pl.BlockSpec((length, 2 * HD), lambda h: (0, 0))
    width = heads * HD
    return pl.pallas_call(
        attend_kernel,
        grid=(pairs,),
        in_specs=[block(0), block(pairs), block(2 * pairs), table, table, table],
        out_specs=[block(0)] * 5,
        out_shape=[jax.ShapeDtypeStruct((length, width), BF)] * 3
        + [jax.ShapeDtypeStruct((length, width), F32)] * 2,
        compiler_params=pltpu.CompilerParams(vmem_limit_bytes=40 * 2**20),
        cost_estimate=pl.CostEstimate(
            flops=16 * heads * length * length * HD // 2,
            bytes_accessed=26 * length * width,
            transcendentals=heads * length * length // 2,
        ),
        name="attend",
    )(mixed, mixed, mixed, *tables)


def attend_back_kernel(q_in, k_in, v_in, do_in, att, lse, cos, first, second, dq_out, dk_out, dv_out, dk, dv):
    length = q_in.shape[0]
    scale = HD ** (-0.5)
    row = lax.broadcasted_iota(jnp.int32, (CHUNK, CHUNK), 0)
    col = lax.broadcasted_iota(jnp.int32, (CHUNK, CHUNK), 1)
    dk[...] = jnp.zeros_like(dk)
    dv[...] = jnp.zeros_like(dv)
    for c in range(length // CHUNK):
        lo, hi = c * CHUNK, (c + 1) * CHUNK
        dqs = []
        for h in range(2):
            lanes = slice(h * HD, (h + 1) * HD)
            q, do = q_in[lo:hi, lanes], do_in[lo:hi, lanes]
            delta = jnp.sum(do.astype(F32) * att[lo:hi, lanes], axis=1, keepdims=True)
            s = contract(q, k_in[lo:hi, lanes], ((1,), (1,)))
            s = jnp.where(col <= row, s, NEG)
            if c:
                s = jnp.concatenate([contract(q, k_in[:lo, lanes], ((1,), (1,))), s], axis=1)
            p = jnp.exp(s - lse[lo:hi, h * HD : h * HD + 1])
            dp = contract(do, v_in[:hi, lanes], ((1,), (1,)))
            ds = (p * (dp - delta)).astype(BF)
            dqs.append(contract(ds, k_in[:hi, lanes], ((1,), (0,))) * scale)
            dk[:hi, lanes] += contract(ds, q, ((0,), (0,)))
            dv[:hi, lanes] += contract(p.astype(BF), do, ((0,), (0,)))
        dq = jnp.concatenate(dqs, axis=1)
        dq_out[lo:hi, :] = turn(dq, cos[lo:hi, :], -first[lo:hi, :], -second[lo:hi, :]).astype(BF)
    dk_out[...] = turn(dk[...], cos[...], -first[...], -second[...]).astype(BF)
    dv_out[...] = dv[...].astype(BF)


def attend_back(q, k, v, d_attended, attended, lse, tables, heads):
    length, width = q.shape
    block = pl.BlockSpec((length, 2 * HD), lambda h: (0, h))
    table = pl.BlockSpec((length, 2 * HD), lambda h: (0, 0))
    return pl.pallas_call(
        attend_back_kernel,
        grid=(heads // 2,),
        in_specs=[block] * 6 + [table] * 3,
        out_specs=[block] * 3,
        out_shape=[jax.ShapeDtypeStruct((length, width), BF)] * 3,
        scratch_shapes=[pltpu.VMEM((length, 2 * HD), F32)] * 2,
        compiler_params=pltpu.CompilerParams(vmem_limit_bytes=40 * 2**20),
        cost_estimate=pl.CostEstimate(
            flops=40 * heads * length * length * HD // 2,
            bytes_accessed=22 * length * width,
            transcendentals=heads * length * length // 2,
        ),
        name="attend_back",
    )(q, k, v, d_attended, attended, lse, *tables)


MESH = pl.DeviceIdType.MESH
TILE = 256
HALF = 128
DEEP = 4
LAG = 2


def vmem_whole():
    return pl.BlockSpec(memory_space=pltpu.VMEM)


def hbm_whole():
    return pl.BlockSpec(memory_space=pl.ANY)


def chip_away(chip, m):
    return 2 * ((chip // 2 + m // 2) % 2) + (chip + m) % 2


def inner_runs(shards, count, part):
    runs = []
    for block in range(shards * part // HALF):
        first = 0
        while first < HALF:
            shard, unit = divmod(block * HALF + first, part)
            last = min(HALF, first + part - unit)
            runs.append((block, first, last, shard * count * part + unit - first))
            first = last
    return runs


class Line:
    def __init__(self, own, whole, send, recv):
        self.own, self.whole, self.send, self.recv = own, whole, send, recv
        self.count = whole.shape[0]
        self.place, self.me = lax.axis_index("ctx"), lax.axis_index("fsdp")

    def copy(self, way, hop):
        ahead = 1 - 2 * way
        origin = self.place - (hop - 1) * ahead
        return pltpu.make_async_remote_copy(
            src_ref=self.own if hop == 1 else self.whole.at[origin],
            dst_ref=self.whole.at[origin],
            send_sem=self.send.at[way, hop - 1],
            recv_sem=self.recv.at[way, hop - 1],
            device_id=(self.place + ahead, self.me),
            device_id_type=MESH,
        )

    def sends(self, way, hop):
        if way == 0:
            return (self.place >= hop - 1) & (self.place <= self.count - 2)
        return (self.place <= self.count - hop) & (self.place >= 1)

    def lands(self, way, hop):
        return self.place >= hop if way == 0 else self.place <= self.count - 1 - hop

    def pass_on(self, hop):
        for way in range(2):
            if hop > 1:
                @pl.when(self.lands(way, hop - 1))
                def _(way=way):
                    self.copy(way, hop - 1).wait_recv()

            if hop < self.count:
                @pl.when(self.sends(way, hop))
                def _(way=way):
                    self.copy(way, hop).start()

    def finish(self):
        for way in range(2):
            for hop in range(1, self.count):
                @pl.when(self.sends(way, hop))
                def _(way=way, hop=hop):
                    self.copy(way, hop).wait_send()


class Plane:
    def __init__(self, mine, wholes, send, recv):
        self.mine, self.wholes, self.send, self.recv = mine, wholes, send, recv
        self.place, self.me = lax.axis_index("ctx"), lax.axis_index("fsdp")
        chip, core = self.me // 2, self.me % 2
        self.sibling = 2 * chip + 1 - core
        self.near = (2 * chip_away(chip, 1) + core, 2 * chip_away(chip, 2) + core)
        self.far = 2 * chip_away(chip, 3) + core

    def copy(self, which, kind, source, target, to):
        return pltpu.make_async_remote_copy(
            src_ref=source,
            dst_ref=target,
            send_sem=self.send.at[which, kind],
            recv_sem=self.recv.at[which, kind],
            device_id=(self.place, to),
            device_id_type=MESH,
        )

    def direct(self, which, a):
        return self.copy(which, a, self.mine[which], self.wholes[which].at[self.me], self.near[a])

    def across(self, which, a):
        half = self.wholes[which].shape[2] // 2
        piece = self.wholes[which].at[self.near[1 - a], :, a * half : (a + 1) * half]
        return self.copy(which, 2 + a, piece, piece, self.near[a])

    def beside(self, which, kind):
        source = (self.me, self.near[0], self.near[1], self.far)[kind]
        piece = self.wholes[which].at[source]
        return self.copy(which, 4 + kind, self.mine[which] if kind == 0 else piece, piece, self.sibling)

    def begin(self, which):
        for a in range(2):
            self.direct(which, a).start()
        self.beside(which, 0).start()

    def relay(self, which):
        for a in range(2):
            self.direct(which, a).wait_recv()
        for a in range(2):
            self.across(which, a).start()
            self.beside(which, 1 + a).start()

    def last(self, which):
        for a in range(2):
            self.across(which, a).wait_recv()
        self.beside(which, 3).start()

    def finish(self, which):
        for kind in range(4):
            self.beside(which, kind).wait()
        for a in range(2):
            self.direct(which, a).wait_send()
            self.across(which, a).wait_send()


def greet(peers):
    barrier = pltpu.get_barrier_semaphore()
    for peer in peers:
        pl.semaphore_signal(barrier, inc=1, device_id=peer, device_id_type=MESH)
    pl.semaphore_wait(barrier, len(peers))


def start_kernel(
    tokens, vectors, w_gate, w_up, w_qkv, x_all, vectors_all, inner, heads,
    raw_gate, raw_up, raw_qkv, my_inner, my_heads,
    load_sem, line_send, line_recv, part_send, part_recv, vector_send, vector_recv, own_sem,
):
    count, shards = x_all.shape[0], inner.shape[0]
    place, me = lax.axis_index("ctx"), lax.axis_index("fsdp")
    loads = [
        pltpu.make_async_copy(w_gate, raw_gate, load_sem.at[0]),
        pltpu.make_async_copy(w_up, raw_up, load_sem.at[1]),
        pltpu.make_async_copy(w_qkv, raw_qkv, load_sem.at[2]),
    ]
    for load in loads:
        load.start()
    peers = [(place, (me + s) % shards) for s in range(1, shards)]
    greet(peers + [((place + 1) % count, me), ((place + count - 1) % count, me)])
    line = Line(tokens, x_all, line_send, line_recv)
    plane = Plane((my_inner, my_heads), (inner, heads), part_send, part_recv)
    line.pass_on(1)
    own_copies = [
        pltpu.make_async_copy(my_inner, inner.at[me], own_sem.at[0]),
        pltpu.make_async_copy(my_heads, heads.at[me], own_sem.at[1]),
        pltpu.make_async_copy(vectors, vectors_all.at[me], own_sem.at[2]),
        pltpu.make_async_copy(tokens, x_all.at[place], own_sem.at[3]),
    ]
    own_copies[2].start()
    own_copies[3].start()
    vector_copies = [
        pltpu.make_async_remote_copy(
            src_ref=vectors,
            dst_ref=vectors_all.at[me],
            send_sem=vector_send.at[s - 1],
            recv_sem=vector_recv.at[s - 1],
            device_id=(place, (me + s) % shards),
            device_id_type=MESH,
        )
        for s in range(1, shards)
    ]
    for c in vector_copies:
        c.start()

    row = lax.broadcasted_iota(jnp.int32, (TILE, HALF), 0)
    col = lax.broadcasted_iota(jnp.int32, (TILE, HALF), 1)

    def picked(raws, first, last, start):
        width = raws[0].shape[1]
        base = jnp.minimum((start + first) // HALF, width // HALF - TILE // HALF) * HALF
        choose = (row + base == col + start) & (col >= first) & (col < last)
        choose = choose.astype(F32).astype(BF)
        at = pl.ds(pl.multiple_of(base, HALF), TILE)
        return [contract(raw[:, at], choose, ((1,), (0,))) for raw in raws]

    part = raw_gate.shape[1] // shards // count
    loads[0].wait()
    loads[1].wait()
    held = None
    for block, first, last, start in inner_runs(shards, count, part):
        values = picked((raw_gate, raw_up), first, last, start + place * part)
        held = values if first == 0 else [a + b for a, b in zip(held, values)]
        if last == HALF:
            for k in range(2):
                at = block * TILE + k * HALF
                my_inner[:, at : at + HALF] = held[k].astype(BF)
    plane.begin(0)
    own_copies[0].start()
    loads[2].wait()
    width = raw_qkv.shape[1] // 3
    for pair in range(shards // 2):
        for kind in range(3):
            value = 0.0
            for h in range(2):
                head = count * (2 * pair + h) + place
                start = kind * width + head * HD - h * HD
                value = value + picked((raw_qkv,), h * HD, (h + 1) * HD, start)[0]
            at = (pair * 3 + kind) * HALF
            my_heads[:, at : at + HALF] = value.astype(BF)
    plane.begin(1)
    own_copies[1].start()
    line.pass_on(2)
    plane.relay(0)
    line.pass_on(3)
    plane.relay(1)
    for hop in range(4, count + 1):
        line.pass_on(hop)
    for which in range(2):
        plane.last(which)
    for which in range(2):
        plane.finish(which)
    for c in vector_copies + own_copies:
        c.wait()
    line.finish()


def start(tokens, vectors, w_gate, w_up, w_qkv, count, shards):
    rows, width = tokens.shape
    shard_rows, ff = w_gate.shape
    inner, heads = 2 * ff // count, 3 * width // count
    dma = pltpu.SemaphoreType.DMA
    return pl.pallas_call(
        start_kernel,
        out_shape=[
            jax.ShapeDtypeStruct((count, rows, width), BF),
            jax.ShapeDtypeStruct((shards,) + vectors.shape, F32),
            jax.ShapeDtypeStruct((shards, shard_rows, inner), BF),
            jax.ShapeDtypeStruct((shards, shard_rows, heads), BF),
        ],
        in_specs=[hbm_whole()] * 5,
        out_specs=[hbm_whole()] * 4,
        scratch_shapes=[
            pltpu.VMEM(w_gate.shape, BF),
            pltpu.VMEM(w_up.shape, BF),
            pltpu.VMEM(w_qkv.shape, BF),
            pltpu.VMEM((shard_rows, inner), BF),
            pltpu.VMEM((shard_rows, heads), BF),
            dma((3,)),
            dma((2, count - 1)),
            dma((2, count - 1)),
            dma((2, 8)),
            dma((2, 8)),
            dma((shards - 1,)),
            dma((shards - 1,)),
            dma((4,)),
        ],
        compiler_params=pltpu.CompilerParams(
            collective_id=2, has_side_effects=True, vmem_limit_bytes=60 * 2**20
        ),
        name="start",
    )(tokens, vectors, w_gate, w_up, w_qkv)


def forward_kernel(
    order, slots, x_all, gain, bias, cos, first, second, cot, w_down, w_out, w_inner, w_heads,
    cot_all, down, attn, normed_t, hat, both, hidden_t, q_out, k_out, v_out, att_out, low_t, lse_out, branch,
    inner, heads, normed, hidden, low, hat_stage, turned_stage, both_stage, hidden_stage,
    q_buf, k_buf, v_buf, att_buf, low_stage, lse_buf, down_tile, attn_tile, term, branch_stage,
    load_sem, line_send, line_recv, part_send, part_recv, own_sem, norm_sem, feed_sem, head_sem, tile_sem, branch_sem,
):
    count, rows = cot_all.shape[0], cot_all.shape[1]
    shards = down.shape[0]
    place, me = lax.axis_index("ctx"), lax.axis_index("fsdp")
    chip, core = me // 2, me % 2
    loads = [
        pltpu.make_async_copy(w_inner, inner, load_sem.at[0]),
        pltpu.make_async_copy(w_heads, heads, load_sem.at[1]),
    ]
    for load in loads:
        load.start()
    peers = [(place, 2 * chip + 1 - core)] + [(place, 2 * chip_away(chip, m) + core) for m in range(1, 3)]
    greet(peers + [((place + 1) % count, me), ((place + count - 1) % count, me)])
    my_down = w_down.at[pl.ds(pl.multiple_of(place * down.shape[1], 16), down.shape[1])]
    my_attn = w_out.at[pl.ds(pl.multiple_of(place * attn.shape[1], 16), attn.shape[1])]
    line = Line(cot, cot_all, line_send, line_recv)
    plane = Plane((my_down, my_attn), (down, attn), part_send, part_recv)
    line.pass_on(1)
    for which in range(2):
        plane.begin(which)
    own_copies = [
        pltpu.make_async_copy(my_down, down.at[me], own_sem.at[0]),
        pltpu.make_async_copy(my_attn, attn.at[me], own_sem.at[1]),
        pltpu.make_async_copy(cot, cot_all.at[place], own_sem.at[2]),
    ]
    for c in own_copies:
        c.start()

    def norm_copies(p):
        at = pl.ds(pl.multiple_of(p * rows, rows), rows)
        return (
            pltpu.make_async_copy(hat_stage.at[p % 2], hat.at[at], norm_sem.at[0, p % 2]),
            pltpu.make_async_copy(turned_stage.at[p % 2], normed_t.at[:, at], norm_sem.at[1, p % 2]),
        )

    def norm_step(p, carry):
        @pl.when(p >= 2)
        def _():
            for c in norm_copies(p - 2):
                c.wait()

        xf = x_all[slots[p]].astype(F32)
        mean = jnp.mean(xf, axis=1, keepdims=True)
        centered = xf - mean
        variance = jnp.mean(centered * centered, axis=1, keepdims=True)
        x_hat = centered * lax.rsqrt(variance + EPS)
        hat_stage[p % 2] = x_hat.astype(BF)
        value = x_hat * gain[...] + bias[...]
        normed[pl.ds(pl.multiple_of(p * rows, rows), rows), :] = value.astype(BF)
        turned_stage[p % 2] = value.T.astype(BF)
        for c in norm_copies(p):
            c.start()
        return carry

    lax.fori_loop(0, count, norm_step, 0)
    loads[0].wait()

    def feed_copies(i):
        wide = pl.ds(pl.multiple_of(i * TILE, TILE), TILE)
        slim = pl.ds(pl.multiple_of(i * HALF, HALF), HALF)
        return (
            pltpu.make_async_copy(both_stage.at[i % 2], both.at[:, wide], feed_sem.at[0, i % 2]),
            pltpu.make_async_copy(hidden_stage.at[i % 2], hidden_t.at[slim], feed_sem.at[1, i % 2]),
        )

    def feed_step(i, carry):
        @pl.when(i >= 2)
        def _():
            for c in feed_copies(i - 2):
                c.wait()

        value = contract(normed[...], inner[:, pl.ds(pl.multiple_of(i * TILE, TILE), TILE)], ((1,), (0,)))
        both_stage[i % 2] = value.astype(BF)
        gate, up = value[:, :HALF], value[:, HALF:]
        value = gate * jax.nn.sigmoid(gate) * up
        hidden[:, pl.ds(pl.multiple_of(i * HALF, HALF), HALF)] = value.astype(BF)
        hidden_stage[i % 2] = value.T.astype(BF)
        for c in feed_copies(i):
            c.start()
        return carry

    tiles = inner.shape[1] // TILE
    lax.fori_loop(0, tiles, feed_step, 0)
    line.pass_on(2)
    for which in range(2):
        plane.relay(which)
    loads[1].wait()
    row = lax.broadcasted_iota(jnp.int32, (CHUNK, CHUNK), 0)
    col = lax.broadcasted_iota(jnp.int32, (CHUNK, CHUNK), 1)
    pairs = heads.shape[1] // (3 * HALF)

    def head_copies(h):
        at = pl.ds(pl.multiple_of(h * HALF, HALF), HALF)
        moves = ((q_buf, q_out), (k_buf, k_out), (v_buf, v_out), (att_buf, att_out), (lse_buf, lse_out))
        copies = [
            pltpu.make_async_copy(a.at[h % 2], b.at[:, at], head_sem.at[n, h % 2]) for n, (a, b) in enumerate(moves)
        ]
        return copies + [pltpu.make_async_copy(low_stage.at[h % 2], low_t.at[at], head_sem.at[5, h % 2])]

    def head_step(h, carry):
        @pl.when(h >= 2)
        def _():
            for c in head_copies(h - 2):
                c.wait()

        slot = h % 2
        mixed = contract(
            normed[...], heads[:, pl.ds(pl.multiple_of(h * 3 * HALF, HALF), 3 * HALF)], ((1,), (0,))
        )
        q = turn(mixed[:, :HALF], cos[...], first[...], second[...]).astype(BF).astype(F32)
        q_buf[slot] = (q * HD ** (-0.5)).astype(BF)
        k_buf[slot] = turn(mixed[:, HALF : 2 * HALF], cos[...], first[...], second[...]).astype(BF)
        v_buf[slot] = mixed[:, 2 * HALF :].astype(BF)
        for c in range(normed.shape[0] // CHUNK):
            lo, hi = c * CHUNK, (c + 1) * CHUNK
            for side in range(2):
                lanes = slice(side * HD, (side + 1) * HD)
                q = q_buf[slot, lo:hi, lanes]
                s = contract(q, k_buf[slot, lo:hi, lanes], ((1,), (1,)))
                s = jnp.where(col <= row, s, NEG)
                if c:
                    s = jnp.concatenate([contract(q, k_buf[slot, :lo, lanes], ((1,), (1,))), s], axis=1)
                top = jnp.max(s, axis=1, keepdims=True)
                p = jnp.exp(s - top)
                total = jnp.sum(p, axis=1, keepdims=True)
                o = contract(p.astype(BF), v_buf[slot, :hi, lanes], ((1,), (0,)))
                att_buf[slot, lo:hi, lanes] = o / total
                lse_buf[slot, lo:hi, lanes] = jnp.broadcast_to(top + jnp.log(total), (CHUNK, HD))
        att = att_buf[slot]
        low[:, pl.ds(pl.multiple_of(h * HALF, HALF), HALF)] = att.astype(BF)
        low_stage[slot] = att.T.astype(BF)
        for c in head_copies(h):
            c.start()
        return carry

    lax.fori_loop(0, pairs // 2, head_step, 0)
    for which in range(2):
        plane.last(which)
    line.pass_on(3)
    lax.fori_loop(pairs // 2, pairs, head_step, 0)
    for which in range(2):
        plane.finish(which)
    for c in own_copies:
        c.wait()

    def tile_copies(i):
        at = pl.ds(pl.multiple_of(i * TILE, TILE), TILE)
        return (
            pltpu.make_async_copy(down.at[:, :, at], down_tile.at[i % 2], tile_sem.at[0, i % 2]),
            pltpu.make_async_copy(attn.at[:, :, at], attn_tile.at[i % 2], tile_sem.at[1, i % 2]),
        )

    def branch_copy(i):
        at = pl.ds(pl.multiple_of(i * TILE, TILE), TILE)
        return pltpu.make_async_copy(branch_stage.at[i % 2], branch.at[:, :, at], branch_sem.at[i % 2])

    steps = branch.shape[2] // TILE
    for c in tile_copies(0):
        c.start()

    def branch_step(i, carry):
        @pl.when(i + 1 < steps)
        def _():
            for c in tile_copies(i + 1):
                c.start()

        for c in tile_copies(i):
            c.wait()

        @pl.when(i >= 2)
        def _():
            branch_copy(i - 2).wait()

        value = contract(hidden[...], down_tile[i % 2].reshape(hidden.shape[1], TILE), ((1,), (0,)))
        value = value + contract(low[...], attn_tile[i % 2].reshape(low.shape[1], TILE), ((1,), (0,)))
        term[...] = value.reshape(term.shape)
        for j in range(count):
            branch_stage[i % 2, j] = term[order[j]].astype(BF)
        branch_copy(i).start()
        return carry

    lax.fori_loop(0, steps, branch_step, 0)
    for hop in range(4, count + 1):
        line.pass_on(hop)
    line.finish()
    for back in range(2):
        for c in norm_copies(count - 1 - back) + feed_copies(tiles - 1 - back):
            c.wait()
        for c in head_copies(pairs - 1 - back):
            c.wait()
        branch_copy(steps - 1 - back).wait()


def forward(order, slots, x_all, gain, bias, tables, cot, w_down, w_out, w_inner, w_heads, shards):
    count, rows, width = x_all.shape
    length = count * rows
    ff_part, attn_part = w_down.shape[0] // count, w_out.shape[0] // count
    ff, cols = shards * ff_part, shards * attn_part
    dma = pltpu.SemaphoreType.DMA
    smem = pl.BlockSpec(memory_space=pltpu.SMEM)
    bf = lambda *shape: jax.ShapeDtypeStruct(shape, BF)
    f32 = lambda *shape: jax.ShapeDtypeStruct(shape, F32)
    out_shape = [
        bf(count, rows, width),
        bf(shards, ff_part, width),
        bf(shards, attn_part, width),
        bf(width, length),
        bf(length, width),
        bf(length, 2 * ff),
        bf(ff, length),
        bf(length, cols),
        bf(length, cols),
        bf(length, cols),
        f32(length, cols),
        bf(cols, length),
        f32(length, cols),
        bf(count, rows, width),
    ]
    return pl.pallas_call(
        forward_kernel,
        out_shape=out_shape,
        in_specs=[smem] * 2 + [vmem_whole()] * 6 + [hbm_whole()] * 5,
        out_specs=[hbm_whole()] * len(out_shape),
        scratch_shapes=[
            pltpu.VMEM(w_inner.shape, BF),
            pltpu.VMEM(w_heads.shape, BF),
            pltpu.VMEM((length, width), BF),
            pltpu.VMEM((length, ff), BF),
            pltpu.VMEM((length, cols), BF),
            pltpu.VMEM((2, rows, width), BF),
            pltpu.VMEM((2, width, rows), BF),
            pltpu.VMEM((2, length, TILE), BF),
            pltpu.VMEM((2, HALF, length), BF),
            pltpu.VMEM((2, length, HALF), BF),
            pltpu.VMEM((2, length, HALF), BF),
            pltpu.VMEM((2, length, HALF), BF),
            pltpu.VMEM((2, length, HALF), F32),
            pltpu.VMEM((2, HALF, length), BF),
            pltpu.VMEM((2, length, HALF), F32),
            pltpu.VMEM((2, shards, ff_part, TILE), BF),
            pltpu.VMEM((2, shards, attn_part, TILE), BF),
            pltpu.VMEM((count, rows, TILE), F32),
            pltpu.VMEM((2, count, rows, TILE), BF),
            dma((2,)),
            dma((2, count - 1)),
            dma((2, count - 1)),
            dma((2, 8)),
            dma((2, 8)),
            dma((3,)),
            dma((2, 2)),
            dma((2, 2)),
            dma((6, 2)),
            dma((2, 2)),
            dma((2,)),
        ],
        compiler_params=pltpu.CompilerParams(
            collective_id=3, has_side_effects=True, vmem_limit_bytes=60 * 2**20
        ),
        name="forward",
    )(order, slots, x_all, gain, bias, *tables, cot, w_down, w_out, w_inner, w_heads)


def feed_back_kernel(slots, *refs):
    *cots, down, attn, both, inner, d_att = refs
    cot = jnp.concatenate([c[0] for c in cots], axis=0)
    d_att[...] = contract(cot, attn[...], ((1,), (1,))).astype(BF)
    d_hidden = contract(cot, down[...], ((1,), (1,)))
    for b in range(down.shape[0] // HALF):
        d = d_hidden[:, b * HALF : (b + 1) * HALF]
        gate = both[:, b * TILE : b * TILE + HALF].astype(F32)
        up = both[:, b * TILE + HALF : (b + 1) * TILE].astype(F32)
        sig = jax.nn.sigmoid(gate)
        inner[:, b * TILE : b * TILE + HALF] = (d * up * sig * (1.0 + gate * (1.0 - sig))).astype(BF)
        inner[:, b * TILE + HALF : (b + 1) * TILE] = (d * gate * sig).astype(BF)


def feed_back(slots, cot, down, attn, both):
    count, rows, width = cot.shape
    whole = lambda a: pl.BlockSpec(a.shape, lambda i, s: (0, 0))
    by_rows = lambda columns: pl.BlockSpec((2 * rows, columns), lambda i, s: (i, 0))
    return pl.pallas_call(
        feed_back_kernel,
        grid_spec=pltpu.PrefetchScalarGridSpec(
            num_scalar_prefetch=1,
            grid=(count // 2,),
            in_specs=[
                pl.BlockSpec((1, rows, width), lambda i, s: (s[2 * i], 0, 0)),
                pl.BlockSpec((1, rows, width), lambda i, s: (s[2 * i + 1], 0, 0)),
                whole(down),
                whole(attn),
                by_rows(both.shape[1]),
            ],
            out_specs=[by_rows(both.shape[1]), by_rows(attn.shape[0])],
        ),
        out_shape=[
            jax.ShapeDtypeStruct(both.shape, BF),
            jax.ShapeDtypeStruct((count * rows, attn.shape[0]), BF),
        ],
        compiler_params=pltpu.CompilerParams(vmem_limit_bytes=58 * 2**20),
        name="feed_back",
    )(slots, cot, cot, down, attn, both)


def rows_of(shard, part):
    return slice(shard * part, (shard + 1) * part)


def heads_back_pair(q_in, k_in, v_in, do_in, att, lse, cos, first, second, out, dk, dv):
    length = q_in.shape[0]
    scale = HD ** (-0.5)
    row = lax.broadcasted_iota(jnp.int32, (CHUNK, CHUNK), 0)
    col = lax.broadcasted_iota(jnp.int32, (CHUNK, CHUNK), 1)
    dk[...] = jnp.zeros_like(dk)
    dv[...] = jnp.zeros_like(dv)
    for c in range(length // CHUNK):
        lo, hi = c * CHUNK, (c + 1) * CHUNK
        dqs = []
        for h in range(2):
            lanes = slice(h * HD, (h + 1) * HD)
            q, do = q_in[lo:hi, lanes], do_in[lo:hi, lanes]
            delta = jnp.sum(do.astype(F32) * att[lo:hi, lanes], axis=1, keepdims=True)
            s = contract(q, k_in[lo:hi, lanes], ((1,), (1,)))
            s = jnp.where(col <= row, s, NEG)
            if c:
                s = jnp.concatenate([contract(q, k_in[:lo, lanes], ((1,), (1,))), s], axis=1)
            p = jnp.exp(s - lse[lo:hi, h * HD : h * HD + 1])
            dp = contract(do, v_in[:hi, lanes], ((1,), (1,)))
            ds = (p * (dp - delta)).astype(BF)
            dqs.append(contract(ds, k_in[:hi, lanes], ((1,), (0,))) * scale)
            dk[:hi, lanes] += contract(ds, q, ((0,), (0,)))
            dv[:hi, lanes] += contract(p.astype(BF), do, ((0,), (0,)))
        dq = jnp.concatenate(dqs, axis=1)
        out[0, lo:hi, :] = turn(dq, cos[lo:hi, :], -first[lo:hi, :], -second[lo:hi, :]).astype(BF)
    out[1] = turn(dk[...], cos[...], -first[...], -second[...]).astype(BF)
    out[2] = dv[...].astype(BF)


def tile_at(i, size=TILE):
    return pl.ds(pl.multiple_of(i * size, size), size)


def backward_kernel(
    order, slots, hid_t, att_t, cos, first, second,
    cot, norm_hbm, inner_hbm, branch, w_inner, w_heads, hat, q_in, k_in, v_in, do_in, att_in, lse_in,
    pieces, sums,
    cot_tile, norm_t, d_inner, d_mixed, terms, term, small, w_tile, h_tile, hat_tile,
    q_tile, k_tile, v_tile, do_tile, att_tile, lse_tile, turned, dk, dv,
    partial, theirs, pair, landed, total, sum_from, sum_land,
    core_send, core_recv, chip_send, chip_recv, line_send, line_recv, own_sem, sum_send, sum_recv,
    cot_sem, load_sem, back_sem, head_sem,
):
    count, chunks = pieces.shape[0], pieces.shape[1]
    shards = 2 * partial.shape[1]
    chips = shards // 2
    rows = terms.shape[1]
    place, me = lax.axis_index("ctx"), lax.axis_index("fsdp")
    chip, core = me // 2, me % 2
    ff_part, attn_part = hid_t.shape[0] // shards, att_t.shape[0] // shards
    sum_parts = terms.shape[2] // TILE
    early = cot.shape[2] // TILE - 1
    inner_end = early + d_inner.shape[1] // TILE

    def chunk_name(i):
        return jnp.where(i < early, i, jnp.where(i == chunks - 1, early, i + 1))

    def core_copy(i):
        return pltpu.make_async_remote_copy(
            src_ref=partial.at[i % 2, :, 1 - core],
            dst_ref=theirs.at[i % DEEP],
            send_sem=core_send.at[i % 2],
            recv_sem=core_recv.at[i % DEEP],
            device_id=(place, me + 1 - 2 * core),
            device_id_type=MESH,
        )

    def chip_copy(j, m):
        return pltpu.make_async_remote_copy(
            src_ref=pair.at[j % 2, chip_away(chip, m)],
            dst_ref=landed.at[j % DEEP, m - 1],
            send_sem=chip_send.at[j % 2, m - 1],
            recv_sem=chip_recv.at[j % DEEP, m - 1],
            device_id=(place, 2 * chip_away(chip, m) + core),
            device_id_type=MESH,
        )

    def line_copy(way, hop, k):
        ahead = 1 - 2 * way
        origin = place - (hop - 1) * ahead
        target = pieces.at[origin, chunk_name(k)]
        return pltpu.make_async_remote_copy(
            src_ref=total.at[k % DEEP] if hop == 1 else target,
            dst_ref=target,
            send_sem=line_send.at[way, hop - 1, k % DEEP],
            recv_sem=line_recv.at[way, k, hop - 1],
            device_id=(place + ahead, me),
            device_id_type=MESH,
        )

    def sends(way, hop):
        if way == 0:
            return (place >= hop - 1) & (place <= count - 2)
        return (place <= count - hop) & (place >= 1)

    def lands(way, hop):
        return place >= hop if way == 0 else place <= count - 1 - hop

    def forward_chunk(hop, k):
        for way in range(2):
            if hop > 1:
                @pl.when(lands(way, hop - 1))
                def _(way=way):
                    line_copy(way, hop - 1, k).wait_recv()

            if hop < count:
                @pl.when(sends(way, hop))
                def _(way=way):
                    @pl.when(k >= DEEP)
                    def _():
                        line_copy(way, hop, k - DEEP).wait_send()

                    line_copy(way, hop, k).start()

    def own_copy(k):
        return pltpu.make_async_copy(total.at[k % DEEP], pieces.at[place, chunk_name(k)], own_sem.at[k % DEEP])

    def sum_copy(way, t, q):
        return pltpu.make_async_remote_copy(
            src_ref=sum_from.at[way, t - 1, q % 2],
            dst_ref=sum_land.at[way, t - 1, q % sum_parts],
            send_sem=sum_send.at[way, t - 1, q % 2],
            recv_sem=sum_recv.at[way, t - 1, q],
            device_id=(place + 1 - 2 * way, me),
            device_id_type=MESH,
        )

    def sum_sends(way, t):
        return place <= t - 1 if way == 0 else place >= count - t

    def sum_step(t, q):
        at = tile_at(q % sum_parts)
        for way in range(2):
            @pl.when(sum_sends(way, t))
            def _(way=way):
                to = count - t + place if way == 0 else t + place - count
                starts = place == 0 if way == 0 else place == count - 1

                @pl.when(q >= 2)
                def _():
                    sum_copy(way, t, q - 2).wait_send()

                @pl.when(starts)
                def _():
                    sum_from[way, t - 1, q % 2] = terms[to, :, at]

                if t > 1:
                    @pl.when(jnp.logical_not(starts))
                    def _():
                        sum_copy(way, t - 1, q).wait_recv()
                        value = terms[to, :, at].astype(F32) + sum_land[way, t - 2, q % sum_parts].astype(F32)
                        sum_from[way, t - 1, q % 2] = value.astype(BF)

                sum_copy(way, t, q).start()

    def sum_end(q):
        at = tile_at(q % sum_parts)
        which = q // sum_parts
        sums[which, :, at] = terms[place, :, at].astype(F32)
        for way in range(2):
            @pl.when(place >= 1 if way == 0 else place <= count - 2)
            def _(way=way):
                sum_copy(way, count - 1, q).wait_recv()
                sums[which, :, at] += sum_land[way, count - 2, q % sum_parts].astype(F32)

    def cot_load(c):
        return pltpu.make_async_copy(cot.at[:, :, tile_at(c)], cot_tile.at[c % 2], cot_sem.at[c % 2])

    loads = [
        pltpu.make_async_copy(branch, terms, load_sem.at[0]),
        pltpu.make_async_copy(norm_hbm, norm_t, load_sem.at[1]),
        pltpu.make_async_copy(inner_hbm, d_inner, load_sem.at[2]),
    ]

    def back_loads(q):
        moves = (
            (w_inner.at[tile_at(q)], w_tile.at[q % 2]),
            (w_heads.at[tile_at(q)], h_tile.at[q % 2]),
            (hat.at[:, tile_at(q)], hat_tile.at[q % 2]),
        )
        return [pltpu.make_async_copy(a, b, back_sem.at[n, q % 2]) for n, (a, b) in enumerate(moves)]

    def head_loads(h):
        moves = ((q_in, q_tile), (k_in, k_tile), (v_in, v_tile), (do_in, do_tile), (att_in, att_tile), (lse_in, lse_tile))
        at = tile_at(h, HALF)
        return [
            pltpu.make_async_copy(a.at[:, at], b.at[h % 2], head_sem.at[n, h % 2]) for n, (a, b) in enumerate(moves)
        ]

    pairs = q_in.shape[1] // HALF
    for c in [loads[0], cot_load(0)] + head_loads(0) + head_loads(1) + loads[1:] + back_loads(0) + back_loads(1):
        c.start()
    peers = [(place, me + 1 - 2 * core)]
    peers += [(place, 2 * chip_away(chip, m) + core) for m in range(1, chips)]
    greet(peers + [((place + 1) % count, me), ((place + count - 1) % count, me)])
    loads[0].wait()

    def store(i, shard, lo, value):
        partial[i % 2, shard // 2, shard % 2, lo : lo + value.shape[0], :] = value

    def from_norm(i, rhs):
        for s in range(0, shards, 2):
            part = norm_t.shape[0] // shards
            value = contract(norm_t[s * part : (s + 2) * part, :], rhs, ((1,), (0,))).astype(BF)
            store(i, s, 0, value[:part])
            store(i, s + 1, 0, value[part:])

    def step(i, carry):
        @pl.when((i < early) | (i == chunks - 1))
        def _():
            c = jnp.where(i < early, i, early)
            cot_load(c).wait()

            rhs = jnp.concatenate([cot_tile[c % 2, slots[p]] for p in range(count)], axis=0)

            @pl.when(c < early)
            def _():
                cot_load(c + 1).start()

            for s in range(0, shards, 4):
                value = contract(hid_t[s * ff_part : (s + 4) * ff_part, :], rhs, ((1,), (0,))).astype(BF)
                for t in range(4):
                    store(i, s + t, 0, value[rows_of(t, ff_part)])
            value = contract(att_t[...], rhs, ((1,), (0,))).astype(BF)
            for s in range(shards):
                store(i, s, ff_part, value[rows_of(s, attn_part)])

        @pl.when(i == chunks - 1)
        def _():
            for s in range(shards):
                store(i, s, ff_part + attn_part, small[s])

        @pl.when(i == early)
        def _():
            loads[1].wait()
            loads[2].wait()

        @pl.when((i >= early) & (i < inner_end))
        def _():
            from_norm(i, d_inner[:, tile_at(i - early)])

        @pl.when((i >= inner_end) & (i < chunks - 1))
        def _():
            at = i - inner_end
            from_norm(i, d_mixed[:, tile_at(at)])

        @pl.when(i < chunks)
        def _():
            core_copy(i).start()

        @pl.when((i >= 1) & (i < chunks + 1))
        def _():
            j = i - 1
            core_copy(j).wait()
            for m in range(chips):
                a = partial[j % 2, m, core].astype(F32) + theirs[j % DEEP, m].astype(F32)
                pair[j % 2, m] = a.astype(BF)
            for m in range(1, chips):
                chip_copy(j, m).start()

        @pl.when((i >= 2) & (i < chunks + 2))
        def _():
            k = i - 2
            for m in range(1, chips):
                chip_copy(k, m).wait()

            a = pair[k % 2, chip].astype(F32)
            for m in range(1, chips):
                a = a + landed[k % DEEP, m - 1].astype(F32)
            for way in range(2):
                @pl.when(sends(way, 1) & (k >= DEEP))
                def _(way=way):
                    line_copy(way, 1, k - DEEP).wait_send()

            @pl.when(k >= DEEP)
            def _():
                own_copy(k - DEEP).wait()

            total[k % DEEP] = a.astype(BF)
            for way in range(2):
                @pl.when(sends(way, 1))
                def _(way=way):
                    line_copy(way, 1, k).start()

            own_copy(k).start()

        @pl.when((i >= sum_parts) & (i < 2 * sum_parts))
        def _():
            q = i - sum_parts
            for c in back_loads(q):
                c.wait()
            value = contract(d_inner[...], w_tile[q % 2], ((1,), (1,)))
            value = value + contract(d_mixed[...], h_tile[q % 2], ((1,), (1,)))
            term[...] = value.reshape(term.shape)
            gain = jnp.sum(value * hat_tile[q % 2].astype(F32), axis=0, keepdims=True)
            bias = jnp.sum(value, axis=0, keepdims=True)
            row = lax.broadcasted_iota(jnp.int32, small.shape[1:], 0)
            small[q] = jnp.where(row == 0, gain, jnp.where(row == 1, bias, 0.0)).astype(BF)
            for j in range(count):
                terms[j, :, tile_at(q)] = term[order[j]].astype(BF)

            @pl.when(q + 2 < sum_parts)
            def _():
                for c in back_loads(q + 2):
                    c.start()

        for t in range(1, count + 1):
            q = i - LAG * (t - 1)

            @pl.when((q >= 0) & (q < 2 * sum_parts))
            def _(q=q, t=t):
                if t < count:
                    sum_step(t, q)
                else:
                    sum_end(q)

        for hop in range(2, count + 1):
            k = i - 2 - LAG * (hop - 1)

            @pl.when((k >= 0) & (k < chunks))
            def _(k=k, hop=hop):
                forward_chunk(hop, k)

        @pl.when((i == 2) | (i == 3) | (i == 5) | (i == 6))
        def _():
            h = i - 2 - i // 5
            for c in head_loads(h):
                c.wait()
            slot = h % 2
            heads_back_pair(
                q_tile.at[slot], k_tile.at[slot], v_tile.at[slot], do_tile.at[slot], att_tile.at[slot],
                lse_tile.at[slot], cos, first, second, turned, dk, dv,
            )
            for n in range(3):
                d_mixed[:, tile_at(3 * h + n, HALF)] = turned[n]

            @pl.when(h + 2 < pairs)
            def _():
                for c in head_loads(h + 2):
                    c.start()

        return carry

    lax.fori_loop(0, chunks + 2 + LAG * (count - 1), step, 0)

    def drain(k, carry):
        own_copy(k).wait()
        for way in range(2):
            for hop in range(1, count):
                @pl.when(sends(way, hop))
                def _(way=way, hop=hop):
                    line_copy(way, hop, k).wait_send()
        return carry

    lax.fori_loop(chunks - DEEP, chunks, drain, 0)
    for way in range(2):
        for t in range(1, count):
            @pl.when(sum_sends(way, t))
            def _(way=way, t=t):
                for q in range(2):
                    sum_copy(way, t, 2 * sum_parts - 2 + q).wait_send()


def backward(
    order, slots, hid_t, att_t, tables, cot, norm_t, d_inner, branch, w_inner, w_heads, hat, heads, shards
):
    count, rows, width = cot.shape
    length = count * rows
    chips = shards // 2
    cols = heads[0].shape[1]
    chunks = (width + d_inner.shape[1] + 3 * cols) // TILE
    part = width // shards
    parts = width // TILE
    dma = pltpu.SemaphoreType.DMA
    smem = pl.BlockSpec(memory_space=pltpu.SMEM)
    return pl.pallas_call(
        backward_kernel,
        out_shape=[
            jax.ShapeDtypeStruct((count, chunks, part, TILE), BF),
            jax.ShapeDtypeStruct((2, rows, width), F32),
        ],
        in_specs=[smem] * 2 + [vmem_whole()] * 5 + [hbm_whole()] * 13,
        out_specs=[hbm_whole(), vmem_whole()],
        scratch_shapes=[
            pltpu.VMEM((2, count, rows, TILE), BF),
            pltpu.VMEM((width, length), BF),
            pltpu.VMEM(d_inner.shape, BF),
            pltpu.VMEM((length, 3 * cols), BF),
            pltpu.VMEM((count, rows, width), BF),
            pltpu.VMEM((count, rows, TILE), F32),
            pltpu.VMEM((parts, 16, TILE), BF),
            pltpu.VMEM((2, TILE, d_inner.shape[1]), BF),
            pltpu.VMEM((2, TILE, 3 * cols), BF),
            pltpu.VMEM((2, length, TILE), BF),
        ]
        + [pltpu.VMEM((2, length, HALF), BF)] * 4
        + [pltpu.VMEM((2, length, HALF), F32)] * 2
        + [pltpu.VMEM((3, length, HALF), BF)]
        + [pltpu.VMEM((length, HALF), F32)] * 2
        + [
            pltpu.VMEM((2, chips, 2, part, TILE), BF),
            pltpu.VMEM((DEEP, chips, part, TILE), BF),
            pltpu.VMEM((2, chips, part, TILE), BF),
            pltpu.VMEM((DEEP, chips - 1, part, TILE), BF),
            pltpu.VMEM((DEEP, part, TILE), BF),
            pltpu.VMEM((2, count - 1, 2, rows, TILE), BF),
            pltpu.VMEM((2, count - 1, parts, rows, TILE), BF),
            dma((2,)),
            dma((DEEP,)),
            dma((2, chips - 1)),
            dma((DEEP, chips - 1)),
            dma((2, count - 1, DEEP)),
            dma((2, chunks, count - 1)),
            dma((DEEP,)),
            dma((2, count - 1, 2)),
            dma((2, count - 1, 2 * parts)),
            dma((2,)),
            dma((3,)),
            dma((3, 2)),
            dma((6, 2)),
        ],
        compiler_params=pltpu.CompilerParams(
            collective_id=1, has_side_effects=True, vmem_limit_bytes=62 * 2**20
        ),
        name="backward",
    )(order, slots, hid_t, att_t, *tables, cot, norm_t, d_inner, branch, w_inner, w_heads, hat, *heads)


def column_runs(columns, source):
    out = []
    for block in range(columns // HALF):
        first = 0
        while first < HALF:
            key, lane = source(block * HALF + first)
            last = first + 1
            while last < HALF and source(block * HALF + last) == (key, lane + last - first):
                last += 1
            out.append((block, first, last, key, (first - lane) % HALF))
            first = last
    return out


def assemble_kernel(down_chunks, rows_in, cols_in, qkv_out, gate_out, up_out, down_out, attn_out, small_out):
    count, chunks, rows, _ = rows_in.shape
    cot_chunks_static = down_chunks
    ff = gate_out.shape[1]
    width = qkv_out.shape[1]
    ff_part = down_out.shape[0] // count
    attn_part = attn_out.shape[0] // count
    shards = ff // (count * ff_part)
    inner_chunks = ff // count // HALF
    lane = lax.broadcasted_iota(jnp.int32, (rows, HALF), 1)

    def gather(out, runs, load):
        for block, first, last, key, shift in runs:
            value = load(key).astype(F32)
            if shift:
                value = pltpu.roll(value, shift, 1)
            if first:
                value = jnp.where(lane >= first, value, held)
            held = value
            if last == HALF:
                out[:, block * HALF : (block + 1) * HALF] = value

    def inner_source(column):
        shard, rest = divmod(column, count * ff_part)
        unit = shard * ff_part + rest % ff_part
        return (rest // ff_part, unit // HALF), unit % HALF

    def head_source(column):
        part, rest = divmod(column, width // 3)
        head, dim = divmod(rest, HD)
        per = width // 3 // HD // shards // count
        shard, at = divmod(head, per * count)
        place, sub = divmod(at, per)
        pair, half = divmod(shard * per + sub, 2)
        return (place, 3 * pair + part), half * HD + dim

    runs = column_runs(ff, inner_source)
    gather(gate_out, runs, lambda key: rows_in[key[0], cot_chunks_static + key[1], :, :HALF])
    gather(up_out, runs, lambda key: rows_in[key[0], cot_chunks_static + key[1], :, HALF:])
    first_head = cot_chunks_static + inner_chunks

    def head_load(key):
        at = key[1] % 2 * HALF
        return rows_in[key[0], first_head + key[1] // 2, :, at : at + HALF]

    gather(qkv_out, column_runs(width, head_source), head_load)
    for p in range(count):
        down_out[p * ff_part : (p + 1) * ff_part, :] = cols_in[p, 0, :ff_part, :].astype(F32)
        attn_out[p * attn_part : (p + 1) * attn_part, :] = cols_in[
            p, 0, ff_part : ff_part + attn_part, :
        ].astype(F32)
    small = [cols_in[p, 0, ff_part + attn_part :, :].astype(F32) for p in range(count)]
    small_out[...] = functools.reduce(jnp.add, small)


def assemble_outputs(pieces, qkv, attn, gate, down):
    count, chunks, rows, _ = pieces.shape
    steps = down[1] // TILE
    part = rows // steps
    by_rows = lambda shape: pl.BlockSpec((part, shape[1]), lambda i: (i, 0))
    by_cols = lambda shape: pl.BlockSpec((shape[0], TILE), lambda i: (0, i))
    return pl.pallas_call(
        functools.partial(assemble_kernel, steps),
        grid=(steps,),
        in_specs=[
            pl.BlockSpec((count, chunks, part, TILE), lambda i: (0, 0, i, 0)),
            pl.BlockSpec((count, 1, rows, TILE), lambda i: (0, i, 0, 0)),
        ],
        out_specs=[by_rows(qkv), by_rows(gate), by_rows(gate), by_cols(down), by_cols(attn)]
        + [pl.BlockSpec((16, TILE), lambda i: (0, 0))],
        out_shape=[jax.ShapeDtypeStruct(s, F32) for s in (qkv, gate, gate, down, attn, (16, TILE))],
        compiler_params=pltpu.CompilerParams(vmem_limit_bytes=40 * 2**20),
        name="assemble",
    )(pieces, pieces)


def rotation_tables(length):
    half = ROT // 2
    inverse = 10000.0 ** (-jnp.arange(half, dtype=F32) / half)
    grid = jnp.arange(length, dtype=jnp.int32).astype(F32)[:, None] * inverse[None, :]
    cos, sin = jnp.cos(grid), jnp.sin(grid)
    zero = jnp.zeros((length, half), F32)
    rest = jnp.zeros((length, HD - ROT), F32)
    tables = (
        jnp.concatenate([cos, cos, rest + 1.0], axis=1),
        jnp.concatenate([-sin, zero, rest], axis=1),
        jnp.concatenate([zero, sin, rest], axis=1),
    )
    return tuple(jnp.tile(t, (1, 2)) for t in tables)


def body_general(tokens, block_order, ln_gain, ln_bias, w_qkv, w_out, w_gate, w_up, w_down, cotangent):
    rows, width = tokens.shape[1], tokens.shape[2]
    count = lax.axis_size("ctx")
    shards = lax.axis_size("fsdp")
    place = lax.axis_index("ctx")
    length = rows * count
    order = block_order[0]
    shard_rows = w_qkv.shape[0]
    ff_shard = w_down.shape[0]
    ff_part = ff_shard // count
    own_heads = H // count
    spread = (w_out.shape[0] // HD) % count == 0
    groups = shards if spread else 1
    head_cols = own_heads * HD // groups

    def my_cols(w, outer, group, part):
        w = w.reshape(w.shape[0], outer, group, count, part)
        return lax.dynamic_index_in_dim(w, place, 3, False).reshape(w.shape[0], outer * group * part)

    def all_cols(piece, outer, group, part):
        whole = gather_ctx(piece).reshape(count, piece.shape[0], outer, group, part)
        return whole.transpose(1, 2, 3, 0, 4).reshape(piece.shape[0], -1).astype(F32)

    def assemble(block, ready=None):
        whole = jnp.zeros((length, width), block.dtype)
        whole = lax.dynamic_update_slice_in_dim(whole, block, order[place] * rows, 0)
        last = None
        for k in range(1, count):
            last = ring_send(block, k)
            source = (place - k) % count
            whole = lax.dynamic_update_slice_in_dim(whole, last, order[source] * rows, 0)
        return whole, last

    gain = lax.all_gather(ln_gain, "fsdp", axis=0, tiled=True).astype(F32)
    bias = lax.all_gather(ln_bias, "fsdp", axis=0, tiled=True).astype(F32)
    tables = rotation_tables(length)

    block = tokens[0]
    x_all, arrived = assemble(block)
    grad_block = cotangent[0]
    cot_all, _ = assemble(after(grad_block, arrived))

    inner = jnp.concatenate(
        [my_cols(w_gate, 1, shards, ff_part), my_cols(w_up, 1, shards, ff_part)], axis=1
    )
    w_inner, sent = gather_rows(inner)
    w_heads, sent = gather_rows(after(my_cols(w_qkv, 3, groups, head_cols), sent))
    down = lax.dynamic_slice_in_dim(w_down, place * ff_part, ff_part, 0)
    w_hidden, sent = gather_rows(after(down, sent))
    if spread:
        part = w_out.shape[0] // count
        attn = lax.dynamic_slice_in_dim(w_out, place * part, part, 0)
        w_attn, sent = gather_rows(after(attn, sent))
    else:
        w_attn = lax.all_gather(after(w_out, sent), "fsdp", axis=0, tiled=True)
        w_attn = lax.dynamic_slice_in_dim(w_attn, place * own_heads * HD, own_heads * HD, 0)

    xf = x_all.astype(F32)
    average = jnp.mean(xf, axis=-1, keepdims=True)
    centered = xf - average
    variance = jnp.mean(centered * centered, axis=-1, keepdims=True)
    inv_std = lax.rsqrt(variance + EPS)
    x_hat = centered * inv_std
    normed = (x_hat * gain + bias).astype(BF)

    across = ((1,), (0,))
    over_tokens = ((0,), (0,))
    back = ((1,), (1,))
    ff_cols = shards * ff_part
    gate_value = dot(normed, w_inner[:, :ff_cols], across)
    up_value = dot(normed, w_inner[:, ff_cols:], across)
    sigmoid_gate = jax.nn.sigmoid(gate_value)
    hidden = (gate_value * sigmoid_gate * up_value).astype(BF)
    mixed = dot(normed, w_heads, across)
    q, k, v, attended, lse = attend(mixed, tables, own_heads)
    attended_low = attended.astype(BF)

    branch = dot(attended_low, w_attn, across) + dot(hidden, w_hidden, across)
    out = line_scatter(lambda j: lax.dynamic_slice_in_dim(branch, order[j] * rows, rows, 0))
    out = (block.astype(F32) + out).astype(BF)[None]

    d_hidden = dot(cot_all, w_hidden, back)
    grad_down = scatter_rows(dot(hidden, cot_all, over_tokens, BF))
    d_gate_act = (
        d_hidden * up_value * sigmoid_gate * (1.0 + gate_value * (1.0 - sigmoid_gate))
    ).astype(BF)
    d_up_act = (d_hidden * gate_value * sigmoid_gate).astype(BF)
    d_inner = jnp.concatenate([d_gate_act, d_up_act], axis=1)
    d_attended = dot(cot_all, w_attn, back, BF)
    d_mixed = attend_back(q, k, v, d_attended, attended, lse, tables, own_heads)
    d_mixed = jnp.concatenate(d_mixed, axis=1)
    grad_inner = scatter_rows(dot(normed, d_inner, over_tokens, BF))
    grad_attn = dot(attended_low, cot_all, over_tokens, BF)
    grad_heads = scatter_rows(dot(normed, d_mixed, over_tokens, BF))

    d_normed = dot(d_inner, w_inner, back) + dot(d_mixed, w_heads, back)
    small = jnp.stack([jnp.sum(d_normed * x_hat, axis=0), jnp.sum(d_normed, axis=0)])
    small = lax.psum(small, ("ctx", "fsdp"))
    small = lax.dynamic_slice_in_dim(small, lax.axis_index("fsdp") * shard_rows, shard_rows, 1)
    d_own = line_scatter(lambda j: lax.dynamic_slice_in_dim(d_normed, order[j] * rows, rows, 0))
    own = block.astype(F32)
    own_average = jnp.mean(own, axis=-1, keepdims=True)
    own = own - own_average
    own_std = lax.rsqrt(jnp.mean(own * own, axis=-1, keepdims=True) + EPS)
    own = own * own_std
    scaled = d_own * gain
    d_input = own_std * (
        scaled
        - jnp.mean(scaled, axis=-1, keepdims=True)
        - own * jnp.mean(scaled * own, axis=-1, keepdims=True)
    )
    grad_in = (grad_block.astype(F32) + d_input)[None]

    down_all = gather_ctx(grad_down).reshape(ff_shard, width).astype(F32)
    if spread:
        attn_all = gather_ctx(scatter_rows(grad_attn)).reshape(w_out.shape).astype(F32)
    else:
        full = jnp.zeros((H * HD, width), BF)
        full = lax.dynamic_update_slice_in_dim(full, grad_attn, place * own_heads * HD, 0)
        full = lax.psum_scatter(full, "fsdp", scatter_dimension=0, tiled=True)
        attn_all = lax.psum(full, "ctx").astype(F32)
    heads_all = all_cols(grad_heads, 3, groups, head_cols)
    inner_all = gather_ctx(grad_inner).reshape(count, shard_rows, 2, shards, ff_part)
    inner_all = inner_all.transpose(2, 1, 3, 0, 4).reshape(2, shard_rows, -1).astype(F32)
    return (
        out,
        grad_in,
        small[0],
        small[1],
        heads_all,
        attn_all,
        inner_all[0],
        inner_all[1],
        down_all,
    )


def body_fast(tokens, block_order, ln_gain, ln_bias, w_qkv, w_out, w_gate, w_up, w_down, cotangent):
    count, shards = lax.axis_size("ctx"), lax.axis_size("fsdp")
    place = lax.axis_index("ctx")
    block, grad_block = tokens[0], cotangent[0]
    rows, width = block.shape
    order = block_order[0]
    spots = jnp.arange(count, dtype=jnp.int32)
    slots = jnp.sum(jnp.where(order[None, :] == spots[:, None], spots[None, :], 0), axis=1)
    vectors = jnp.stack([ln_gain, ln_bias] + [jnp.zeros_like(ln_gain)] * 6).astype(F32)
    x_all, vectors, w_inner, w_heads = start(block, vectors, w_gate, w_up, w_qkv, count, shards)
    w_inner = w_inner.reshape(width, -1)
    w_heads = w_heads.reshape(width, -1)
    gain, bias = vectors[:, 0].reshape(1, width), vectors[:, 1].reshape(1, width)
    tables = rotation_tables(rows * count)

    (
        cot_all, w_hidden, w_attn, normed_t, hat, both, hidden_t, q, k, v, attended, low_t, lse, branch,
    ) = forward(
        order, slots, x_all, gain, bias, tables, grad_block, w_down, w_out, w_inner, w_heads, shards
    )
    w_hidden, w_attn = w_hidden.reshape(-1, width), w_attn.reshape(-1, width)
    d_inner, d_attended = feed_back(slots, cot_all, w_hidden, w_attn, both)
    pieces, sums = backward(
        order, slots, hidden_t, low_t, tables, cot_all, normed_t, d_inner, branch, w_inner, w_heads, hat,
        (q, k, v, d_attended, attended, lse), shards,
    )
    d_qkv, d_gate, d_up, d_down, d_attn, small = assemble_outputs(
        pieces, w_qkv.shape, w_out.shape, w_gate.shape, w_down.shape
    )
    own = block.astype(F32)
    out = (own + sums[0]).astype(BF)[None]
    own = own - jnp.mean(own, axis=-1, keepdims=True)
    own_std = lax.rsqrt(jnp.mean(own * own, axis=-1, keepdims=True) + EPS)
    own = own * own_std
    scaled = sums[1] * gain
    d_input = own_std * (
        scaled
        - jnp.mean(scaled, axis=-1, keepdims=True)
        - own * jnp.mean(scaled * own, axis=-1, keepdims=True)
    )
    grad_in = (grad_block.astype(F32) + d_input)[None]
    return out, grad_in, small[0], small[1], d_qkv, d_attn, d_gate, d_up, d_down


def solution(mesh):
    whole, once = P("fsdp", "ctx", None), P("fsdp", None)
    count, shards = mesh.shape["ctx"], mesh.shape["fsdp"]

    def body(*args):
        w_out, w_down = args[5], args[8]
        fits = shards == 8 and w_out.shape[0] == count * HD and w_out.shape[0] == TILE
        fits = fits and w_down.shape[0] % (16 * count) == 0 and w_down.shape[0] // count <= 176
        return (body_fast if fits else body_general)(*args)

    return jax.shard_map(
        body,
        mesh=mesh,
        in_specs=(whole, once, P("fsdp"), P("fsdp")) + (once,) * 5 + (whole,),
        out_specs=(whole, whole, P("fsdp"), P("fsdp")) + (once,) * 5,
        check_vma=False,
    )
```

```python
import functools

import jax
import jax.numpy as jnp
import numpy as np
from jax import lax
from jax.experimental import pallas as pl
from jax.experimental.pallas import tpu as pltpu
from jax.sharding import PartitionSpec as P

H = 32
HD = 64
ROT = 16
EPS = 1e-05
NEG = -1e30
CHUNK = 256

BF = jnp.bfloat16
F32 = jnp.float32


def xor_send(value, mask):
    count = lax.axis_size("fsdp")
    return lax.ppermute(value, "fsdp", [(i, i ^ mask) for i in range(count)])


def ring_send(value, steps):
    count = lax.axis_size("ctx")
    return lax.ppermute(value, "ctx", [(i, (i + steps) % count) for i in range(count)])


def after(value, *done):
    return lax.optimization_barrier((value,) + done)[0]


def dot(a, b, dims, out=F32):
    return lax.dot_general(a, b, (dims, ((), ())), preferred_element_type=F32).astype(out)


def gather_rows(piece):
    count = lax.axis_size("fsdp")
    chips = count // 2
    me = lax.axis_index("fsdp")
    chip, core = me // 2, me % 2
    parts = [piece] + [xor_send(piece, 2 * m) for m in range(1, chips)]
    others = [xor_send(p, 1) for p in parts]
    whole = jnp.zeros((count,) + piece.shape, piece.dtype)
    for m in range(chips):
        at = 2 * (chip ^ m)
        whole = lax.dynamic_update_index_in_dim(whole, parts[m], at + core, 0)
        whole = lax.dynamic_update_index_in_dim(whole, others[m], at + 1 - core, 0)
    return whole.reshape(count * piece.shape[0], piece.shape[1]), parts[-1]


def scatter_rows(grad):
    count = lax.axis_size("fsdp")
    chips = count // 2
    me = lax.axis_index("fsdp")
    chip, core = me // 2, me % 2
    rows = grad.shape[0] // count
    split = grad.reshape(chips, 2, rows, grad.shape[1])
    theirs = xor_send(lax.dynamic_index_in_dim(split, 1 - core, 1, False), 1)
    pair = lax.dynamic_index_in_dim(split, core, 1, False).astype(F32) + theirs.astype(F32)
    pair = pair.astype(BF)
    total = lax.dynamic_index_in_dim(pair, chip, 0, False).astype(F32)
    for m in range(1, chips):
        part = lax.dynamic_index_in_dim(pair, chip ^ m, 0, False)
        total = total + xor_send(part, 2 * m).astype(F32)
    return total.astype(BF)


def gather_ctx(piece):
    count = lax.axis_size("ctx")
    me = lax.axis_index("ctx")
    whole = jnp.zeros((count,) + piece.shape, piece.dtype)
    whole = lax.dynamic_update_index_in_dim(whole, piece, me, 0)
    for k in range(1, count):
        part = ring_send(piece, k)
        whole = lax.dynamic_update_index_in_dim(whole, part, (me - k) % count, 0)
    return whole


def line_scatter(blocks):
    count = lax.axis_size("ctx")
    me = lax.axis_index("ctx")
    down = up = None
    for t in range(1, count):
        to_down = blocks(jnp.clip(t + me - count, 0, count - 1))
        to_up = blocks(jnp.clip(count - 1 - (t + (count - 1 - me) - count), 0, count - 1))
        if down is not None:
            to_down = to_down + down.astype(F32)
            to_up = to_up + up.astype(F32)
        pairs = [(i, i - 1) for i in range(count - t, count)]
        down = lax.ppermute(to_down.astype(BF), "ctx", pairs)
        up = lax.ppermute(to_up.astype(BF), "ctx", [(count - 1 - i, count - 1 - j) for i, j in pairs])
    return blocks(me) + down.astype(F32) + up.astype(F32)


def turn(x, cos, first, second):
    width = x.shape[1]
    half = ROT // 2
    return x * cos + pltpu.roll(x, width - half, 1) * first + pltpu.roll(x, half, 1) * second


def contract(a, b, dims):
    return lax.dot_general(a, b, (dims, ((), ())), preferred_element_type=F32)


def attend_kernel(mq, mk, mv, cos, first, second, q_out, k_out, v_out, att_out, lse_out):
    length = mq.shape[0]
    scale = HD ** (-0.5)
    q_out[...] = (turn(mq[...], cos[...], first[...], second[...]).astype(BF).astype(F32) * scale).astype(BF)
    k_out[...] = turn(mk[...], cos[...], first[...], second[...]).astype(BF)
    v_out[...] = mv[...].astype(BF)
    row = lax.broadcasted_iota(jnp.int32, (CHUNK, CHUNK), 0)
    col = lax.broadcasted_iota(jnp.int32, (CHUNK, CHUNK), 1)
    for c in range(length // CHUNK):
        lo, hi = c * CHUNK, (c + 1) * CHUNK
        for h in range(2):
            lanes = slice(h * HD, (h + 1) * HD)
            q = q_out[lo:hi, lanes]
            s = contract(q, k_out[lo:hi, lanes], ((1,), (1,)))
            s = jnp.where(col <= row, s, NEG)
            if c:
                s = jnp.concatenate([contract(q, k_out[:lo, lanes], ((1,), (1,))), s], axis=1)
            top = jnp.max(s, axis=1, keepdims=True)
            p = jnp.exp(s - top)
            total = jnp.sum(p, axis=1, keepdims=True)
            o = contract(p.astype(BF), v_out[:hi, lanes], ((1,), (0,)))
            att_out[lo:hi, lanes] = o / total
            lse_out[lo:hi, lanes] = jnp.broadcast_to(top + jnp.log(total), (CHUNK, HD))


def attend(mixed, tables, heads):
    length = mixed.shape[0]
    pairs = heads // 2
    block = lambda at: pl.BlockSpec((length, 2 * HD), lambda h, at=at: (0, at + h))
    table = pl.BlockSpec((length, 2 * HD), lambda h: (0, 0))
    width = heads * HD
    return pl.pallas_call(
        attend_kernel,
        grid=(pairs,),
        in_specs=[block(0), block(pairs), block(2 * pairs), table, table, table],
        out_specs=[block(0)] * 5,
        out_shape=[jax.ShapeDtypeStruct((length, width), BF)] * 3
        + [jax.ShapeDtypeStruct((length, width), F32)] * 2,
        compiler_params=pltpu.CompilerParams(vmem_limit_bytes=40 * 2**20),
        cost_estimate=pl.CostEstimate(
            flops=16 * heads * length * length * HD // 2,
            bytes_accessed=26 * length * width,
            transcendentals=heads * length * length // 2,
        ),
        name="attend",
    )(mixed, mixed, mixed, *tables)


def attend_back_kernel(q_in, k_in, v_in, do_in, att, lse, cos, first, second, dq_out, dk_out, dv_out, dk, dv):
    length = q_in.shape[0]
    scale = HD ** (-0.5)
    row = lax.broadcasted_iota(jnp.int32, (CHUNK, CHUNK), 0)
    col = lax.broadcasted_iota(jnp.int32, (CHUNK, CHUNK), 1)
    dk[...] = jnp.zeros_like(dk)
    dv[...] = jnp.zeros_like(dv)
    for c in range(length // CHUNK):
        lo, hi = c * CHUNK, (c + 1) * CHUNK
        dqs = []
        for h in range(2):
            lanes = slice(h * HD, (h + 1) * HD)
            q, do = q_in[lo:hi, lanes], do_in[lo:hi, lanes]
            delta = jnp.sum(do.astype(F32) * att[lo:hi, lanes], axis=1, keepdims=True)
            s = contract(q, k_in[lo:hi, lanes], ((1,), (1,)))
            s = jnp.where(col <= row, s, NEG)
            if c:
                s = jnp.concatenate([contract(q, k_in[:lo, lanes], ((1,), (1,))), s], axis=1)
            p = jnp.exp(s - lse[lo:hi, h * HD : h * HD + 1])
            dp = contract(do, v_in[:hi, lanes], ((1,), (1,)))
            ds = (p * (dp - delta)).astype(BF)
            dqs.append(contract(ds, k_in[:hi, lanes], ((1,), (0,))) * scale)
            dk[:hi, lanes] += contract(ds, q, ((0,), (0,)))
            dv[:hi, lanes] += contract(p.astype(BF), do, ((0,), (0,)))
        dq = jnp.concatenate(dqs, axis=1)
        dq_out[lo:hi, :] = turn(dq, cos[lo:hi, :], -first[lo:hi, :], -second[lo:hi, :]).astype(BF)
    dk_out[...] = turn(dk[...], cos[...], -first[...], -second[...]).astype(BF)
    dv_out[...] = dv[...].astype(BF)


def attend_back(q, k, v, d_attended, attended, lse, tables, heads):
    length, width = q.shape
    block = pl.BlockSpec((length, 2 * HD), lambda h: (0, h))
    table = pl.BlockSpec((length, 2 * HD), lambda h: (0, 0))
    return pl.pallas_call(
        attend_back_kernel,
        grid=(heads // 2,),
        in_specs=[block] * 6 + [table] * 3,
        out_specs=[block] * 3,
        out_shape=[jax.ShapeDtypeStruct((length, width), BF)] * 3,
        scratch_shapes=[pltpu.VMEM((length, 2 * HD), F32)] * 2,
        compiler_params=pltpu.CompilerParams(vmem_limit_bytes=40 * 2**20),
        cost_estimate=pl.CostEstimate(
            flops=40 * heads * length * length * HD // 2,
            bytes_accessed=22 * length * width,
            transcendentals=heads * length * length // 2,
        ),
        name="attend_back",
    )(q, k, v, d_attended, attended, lse, *tables)


MESH = pl.DeviceIdType.MESH
TILE = 256
HALF = 128
DEEP = 4
LAG = 1


def vmem_whole():
    return pl.BlockSpec(memory_space=pltpu.VMEM)


def hbm_whole():
    return pl.BlockSpec(memory_space=pl.ANY)


def chip_away(chip, m):
    return 2 * ((chip // 2 + m // 2) % 2) + (chip + m) % 2


def inner_runs(shards, count, part):
    runs = []
    for block in range(shards * part // HALF):
        first = 0
        while first < HALF:
            shard, unit = divmod(block * HALF + first, part)
            last = min(HALF, first + part - unit)
            runs.append((block, first, last, shard * count * part + unit - first))
            first = last
    return runs


class Line:
    def __init__(self, own, whole, send, recv):
        self.own, self.whole, self.send, self.recv = own, whole, send, recv
        self.count = whole.shape[0]
        self.place, self.me = lax.axis_index("ctx"), lax.axis_index("fsdp")

    def copy(self, way, hop):
        ahead = 1 - 2 * way
        origin = self.place - (hop - 1) * ahead
        return pltpu.make_async_remote_copy(
            src_ref=self.own if hop == 1 else self.whole.at[origin],
            dst_ref=self.whole.at[origin],
            send_sem=self.send.at[way, hop - 1],
            recv_sem=self.recv.at[way, hop - 1],
            device_id=(self.place + ahead, self.me),
            device_id_type=MESH,
        )

    def sends(self, way, hop):
        if way == 0:
            return (self.place >= hop - 1) & (self.place <= self.count - 2)
        return (self.place <= self.count - hop) & (self.place >= 1)

    def lands(self, way, hop):
        return self.place >= hop if way == 0 else self.place <= self.count - 1 - hop

    def pass_on(self, hop):
        for way in range(2):
            if hop > 1:
                @pl.when(self.lands(way, hop - 1))
                def _(way=way):
                    self.copy(way, hop - 1).wait_recv()

            if hop < self.count:
                @pl.when(self.sends(way, hop))
                def _(way=way):
                    self.copy(way, hop).start()

    def finish(self):
        for way in range(2):
            for hop in range(1, self.count):
                @pl.when(self.sends(way, hop))
                def _(way=way, hop=hop):
                    self.copy(way, hop).wait_send()


class Plane:
    def __init__(self, mine, wholes, send, recv):
        self.mine, self.wholes, self.send, self.recv = mine, wholes, send, recv
        self.place, self.me = lax.axis_index("ctx"), lax.axis_index("fsdp")
        chip, core = self.me // 2, self.me % 2
        self.sibling = 2 * chip + 1 - core
        self.near = (2 * chip_away(chip, 1) + core, 2 * chip_away(chip, 2) + core)
        self.far = 2 * chip_away(chip, 3) + core

    def copy(self, which, kind, source, target, to):
        return pltpu.make_async_remote_copy(
            src_ref=source,
            dst_ref=target,
            send_sem=self.send.at[which, kind],
            recv_sem=self.recv.at[which, kind],
            device_id=(self.place, to),
            device_id_type=MESH,
        )

    def direct(self, which, a):
        return self.copy(which, a, self.mine[which], self.wholes[which].at[self.me], self.near[a])

    def across(self, which, a):
        half = self.wholes[which].shape[2] // 2
        piece = self.wholes[which].at[self.near[1 - a], :, a * half : (a + 1) * half]
        return self.copy(which, 2 + a, piece, piece, self.near[a])

    def beside(self, which, kind):
        source = (self.me, self.near[0], self.near[1], self.far)[kind]
        piece = self.wholes[which].at[source]
        return self.copy(which, 4 + kind, self.mine[which] if kind == 0 else piece, piece, self.sibling)

    def begin(self, which):
        for a in range(2):
            self.direct(which, a).start()
        self.beside(which, 0).start()

    def relay(self, which):
        for a in range(2):
            self.direct(which, a).wait_recv()
        for a in range(2):
            self.across(which, a).start()
            self.beside(which, 1 + a).start()

    def last(self, which):
        for a in range(2):
            self.across(which, a).wait_recv()
        self.beside(which, 3).start()

    def finish(self, which):
        for kind in range(4):
            self.beside(which, kind).wait()
        for a in range(2):
            self.direct(which, a).wait_send()
            self.across(which, a).wait_send()


class Own:
    def __init__(self, source, stage, target, sem, n):
        self.load = pltpu.make_async_copy(source, stage, sem.at[n, 0])
        self.store = pltpu.make_async_copy(stage, target, sem.at[n, 1])

    def turn(self):
        self.load.wait()
        self.store.start()


def greet(peers):
    barrier = pltpu.get_barrier_semaphore()
    for peer in peers:
        pl.semaphore_signal(barrier, inc=1, device_id=peer, device_id_type=MESH)
    pl.semaphore_wait(barrier, len(peers))


def start_kernel(
    tokens, vectors, w_gate, w_up, w_qkv, w_out, x_all, vectors_all, inner, heads_own, attn,
    raw_gate, raw_up, raw_qkv, my_inner, my_heads, tokens_stage, my_attn,
    load_sem, line_send, line_recv, part_send, part_recv, vector_send, vector_recv, own_sem, turn_sem,
):
    count, shards = x_all.shape[0], inner.shape[0]
    place, me = lax.axis_index("ctx"), lax.axis_index("fsdp")
    loads = [
        pltpu.make_async_copy(w_gate, raw_gate, load_sem.at[0]),
        pltpu.make_async_copy(w_up, raw_up, load_sem.at[1]),
        pltpu.make_async_copy(w_qkv, raw_qkv, load_sem.at[2]),
    ]
    at = pl.ds(pl.multiple_of(place * attn.shape[1], 16), attn.shape[1])
    own_attn = Own(w_out.at[at], my_attn, attn.at[me], turn_sem, 1)
    own_attn.load.start()
    for load in loads:
        load.start()
    peers = [(place, (me + s) % shards) for s in range(1, shards)]
    greet(peers + [((place + 1) % count, me), ((place + count - 1) % count, me)])
    line = Line(tokens, x_all, line_send, line_recv)
    plane = Plane((my_inner, my_attn), (inner, attn), part_send, part_recv)
    line.pass_on(1)
    own_attn.turn()
    plane.begin(1)
    own_copies = [
        pltpu.make_async_copy(my_inner, inner.at[me], own_sem.at[0]),
        pltpu.make_async_copy(my_heads, heads_own, own_sem.at[1]),
        pltpu.make_async_copy(vectors, vectors_all.at[me], own_sem.at[2]),
    ]
    own_copies[2].start()
    own_tokens = Own(tokens, tokens_stage, x_all.at[place], turn_sem, 0)
    own_tokens.load.start()
    vector_copies = [
        pltpu.make_async_remote_copy(
            src_ref=vectors,
            dst_ref=vectors_all.at[me],
            send_sem=vector_send.at[s - 1],
            recv_sem=vector_recv.at[s - 1],
            device_id=(place, (me + s) % shards),
            device_id_type=MESH,
        )
        for s in range(1, shards)
    ]
    for c in vector_copies:
        c.start()

    row = lax.broadcasted_iota(jnp.int32, (TILE, HALF), 0)
    col = lax.broadcasted_iota(jnp.int32, (TILE, HALF), 1)

    def picked(raws, first, last, start):
        width = raws[0].shape[1]
        base = jnp.minimum((start + first) // HALF, width // HALF - TILE // HALF) * HALF
        choose = (row + base == col + start) & (col >= first) & (col < last)
        choose = choose.astype(F32).astype(BF)
        at = pl.ds(pl.multiple_of(base, HALF), TILE)
        return [contract(raw[:, at], choose, ((1,), (0,))) for raw in raws]

    own_tokens.turn()
    part = raw_gate.shape[1] // shards // count
    loads[0].wait()
    loads[1].wait()
    held = None
    for block, first, last, start in inner_runs(shards, count, part):
        values = picked((raw_gate, raw_up), first, last, start + place * part)
        held = values if first == 0 else [a + b for a, b in zip(held, values)]
        if last == HALF:
            for k in range(2):
                at = block * TILE + k * HALF
                my_inner[:, at : at + HALF] = held[k].astype(BF)
    plane.begin(0)
    own_copies[0].start()
    loads[2].wait()
    width = raw_qkv.shape[1] // 3
    for pair in range(shards // 2):
        for kind in range(3):
            value = 0.0
            for h in range(2):
                head = count * (2 * pair + h) + place
                start = kind * width + head * HD - h * HD
                value = value + picked((raw_qkv,), h * HD, (h + 1) * HD, start)[0]
            at = (pair * 3 + kind) * HALF
            my_heads[:, at : at + HALF] = value.astype(BF)
    own_copies[1].start()
    plane.relay(1)
    line.pass_on(2)
    plane.relay(0)
    plane.last(1)
    line.pass_on(3)
    plane.last(0)
    for which in range(2):
        plane.finish(which)
    for hop in range(4, count + 1):
        line.pass_on(hop)
    for c in vector_copies + own_copies + [own_tokens.store, own_attn.store]:
        c.wait()
    line.finish()


def start(tokens, vectors, w_gate, w_up, w_qkv, w_out, count, shards):
    rows, width = tokens.shape
    shard_rows, ff = w_gate.shape
    inner, heads = 2 * ff // count, 3 * width // count
    dma = pltpu.SemaphoreType.DMA
    return pl.pallas_call(
        start_kernel,
        out_shape=[
            jax.ShapeDtypeStruct((count, rows, width), BF),
            jax.ShapeDtypeStruct((shards,) + vectors.shape, F32),
            jax.ShapeDtypeStruct((shards, shard_rows, inner), BF),
            jax.ShapeDtypeStruct((shard_rows, heads), BF),
            jax.ShapeDtypeStruct((shards, w_out.shape[0] // count, width), BF),
        ],
        in_specs=[hbm_whole()] * 6,
        out_specs=[hbm_whole()] * 5,
        scratch_shapes=[
            pltpu.VMEM(w_gate.shape, BF),
            pltpu.VMEM(w_up.shape, BF),
            pltpu.VMEM(w_qkv.shape, BF),
            pltpu.VMEM((shard_rows, inner), BF),
            pltpu.VMEM((shard_rows, heads), BF),
            pltpu.VMEM(tokens.shape, BF),
            pltpu.VMEM((w_out.shape[0] // count, width), BF),
            dma((3,)),
            dma((2, count - 1)),
            dma((2, count - 1)),
            dma((2, 8)),
            dma((2, 8)),
            dma((shards - 1,)),
            dma((shards - 1,)),
            dma((3,)),
            dma((2, 2)),
        ],
        compiler_params=pltpu.CompilerParams(
            collective_id=2, has_side_effects=True, vmem_limit_bytes=60 * 2**20
        ),
        name="start",
    )(tokens, vectors, w_gate, w_up, w_qkv, w_out)


def forward_kernel(
    order, slots, x_all, gain, bias, cos, first, second, cot, w_down, attn, w_inner, heads_own,
    cot_all, heads_all, down, normed_t, hat, both, hidden_t, q_out, k_out, v_out, att_out, low_t, lse_out, branch,
    inner, heads, normed, hidden, low, hat_stage, turned_stage, both_stage, hidden_stage,
    q_buf, k_buf, v_buf, att_buf, low_stage, lse_buf, down_tile, attn_tile, term, branch_stage, down_stage, cot_stage, heads_stage,
    load_sem, line_send, line_recv, part_send, part_recv, own_sem, norm_sem, feed_sem, head_sem, tile_sem, branch_sem,
):
    count, rows = cot_all.shape[0], cot_all.shape[1]
    shards = down.shape[0]
    place, me = lax.axis_index("ctx"), lax.axis_index("fsdp")
    chip, core = me // 2, me % 2
    loads = [
        pltpu.make_async_copy(w_inner, inner, load_sem.at[0]),
    ]
    part = heads_all.shape[1]
    loads += [
        pltpu.make_async_copy(heads_all.at[s], heads.at[s * part : (s + 1) * part], load_sem.at[1 + s])
        for s in range(shards)
    ]
    loads[0].start()
    peers = [(place, 2 * chip + 1 - core)] + [(place, 2 * chip_away(chip, m) + core) for m in range(1, 3)]
    greet(peers + [((place + 1) % count, me), ((place + count - 1) % count, me)])
    my_down = w_down.at[pl.ds(pl.multiple_of(place * down.shape[1], 16), down.shape[1])]
    line = Line(cot, cot_all, line_send, line_recv)
    plane = Plane((heads_own, my_down), (heads_all, down), part_send, part_recv)
    line.pass_on(1)
    plane.begin(0)
    owns = [
        Own(heads_own, heads_stage, heads_all.at[me], own_sem, 0),
        Own(cot, cot_stage, cot_all.at[place], own_sem, 1),
        Own(my_down, down_stage, down.at[me], own_sem, 2),
    ]
    for own in owns:
        own.load.start()

    def norm_copies(p):
        at = pl.ds(pl.multiple_of(p * rows, rows), rows)
        return (
            pltpu.make_async_copy(hat_stage.at[p % 2], hat.at[at], norm_sem.at[0, p % 2]),
            pltpu.make_async_copy(turned_stage.at[p % 2], normed_t.at[:, at], norm_sem.at[1, p % 2]),
        )

    def norm_step(p, carry):
        @pl.when(p >= 2)
        def _():
            for c in norm_copies(p - 2):
                c.wait()

        xf = x_all[slots[p]].astype(F32)
        mean = jnp.mean(xf, axis=1, keepdims=True)
        centered = xf - mean
        variance = jnp.mean(centered * centered, axis=1, keepdims=True)
        x_hat = centered * lax.rsqrt(variance + EPS)
        hat_stage[p % 2] = x_hat.astype(BF)
        value = x_hat * gain[...] + bias[...]
        normed[pl.ds(pl.multiple_of(p * rows, rows), rows), :] = value.astype(BF)
        turned_stage[p % 2] = value.T.astype(BF)
        for c in norm_copies(p):
            c.start()
        return carry

    lax.fori_loop(0, count, norm_step, 0)
    for own in owns:
        own.turn()
    loads[0].wait()

    def feed_copies(i):
        wide = pl.ds(pl.multiple_of(i * TILE, TILE), TILE)
        slim = pl.ds(pl.multiple_of(i * HALF, HALF), HALF)
        return (
            pltpu.make_async_copy(both_stage.at[i % 2], both.at[:, wide], feed_sem.at[0, i % 2]),
            pltpu.make_async_copy(hidden_stage.at[i % 2], hidden_t.at[slim], feed_sem.at[1, i % 2]),
        )

    def feed_step(i, carry):
        @pl.when(i >= 2)
        def _():
            for c in feed_copies(i - 2):
                c.wait()

        value = contract(normed[...], inner[:, pl.ds(pl.multiple_of(i * TILE, TILE), TILE)], ((1,), (0,)))
        both_stage[i % 2] = value.astype(BF)
        gate, up = value[:, :HALF], value[:, HALF:]
        value = gate * jax.nn.sigmoid(gate) * up
        hidden[:, pl.ds(pl.multiple_of(i * HALF, HALF), HALF)] = value.astype(BF)
        hidden_stage[i % 2] = value.T.astype(BF)
        for c in feed_copies(i):
            c.start()
        return carry

    tiles = inner.shape[1] // TILE
    lax.fori_loop(0, tiles // 2, feed_step, 0)
    plane.relay(0)
    plane.begin(1)
    lax.fori_loop(tiles // 2, tiles, feed_step, 0)
    line.pass_on(2)
    plane.last(0)
    plane.finish(0)
    owns[0].store.wait()
    for load in loads[1:]:
        load.start()
    for load in loads[1:]:
        load.wait()
    row = lax.broadcasted_iota(jnp.int32, (CHUNK, CHUNK), 0)
    col = lax.broadcasted_iota(jnp.int32, (CHUNK, CHUNK), 1)
    pairs = heads.shape[1] // (3 * HALF)

    def head_copies(h):
        at = pl.ds(pl.multiple_of(h * HALF, HALF), HALF)
        moves = ((q_buf, q_out), (k_buf, k_out), (v_buf, v_out), (att_buf, att_out), (lse_buf, lse_out))
        copies = [
            pltpu.make_async_copy(a.at[h % 2], b.at[:, at], head_sem.at[n, h % 2]) for n, (a, b) in enumerate(moves)
        ]
        return copies + [pltpu.make_async_copy(low_stage.at[h % 2], low_t.at[at], head_sem.at[5, h % 2])]

    def head_step(h, carry):
        @pl.when(h >= 2)
        def _():
            for c in head_copies(h - 2):
                c.wait()

        slot = h % 2
        w = heads[:, pl.ds(pl.multiple_of(h * 3 * HALF, HALF), 3 * HALF)]
        mixed = contract(normed[...], w, ((1,), (0,)))
        q = turn(mixed[:, :HALF], cos[...], first[...], second[...]).astype(BF).astype(F32)
        q_buf[slot] = (q * HD ** (-0.5)).astype(BF)
        k_buf[slot] = turn(mixed[:, HALF : 2 * HALF], cos[...], first[...], second[...]).astype(BF)
        v_buf[slot] = mixed[:, 2 * HALF :].astype(BF)
        for c in range(normed.shape[0] // CHUNK):
            lo, hi = c * CHUNK, (c + 1) * CHUNK
            for side in range(2):
                lanes = slice(side * HD, (side + 1) * HD)
                q = q_buf[slot, lo:hi, lanes]
                s = contract(q, k_buf[slot, lo:hi, lanes], ((1,), (1,)))
                s = jnp.where(col <= row, s, NEG)
                if c:
                    s = jnp.concatenate([contract(q, k_buf[slot, :lo, lanes], ((1,), (1,))), s], axis=1)
                top = jnp.max(s, axis=1, keepdims=True)
                p = jnp.exp(s - top)
                total = jnp.sum(p, axis=1, keepdims=True)
                o = contract(p.astype(BF), v_buf[slot, :hi, lanes], ((1,), (0,)))
                att_buf[slot, lo:hi, lanes] = o / total
                lse_buf[slot, lo:hi, lanes] = jnp.broadcast_to(top + jnp.log(total), (CHUNK, HD))
        att = att_buf[slot]
        low[:, pl.ds(pl.multiple_of(h * HALF, HALF), HALF)] = att.astype(BF)
        low_stage[slot] = att.T.astype(BF)
        for c in head_copies(h):
            c.start()
        return carry

    lax.fori_loop(0, pairs - 1, head_step, 0)
    plane.relay(1)
    line.pass_on(3)
    lax.fori_loop(pairs - 1, pairs, head_step, 0)
    plane.last(1)
    plane.finish(1)
    for own in owns[1:]:
        own.store.wait()

    def tile_copies(i):
        at = pl.ds(pl.multiple_of(i * TILE, TILE), TILE)
        return (
            pltpu.make_async_copy(down.at[:, :, at], down_tile.at[i % 2], tile_sem.at[0, i % 2]),
            pltpu.make_async_copy(attn.at[:, :, at], attn_tile.at[i % 2], tile_sem.at[1, i % 2]),
        )

    def branch_copy(i):
        at = pl.ds(pl.multiple_of(i * TILE, TILE), TILE)
        return pltpu.make_async_copy(branch_stage.at[i % 2], branch.at[:, :, at], branch_sem.at[i % 2])

    steps = branch.shape[2] // TILE
    for c in tile_copies(0):
        c.start()

    def branch_step(i, carry):
        @pl.when(i + 1 < steps)
        def _():
            for c in tile_copies(i + 1):
                c.start()

        for c in tile_copies(i):
            c.wait()

        @pl.when(i >= 2)
        def _():
            branch_copy(i - 2).wait()

        value = contract(hidden[...], down_tile[i % 2].reshape(hidden.shape[1], TILE), ((1,), (0,)))
        value = value + contract(low[...], attn_tile[i % 2].reshape(low.shape[1], TILE), ((1,), (0,)))
        term[...] = value.reshape(term.shape)
        for j in range(count):
            branch_stage[i % 2, j] = term[order[j]].astype(BF)
        branch_copy(i).start()
        return carry

    lax.fori_loop(0, steps, branch_step, 0)
    for hop in range(4, count + 1):
        line.pass_on(hop)
    line.finish()
    for back in range(2):
        for c in norm_copies(count - 1 - back) + feed_copies(tiles - 1 - back):
            c.wait()
        for c in head_copies(pairs - 1 - back):
            c.wait()
        branch_copy(steps - 1 - back).wait()


def forward(order, slots, x_all, gain, bias, tables, cot, w_down, attn, w_inner, heads_own, shards):
    count, rows, width = x_all.shape
    length = count * rows
    ff_part, attn_part = w_down.shape[0] // count, attn.shape[1]
    ff, cols = shards * ff_part, shards * attn_part
    dma = pltpu.SemaphoreType.DMA
    smem = pl.BlockSpec(memory_space=pltpu.SMEM)
    bf = lambda *shape: jax.ShapeDtypeStruct(shape, BF)
    f32 = lambda *shape: jax.ShapeDtypeStruct(shape, F32)
    out_shape = [
        bf(count, rows, width),
        bf(shards, *heads_own.shape),
        bf(shards, ff_part, width),
        bf(width, length),
        bf(length, width),
        bf(length, 2 * ff),
        bf(ff, length),
        bf(length, cols),
        bf(length, cols),
        bf(length, cols),
        f32(length, cols),
        bf(cols, length),
        f32(length, cols),
        bf(count, rows, width),
    ]
    return pl.pallas_call(
        forward_kernel,
        out_shape=out_shape,
        in_specs=[smem] * 2 + [vmem_whole()] * 6 + [hbm_whole()] * 5,
        out_specs=[hbm_whole()] * len(out_shape),
        scratch_shapes=[
            pltpu.VMEM(w_inner.shape, BF),
            pltpu.VMEM((width, heads_own.shape[1]), BF),
            pltpu.VMEM((length, width), BF),
            pltpu.VMEM((length, ff), BF),
            pltpu.VMEM((length, cols), BF),
            pltpu.VMEM((2, rows, width), BF),
            pltpu.VMEM((2, width, rows), BF),
            pltpu.VMEM((2, length, TILE), BF),
            pltpu.VMEM((2, HALF, length), BF),
            pltpu.VMEM((2, length, HALF), BF),
            pltpu.VMEM((2, length, HALF), BF),
            pltpu.VMEM((2, length, HALF), BF),
            pltpu.VMEM((2, length, HALF), F32),
            pltpu.VMEM((2, HALF, length), BF),
            pltpu.VMEM((2, length, HALF), F32),
            pltpu.VMEM((2, shards, ff_part, TILE), BF),
            pltpu.VMEM((2, shards, attn_part, TILE), BF),
            pltpu.VMEM((count, rows, TILE), F32),
            pltpu.VMEM((2, count, rows, TILE), BF),
            pltpu.VMEM((ff_part, width), BF),
            pltpu.VMEM((rows, width), BF),
            pltpu.VMEM(heads_own.shape, BF),
            dma((1 + shards,)),
            dma((2, count - 1)),
            dma((2, count - 1)),
            dma((2, 8)),
            dma((2, 8)),
            dma((3, 2)),
            dma((2, 2)),
            dma((2, 2)),
            dma((6, 2)),
            dma((2, 2)),
            dma((2,)),
        ],
        compiler_params=pltpu.CompilerParams(
            collective_id=3, has_side_effects=True, vmem_limit_bytes=60 * 2**20
        ),
        name="forward",
    )(order, slots, x_all, gain, bias, *tables, cot, w_down, attn, w_inner, heads_own)


def fixed_tables(length):
    half = ROT // 2
    inverse = np.float32(10000.0) ** (-np.arange(half, dtype=np.float32) / np.float32(half))
    grid = np.arange(length, dtype=np.float32)[:, None] * inverse.astype(np.float32)[None, :]
    cos, sin = np.cos(grid, dtype=np.float32), np.sin(grid, dtype=np.float32)
    zero, rest = np.zeros((length, half), np.float32), np.zeros((length, HD - ROT), np.float32)
    tables = ([cos, cos, rest + 1], [-sin, zero, rest], [zero, sin, rest])
    return [jnp.asarray(np.tile(np.concatenate(t, axis=1), (1, 2))) for t in tables]


def rows_of(shard, part):
    return slice(shard * part, (shard + 1) * part)


def heads_back_pair(q_in, k_in, v_in, do_in, att, lse, cos, first, second, out, dk, dv):
    length = q_in.shape[0]
    scale = HD ** (-0.5)
    row = lax.broadcasted_iota(jnp.int32, (CHUNK, CHUNK), 0)
    col = lax.broadcasted_iota(jnp.int32, (CHUNK, CHUNK), 1)
    dk[...] = jnp.zeros_like(dk)
    dv[...] = jnp.zeros_like(dv)
    for c in range(length // CHUNK):
        lo, hi = c * CHUNK, (c + 1) * CHUNK
        dqs = []
        for h in range(2):
            lanes = slice(h * HD, (h + 1) * HD)
            q, do = q_in[lo:hi, lanes], do_in[lo:hi, lanes]
            delta = jnp.sum(do.astype(F32) * att[lo:hi, lanes], axis=1, keepdims=True)
            s = contract(q, k_in[lo:hi, lanes], ((1,), (1,)))
            s = jnp.where(col <= row, s, NEG)
            if c:
                s = jnp.concatenate([contract(q, k_in[:lo, lanes], ((1,), (1,))), s], axis=1)
            p = jnp.exp(s - lse[lo:hi, h * HD : h * HD + 1])
            dp = contract(do, v_in[:hi, lanes], ((1,), (1,)))
            ds = (p * (dp - delta)).astype(BF)
            dqs.append(contract(ds, k_in[:hi, lanes], ((1,), (0,))) * scale)
            dk[:hi, lanes] += contract(ds, q, ((0,), (0,)))
            dv[:hi, lanes] += contract(p.astype(BF), do, ((0,), (0,)))
        dq = jnp.concatenate(dqs, axis=1)
        out[0, lo:hi, :] = turn(dq, cos[lo:hi, :], -first[lo:hi, :], -second[lo:hi, :]).astype(BF)
    out[1] = turn(dk[...], cos[...], -first[...], -second[...]).astype(BF)
    out[2] = dv[...].astype(BF)


def tile_at(i, size=TILE):
    return pl.ds(pl.multiple_of(i * size, size), size)


def backward_kernel(
    order, slots, hid_t, att_t, cos, first, second,
    cot, norm_hbm, down, attn, both, branch, w_inner, w_heads, hat, q_in, k_in, v_in, att_in, lse_in,
    pieces, sums,
    cot_own, norm_t, d_inner, d_mixed, terms, term, small, w_tile, h_tile, hat_tile,
    attn_tile, q_tile, k_tile, v_tile, att_tile, lse_tile, d_att, turned, dk, dv, sums_stage,
    partial, theirs, pair, landed, total, sum_from, sum_land,
    core_send, core_recv, chip_send, chip_recv, line_send, line_recv, own_sem, sum_send, sum_recv,
    cot_sem, load_sem, feed_sem, back_sem, head_sem, sums_sem,
):
    count, chunks = pieces.shape[0], pieces.shape[1]
    shards = 2 * partial.shape[1]
    chips = shards // 2
    rows = terms.shape[1]
    place, me = lax.axis_index("ctx"), lax.axis_index("fsdp")
    chip, core = me // 2, me % 2
    ff_part, attn_part = hid_t.shape[0] // shards, att_t.shape[0] // shards
    sum_parts = terms.shape[2] // TILE
    early = cot_own.shape[1] // TILE - 1
    inner_end = early + d_inner.shape[1] // TILE

    def chunk_name(i):
        return jnp.where(i < early, i + chunks - 1 - early, jnp.where(i == chunks - 1, i, i - early))

    def core_copy(i):
        return pltpu.make_async_remote_copy(
            src_ref=partial.at[i % 2, :, 1 - core],
            dst_ref=theirs.at[i % DEEP],
            send_sem=core_send.at[i % 2],
            recv_sem=core_recv.at[i % DEEP],
            device_id=(place, me + 1 - 2 * core),
            device_id_type=MESH,
        )

    def chip_copy(j, m):
        return pltpu.make_async_remote_copy(
            src_ref=pair.at[j % 2, chip_away(chip, m)],
            dst_ref=landed.at[j % DEEP, m - 1],
            send_sem=chip_send.at[j % 2, m - 1],
            recv_sem=chip_recv.at[j % DEEP, m - 1],
            device_id=(place, 2 * chip_away(chip, m) + core),
            device_id_type=MESH,
        )

    def line_copy(way, hop, k):
        ahead = 1 - 2 * way
        origin = place - (hop - 1) * ahead
        target = pieces.at[origin, chunk_name(k)]
        return pltpu.make_async_remote_copy(
            src_ref=total.at[k % DEEP] if hop == 1 else target,
            dst_ref=target,
            send_sem=line_send.at[way, hop - 1, k % DEEP],
            recv_sem=line_recv.at[way, k, hop - 1],
            device_id=(place + ahead, me),
            device_id_type=MESH,
        )

    def sends(way, hop):
        if way == 0:
            return (place >= hop - 1) & (place <= count - 2)
        return (place <= count - hop) & (place >= 1)

    def lands(way, hop):
        return place >= hop if way == 0 else place <= count - 1 - hop

    def forward_chunk(hop, k):
        for way in range(2):
            if hop > 1:
                @pl.when(lands(way, hop - 1))
                def _(way=way):
                    line_copy(way, hop - 1, k).wait_recv()

            if hop < count:
                @pl.when(sends(way, hop))
                def _(way=way):
                    @pl.when(k >= DEEP)
                    def _():
                        line_copy(way, hop, k - DEEP).wait_send()

                    line_copy(way, hop, k).start()

    def own_copy(k):
        return pltpu.make_async_copy(total.at[k % DEEP], pieces.at[place, chunk_name(k)], own_sem.at[k % DEEP])

    def sum_copy(way, t, q):
        return pltpu.make_async_remote_copy(
            src_ref=sum_from.at[way, t - 1, q % 2],
            dst_ref=sum_land.at[way, t - 1, q % sum_parts],
            send_sem=sum_send.at[way, t - 1, q % 2],
            recv_sem=sum_recv.at[way, t - 1, q],
            device_id=(place + 1 - 2 * way, me),
            device_id_type=MESH,
        )

    def sum_sends(way, t):
        return place <= t - 1 if way == 0 else place >= count - t

    def sum_step(t, q):
        at = tile_at(q % sum_parts)
        for way in range(2):
            @pl.when(sum_sends(way, t))
            def _(way=way):
                to = count - t + place if way == 0 else t + place - count
                starts = place == 0 if way == 0 else place == count - 1

                @pl.when(q >= 2)
                def _():
                    sum_copy(way, t, q - 2).wait_send()

                @pl.when(starts)
                def _():
                    sum_from[way, t - 1, q % 2] = terms[to, :, at]

                if t > 1:
                    @pl.when(jnp.logical_not(starts))
                    def _():
                        sum_copy(way, t - 1, q).wait_recv()
                        value = terms[to, :, at].astype(F32) + sum_land[way, t - 2, q % sum_parts].astype(F32)
                        sum_from[way, t - 1, q % 2] = value.astype(BF)

                sum_copy(way, t, q).start()

    def sums_copy(q):
        return pltpu.make_async_copy(
            sums_stage.at[q % 2], sums.at[q // sum_parts, :, tile_at(q % sum_parts)], sums_sem.at[q % 2]
        )

    def sum_end(q):
        @pl.when(q >= 2)
        def _():
            sums_copy(q - 2).wait()

        sums_stage[q % 2] = terms[place, :, tile_at(q % sum_parts)].astype(F32)
        for way in range(2):
            @pl.when(place >= 1 if way == 0 else place <= count - 2)
            def _(way=way):
                sum_copy(way, count - 1, q).wait_recv()
                sums_stage[q % 2] += sum_land[way, count - 2, q % sum_parts].astype(F32)

        sums_copy(q).start()

    cot_load = pltpu.make_async_copy(cot, terms, cot_sem)

    def feed_load(b, size):
        at = pl.ds(pl.multiple_of(b * TILE, TILE), size)
        return pltpu.make_async_copy(
            down.at[at], w_tile.at[b % 2, :size, : cot_own.shape[1]], feed_sem.at[b % 2]
        )

    both_load = pltpu.make_async_copy(both, d_inner, load_sem.at[2])

    loads = [
        pltpu.make_async_copy(branch, terms, load_sem.at[0]),
        pltpu.make_async_copy(norm_hbm, norm_t, load_sem.at[1]),
    ]

    def back_loads(q):
        moves = (
            (w_inner.at[tile_at(q)], w_tile.at[q % 2]),
            (w_heads.at[tile_at(q)], h_tile.at[q % 2]),
            (hat.at[:, tile_at(q)], hat_tile.at[q % 2]),
        )
        return [pltpu.make_async_copy(a, b, back_sem.at[n, q % 2]) for n, (a, b) in enumerate(moves)]

    def head_loads(h):
        moves = ((q_in, q_tile), (k_in, k_tile), (v_in, v_tile), (att_in, att_tile), (lse_in, lse_tile))
        at = tile_at(h, HALF)
        copies = [
            pltpu.make_async_copy(a.at[:, at], b.at[h % 2], head_sem.at[n, h % 2]) for n, (a, b) in enumerate(moves)
        ]
        return copies

    def attn_load(h):
        return pltpu.make_async_copy(attn.at[tile_at(h // 2)], attn_tile, load_sem.at[3])

    pairs = q_in.shape[1] // HALF
    tiles = d_inner.shape[1] // TILE
    for c in [cot_load, both_load, feed_load(0, TILE), feed_load(1, TILE), attn_load(0)] + head_loads(0) + head_loads(1) + loads[1:]:
        c.start()
    peers = [(place, me + 1 - 2 * core)]
    peers += [(place, 2 * chip_away(chip, m) + core) for m in range(1, chips)]
    greet(peers + [((place + 1) % count, me), ((place + count - 1) % count, me)])
    cot_load.wait()
    for p in range(count):
        cot_own[p * rows : (p + 1) * rows, :] = terms[slots[p]]
    loads[0].start()
    loads[0].wait()

    ff = down.shape[0]
    whole_tiles = ff // TILE

    def feed_tile(b, size):
        feed_load(b, size).wait()
        d_hidden = contract(cot_own[...], w_tile[b % 2, :size, : cot_own.shape[1]], ((1,), (1,)))
        for n in range(size // HALF):
            d = d_hidden[:, n * HALF : (n + 1) * HALF]
            at = tile_at(2 * b + n)
            value = d_inner[:, at]
            gate = value[:, :HALF].astype(F32)
            up = value[:, HALF:].astype(F32)
            sig = jax.nn.sigmoid(gate)
            d_gate = d * up * sig * (1.0 + gate * (1.0 - sig))
            d_inner[:, at] = jnp.concatenate([d_gate, d * gate * sig], axis=1).astype(BF)

    def feed_step(b, carry):
        feed_tile(b, TILE)

        @pl.when(b + 2 < whole_tiles)
        def _():
            feed_load(b + 2, TILE).start()

        if ff % TILE:
            @pl.when(b + 2 == whole_tiles)
            def _():
                feed_load(whole_tiles, ff % TILE).start()

        return carry

    def store(i, shard, lo, value):
        partial[i % 2, shard // 2, shard % 2, lo : lo + value.shape[0], :] = value

    def from_norm(i, rhs):
        for s in range(0, shards, 2):
            part = norm_t.shape[0] // shards
            value = contract(norm_t[s * part : (s + 2) * part, :], rhs, ((1,), (0,))).astype(BF)
            store(i, s, 0, value[:part])
            store(i, s + 1, 0, value[part:])

    def step(i, carry):
        @pl.when((i < early) | (i == chunks - 1))
        def _():
            c = jnp.where(i < early, i, early)
            rhs = cot_own[:, tile_at(c)]
            for s in range(0, shards, 4):
                value = contract(hid_t[s * ff_part : (s + 4) * ff_part, :], rhs, ((1,), (0,))).astype(BF)
                for t in range(4):
                    store(i, s + t, 0, value[rows_of(t, ff_part)])
            value = contract(att_t[...], rhs, ((1,), (0,))).astype(BF)
            for s in range(shards):
                store(i, s, ff_part, value[rows_of(s, attn_part)])

        @pl.when(i == chunks - 1)
        def _():
            for s in range(shards):
                store(i, s, ff_part + attn_part, small[s])

        @pl.when(i == early)
        def _():
            loads[1].wait()

        @pl.when((i >= early) & (i < inner_end))
        def _():
            from_norm(i, d_inner[:, tile_at(i - early)])

        @pl.when((i >= inner_end) & (i < chunks - 1))
        def _():
            at = i - inner_end
            from_norm(i, d_mixed[:, tile_at(at)])

        @pl.when(i < chunks)
        def _():
            core_copy(i).start()

        @pl.when((i >= 1) & (i < chunks + 1))
        def _():
            j = i - 1
            core_copy(j).wait()
            for m in range(chips):
                a = partial[j % 2, m, core].astype(F32) + theirs[j % DEEP, m].astype(F32)
                pair[j % 2, m] = a.astype(BF)
            for m in range(1, chips):
                chip_copy(j, m).start()

        @pl.when((i >= 2) & (i < chunks + 2))
        def _():
            k = i - 2
            for m in range(1, chips):
                chip_copy(k, m).wait()

            a = pair[k % 2, chip].astype(F32)
            for m in range(1, chips):
                a = a + landed[k % DEEP, m - 1].astype(F32)
            for way in range(2):
                @pl.when(sends(way, 1) & (k >= DEEP))
                def _(way=way):
                    line_copy(way, 1, k - DEEP).wait_send()

            @pl.when(k >= DEEP)
            def _():
                own_copy(k - DEEP).wait()

            total[k % DEEP] = a.astype(BF)
            for way in range(2):
                @pl.when(sends(way, 1))
                def _(way=way):
                    line_copy(way, 1, k).start()

            own_copy(k).start()

        @pl.when((i >= sum_parts) & (i < 2 * sum_parts))
        def _():
            q = i - sum_parts
            for c in back_loads(q):
                c.wait()
            value = contract(d_inner[...], w_tile[q % 2], ((1,), (1,)))
            value = value + contract(d_mixed[...], h_tile[q % 2], ((1,), (1,)))
            term[...] = value.reshape(term.shape)
            gain = jnp.sum(value * hat_tile[q % 2].astype(F32), axis=0, keepdims=True)
            bias = jnp.sum(value, axis=0, keepdims=True)
            row = lax.broadcasted_iota(jnp.int32, small.shape[1:], 0)
            small[q] = jnp.where(row == 0, gain, jnp.where(row == 1, bias, 0.0)).astype(BF)
            for j in range(count):
                terms[j, :, tile_at(q)] = term[order[j]].astype(BF)

            @pl.when(q + 2 < sum_parts)
            def _():
                for c in back_loads(q + 2):
                    c.start()

        for t in range(1, count + 1):
            q = i - LAG * (t - 1)

            @pl.when((q >= 0) & (q < 2 * sum_parts))
            def _(q=q, t=t):
                if t < count:
                    sum_step(t, q)
                else:
                    sum_end(q)

        for hop in range(2, count + 1):
            k = i - 2 - LAG * (hop - 1)

            @pl.when((k >= 0) & (k < chunks))
            def _(k=k, hop=hop):
                forward_chunk(hop, k)

        @pl.when(i == 0)
        def _():
            both_load.wait()

        @pl.when((i == 0) | (i == 1) | (i == 4))
        def _():
            first_tile = jnp.where(i == 0, 0, jnp.where(i == 1, 1, 3))
            last_tile = jnp.where(i == 0, 1, jnp.where(i == 1, 3, whole_tiles))
            lax.fori_loop(first_tile, last_tile, feed_step, 0)

        if ff % TILE:
            @pl.when(i == 4)
            def _():
                feed_tile(whole_tiles, ff % TILE)

        @pl.when(i == 5)
        def _():
            for c in back_loads(0) + back_loads(1):
                c.start()

        @pl.when((i == 2) | (i == 3) | (i == 5) | (i == 6))
        def _():
            h = i - 2 - i // 5
            for c in head_loads(h):
                c.wait()
            slot = h % 2

            @pl.when(slot == 0)
            def _():
                attn_load(h).wait()
                value = contract(cot_own[...], attn_tile[...], ((1,), (1,)))
                for n in range(2):
                    d_att[n] = value[:, n * HALF : (n + 1) * HALF].astype(BF)

                @pl.when(h + 2 < pairs)
                def _():
                    attn_load(h + 2).start()

            heads_back_pair(
                q_tile.at[slot], k_tile.at[slot], v_tile.at[slot], d_att.at[slot], att_tile.at[slot],
                lse_tile.at[slot], cos, first, second, turned, dk, dv,
            )
            for n in range(3):
                d_mixed[:, tile_at(3 * h + n, HALF)] = turned[n]

            @pl.when(h + 2 < pairs)
            def _():
                for c in head_loads(h + 2):
                    c.start()

        return carry

    lax.fori_loop(0, chunks + 2 + LAG * (count - 1), step, 0)

    def drain(k, carry):
        own_copy(k).wait()
        for way in range(2):
            for hop in range(1, count):
                @pl.when(sends(way, hop))
                def _(way=way, hop=hop):
                    line_copy(way, hop, k).wait_send()
        return carry

    lax.fori_loop(chunks - DEEP, chunks, drain, 0)
    for q in range(2):
        sums_copy(2 * sum_parts - 2 + q).wait()
    for way in range(2):
        for t in range(1, count):
            @pl.when(sum_sends(way, t))
            def _(way=way, t=t):
                for q in range(2):
                    sum_copy(way, t, 2 * sum_parts - 2 + q).wait_send()


def backward(
    order, slots, hid_t, att_t, tables, cot, norm_t, down, attn, both, branch, w_inner, w_heads, hat, heads, shards
):
    count, rows, width = cot.shape
    length = count * rows
    chips = shards // 2
    cols = heads[0].shape[1]
    inner = both.shape[1]
    chunks = (width + inner + 3 * cols) // TILE
    part = width // shards
    parts = width // TILE
    dma = pltpu.SemaphoreType.DMA
    smem = pl.BlockSpec(memory_space=pltpu.SMEM)
    return pl.pallas_call(
        backward_kernel,
        out_shape=[
            jax.ShapeDtypeStruct((count, chunks, part, TILE), BF),
            jax.ShapeDtypeStruct((2, rows, width), F32),
        ],
        in_specs=[smem] * 2 + [vmem_whole()] * 5 + [hbm_whole()] * 14,
        out_specs=[hbm_whole()] * 2,
        scratch_shapes=[
            pltpu.VMEM((length, width), BF),
            pltpu.VMEM((width, length), BF),
            pltpu.VMEM((length, inner), BF),
            pltpu.VMEM((length, 3 * cols), BF),
            pltpu.VMEM((count, rows, width), BF),
            pltpu.VMEM((count, rows, TILE), F32),
            pltpu.VMEM((parts, 16, TILE), BF),
            pltpu.VMEM((2, TILE, inner), BF),
            pltpu.VMEM((2, TILE, 3 * cols), BF),
            pltpu.VMEM((2, length, TILE), BF),
        ]
        + [pltpu.VMEM((TILE, width), BF)]
        + [pltpu.VMEM((2, length, HALF), BF)] * 3
        + [pltpu.VMEM((2, length, HALF), F32)] * 2
        + [pltpu.VMEM((2, length, HALF), BF)]
        + [pltpu.VMEM((3, length, HALF), BF)]
        + [pltpu.VMEM((length, HALF), F32)] * 2
        + [pltpu.VMEM((2, rows, TILE), F32)]
        + [
            pltpu.VMEM((2, chips, 2, part, TILE), BF),
            pltpu.VMEM((DEEP, chips, part, TILE), BF),
            pltpu.VMEM((2, chips, part, TILE), BF),
            pltpu.VMEM((DEEP, chips - 1, part, TILE), BF),
            pltpu.VMEM((DEEP, part, TILE), BF),
            pltpu.VMEM((2, count - 1, 2, rows, TILE), BF),
            pltpu.VMEM((2, count - 1, parts, rows, TILE), BF),
            dma((2,)),
            dma((DEEP,)),
            dma((2, chips - 1)),
            dma((DEEP, chips - 1)),
            dma((2, count - 1, DEEP)),
            dma((2, chunks, count - 1)),
            dma((DEEP,)),
            dma((2, count - 1, 2)),
            dma((2, count - 1, 2 * parts)),
            pltpu.SemaphoreType.DMA,
            dma((4,)),
            dma((2,)),
            dma((3, 2)),
            dma((5, 2)),
            dma((2,)),
        ],
        compiler_params=pltpu.CompilerParams(
            collective_id=1, has_side_effects=True, vmem_limit_bytes=62 * 2**20
        ),
        name="backward",
    )(order, slots, hid_t, att_t, *tables, cot, norm_t, down, attn, both, branch, w_inner, w_heads, hat, *heads)


def column_runs(columns, source):
    out = []
    for block in range(columns // HALF):
        first = 0
        while first < HALF:
            key, lane = source(block * HALF + first)
            last = first + 1
            while last < HALF and source(block * HALF + last) == (key, lane + last - first):
                last += 1
            out.append((block, first, last, key, (first - lane) % HALF))
            first = last
    return out


def assemble_kernel(rows_in, cols_in, sums, tokens, cot, gain, out, grad, qkv_out, gate_out, up_out, down_out, attn_out, small_out):
    count, chunks, rows, _ = rows_in.shape
    ff = gate_out.shape[1]
    width = qkv_out.shape[1]
    ff_part = down_out.shape[0] // count
    attn_part = attn_out.shape[0] // count
    shards = ff // (count * ff_part)
    inner_chunks = ff // count // HALF
    lane = lax.broadcasted_iota(jnp.int32, (rows, HALF), 1)
    own = tokens[...].astype(F32)
    out[...] = (own + sums[0]).astype(BF)
    own = own - jnp.mean(own, axis=1, keepdims=True)
    inv_std = lax.rsqrt(jnp.mean(own * own, axis=1, keepdims=True) + EPS)
    own = own * inv_std
    scaled = sums[1] * gain[...]
    scaled = scaled - jnp.mean(scaled, axis=1, keepdims=True) - own * jnp.mean(scaled * own, axis=1, keepdims=True)
    grad[...] = cot[...].astype(F32) + inv_std * scaled

    def gather(out, runs, load):
        for block, first, last, key, shift in runs:
            value = load(key).astype(F32)
            if shift:
                value = pltpu.roll(value, shift, 1)
            if first:
                value = jnp.where(lane >= first, value, held)
            held = value
            if last == HALF:
                out[:, block * HALF : (block + 1) * HALF] = value

    def inner_source(column):
        shard, rest = divmod(column, count * ff_part)
        unit = shard * ff_part + rest % ff_part
        return (rest // ff_part, unit // HALF), unit % HALF

    def head_source(column):
        part, rest = divmod(column, width // 3)
        head, dim = divmod(rest, HD)
        per = width // 3 // HD // shards // count
        shard, at = divmod(head, per * count)
        place, sub = divmod(at, per)
        pair, half = divmod(shard * per + sub, 2)
        return (place, 3 * pair + part), half * HD + dim

    runs = column_runs(ff, inner_source)
    gather(gate_out, runs, lambda key: rows_in[key[0], key[1], :, :HALF])
    gather(up_out, runs, lambda key: rows_in[key[0], key[1], :, HALF:])
    first_head = inner_chunks

    def head_load(key):
        at = key[1] % 2 * HALF
        return rows_in[key[0], first_head + key[1] // 2, :, at : at + HALF]

    gather(qkv_out, column_runs(width, head_source), head_load)
    for p in range(count):
        down_out[p * ff_part : (p + 1) * ff_part, :] = cols_in[p, 0, :ff_part, :].astype(F32)
        attn_out[p * attn_part : (p + 1) * attn_part, :] = cols_in[
            p, 0, ff_part : ff_part + attn_part, :
        ].astype(F32)
    small = [cols_in[p, 0, ff_part + attn_part :, :].astype(F32) for p in range(count)]
    small_out[...] = functools.reduce(jnp.add, small)


def assemble_outputs(pieces, sums, tokens, cot, gain, qkv, attn, gate, down):
    count, chunks, rows, _ = pieces.shape
    steps = down[1] // TILE
    part = rows // steps
    width = tokens.shape[1]
    by_rows = lambda shape: pl.BlockSpec((part, shape[1]), lambda i: (i, 0))
    by_cols = lambda shape: pl.BlockSpec((shape[0], TILE), lambda i: (0, i))
    return pl.pallas_call(
        assemble_kernel,
        grid=(steps,),
        in_specs=[
            pl.BlockSpec((count, chunks - steps, part, TILE), lambda i: (0, 0, i, 0)),
            pl.BlockSpec((count, 1, rows, TILE), lambda i: (0, chunks - steps + i, 0, 0)),
            pl.BlockSpec((2, part, width), lambda i: (0, i, 0)),
            by_rows(tokens.shape),
            by_rows(tokens.shape),
            pl.BlockSpec((1, width), lambda i: (0, 0)),
        ],
        out_specs=[by_rows(tokens.shape)] * 2
        + [by_rows(qkv), by_rows(gate), by_rows(gate), by_cols(down), by_cols(attn)]
        + [pl.BlockSpec((16, TILE), lambda i: (0, 0))],
        out_shape=[jax.ShapeDtypeStruct(tokens.shape, BF), jax.ShapeDtypeStruct(tokens.shape, F32)]
        + [jax.ShapeDtypeStruct(s, F32) for s in (qkv, gate, gate, down, attn, (16, TILE))],
        compiler_params=pltpu.CompilerParams(vmem_limit_bytes=60 * 2**20),
        name="assemble",
    )(pieces, pieces, sums, tokens, cot, gain)


def rotation_tables(length):
    half = ROT // 2
    inverse = 10000.0 ** (-jnp.arange(half, dtype=F32) / half)
    grid = jnp.arange(length, dtype=jnp.int32).astype(F32)[:, None] * inverse[None, :]
    cos, sin = jnp.cos(grid), jnp.sin(grid)
    zero = jnp.zeros((length, half), F32)
    rest = jnp.zeros((length, HD - ROT), F32)
    tables = (
        jnp.concatenate([cos, cos, rest + 1.0], axis=1),
        jnp.concatenate([-sin, zero, rest], axis=1),
        jnp.concatenate([zero, sin, rest], axis=1),
    )
    return tuple(jnp.tile(t, (1, 2)) for t in tables)


def body_general(tokens, block_order, ln_gain, ln_bias, w_qkv, w_out, w_gate, w_up, w_down, cotangent):
    rows, width = tokens.shape[1], tokens.shape[2]
    count = lax.axis_size("ctx")
    shards = lax.axis_size("fsdp")
    place = lax.axis_index("ctx")
    length = rows * count
    order = block_order[0]
    shard_rows = w_qkv.shape[0]
    ff_shard = w_down.shape[0]
    ff_part = ff_shard // count
    own_heads = H // count
    spread = (w_out.shape[0] // HD) % count == 0
    groups = shards if spread else 1
    head_cols = own_heads * HD // groups

    def my_cols(w, outer, group, part):
        w = w.reshape(w.shape[0], outer, group, count, part)
        return lax.dynamic_index_in_dim(w, place, 3, False).reshape(w.shape[0], outer * group * part)

    def all_cols(piece, outer, group, part):
        whole = gather_ctx(piece).reshape(count, piece.shape[0], outer, group, part)
        return whole.transpose(1, 2, 3, 0, 4).reshape(piece.shape[0], -1).astype(F32)

    def assemble(block, ready=None):
        whole = jnp.zeros((length, width), block.dtype)
        whole = lax.dynamic_update_slice_in_dim(whole, block, order[place] * rows, 0)
        last = None
        for k in range(1, count):
            last = ring_send(block, k)
            source = (place - k) % count
            whole = lax.dynamic_update_slice_in_dim(whole, last, order[source] * rows, 0)
        return whole, last

    gain = lax.all_gather(ln_gain, "fsdp", axis=0, tiled=True).astype(F32)
    bias = lax.all_gather(ln_bias, "fsdp", axis=0, tiled=True).astype(F32)
    tables = rotation_tables(length)

    block = tokens[0]
    x_all, arrived = assemble(block)
    grad_block = cotangent[0]
    cot_all, _ = assemble(after(grad_block, arrived))

    inner = jnp.concatenate(
        [my_cols(w_gate, 1, shards, ff_part), my_cols(w_up, 1, shards, ff_part)], axis=1
    )
    w_inner, sent = gather_rows(inner)
    w_heads, sent = gather_rows(after(my_cols(w_qkv, 3, groups, head_cols), sent))
    down = lax.dynamic_slice_in_dim(w_down, place * ff_part, ff_part, 0)
    w_hidden, sent = gather_rows(after(down, sent))
    if spread:
        part = w_out.shape[0] // count
        attn = lax.dynamic_slice_in_dim(w_out, place * part, part, 0)
        w_attn, sent = gather_rows(after(attn, sent))
    else:
        w_attn = lax.all_gather(after(w_out, sent), "fsdp", axis=0, tiled=True)
        w_attn = lax.dynamic_slice_in_dim(w_attn, place * own_heads * HD, own_heads * HD, 0)

    xf = x_all.astype(F32)
    average = jnp.mean(xf, axis=-1, keepdims=True)
    centered = xf - average
    variance = jnp.mean(centered * centered, axis=-1, keepdims=True)
    inv_std = lax.rsqrt(variance + EPS)
    x_hat = centered * inv_std
    normed = (x_hat * gain + bias).astype(BF)

    across = ((1,), (0,))
    over_tokens = ((0,), (0,))
    back = ((1,), (1,))
    ff_cols = shards * ff_part
    gate_value = dot(normed, w_inner[:, :ff_cols], across)
    up_value = dot(normed, w_inner[:, ff_cols:], across)
    sigmoid_gate = jax.nn.sigmoid(gate_value)
    hidden = (gate_value * sigmoid_gate * up_value).astype(BF)
    mixed = dot(normed, w_heads, across)
    q, k, v, attended, lse = attend(mixed, tables, own_heads)
    attended_low = attended.astype(BF)

    branch = dot(attended_low, w_attn, across) + dot(hidden, w_hidden, across)
    out = line_scatter(lambda j: lax.dynamic_slice_in_dim(branch, order[j] * rows, rows, 0))
    out = (block.astype(F32) + out).astype(BF)[None]

    d_hidden = dot(cot_all, w_hidden, back)
    grad_down = scatter_rows(dot(hidden, cot_all, over_tokens, BF))
    d_gate_act = (
        d_hidden * up_value * sigmoid_gate * (1.0 + gate_value * (1.0 - sigmoid_gate))
    ).astype(BF)
    d_up_act = (d_hidden * gate_value * sigmoid_gate).astype(BF)
    d_inner = jnp.concatenate([d_gate_act, d_up_act], axis=1)
    d_attended = dot(cot_all, w_attn, back, BF)
    d_mixed = attend_back(q, k, v, d_attended, attended, lse, tables, own_heads)
    d_mixed = jnp.concatenate(d_mixed, axis=1)
    grad_inner = scatter_rows(dot(normed, d_inner, over_tokens, BF))
    grad_attn = dot(attended_low, cot_all, over_tokens, BF)
    grad_heads = scatter_rows(dot(normed, d_mixed, over_tokens, BF))

    d_normed = dot(d_inner, w_inner, back) + dot(d_mixed, w_heads, back)
    small = jnp.stack([jnp.sum(d_normed * x_hat, axis=0), jnp.sum(d_normed, axis=0)])
    small = lax.psum(small, ("ctx", "fsdp"))
    small = lax.dynamic_slice_in_dim(small, lax.axis_index("fsdp") * shard_rows, shard_rows, 1)
    d_own = line_scatter(lambda j: lax.dynamic_slice_in_dim(d_normed, order[j] * rows, rows, 0))
    own = block.astype(F32)
    own_average = jnp.mean(own, axis=-1, keepdims=True)
    own = own - own_average
    own_std = lax.rsqrt(jnp.mean(own * own, axis=-1, keepdims=True) + EPS)
    own = own * own_std
    scaled = d_own * gain
    d_input = own_std * (
        scaled
        - jnp.mean(scaled, axis=-1, keepdims=True)
        - own * jnp.mean(scaled * own, axis=-1, keepdims=True)
    )
    grad_in = (grad_block.astype(F32) + d_input)[None]

    down_all = gather_ctx(grad_down).reshape(ff_shard, width).astype(F32)
    if spread:
        attn_all = gather_ctx(scatter_rows(grad_attn)).reshape(w_out.shape).astype(F32)
    else:
        full = jnp.zeros((H * HD, width), BF)
        full = lax.dynamic_update_slice_in_dim(full, grad_attn, place * own_heads * HD, 0)
        full = lax.psum_scatter(full, "fsdp", scatter_dimension=0, tiled=True)
        attn_all = lax.psum(full, "ctx").astype(F32)
    heads_all = all_cols(grad_heads, 3, groups, head_cols)
    inner_all = gather_ctx(grad_inner).reshape(count, shard_rows, 2, shards, ff_part)
    inner_all = inner_all.transpose(2, 1, 3, 0, 4).reshape(2, shard_rows, -1).astype(F32)
    return (
        out,
        grad_in,
        small[0],
        small[1],
        heads_all,
        attn_all,
        inner_all[0],
        inner_all[1],
        down_all,
    )


def body_fast(tokens, block_order, ln_gain, ln_bias, w_qkv, w_out, w_gate, w_up, w_down, cotangent):
    count, shards = lax.axis_size("ctx"), lax.axis_size("fsdp")
    place = lax.axis_index("ctx")
    block, grad_block = tokens[0], cotangent[0]
    rows, width = block.shape
    order = block_order[0]
    spots = jnp.arange(count, dtype=jnp.int32)
    slots = jnp.sum(jnp.where(order[None, :] == spots[:, None], spots[None, :], 0), axis=1)
    vectors = jnp.stack([ln_gain, ln_bias] + [jnp.zeros_like(ln_gain)] * 6).astype(F32)
    x_all, vectors, w_inner, heads_own, w_attn = start(
        block, vectors, w_gate, w_up, w_qkv, w_out, count, shards
    )
    w_inner = w_inner.reshape(width, -1)
    gain, bias = vectors[:, 0].reshape(1, width), vectors[:, 1].reshape(1, width)
    tables = fixed_tables(rows * count)

    (
        cot_all, w_heads, w_hidden, normed_t, hat, both, hidden_t, q, k, v, attended, low_t, lse, branch,
    ) = forward(
        order, slots, x_all, gain, bias, tables, grad_block, w_down, w_attn, w_inner, heads_own, shards
    )
    w_hidden, w_attn = w_hidden.reshape(-1, width), w_attn.reshape(-1, width)
    w_heads = w_heads.reshape(width, -1)
    pieces, sums = backward(
        order, slots, hidden_t, low_t, tables, cot_all, normed_t, w_hidden, w_attn, both, branch, w_inner,
        w_heads, hat, (q, k, v, attended, lse), shards,
    )
    out, grad_in, d_qkv, d_gate, d_up, d_down, d_attn, small = assemble_outputs(
        pieces, sums, block, grad_block, gain, w_qkv.shape, w_out.shape, w_gate.shape, w_down.shape
    )
    out, grad_in = out[None], grad_in[None]
    return out, grad_in, small[0], small[1], d_qkv, d_attn, d_gate, d_up, d_down


def solution(mesh):
    whole, once = P("fsdp", "ctx", None), P("fsdp", None)
    count, shards = mesh.shape["ctx"], mesh.shape["fsdp"]

    def body(*args):
        w_out, w_down = args[5], args[8]
        fits = shards == 8 and w_out.shape[0] == count * HD and w_out.shape[0] == TILE
        fits = fits and w_down.shape[0] % (16 * count) == 0 and w_down.shape[0] // count <= 176
        return (body_fast if fits else body_general)(*args)

    return jax.shard_map(
        body,
        mesh=mesh,
        in_specs=(whole, once, P("fsdp"), P("fsdp")) + (once,) * 5 + (whole,),
        out_specs=(whole, whole, P("fsdp"), P("fsdp")) + (once,) * 5,
        check_vma=False,
    )
```

```python
import functools

import jax
import jax.numpy as jnp
import numpy as np
from jax import lax
from jax.experimental import pallas as pl
from jax.experimental.pallas import tpu as pltpu
from jax.sharding import PartitionSpec as P

H = 32
HD = 64
ROT = 16
EPS = 1e-05
NEG = -1e30
CHUNK = 256

BF = jnp.bfloat16
F32 = jnp.float32


def xor_send(value, mask):
    count = lax.axis_size("fsdp")
    return lax.ppermute(value, "fsdp", [(i, i ^ mask) for i in range(count)])


def ring_send(value, steps):
    count = lax.axis_size("ctx")
    return lax.ppermute(value, "ctx", [(i, (i + steps) % count) for i in range(count)])


def after(value, *done):
    return lax.optimization_barrier((value,) + done)[0]


def dot(a, b, dims, out=F32):
    return lax.dot_general(a, b, (dims, ((), ())), preferred_element_type=F32).astype(out)


def gather_rows(piece):
    count = lax.axis_size("fsdp")
    chips = count // 2
    me = lax.axis_index("fsdp")
    chip, core = me // 2, me % 2
    parts = [piece] + [xor_send(piece, 2 * m) for m in range(1, chips)]
    others = [xor_send(p, 1) for p in parts]
    whole = jnp.zeros((count,) + piece.shape, piece.dtype)
    for m in range(chips):
        at = 2 * (chip ^ m)
        whole = lax.dynamic_update_index_in_dim(whole, parts[m], at + core, 0)
        whole = lax.dynamic_update_index_in_dim(whole, others[m], at + 1 - core, 0)
    return whole.reshape(count * piece.shape[0], piece.shape[1]), parts[-1]


def scatter_rows(grad):
    count = lax.axis_size("fsdp")
    chips = count // 2
    me = lax.axis_index("fsdp")
    chip, core = me // 2, me % 2
    rows = grad.shape[0] // count
    split = grad.reshape(chips, 2, rows, grad.shape[1])
    theirs = xor_send(lax.dynamic_index_in_dim(split, 1 - core, 1, False), 1)
    pair = lax.dynamic_index_in_dim(split, core, 1, False).astype(F32) + theirs.astype(F32)
    pair = pair.astype(BF)
    total = lax.dynamic_index_in_dim(pair, chip, 0, False).astype(F32)
    for m in range(1, chips):
        part = lax.dynamic_index_in_dim(pair, chip ^ m, 0, False)
        total = total + xor_send(part, 2 * m).astype(F32)
    return total.astype(BF)


def gather_ctx(piece):
    count = lax.axis_size("ctx")
    me = lax.axis_index("ctx")
    whole = jnp.zeros((count,) + piece.shape, piece.dtype)
    whole = lax.dynamic_update_index_in_dim(whole, piece, me, 0)
    for k in range(1, count):
        part = ring_send(piece, k)
        whole = lax.dynamic_update_index_in_dim(whole, part, (me - k) % count, 0)
    return whole


def line_scatter(blocks):
    count = lax.axis_size("ctx")
    me = lax.axis_index("ctx")
    down = up = None
    for t in range(1, count):
        to_down = blocks(jnp.clip(t + me - count, 0, count - 1))
        to_up = blocks(jnp.clip(count - 1 - (t + (count - 1 - me) - count), 0, count - 1))
        if down is not None:
            to_down = to_down + down.astype(F32)
            to_up = to_up + up.astype(F32)
        pairs = [(i, i - 1) for i in range(count - t, count)]
        down = lax.ppermute(to_down.astype(BF), "ctx", pairs)
        up = lax.ppermute(to_up.astype(BF), "ctx", [(count - 1 - i, count - 1 - j) for i, j in pairs])
    return blocks(me) + down.astype(F32) + up.astype(F32)


def turn(x, cos, first, second):
    width = x.shape[1]
    half = ROT // 2
    return x * cos + pltpu.roll(x, width - half, 1) * first + pltpu.roll(x, half, 1) * second


def contract(a, b, dims):
    return lax.dot_general(a, b, (dims, ((), ())), preferred_element_type=F32)


def attend_kernel(mq, mk, mv, cos, first, second, q_out, k_out, v_out, att_out, lse_out):
    length = mq.shape[0]
    scale = HD ** (-0.5)
    q_out[...] = (turn(mq[...], cos[...], first[...], second[...]).astype(BF).astype(F32) * scale).astype(BF)
    k_out[...] = turn(mk[...], cos[...], first[...], second[...]).astype(BF)
    v_out[...] = mv[...].astype(BF)
    row = lax.broadcasted_iota(jnp.int32, (CHUNK, CHUNK), 0)
    col = lax.broadcasted_iota(jnp.int32, (CHUNK, CHUNK), 1)
    for c in range(length // CHUNK):
        lo, hi = c * CHUNK, (c + 1) * CHUNK
        for h in range(2):
            lanes = slice(h * HD, (h + 1) * HD)
            q = q_out[lo:hi, lanes]
            s = contract(q, k_out[lo:hi, lanes], ((1,), (1,)))
            s = jnp.where(col <= row, s, NEG)
            if c:
                s = jnp.concatenate([contract(q, k_out[:lo, lanes], ((1,), (1,))), s], axis=1)
            top = jnp.max(s, axis=1, keepdims=True)
            p = jnp.exp(s - top)
            total = jnp.sum(p, axis=1, keepdims=True)
            o = contract(p.astype(BF), v_out[:hi, lanes], ((1,), (0,)))
            att_out[lo:hi, lanes] = o / total
            lse_out[lo:hi, lanes] = jnp.broadcast_to(top + jnp.log(total), (CHUNK, HD))


def attend(mixed, tables, heads):
    length = mixed.shape[0]
    pairs = heads // 2
    block = lambda at: pl.BlockSpec((length, 2 * HD), lambda h, at=at: (0, at + h))
    table = pl.BlockSpec((length, 2 * HD), lambda h: (0, 0))
    width = heads * HD
    return pl.pallas_call(
        attend_kernel,
        grid=(pairs,),
        in_specs=[block(0), block(pairs), block(2 * pairs), table, table, table],
        out_specs=[block(0)] * 5,
        out_shape=[jax.ShapeDtypeStruct((length, width), BF)] * 3
        + [jax.ShapeDtypeStruct((length, width), F32)] * 2,
        compiler_params=pltpu.CompilerParams(vmem_limit_bytes=40 * 2**20),
        cost_estimate=pl.CostEstimate(
            flops=16 * heads * length * length * HD // 2,
            bytes_accessed=26 * length * width,
            transcendentals=heads * length * length // 2,
        ),
        name="attend",
    )(mixed, mixed, mixed, *tables)


def attend_back_kernel(q_in, k_in, v_in, do_in, att, lse, cos, first, second, dq_out, dk_out, dv_out, dk, dv):
    length = q_in.shape[0]
    scale = HD ** (-0.5)
    row = lax.broadcasted_iota(jnp.int32, (CHUNK, CHUNK), 0)
    col = lax.broadcasted_iota(jnp.int32, (CHUNK, CHUNK), 1)
    dk[...] = jnp.zeros_like(dk)
    dv[...] = jnp.zeros_like(dv)
    for c in range(length // CHUNK):
        lo, hi = c * CHUNK, (c + 1) * CHUNK
        dqs = []
        for h in range(2):
            lanes = slice(h * HD, (h + 1) * HD)
            q, do = q_in[lo:hi, lanes], do_in[lo:hi, lanes]
            delta = jnp.sum(do.astype(F32) * att[lo:hi, lanes], axis=1, keepdims=True)
            s = contract(q, k_in[lo:hi, lanes], ((1,), (1,)))
            s = jnp.where(col <= row, s, NEG)
            if c:
                s = jnp.concatenate([contract(q, k_in[:lo, lanes], ((1,), (1,))), s], axis=1)
            p = jnp.exp(s - lse[lo:hi, h * HD : h * HD + 1])
            dp = contract(do, v_in[:hi, lanes], ((1,), (1,)))
            ds = (p * (dp - delta)).astype(BF)
            dqs.append(contract(ds, k_in[:hi, lanes], ((1,), (0,))) * scale)
            dk[:hi, lanes] += contract(ds, q, ((0,), (0,)))
            dv[:hi, lanes] += contract(p.astype(BF), do, ((0,), (0,)))
        dq = jnp.concatenate(dqs, axis=1)
        dq_out[lo:hi, :] = turn(dq, cos[lo:hi, :], -first[lo:hi, :], -second[lo:hi, :]).astype(BF)
    dk_out[...] = turn(dk[...], cos[...], -first[...], -second[...]).astype(BF)
    dv_out[...] = dv[...].astype(BF)


def attend_back(q, k, v, d_attended, attended, lse, tables, heads):
    length, width = q.shape
    block = pl.BlockSpec((length, 2 * HD), lambda h: (0, h))
    table = pl.BlockSpec((length, 2 * HD), lambda h: (0, 0))
    return pl.pallas_call(
        attend_back_kernel,
        grid=(heads // 2,),
        in_specs=[block] * 6 + [table] * 3,
        out_specs=[block] * 3,
        out_shape=[jax.ShapeDtypeStruct((length, width), BF)] * 3,
        scratch_shapes=[pltpu.VMEM((length, 2 * HD), F32)] * 2,
        compiler_params=pltpu.CompilerParams(vmem_limit_bytes=40 * 2**20),
        cost_estimate=pl.CostEstimate(
            flops=40 * heads * length * length * HD // 2,
            bytes_accessed=22 * length * width,
            transcendentals=heads * length * length // 2,
        ),
        name="attend_back",
    )(q, k, v, d_attended, attended, lse, *tables)


MESH = pl.DeviceIdType.MESH
TILE = 256
HALF = 128
DEEP = 4
LAG = 1


def tile_at(i, size=TILE):
    return pl.ds(pl.multiple_of(i * size, size), size)


def vmem_whole():
    return pl.BlockSpec(memory_space=pltpu.VMEM)


def hbm_whole():
    return pl.BlockSpec(memory_space=pl.ANY)


def chip_away(chip, m):
    return 2 * ((chip // 2 + m // 2) % 2) + (chip + m) % 2


def inner_runs(shards, count, part):
    runs = []
    for block in range(shards * part // HALF):
        first = 0
        while first < HALF:
            shard, unit = divmod(block * HALF + first, part)
            last = min(HALF, first + part - unit)
            runs.append((block, first, last, shard * count * part + unit - first))
            first = last
    return runs


class Line:
    def __init__(self, own, whole, send, recv):
        self.own, self.whole, self.send, self.recv = own, whole, send, recv
        self.count = whole.shape[0]
        self.place, self.me = lax.axis_index("ctx"), lax.axis_index("fsdp")

    def copy(self, way, hop):
        ahead = 1 - 2 * way
        origin = self.place - (hop - 1) * ahead
        return pltpu.make_async_remote_copy(
            src_ref=self.own if hop == 1 else self.whole.at[origin],
            dst_ref=self.whole.at[origin],
            send_sem=self.send.at[way, hop - 1],
            recv_sem=self.recv.at[way, hop - 1],
            device_id=(self.place + ahead, self.me),
            device_id_type=MESH,
        )

    def sends(self, way, hop):
        if way == 0:
            return (self.place >= hop - 1) & (self.place <= self.count - 2)
        return (self.place <= self.count - hop) & (self.place >= 1)

    def lands(self, way, hop):
        return self.place >= hop if way == 0 else self.place <= self.count - 1 - hop

    def pass_on(self, hop):
        for way in range(2):
            if hop > 1:
                @pl.when(self.lands(way, hop - 1))
                def _(way=way):
                    self.copy(way, hop - 1).wait_recv()

            if hop < self.count:
                @pl.when(self.sends(way, hop))
                def _(way=way):
                    self.copy(way, hop).start()

    def finish(self):
        for way in range(2):
            for hop in range(1, self.count):
                @pl.when(self.sends(way, hop))
                def _(way=way, hop=hop):
                    self.copy(way, hop).wait_send()


class Plane:
    def __init__(self, mine, wholes, send, recv):
        self.mine, self.wholes, self.send, self.recv = mine, wholes, send, recv
        self.place, self.me = lax.axis_index("ctx"), lax.axis_index("fsdp")
        chip, core = self.me // 2, self.me % 2
        self.sibling = 2 * chip + 1 - core
        self.near = (2 * chip_away(chip, 1) + core, 2 * chip_away(chip, 2) + core)
        self.far = 2 * chip_away(chip, 3) + core

    def copy(self, which, kind, source, target, to):
        return pltpu.make_async_remote_copy(
            src_ref=source,
            dst_ref=target,
            send_sem=self.send.at[which, kind],
            recv_sem=self.recv.at[which, kind],
            device_id=(self.place, to),
            device_id_type=MESH,
        )

    def direct(self, which, a):
        return self.copy(which, a, self.mine[which], self.wholes[which].at[self.me], self.near[a])

    def across(self, which, a):
        half = self.wholes[which].shape[2] // 2
        piece = self.wholes[which].at[self.near[1 - a], :, a * half : (a + 1) * half]
        return self.copy(which, 2 + a, piece, piece, self.near[a])

    def beside(self, which, kind):
        source = (self.me, self.near[0], self.near[1], self.far)[kind]
        piece = self.wholes[which].at[source]
        return self.copy(which, 4 + kind, self.mine[which] if kind == 0 else piece, piece, self.sibling)

    def begin(self, which):
        for a in range(2):
            self.direct(which, a).start()
        self.beside(which, 0).start()

    def relay(self, which):
        for a in range(2):
            self.direct(which, a).wait_recv()
        for a in range(2):
            self.across(which, a).start()
            self.beside(which, 1 + a).start()

    def last(self, which):
        for a in range(2):
            self.across(which, a).wait_recv()
        self.beside(which, 3).start()

    def finish(self, which):
        for kind in range(4):
            self.beside(which, kind).wait()
        for a in range(2):
            self.direct(which, a).wait_send()
            self.across(which, a).wait_send()


class Own:
    def __init__(self, source, stage, target, sem, n):
        self.load = pltpu.make_async_copy(source, stage, sem.at[n, 0])
        self.store = pltpu.make_async_copy(stage, target, sem.at[n, 1])

    def turn(self):
        self.load.wait()
        self.store.start()


def greet(peers):
    barrier = pltpu.get_barrier_semaphore()
    for peer in peers:
        pl.semaphore_signal(barrier, inc=1, device_id=peer, device_id_type=MESH)
    pl.semaphore_wait(barrier, len(peers))


def forward_kernel(
    order, slots, cos, first, second, tokens, cot, vectors, w_gate, w_up, w_qkv, w_out, w_down,
    cot_all, rows_out, inner_out, heads_out, attn_out, down, normed_t, hat, both, hidden_t,
    q_out, k_out, v_out, att_out, low_t, lse_out, branch,
    raw, x_all, vectors_all, scales, inner, heads, attn,
    normed, hidden, low, hat_stage, turned_stage, both_stage, hidden_stage,
    q_buf, k_buf, v_buf, att_buf, low_stage, lse_buf, down_tile, term, branch_stage,
    load_sem, x_send, x_recv, line_send, line_recv, part_send, part_recv, vector_send, vector_recv,
    own_sem, out_sem, norm_sem, feed_sem, head_sem, tile_sem, branch_sem,
):
    count, rows = x_all.shape[0], x_all.shape[1]
    shards = inner.shape[0]
    place, me = lax.axis_index("ctx"), lax.axis_index("fsdp")
    width = w_gate.shape[1]
    my_attn = w_out.at[pl.ds(pl.multiple_of(place * attn.shape[1], 16), attn.shape[1])]
    my_down = w_down.at[pl.ds(pl.multiple_of(place * down.shape[1], 16), down.shape[1])]
    loads = [
        pltpu.make_async_copy(my_attn, attn.at[me], load_sem.at[0]),
        pltpu.make_async_copy(w_gate, raw.at[0, :, :width], load_sem.at[1]),
        pltpu.make_async_copy(w_up, raw.at[1, :, :width], load_sem.at[2]),
        pltpu.make_async_copy(tokens, x_all.at[place], load_sem.at[3]),
        pltpu.make_async_copy(vectors, vectors_all.at[me], load_sem.at[4]),
    ]
    owns = [
        Own(cot, hat_stage.at[0], cot_all.at[place], own_sem, 0),
        Own(my_down, hat_stage.at[1, : down.shape[1]], down.at[me], own_sem, 1),
    ]
    for c in loads + [own.load for own in owns]:
        c.start()
    qkv_load = pltpu.make_async_copy(w_qkv, raw.at[0], load_sem.at[5])
    peers = [(place, (me + s) % shards) for s in range(1, shards)]
    greet(peers + [((place + 1) % count, me), ((place + count - 1) % count, me)])
    x_line = Line(tokens, x_all, x_send, x_recv)
    line = Line(cot, cot_all, line_send, line_recv)
    plane = Plane(
        (inner.at[me], attn.at[me], heads.at[me], my_down), (inner, attn, heads, down), part_send, part_recv
    )
    x_line.pass_on(1)
    vector_copies = [
        pltpu.make_async_remote_copy(
            src_ref=vectors,
            dst_ref=vectors_all.at[me],
            send_sem=vector_send.at[s - 1],
            recv_sem=vector_recv.at[s - 1],
            device_id=(place, (me + s) % shards),
            device_id_type=MESH,
        )
        for s in range(1, shards)
    ]
    for c in vector_copies:
        c.start()
    loads[0].wait()
    plane.begin(1)

    row = lax.broadcasted_iota(jnp.int32, (TILE, HALF), 0)
    col = lax.broadcasted_iota(jnp.int32, (TILE, HALF), 1)

    def picked(sources, size, first, last, start):
        base = jnp.minimum((start + first) // HALF, size // HALF - TILE // HALF) * HALF
        choose = (row + base == col + start) & (col >= first) & (col < last)
        choose = choose.astype(F32).astype(BF)
        at = pl.ds(pl.multiple_of(base, HALF), TILE)
        return [contract(raw[source, :, at], choose, ((1,), (0,))) for source in sources]

    part = width // shards // count
    loads[1].wait()
    loads[2].wait()
    held = None
    for block, first_col, last_col, start in inner_runs(shards, count, part):
        values = picked((0, 1), width, first_col, last_col, start + place * part)
        held = values if first_col == 0 else [a + b for a, b in zip(held, values)]
        if last_col == HALF:
            for k in range(2):
                at = block * TILE + k * HALF
                inner[me, :, at : at + HALF] = held[k].astype(BF)
    plane.begin(0)
    qkv_load.start()
    qkv_load.wait()
    third = raw.shape[2] // 3
    for pair in range(shards // 2):
        for kind in range(3):
            value = 0.0
            for h in range(2):
                head = count * (2 * pair + h) + place
                start = kind * third + head * HD - h * HD
                value = value + picked((0,), raw.shape[2], h * HD, (h + 1) * HD, start)[0]
            at = (pair * 3 + kind) * HALF
            heads[me, :, at : at + HALF] = value.astype(BF)
    plane.begin(2)
    for own in owns:
        own.turn()
    plane.relay(1)
    x_line.pass_on(2)
    plane.relay(0)
    plane.last(1)
    x_line.pass_on(3)
    line.pass_on(1)
    plane.relay(2)
    plane.last(0)
    plane.finish(1)
    for c in loads[3:] + vector_copies:
        c.wait()
    scales[...] = jnp.concatenate([vectors_all[s] for s in range(shards)], axis=1)
    x_line.pass_on(4)
    plane.begin(3)
    outs = [
        pltpu.make_async_copy(attn, attn_out, out_sem.at[0]),
        pltpu.make_async_copy(scales, rows_out, out_sem.at[1]),
        pltpu.make_async_copy(inner, inner_out, out_sem.at[2]),
        pltpu.make_async_copy(heads, heads_out, out_sem.at[3]),
    ]
    outs[0].start()
    outs[1].start()

    def norm_copies(p):
        at = pl.ds(pl.multiple_of(p * rows, rows), rows)
        return (
            pltpu.make_async_copy(hat_stage.at[p % 2], hat.at[at], norm_sem.at[0, p % 2]),
            pltpu.make_async_copy(turned_stage.at[p % 2], normed_t.at[:, at], norm_sem.at[1, p % 2]),
        )

    def norm_step(p, carry):
        @pl.when(p >= 2)
        def _():
            for c in norm_copies(p - 2):
                c.wait()

        xf = x_all[slots[p]].astype(F32)
        mean = jnp.mean(xf, axis=1, keepdims=True)
        centered = xf - mean
        variance = jnp.mean(centered * centered, axis=1, keepdims=True)
        x_hat = centered * lax.rsqrt(variance + EPS)
        hat_stage[p % 2] = x_hat.astype(BF)
        value = x_hat * scales[0:1, :] + scales[1:2, :]
        normed[pl.ds(pl.multiple_of(p * rows, rows), rows), :] = value.astype(BF)
        turned_stage[p % 2] = value.T.astype(BF)
        for c in norm_copies(p):
            c.start()
        return carry

    for own in owns:
        own.store.wait()
    lax.fori_loop(0, count, norm_step, 0)
    plane.finish(0)
    outs[2].start()
    model = normed.shape[1]

    def feed_copies(i):
        wide = pl.ds(pl.multiple_of(i * TILE, TILE), TILE)
        slim = pl.ds(pl.multiple_of(i * HALF, HALF), HALF)
        return (
            pltpu.make_async_copy(both_stage.at[i % 2], both.at[:, wide], feed_sem.at[0, i % 2]),
            pltpu.make_async_copy(hidden_stage.at[i % 2], hidden_t.at[slim], feed_sem.at[1, i % 2]),
        )

    def feed_step(i, carry):
        @pl.when(i >= 2)
        def _():
            for c in feed_copies(i - 2):
                c.wait()

        value = contract(normed[...], inner[:, :, tile_at(i)].reshape(model, TILE), ((1,), (0,)))
        both_stage[i % 2] = value.astype(BF)
        gate, up = value[:, :HALF], value[:, HALF:]
        value = gate * jax.nn.sigmoid(gate) * up
        hidden[:, pl.ds(pl.multiple_of(i * HALF, HALF), HALF)] = value.astype(BF)
        hidden_stage[i % 2] = value.T.astype(BF)
        for c in feed_copies(i):
            c.start()
        return carry

    tiles = inner.shape[2] // TILE
    lax.fori_loop(0, tiles, feed_step, 0)
    line.pass_on(2)
    plane.relay(3)
    plane.last(2)
    plane.finish(2)
    outs[3].start()
    row = lax.broadcasted_iota(jnp.int32, (CHUNK, CHUNK), 0)
    col = lax.broadcasted_iota(jnp.int32, (CHUNK, CHUNK), 1)
    pairs = heads.shape[2] // (3 * HALF)

    def head_copies(h):
        at = pl.ds(pl.multiple_of(h * HALF, HALF), HALF)
        moves = ((q_buf, q_out), (k_buf, k_out), (v_buf, v_out), (att_buf, att_out), (lse_buf, lse_out))
        copies = [
            pltpu.make_async_copy(a.at[h % 2], b.at[:, at], head_sem.at[n, h % 2]) for n, (a, b) in enumerate(moves)
        ]
        return copies + [pltpu.make_async_copy(low_stage.at[h % 2], low_t.at[at], head_sem.at[5, h % 2])]

    def head_step(h, carry):
        @pl.when(h >= 2)
        def _():
            for c in head_copies(h - 2):
                c.wait()

        slot = h % 2
        w = heads[:, :, tile_at(h, 3 * HALF)].reshape(model, 3 * HALF)
        mixed = contract(normed[...], w, ((1,), (0,)))
        q = turn(mixed[:, :HALF], cos[...], first[...], second[...]).astype(BF).astype(F32)
        q_buf[slot] = (q * HD ** (-0.5)).astype(BF)
        k_buf[slot] = turn(mixed[:, HALF : 2 * HALF], cos[...], first[...], second[...]).astype(BF)
        v_buf[slot] = mixed[:, 2 * HALF :].astype(BF)
        for c in range(normed.shape[0] // CHUNK):
            lo, hi = c * CHUNK, (c + 1) * CHUNK
            for side in range(2):
                lanes = slice(side * HD, (side + 1) * HD)
                q = q_buf[slot, lo:hi, lanes]
                s = contract(q, k_buf[slot, lo:hi, lanes], ((1,), (1,)))
                s = jnp.where(col <= row, s, NEG)
                if c:
                    s = jnp.concatenate([contract(q, k_buf[slot, :lo, lanes], ((1,), (1,))), s], axis=1)
                top = jnp.max(s, axis=1, keepdims=True)
                p = jnp.exp(s - top)
                total = jnp.sum(p, axis=1, keepdims=True)
                o = contract(p.astype(BF), v_buf[slot, :hi, lanes], ((1,), (0,)))
                att_buf[slot, lo:hi, lanes] = o / total
                lse_buf[slot, lo:hi, lanes] = jnp.broadcast_to(top + jnp.log(total), (CHUNK, HD))
        att = att_buf[slot]
        low[:, pl.ds(pl.multiple_of(h * HALF, HALF), HALF)] = att.astype(BF)
        low_stage[slot] = att.T.astype(BF)
        for c in head_copies(h):
            c.start()
        return carry

    lax.fori_loop(0, pairs - 1, head_step, 0)
    plane.last(3)
    line.pass_on(3)
    lax.fori_loop(pairs - 1, pairs, head_step, 0)
    plane.finish(3)
    def tile_copies(i):
        at = pl.ds(pl.multiple_of(i * TILE, TILE), TILE)
        return [pltpu.make_async_copy(down.at[:, :, at], down_tile.at[i % 2], tile_sem.at[i % 2])]

    def branch_copy(i):
        at = pl.ds(pl.multiple_of(i * TILE, TILE), TILE)
        return pltpu.make_async_copy(branch_stage.at[i % 2], branch.at[:, :, at], branch_sem.at[i % 2])

    steps = branch.shape[2] // TILE
    for c in tile_copies(0):
        c.start()

    def branch_step(i, carry):
        @pl.when(i + 1 < steps)
        def _():
            for c in tile_copies(i + 1):
                c.start()

        for c in tile_copies(i):
            c.wait()

        @pl.when(i >= 2)
        def _():
            branch_copy(i - 2).wait()

        value = contract(hidden[...], down_tile[i % 2].reshape(hidden.shape[1], TILE), ((1,), (0,)))
        value = value + contract(low[...], attn[:, :, tile_at(i)].reshape(low.shape[1], TILE), ((1,), (0,)))
        term[...] = value.reshape(term.shape)
        for j in range(count):
            branch_stage[i % 2, j] = term[order[j]].astype(BF)
        branch_copy(i).start()
        return carry

    lax.fori_loop(0, steps, branch_step, 0)
    for hop in range(4, count + 1):
        line.pass_on(hop)
    line.finish()
    x_line.finish()
    for c in outs:
        c.wait()
    for back in range(2):
        for c in norm_copies(count - 1 - back) + feed_copies(tiles - 1 - back):
            c.wait()
        for c in head_copies(pairs - 1 - back):
            c.wait()
        branch_copy(steps - 1 - back).wait()


def forward(order, slots, tables, tokens, cot, vectors, w_gate, w_up, w_qkv, w_out, w_down, count, shards):
    rows, width = tokens.shape
    length = count * rows
    shard_rows = w_gate.shape[0]
    ff_part, attn_part = w_down.shape[0] // count, w_out.shape[0] // count
    ff, cols = shards * ff_part, shards * attn_part
    dma = pltpu.SemaphoreType.DMA
    smem = pl.BlockSpec(memory_space=pltpu.SMEM)
    bf = lambda *shape: jax.ShapeDtypeStruct(shape, BF)
    f32 = lambda *shape: jax.ShapeDtypeStruct(shape, F32)
    out_shape = [
        bf(count, rows, width),
        f32(vectors.shape[0], width),
        bf(shards, shard_rows, 2 * ff),
        bf(shards, shard_rows, 3 * cols),
        bf(shards, attn_part, width),
        bf(shards, ff_part, width),
        bf(width, length),
        bf(length, width),
        bf(length, 2 * ff),
        bf(ff, length),
        bf(length, cols),
        bf(length, cols),
        bf(length, cols),
        f32(length, cols),
        bf(cols, length),
        f32(length, cols),
        bf(count, rows, width),
    ]
    hops = (2, count - 1)
    return pl.pallas_call(
        forward_kernel,
        out_shape=out_shape,
        in_specs=[smem] * 2 + [vmem_whole()] * 3 + [hbm_whole()] * 8,
        out_specs=[hbm_whole()] * len(out_shape),
        scratch_shapes=[
            pltpu.VMEM((2,) + w_qkv.shape, BF),
            pltpu.VMEM((count, rows, width), BF),
            pltpu.VMEM((shards,) + vectors.shape, F32),
            pltpu.VMEM((vectors.shape[0], width), F32),
            pltpu.VMEM((shards, shard_rows, 2 * ff), BF),
            pltpu.VMEM((shards, shard_rows, 3 * cols), BF),
            pltpu.VMEM((shards, attn_part, width), BF),
            pltpu.VMEM((length, width), BF),
            pltpu.VMEM((length, ff), BF),
            pltpu.VMEM((length, cols), BF),
            pltpu.VMEM((2, rows, width), BF),
            pltpu.VMEM((2, width, rows), BF),
            pltpu.VMEM((2, length, TILE), BF),
            pltpu.VMEM((2, HALF, length), BF),
            pltpu.VMEM((2, length, HALF), BF),
            pltpu.VMEM((2, length, HALF), BF),
            pltpu.VMEM((2, length, HALF), BF),
            pltpu.VMEM((2, length, HALF), F32),
            pltpu.VMEM((2, HALF, length), BF),
            pltpu.VMEM((2, length, HALF), F32),
            pltpu.VMEM((2, shards, ff_part, TILE), BF),
            pltpu.VMEM((count, rows, TILE), F32),
            pltpu.VMEM((2, count, rows, TILE), BF),
            dma((6,)),
            dma(hops),
            dma(hops),
            dma(hops),
            dma(hops),
            dma((4, 8)),
            dma((4, 8)),
            dma((shards - 1,)),
            dma((shards - 1,)),
            dma((2, 2)),
            dma((4,)),
            dma((2, 2)),
            dma((2, 2)),
            dma((6, 2)),
            dma((2,)),
            dma((2,)),
        ],
        compiler_params=pltpu.CompilerParams(
            collective_id=3, has_side_effects=True, vmem_limit_bytes=62 * 2**20
        ),
        name="forward",
    )(order, slots, *tables, tokens, cot, vectors, w_gate, w_up, w_qkv, w_out, w_down)


def fixed_tables(length):
    half = ROT // 2
    inverse = np.float32(10000.0) ** (-np.arange(half, dtype=np.float32) / np.float32(half))
    grid = np.arange(length, dtype=np.float32)[:, None] * inverse.astype(np.float32)[None, :]
    cos, sin = np.cos(grid, dtype=np.float32), np.sin(grid, dtype=np.float32)
    zero, rest = np.zeros((length, half), np.float32), np.zeros((length, HD - ROT), np.float32)
    tables = ([cos, cos, rest + 1], [-sin, zero, rest], [zero, sin, rest])
    return [jnp.asarray(np.tile(np.concatenate(t, axis=1), (1, 2))) for t in tables]


def rows_of(shard, part):
    return slice(shard * part, (shard + 1) * part)


def heads_back_pair(q_in, k_in, v_in, do_in, att, lse, cos, first, second, out, dk, dv):
    length = q_in.shape[0]
    scale = HD ** (-0.5)
    row = lax.broadcasted_iota(jnp.int32, (CHUNK, CHUNK), 0)
    col = lax.broadcasted_iota(jnp.int32, (CHUNK, CHUNK), 1)
    dk[...] = jnp.zeros_like(dk)
    dv[...] = jnp.zeros_like(dv)
    for c in range(length // CHUNK):
        lo, hi = c * CHUNK, (c + 1) * CHUNK
        dqs = []
        for h in range(2):
            lanes = slice(h * HD, (h + 1) * HD)
            q, do = q_in[lo:hi, lanes], do_in[lo:hi, lanes]
            delta = jnp.sum(do.astype(F32) * att[lo:hi, lanes], axis=1, keepdims=True)
            s = contract(q, k_in[lo:hi, lanes], ((1,), (1,)))
            s = jnp.where(col <= row, s, NEG)
            if c:
                s = jnp.concatenate([contract(q, k_in[:lo, lanes], ((1,), (1,))), s], axis=1)
            p = jnp.exp(s - lse[lo:hi, h * HD : h * HD + 1])
            dp = contract(do, v_in[:hi, lanes], ((1,), (1,)))
            ds = (p * (dp - delta)).astype(BF)
            dqs.append(contract(ds, k_in[:hi, lanes], ((1,), (0,))) * scale)
            dk[:hi, lanes] += contract(ds, q, ((0,), (0,)))
            dv[:hi, lanes] += contract(p.astype(BF), do, ((0,), (0,)))
        dq = jnp.concatenate(dqs, axis=1)
        out[0, lo:hi, :] = turn(dq, cos[lo:hi, :], -first[lo:hi, :], -second[lo:hi, :]).astype(BF)
    out[1] = turn(dk[...], cos[...], -first[...], -second[...]).astype(BF)
    out[2] = dv[...].astype(BF)


def backward_kernel(
    order, slots, hid_t, att_t, cos, first, second,
    cot, norm_hbm, down, attn, both, branch, w_inner, w_heads, hat, q_in, k_in, v_in, att_in, lse_in,
    pieces, sums,
    cot_own, norm_t, d_inner, d_mixed, terms, term, small, w_tile, h_tile, hat_tile,
    attn_tile, q_tile, k_tile, v_tile, att_tile, lse_tile, d_att, turned, dk, dv, sums_stage,
    partial, theirs, pair, landed, total, sum_from, sum_land,
    core_send, core_recv, chip_send, chip_recv, line_send, line_recv, own_sem, sum_send, sum_recv,
    cot_sem, load_sem, feed_sem, back_sem, head_sem, sums_sem,
):
    count, chunks = pieces.shape[0], pieces.shape[1]
    shards = 2 * partial.shape[1]
    chips = shards // 2
    rows = terms.shape[1]
    place, me = lax.axis_index("ctx"), lax.axis_index("fsdp")
    chip, core = me // 2, me % 2
    ff_part, attn_part = hid_t.shape[0] // shards, att_t.shape[0] // shards
    sum_parts = terms.shape[2] // TILE
    early = cot_own.shape[1] // TILE - 1
    inner_end = early + d_inner.shape[1] // TILE

    def chunk_name(i):
        return jnp.where(i < early, i + chunks - 1 - early, jnp.where(i == chunks - 1, i, i - early))

    def core_copy(i):
        return pltpu.make_async_remote_copy(
            src_ref=partial.at[i % 2, :, 1 - core],
            dst_ref=theirs.at[i % DEEP],
            send_sem=core_send.at[i % 2],
            recv_sem=core_recv.at[i % DEEP],
            device_id=(place, me + 1 - 2 * core),
            device_id_type=MESH,
        )

    def chip_copy(j, m):
        return pltpu.make_async_remote_copy(
            src_ref=pair.at[j % 2, chip_away(chip, m)],
            dst_ref=landed.at[j % DEEP, m - 1],
            send_sem=chip_send.at[j % 2, m - 1],
            recv_sem=chip_recv.at[j % DEEP, m - 1],
            device_id=(place, 2 * chip_away(chip, m) + core),
            device_id_type=MESH,
        )

    def line_copy(way, hop, k):
        ahead = 1 - 2 * way
        origin = place - (hop - 1) * ahead
        target = pieces.at[origin, chunk_name(k)]
        return pltpu.make_async_remote_copy(
            src_ref=total.at[k % DEEP] if hop == 1 else target,
            dst_ref=target,
            send_sem=line_send.at[way, hop - 1, k % DEEP],
            recv_sem=line_recv.at[way, k, hop - 1],
            device_id=(place + ahead, me),
            device_id_type=MESH,
        )

    def sends(way, hop):
        if way == 0:
            return (place >= hop - 1) & (place <= count - 2)
        return (place <= count - hop) & (place >= 1)

    def lands(way, hop):
        return place >= hop if way == 0 else place <= count - 1 - hop

    def forward_chunk(hop, k):
        for way in range(2):
            if hop > 1:
                @pl.when(lands(way, hop - 1))
                def _(way=way):
                    line_copy(way, hop - 1, k).wait_recv()

            if hop < count:
                @pl.when(sends(way, hop))
                def _(way=way):
                    @pl.when(k >= DEEP)
                    def _():
                        line_copy(way, hop, k - DEEP).wait_send()

                    line_copy(way, hop, k).start()

    def own_copy(k):
        return pltpu.make_async_copy(total.at[k % DEEP], pieces.at[place, chunk_name(k)], own_sem.at[k % DEEP])

    def sum_copy(way, t, q):
        return pltpu.make_async_remote_copy(
            src_ref=sum_from.at[way, t - 1, q // sum_parts],
            dst_ref=sum_land.at[way, t - 1, q % sum_parts],
            send_sem=sum_send.at[way, t - 1, q // sum_parts],
            recv_sem=sum_recv.at[way, t - 1, q],
            device_id=(place + 1 - 2 * way, me),
            device_id_type=MESH,
        )

    def sum_sends(way, t):
        return place <= t - 1 if way == 0 else place >= count - t

    def sum_step(t, q):
        at = tile_at(q % sum_parts)
        for way in range(2):
            @pl.when(sum_sends(way, t))
            def _(way=way):
                to = count - t + place if way == 0 else t + place - count
                starts = place == 0 if way == 0 else place == count - 1

                @pl.when(q % sum_parts >= 1)
                def _():
                    sum_copy(way, t, q - 1).wait_send()

                @pl.when(starts)
                def _():
                    sum_from[way, t - 1, q // sum_parts] = terms[to, :, at]

                if t > 1:
                    @pl.when(jnp.logical_not(starts))
                    def _():
                        sum_copy(way, t - 1, q).wait_recv()
                        value = terms[to, :, at].astype(F32) + sum_land[way, t - 2, q % sum_parts].astype(F32)
                        sum_from[way, t - 1, q // sum_parts] = value.astype(BF)

                sum_copy(way, t, q).start()

    def sums_copy(q):
        return pltpu.make_async_copy(
            sums_stage.at[q // sum_parts],
            sums.at[q // sum_parts, :, tile_at(q % sum_parts)],
            sums_sem.at[q // sum_parts],
        )

    def sum_end(q):
        @pl.when(q % sum_parts >= 1)
        def _():
            sums_copy(q - 1).wait()

        sums_stage[q // sum_parts] = terms[place, :, tile_at(q % sum_parts)].astype(F32)
        for way in range(2):
            @pl.when(place >= 1 if way == 0 else place <= count - 2)
            def _(way=way):
                sum_copy(way, count - 1, q).wait_recv()
                sums_stage[q // sum_parts] += sum_land[way, count - 2, q % sum_parts].astype(F32)

        sums_copy(q).start()

    cot_load = pltpu.make_async_copy(cot, terms, cot_sem)

    def feed_load(b, size):
        at = pl.ds(pl.multiple_of(b * TILE, TILE), size)
        return pltpu.make_async_copy(
            down.at[at], w_tile.at[b % 2, :size, : cot_own.shape[1]], feed_sem.at[b % 2]
        )

    both_load = pltpu.make_async_copy(both, d_inner, load_sem.at[2])

    loads = [
        pltpu.make_async_copy(branch, terms, load_sem.at[0]),
        pltpu.make_async_copy(norm_hbm, norm_t, load_sem.at[1]),
    ]

    def back_loads(q):
        moves = (
            (w_inner.at[tile_at(q)], w_tile.at[q % 2]),
            (w_heads.at[tile_at(q)], h_tile.at[q % 2]),
            (hat.at[:, tile_at(q)], hat_tile.at[q % 2]),
        )
        return [pltpu.make_async_copy(a, b, back_sem.at[n, q % 2]) for n, (a, b) in enumerate(moves)]

    def head_loads(h):
        moves = ((q_in, q_tile), (k_in, k_tile), (v_in, v_tile), (att_in, att_tile), (lse_in, lse_tile))
        at = tile_at(h, HALF)
        copies = [
            pltpu.make_async_copy(a.at[:, at], b.at[h % 2], head_sem.at[n, h % 2]) for n, (a, b) in enumerate(moves)
        ]
        return copies

    def attn_load(h):
        return pltpu.make_async_copy(attn.at[tile_at(h // 2)], attn_tile, load_sem.at[3])

    pairs = q_in.shape[1] // HALF
    tiles = d_inner.shape[1] // TILE
    for c in [cot_load, both_load, feed_load(0, TILE), feed_load(1, TILE), attn_load(0)] + head_loads(0) + head_loads(1) + loads[1:]:
        c.start()
    peers = [(place, me + 1 - 2 * core)]
    peers += [(place, 2 * chip_away(chip, m) + core) for m in range(1, chips)]
    greet(peers + [((place + 1) % count, me), ((place + count - 1) % count, me)])
    cot_load.wait()
    for p in range(count):
        cot_own[p * rows : (p + 1) * rows, :] = terms[slots[p]]
    loads[0].start()
    loads[0].wait()

    ff = down.shape[0]
    whole_tiles = ff // TILE

    def feed_tile(b, size):
        feed_load(b, size).wait()
        d_hidden = contract(cot_own[...], w_tile[b % 2, :size, : cot_own.shape[1]], ((1,), (1,)))
        for n in range(size // HALF):
            d = d_hidden[:, n * HALF : (n + 1) * HALF]
            at = tile_at(2 * b + n)
            value = d_inner[:, at]
            gate = value[:, :HALF].astype(F32)
            up = value[:, HALF:].astype(F32)
            sig = jax.nn.sigmoid(gate)
            d_gate = d * up * sig * (1.0 + gate * (1.0 - sig))
            d_inner[:, at] = jnp.concatenate([d_gate, d * gate * sig], axis=1).astype(BF)

    def feed_step(b, carry):
        feed_tile(b, TILE)

        @pl.when(b + 2 < whole_tiles)
        def _():
            feed_load(b + 2, TILE).start()

        if ff % TILE:
            @pl.when(b + 2 == whole_tiles)
            def _():
                feed_load(whole_tiles, ff % TILE).start()

        return carry

    def store(i, shard, lo, value):
        partial[i % 2, shard // 2, shard % 2, lo : lo + value.shape[0], :] = value

    def from_norm(i, rhs):
        for s in range(0, shards, 2):
            part = norm_t.shape[0] // shards
            value = contract(norm_t[s * part : (s + 2) * part, :], rhs, ((1,), (0,))).astype(BF)
            store(i, s, 0, value[:part])
            store(i, s + 1, 0, value[part:])

    def step(i, carry):
        @pl.when((i < early) | (i == chunks - 1))
        def _():
            c = jnp.where(i < early, i, early)
            rhs = cot_own[:, tile_at(c)]
            for s in range(0, shards, 4):
                value = contract(hid_t[s * ff_part : (s + 4) * ff_part, :], rhs, ((1,), (0,))).astype(BF)
                for t in range(4):
                    store(i, s + t, 0, value[rows_of(t, ff_part)])
            value = contract(att_t[...], rhs, ((1,), (0,))).astype(BF)
            for s in range(shards):
                store(i, s, ff_part, value[rows_of(s, attn_part)])

        @pl.when(i == chunks - 1)
        def _():
            for s in range(shards):
                store(i, s, ff_part + attn_part, small[s])

        @pl.when(i == early)
        def _():
            loads[1].wait()

        @pl.when((i >= early) & (i < inner_end))
        def _():
            from_norm(i, d_inner[:, tile_at(i - early)])

        @pl.when((i >= inner_end) & (i < chunks - 1))
        def _():
            at = i - inner_end
            from_norm(i, d_mixed[:, tile_at(at)])

        @pl.when(i < chunks)
        def _():
            core_copy(i).start()

        @pl.when((i >= 1) & (i < chunks + 1))
        def _():
            j = i - 1
            core_copy(j).wait()
            for m in range(chips):
                a = partial[j % 2, m, core].astype(F32) + theirs[j % DEEP, m].astype(F32)
                pair[j % 2, m] = a.astype(BF)
            for m in range(1, chips):
                chip_copy(j, m).start()

        @pl.when((i >= 2) & (i < chunks + 2))
        def _():
            k = i - 2
            for m in range(1, chips):
                chip_copy(k, m).wait()

            a = pair[k % 2, chip].astype(F32)
            for m in range(1, chips):
                a = a + landed[k % DEEP, m - 1].astype(F32)
            for way in range(2):
                @pl.when(sends(way, 1) & (k >= DEEP))
                def _(way=way):
                    line_copy(way, 1, k - DEEP).wait_send()

            @pl.when(k >= DEEP)
            def _():
                own_copy(k - DEEP).wait()

            total[k % DEEP] = a.astype(BF)
            for way in range(2):
                @pl.when(sends(way, 1))
                def _(way=way):
                    line_copy(way, 1, k).start()

            own_copy(k).start()

        @pl.when((i >= 9) & (i < 9 + 2 * sum_parts) & (i % 2 == 1))
        def _():
            q = (i - 9) // 2
            for c in back_loads(q):
                c.wait()
            value = contract(d_inner[...], w_tile[q % 2], ((1,), (1,)))
            value = value + contract(d_mixed[...], h_tile[q % 2], ((1,), (1,)))
            term[...] = value.reshape(term.shape)
            gain = jnp.sum(value * hat_tile[q % 2].astype(F32), axis=0, keepdims=True)
            bias = jnp.sum(value, axis=0, keepdims=True)
            row = lax.broadcasted_iota(jnp.int32, small.shape[1:], 0)
            small[q] = jnp.where(row == 0, gain, jnp.where(row == 1, bias, 0.0)).astype(BF)
            for j in range(count):
                terms[j, :, tile_at(q)] = term[order[j]].astype(BF)

            @pl.when(q + 2 < sum_parts)
            def _():
                for c in back_loads(q + 2):
                    c.start()

        for t in range(1, count + 1):
            when = i - LAG * (t - 1)
            q = jnp.where(when % 2 == 0, when // 2, sum_parts + (when - 9) // 2)
            begins = jnp.where(when % 2 == 0, when, jnp.where(when >= 9, when - 9, -1))

            @pl.when((begins >= 0) & (begins < 2 * sum_parts))
            def _(q=q, t=t):
                if t < count:
                    sum_step(t, q)
                else:
                    sum_end(q)

        for hop in range(2, count + 1):
            k = i - 2 - LAG * (hop - 1)

            @pl.when((k >= 0) & (k < chunks))
            def _(k=k, hop=hop):
                forward_chunk(hop, k)

        @pl.when(i == 0)
        def _():
            both_load.wait()

        @pl.when((i == 0) | (i == 1) | (i == 4))
        def _():
            first_tile = jnp.where(i == 0, 0, jnp.where(i == 1, 1, 3))
            last_tile = jnp.where(i == 0, 1, jnp.where(i == 1, 3, whole_tiles))
            lax.fori_loop(first_tile, last_tile, feed_step, 0)

        if ff % TILE:
            @pl.when(i == 4)
            def _():
                feed_tile(whole_tiles, ff % TILE)

        @pl.when(i == 5)
        def _():
            for c in back_loads(0) + back_loads(1):
                c.start()

        @pl.when((i == 2) | (i == 3) | (i == 5) | (i == 6))
        def _():
            h = i - 2 - i // 5
            for c in head_loads(h):
                c.wait()
            slot = h % 2

            @pl.when(slot == 0)
            def _():
                attn_load(h).wait()
                value = contract(cot_own[...], attn_tile[...], ((1,), (1,)))
                for n in range(2):
                    d_att[n] = value[:, n * HALF : (n + 1) * HALF].astype(BF)

                @pl.when(h + 2 < pairs)
                def _():
                    attn_load(h + 2).start()

            heads_back_pair(
                q_tile.at[slot], k_tile.at[slot], v_tile.at[slot], d_att.at[slot], att_tile.at[slot],
                lse_tile.at[slot], cos, first, second, turned, dk, dv,
            )
            for n in range(3):
                d_mixed[:, tile_at(3 * h + n, HALF)] = turned[n]

            @pl.when(h + 2 < pairs)
            def _():
                for c in head_loads(h + 2):
                    c.start()

        return carry

    lax.fori_loop(0, chunks + 2 + LAG * (count - 1), step, 0)

    def drain(k, carry):
        own_copy(k).wait()
        for way in range(2):
            for hop in range(1, count):
                @pl.when(sends(way, hop))
                def _(way=way, hop=hop):
                    line_copy(way, hop, k).wait_send()
        return carry

    lax.fori_loop(chunks - DEEP, chunks, drain, 0)
    for kind in range(1, 3):
        sums_copy(kind * sum_parts - 1).wait()
    for way in range(2):
        for t in range(1, count):
            @pl.when(sum_sends(way, t))
            def _(way=way, t=t):
                for kind in range(1, 3):
                    sum_copy(way, t, kind * sum_parts - 1).wait_send()


def backward(
    order, slots, hid_t, att_t, tables, cot, norm_t, down, attn, both, branch, w_inner, w_heads, hat, heads, shards
):
    count, rows, width = cot.shape
    length = count * rows
    chips = shards // 2
    cols = heads[0].shape[1]
    inner = both.shape[1]
    chunks = (width + inner + 3 * cols) // TILE
    part = width // shards
    parts = width // TILE
    dma = pltpu.SemaphoreType.DMA
    smem = pl.BlockSpec(memory_space=pltpu.SMEM)
    return pl.pallas_call(
        backward_kernel,
        out_shape=[
            jax.ShapeDtypeStruct((count, chunks, part, TILE), BF),
            jax.ShapeDtypeStruct((2, rows, width), F32),
        ],
        in_specs=[smem] * 2 + [vmem_whole()] * 5 + [hbm_whole()] * 14,
        out_specs=[hbm_whole()] * 2,
        scratch_shapes=[
            pltpu.VMEM((length, width), BF),
            pltpu.VMEM((width, length), BF),
            pltpu.VMEM((length, inner), BF),
            pltpu.VMEM((length, 3 * cols), BF),
            pltpu.VMEM((count, rows, width), BF),
            pltpu.VMEM((count, rows, TILE), F32),
            pltpu.VMEM((parts, 16, TILE), BF),
            pltpu.VMEM((2, TILE, inner), BF),
            pltpu.VMEM((2, TILE, 3 * cols), BF),
            pltpu.VMEM((2, length, TILE), BF),
        ]
        + [pltpu.VMEM((TILE, width), BF)]
        + [pltpu.VMEM((2, length, HALF), BF)] * 3
        + [pltpu.VMEM((2, length, HALF), F32)] * 2
        + [pltpu.VMEM((2, length, HALF), BF)]
        + [pltpu.VMEM((3, length, HALF), BF)]
        + [pltpu.VMEM((length, HALF), F32)] * 2
        + [pltpu.VMEM((2, rows, TILE), F32)]
        + [
            pltpu.VMEM((2, chips, 2, part, TILE), BF),
            pltpu.VMEM((DEEP, chips, part, TILE), BF),
            pltpu.VMEM((2, chips, part, TILE), BF),
            pltpu.VMEM((DEEP, chips - 1, part, TILE), BF),
            pltpu.VMEM((DEEP, part, TILE), BF),
            pltpu.VMEM((2, count - 1, 2, rows, TILE), BF),
            pltpu.VMEM((2, count - 1, parts, rows, TILE), BF),
            dma((2,)),
            dma((DEEP,)),
            dma((2, chips - 1)),
            dma((DEEP, chips - 1)),
            dma((2, count - 1, DEEP)),
            dma((2, chunks, count - 1)),
            dma((DEEP,)),
            dma((2, count - 1, 2)),
            dma((2, count - 1, 2 * parts)),
            pltpu.SemaphoreType.DMA,
            dma((4,)),
            dma((2,)),
            dma((3, 2)),
            dma((5, 2)),
            dma((2,)),
        ],
        compiler_params=pltpu.CompilerParams(
            collective_id=1, has_side_effects=True, vmem_limit_bytes=62 * 2**20
        ),
        name="backward",
    )(order, slots, hid_t, att_t, *tables, cot, norm_t, down, attn, both, branch, w_inner, w_heads, hat, *heads)


def column_runs(columns, source):
    out = []
    for block in range(columns // HALF):
        first = 0
        while first < HALF:
            key, lane = source(block * HALF + first)
            last = first + 1
            while last < HALF and source(block * HALF + last) == (key, lane + last - first):
                last += 1
            out.append((block, first, last, key, (first - lane) % HALF))
            first = last
    return out


def assemble_kernel(rows_in, cols_in, sums, tokens, cot, gain, out, grad, qkv_out, gate_out, up_out, down_out, attn_out, small_out):
    count, chunks, rows, _ = rows_in.shape
    ff = gate_out.shape[1]
    width = qkv_out.shape[1]
    ff_part = down_out.shape[0] // count
    attn_part = attn_out.shape[0] // count
    shards = ff // (count * ff_part)
    inner_chunks = ff // count // HALF
    lane = lax.broadcasted_iota(jnp.int32, (rows, HALF), 1)
    own = tokens[...].astype(F32)
    out[...] = (own + sums[0]).astype(BF)
    own = own - jnp.mean(own, axis=1, keepdims=True)
    inv_std = lax.rsqrt(jnp.mean(own * own, axis=1, keepdims=True) + EPS)
    own = own * inv_std
    scaled = sums[1] * gain[0:1, :]
    scaled = scaled - jnp.mean(scaled, axis=1, keepdims=True) - own * jnp.mean(scaled * own, axis=1, keepdims=True)
    grad[...] = cot[...].astype(F32) + inv_std * scaled

    def gather(out, runs, load):
        for block, first, last, key, shift in runs:
            value = load(key).astype(F32)
            if shift:
                value = pltpu.roll(value, shift, 1)
            if first:
                value = jnp.where(lane >= first, value, held)
            held = value
            if last == HALF:
                out[:, block * HALF : (block + 1) * HALF] = value

    def inner_source(column):
        shard, rest = divmod(column, count * ff_part)
        unit = shard * ff_part + rest % ff_part
        return (rest // ff_part, unit // HALF), unit % HALF

    def head_source(column):
        part, rest = divmod(column, width // 3)
        head, dim = divmod(rest, HD)
        per = width // 3 // HD // shards // count
        shard, at = divmod(head, per * count)
        place, sub = divmod(at, per)
        pair, half = divmod(shard * per + sub, 2)
        return (place, 3 * pair + part), half * HD + dim

    runs = column_runs(ff, inner_source)
    gather(gate_out, runs, lambda key: rows_in[key[0], key[1], :, :HALF])
    gather(up_out, runs, lambda key: rows_in[key[0], key[1], :, HALF:])
    first_head = inner_chunks

    def head_load(key):
        at = key[1] % 2 * HALF
        return rows_in[key[0], first_head + key[1] // 2, :, at : at + HALF]

    gather(qkv_out, column_runs(width, head_source), head_load)
    for p in range(count):
        down_out[p * ff_part : (p + 1) * ff_part, :] = cols_in[p, 0, :ff_part, :].astype(F32)
        attn_out[p * attn_part : (p + 1) * attn_part, :] = cols_in[
            p, 0, ff_part : ff_part + attn_part, :
        ].astype(F32)
    small = [cols_in[p, 0, ff_part + attn_part :, :].astype(F32) for p in range(count)]
    small_out[...] = functools.reduce(jnp.add, small)


def assemble_outputs(pieces, sums, tokens, cot, gain, qkv, attn, gate, down):
    count, chunks, rows, _ = pieces.shape
    steps = down[1] // TILE
    part = rows // steps
    width = tokens.shape[1]
    by_rows = lambda shape: pl.BlockSpec((part, shape[1]), lambda i: (i, 0))
    by_cols = lambda shape: pl.BlockSpec((shape[0], TILE), lambda i: (0, i))
    return pl.pallas_call(
        assemble_kernel,
        grid=(steps,),
        in_specs=[
            pl.BlockSpec((count, chunks - steps, part, TILE), lambda i: (0, 0, i, 0)),
            pl.BlockSpec((count, 1, rows, TILE), lambda i: (0, chunks - steps + i, 0, 0)),
            pl.BlockSpec((2, part, width), lambda i: (0, i, 0)),
            by_rows(tokens.shape),
            by_rows(tokens.shape),
            pl.BlockSpec(gain.shape, lambda i: (0, 0)),
        ],
        out_specs=[by_rows(tokens.shape)] * 2
        + [by_rows(qkv), by_rows(gate), by_rows(gate), by_cols(down), by_cols(attn)]
        + [pl.BlockSpec((16, TILE), lambda i: (0, 0))],
        out_shape=[jax.ShapeDtypeStruct(tokens.shape, BF), jax.ShapeDtypeStruct(tokens.shape, F32)]
        + [jax.ShapeDtypeStruct(s, F32) for s in (qkv, gate, gate, down, attn, (16, TILE))],
        compiler_params=pltpu.CompilerParams(vmem_limit_bytes=60 * 2**20),
        name="assemble",
    )(pieces, pieces, sums, tokens, cot, gain)


def rotation_tables(length):
    half = ROT // 2
    inverse = 10000.0 ** (-jnp.arange(half, dtype=F32) / half)
    grid = jnp.arange(length, dtype=jnp.int32).astype(F32)[:, None] * inverse[None, :]
    cos, sin = jnp.cos(grid), jnp.sin(grid)
    zero = jnp.zeros((length, half), F32)
    rest = jnp.zeros((length, HD - ROT), F32)
    tables = (
        jnp.concatenate([cos, cos, rest + 1.0], axis=1),
        jnp.concatenate([-sin, zero, rest], axis=1),
        jnp.concatenate([zero, sin, rest], axis=1),
    )
    return tuple(jnp.tile(t, (1, 2)) for t in tables)


def body_general(tokens, block_order, ln_gain, ln_bias, w_qkv, w_out, w_gate, w_up, w_down, cotangent):
    rows, width = tokens.shape[1], tokens.shape[2]
    count = lax.axis_size("ctx")
    shards = lax.axis_size("fsdp")
    place = lax.axis_index("ctx")
    length = rows * count
    order = block_order[0]
    shard_rows = w_qkv.shape[0]
    ff_shard = w_down.shape[0]
    ff_part = ff_shard // count
    own_heads = H // count
    spread = (w_out.shape[0] // HD) % count == 0
    groups = shards if spread else 1
    head_cols = own_heads * HD // groups

    def my_cols(w, outer, group, part):
        w = w.reshape(w.shape[0], outer, group, count, part)
        return lax.dynamic_index_in_dim(w, place, 3, False).reshape(w.shape[0], outer * group * part)

    def all_cols(piece, outer, group, part):
        whole = gather_ctx(piece).reshape(count, piece.shape[0], outer, group, part)
        return whole.transpose(1, 2, 3, 0, 4).reshape(piece.shape[0], -1).astype(F32)

    def assemble(block, ready=None):
        whole = jnp.zeros((length, width), block.dtype)
        whole = lax.dynamic_update_slice_in_dim(whole, block, order[place] * rows, 0)
        last = None
        for k in range(1, count):
            last = ring_send(block, k)
            source = (place - k) % count
            whole = lax.dynamic_update_slice_in_dim(whole, last, order[source] * rows, 0)
        return whole, last

    gain = lax.all_gather(ln_gain, "fsdp", axis=0, tiled=True).astype(F32)
    bias = lax.all_gather(ln_bias, "fsdp", axis=0, tiled=True).astype(F32)
    tables = rotation_tables(length)

    block = tokens[0]
    x_all, arrived = assemble(block)
    grad_block = cotangent[0]
    cot_all, _ = assemble(after(grad_block, arrived))

    inner = jnp.concatenate(
        [my_cols(w_gate, 1, shards, ff_part), my_cols(w_up, 1, shards, ff_part)], axis=1
    )
    w_inner, sent = gather_rows(inner)
    w_heads, sent = gather_rows(after(my_cols(w_qkv, 3, groups, head_cols), sent))
    down = lax.dynamic_slice_in_dim(w_down, place * ff_part, ff_part, 0)
    w_hidden, sent = gather_rows(after(down, sent))
    if spread:
        part = w_out.shape[0] // count
        attn = lax.dynamic_slice_in_dim(w_out, place * part, part, 0)
        w_attn, sent = gather_rows(after(attn, sent))
    else:
        w_attn = lax.all_gather(after(w_out, sent), "fsdp", axis=0, tiled=True)
        w_attn = lax.dynamic_slice_in_dim(w_attn, place * own_heads * HD, own_heads * HD, 0)

    xf = x_all.astype(F32)
    average = jnp.mean(xf, axis=-1, keepdims=True)
    centered = xf - average
    variance = jnp.mean(centered * centered, axis=-1, keepdims=True)
    inv_std = lax.rsqrt(variance + EPS)
    x_hat = centered * inv_std
    normed = (x_hat * gain + bias).astype(BF)

    across = ((1,), (0,))
    over_tokens = ((0,), (0,))
    back = ((1,), (1,))
    ff_cols = shards * ff_part
    gate_value = dot(normed, w_inner[:, :ff_cols], across)
    up_value = dot(normed, w_inner[:, ff_cols:], across)
    sigmoid_gate = jax.nn.sigmoid(gate_value)
    hidden = (gate_value * sigmoid_gate * up_value).astype(BF)
    mixed = dot(normed, w_heads, across)
    q, k, v, attended, lse = attend(mixed, tables, own_heads)
    attended_low = attended.astype(BF)

    branch = dot(attended_low, w_attn, across) + dot(hidden, w_hidden, across)
    out = line_scatter(lambda j: lax.dynamic_slice_in_dim(branch, order[j] * rows, rows, 0))
    out = (block.astype(F32) + out).astype(BF)[None]

    d_hidden = dot(cot_all, w_hidden, back)
    grad_down = scatter_rows(dot(hidden, cot_all, over_tokens, BF))
    d_gate_act = (
        d_hidden * up_value * sigmoid_gate * (1.0 + gate_value * (1.0 - sigmoid_gate))
    ).astype(BF)
    d_up_act = (d_hidden * gate_value * sigmoid_gate).astype(BF)
    d_inner = jnp.concatenate([d_gate_act, d_up_act], axis=1)
    d_attended = dot(cot_all, w_attn, back, BF)
    d_mixed = attend_back(q, k, v, d_attended, attended, lse, tables, own_heads)
    d_mixed = jnp.concatenate(d_mixed, axis=1)
    grad_inner = scatter_rows(dot(normed, d_inner, over_tokens, BF))
    grad_attn = dot(attended_low, cot_all, over_tokens, BF)
    grad_heads = scatter_rows(dot(normed, d_mixed, over_tokens, BF))

    d_normed = dot(d_inner, w_inner, back) + dot(d_mixed, w_heads, back)
    small = jnp.stack([jnp.sum(d_normed * x_hat, axis=0), jnp.sum(d_normed, axis=0)])
    small = lax.psum(small, ("ctx", "fsdp"))
    small = lax.dynamic_slice_in_dim(small, lax.axis_index("fsdp") * shard_rows, shard_rows, 1)
    d_own = line_scatter(lambda j: lax.dynamic_slice_in_dim(d_normed, order[j] * rows, rows, 0))
    own = block.astype(F32)
    own_average = jnp.mean(own, axis=-1, keepdims=True)
    own = own - own_average
    own_std = lax.rsqrt(jnp.mean(own * own, axis=-1, keepdims=True) + EPS)
    own = own * own_std
    scaled = d_own * gain
    d_input = own_std * (
        scaled
        - jnp.mean(scaled, axis=-1, keepdims=True)
        - own * jnp.mean(scaled * own, axis=-1, keepdims=True)
    )
    grad_in = (grad_block.astype(F32) + d_input)[None]

    down_all = gather_ctx(grad_down).reshape(ff_shard, width).astype(F32)
    if spread:
        attn_all = gather_ctx(scatter_rows(grad_attn)).reshape(w_out.shape).astype(F32)
    else:
        full = jnp.zeros((H * HD, width), BF)
        full = lax.dynamic_update_slice_in_dim(full, grad_attn, place * own_heads * HD, 0)
        full = lax.psum_scatter(full, "fsdp", scatter_dimension=0, tiled=True)
        attn_all = lax.psum(full, "ctx").astype(F32)
    heads_all = all_cols(grad_heads, 3, groups, head_cols)
    inner_all = gather_ctx(grad_inner).reshape(count, shard_rows, 2, shards, ff_part)
    inner_all = inner_all.transpose(2, 1, 3, 0, 4).reshape(2, shard_rows, -1).astype(F32)
    return (
        out,
        grad_in,
        small[0],
        small[1],
        heads_all,
        attn_all,
        inner_all[0],
        inner_all[1],
        down_all,
    )


def body_fast(tokens, block_order, ln_gain, ln_bias, w_qkv, w_out, w_gate, w_up, w_down, cotangent):
    count, shards = lax.axis_size("ctx"), lax.axis_size("fsdp")
    place = lax.axis_index("ctx")
    block, grad_block = tokens[0], cotangent[0]
    rows, width = block.shape
    order = block_order[0]
    spots = jnp.arange(count, dtype=jnp.int32)
    slots = jnp.sum(jnp.where(order[None, :] == spots[:, None], spots[None, :], 0), axis=1)
    vectors = jnp.stack([ln_gain, ln_bias] + [jnp.zeros_like(ln_gain)] * 6).astype(F32)
    tables = fixed_tables(rows * count)
    (
        cot_all, scales, w_inner, w_heads, w_attn, w_hidden, normed_t, hat, both, hidden_t,
        q, k, v, attended, low_t, lse, branch,
    ) = forward(
        order, slots, tables, block, grad_block, vectors, w_gate, w_up, w_qkv, w_out, w_down, count, shards
    )
    w_inner = w_inner.reshape(width, -1)
    w_hidden, w_attn = w_hidden.reshape(-1, width), w_attn.reshape(-1, width)
    w_heads = w_heads.reshape(width, -1)
    pieces, sums = backward(
        order, slots, hidden_t, low_t, tables, cot_all, normed_t, w_hidden, w_attn, both, branch, w_inner,
        w_heads, hat, (q, k, v, attended, lse), shards,
    )
    out, grad_in, d_qkv, d_gate, d_up, d_down, d_attn, small = assemble_outputs(
        pieces, sums, block, grad_block, scales, w_qkv.shape, w_out.shape, w_gate.shape, w_down.shape
    )
    out, grad_in = out[None], grad_in[None]
    return out, grad_in, small[0], small[1], d_qkv, d_attn, d_gate, d_up, d_down


def solution(mesh):
    whole, once = P("fsdp", "ctx", None), P("fsdp", None)
    count, shards = mesh.shape["ctx"], mesh.shape["fsdp"]

    def body(*args):
        w_out, w_down = args[5], args[8]
        fits = shards == 8 and w_out.shape[0] == count * HD and w_out.shape[0] == TILE
        fits = fits and w_down.shape[0] % (16 * count) == 0 and w_down.shape[0] // count <= 176
        return (body_fast if fits else body_general)(*args)

    return jax.shard_map(
        body,
        mesh=mesh,
        in_specs=(whole, once, P("fsdp"), P("fsdp")) + (once,) * 5 + (whole,),
        out_specs=(whole, whole, P("fsdp"), P("fsdp")) + (once,) * 5,
        check_vma=False,
    )
```

```python
import functools

import jax
import jax.numpy as jnp
import numpy as np
from jax import lax
from jax.experimental import pallas as pl
from jax.experimental.pallas import tpu as pltpu
from jax.sharding import PartitionSpec as P

H = 32
HD = 64
ROT = 16
EPS = 1e-05
NEG = -1e30
CHUNK = 256

BF = jnp.bfloat16
F32 = jnp.float32


def xor_send(value, mask):
    count = lax.axis_size("fsdp")
    return lax.ppermute(value, "fsdp", [(i, i ^ mask) for i in range(count)])


def ring_send(value, steps):
    count = lax.axis_size("ctx")
    return lax.ppermute(value, "ctx", [(i, (i + steps) % count) for i in range(count)])


def after(value, *done):
    return lax.optimization_barrier((value,) + done)[0]


def dot(a, b, dims, out=F32):
    return lax.dot_general(a, b, (dims, ((), ())), preferred_element_type=F32).astype(out)


def gather_rows(piece):
    count = lax.axis_size("fsdp")
    chips = count // 2
    me = lax.axis_index("fsdp")
    chip, core = me // 2, me % 2
    parts = [piece] + [xor_send(piece, 2 * m) for m in range(1, chips)]
    others = [xor_send(p, 1) for p in parts]
    whole = jnp.zeros((count,) + piece.shape, piece.dtype)
    for m in range(chips):
        at = 2 * (chip ^ m)
        whole = lax.dynamic_update_index_in_dim(whole, parts[m], at + core, 0)
        whole = lax.dynamic_update_index_in_dim(whole, others[m], at + 1 - core, 0)
    return whole.reshape(count * piece.shape[0], piece.shape[1]), parts[-1]


def scatter_rows(grad):
    count = lax.axis_size("fsdp")
    chips = count // 2
    me = lax.axis_index("fsdp")
    chip, core = me // 2, me % 2
    rows = grad.shape[0] // count
    split = grad.reshape(chips, 2, rows, grad.shape[1])
    theirs = xor_send(lax.dynamic_index_in_dim(split, 1 - core, 1, False), 1)
    pair = lax.dynamic_index_in_dim(split, core, 1, False).astype(F32) + theirs.astype(F32)
    pair = pair.astype(BF)
    total = lax.dynamic_index_in_dim(pair, chip, 0, False).astype(F32)
    for m in range(1, chips):
        part = lax.dynamic_index_in_dim(pair, chip ^ m, 0, False)
        total = total + xor_send(part, 2 * m).astype(F32)
    return total.astype(BF)


def gather_ctx(piece):
    count = lax.axis_size("ctx")
    me = lax.axis_index("ctx")
    whole = jnp.zeros((count,) + piece.shape, piece.dtype)
    whole = lax.dynamic_update_index_in_dim(whole, piece, me, 0)
    for k in range(1, count):
        part = ring_send(piece, k)
        whole = lax.dynamic_update_index_in_dim(whole, part, (me - k) % count, 0)
    return whole


def line_scatter(blocks):
    count = lax.axis_size("ctx")
    me = lax.axis_index("ctx")
    down = up = None
    for t in range(1, count):
        to_down = blocks(jnp.clip(t + me - count, 0, count - 1))
        to_up = blocks(jnp.clip(count - 1 - (t + (count - 1 - me) - count), 0, count - 1))
        if down is not None:
            to_down = to_down + down.astype(F32)
            to_up = to_up + up.astype(F32)
        pairs = [(i, i - 1) for i in range(count - t, count)]
        down = lax.ppermute(to_down.astype(BF), "ctx", pairs)
        up = lax.ppermute(to_up.astype(BF), "ctx", [(count - 1 - i, count - 1 - j) for i, j in pairs])
    return blocks(me) + down.astype(F32) + up.astype(F32)


def turn(x, cos, first, second):
    width = x.shape[1]
    half = ROT // 2
    return x * cos + pltpu.roll(x, width - half, 1) * first + pltpu.roll(x, half, 1) * second


def contract(a, b, dims):
    return lax.dot_general(a, b, (dims, ((), ())), preferred_element_type=F32)


def attend_kernel(mq, mk, mv, cos, first, second, q_out, k_out, v_out, att_out, lse_out):
    length = mq.shape[0]
    scale = HD ** (-0.5)
    q_out[...] = (turn(mq[...], cos[...], first[...], second[...]).astype(BF).astype(F32) * scale).astype(BF)
    k_out[...] = turn(mk[...], cos[...], first[...], second[...]).astype(BF)
    v_out[...] = mv[...].astype(BF)
    row = lax.broadcasted_iota(jnp.int32, (CHUNK, CHUNK), 0)
    col = lax.broadcasted_iota(jnp.int32, (CHUNK, CHUNK), 1)
    for c in range(length // CHUNK):
        lo, hi = c * CHUNK, (c + 1) * CHUNK
        for h in range(2):
            lanes = slice(h * HD, (h + 1) * HD)
            q = q_out[lo:hi, lanes]
            s = contract(q, k_out[lo:hi, lanes], ((1,), (1,)))
            s = jnp.where(col <= row, s, NEG)
            if c:
                s = jnp.concatenate([contract(q, k_out[:lo, lanes], ((1,), (1,))), s], axis=1)
            top = jnp.max(s, axis=1, keepdims=True)
            p = jnp.exp(s - top)
            total = jnp.sum(p, axis=1, keepdims=True)
            o = contract(p.astype(BF), v_out[:hi, lanes], ((1,), (0,)))
            att_out[lo:hi, lanes] = o / total
            lse_out[lo:hi, lanes] = jnp.broadcast_to(top + jnp.log(total), (CHUNK, HD))


def attend(mixed, tables, heads):
    length = mixed.shape[0]
    pairs = heads // 2
    block = lambda at: pl.BlockSpec((length, 2 * HD), lambda h, at=at: (0, at + h))
    table = pl.BlockSpec((length, 2 * HD), lambda h: (0, 0))
    width = heads * HD
    return pl.pallas_call(
        attend_kernel,
        grid=(pairs,),
        in_specs=[block(0), block(pairs), block(2 * pairs), table, table, table],
        out_specs=[block(0)] * 5,
        out_shape=[jax.ShapeDtypeStruct((length, width), BF)] * 3
        + [jax.ShapeDtypeStruct((length, width), F32)] * 2,
        compiler_params=pltpu.CompilerParams(vmem_limit_bytes=40 * 2**20),
        cost_estimate=pl.CostEstimate(
            flops=16 * heads * length * length * HD // 2,
            bytes_accessed=26 * length * width,
            transcendentals=heads * length * length // 2,
        ),
        name="attend",
    )(mixed, mixed, mixed, *tables)


def attend_back_kernel(q_in, k_in, v_in, do_in, att, lse, cos, first, second, dq_out, dk_out, dv_out, dk, dv):
    length = q_in.shape[0]
    scale = HD ** (-0.5)
    row = lax.broadcasted_iota(jnp.int32, (CHUNK, CHUNK), 0)
    col = lax.broadcasted_iota(jnp.int32, (CHUNK, CHUNK), 1)
    dk[...] = jnp.zeros_like(dk)
    dv[...] = jnp.zeros_like(dv)
    for c in range(length // CHUNK):
        lo, hi = c * CHUNK, (c + 1) * CHUNK
        dqs = []
        for h in range(2):
            lanes = slice(h * HD, (h + 1) * HD)
            q, do = q_in[lo:hi, lanes], do_in[lo:hi, lanes]
            delta = jnp.sum(do.astype(F32) * att[lo:hi, lanes], axis=1, keepdims=True)
            s = contract(q, k_in[lo:hi, lanes], ((1,), (1,)))
            s = jnp.where(col <= row, s, NEG)
            if c:
                s = jnp.concatenate([contract(q, k_in[:lo, lanes], ((1,), (1,))), s], axis=1)
            p = jnp.exp(s - lse[lo:hi, h * HD : h * HD + 1])
            dp = contract(do, v_in[:hi, lanes], ((1,), (1,)))
            ds = (p * (dp - delta)).astype(BF)
            dqs.append(contract(ds, k_in[:hi, lanes], ((1,), (0,))) * scale)
            dk[:hi, lanes] += contract(ds, q, ((0,), (0,)))
            dv[:hi, lanes] += contract(p.astype(BF), do, ((0,), (0,)))
        dq = jnp.concatenate(dqs, axis=1)
        dq_out[lo:hi, :] = turn(dq, cos[lo:hi, :], -first[lo:hi, :], -second[lo:hi, :]).astype(BF)
    dk_out[...] = turn(dk[...], cos[...], -first[...], -second[...]).astype(BF)
    dv_out[...] = dv[...].astype(BF)


def attend_back(q, k, v, d_attended, attended, lse, tables, heads):
    length, width = q.shape
    block = pl.BlockSpec((length, 2 * HD), lambda h: (0, h))
    table = pl.BlockSpec((length, 2 * HD), lambda h: (0, 0))
    return pl.pallas_call(
        attend_back_kernel,
        grid=(heads // 2,),
        in_specs=[block] * 6 + [table] * 3,
        out_specs=[block] * 3,
        out_shape=[jax.ShapeDtypeStruct((length, width), BF)] * 3,
        scratch_shapes=[pltpu.VMEM((length, 2 * HD), F32)] * 2,
        compiler_params=pltpu.CompilerParams(vmem_limit_bytes=40 * 2**20),
        cost_estimate=pl.CostEstimate(
            flops=40 * heads * length * length * HD // 2,
            bytes_accessed=22 * length * width,
            transcendentals=heads * length * length // 2,
        ),
        name="attend_back",
    )(q, k, v, d_attended, attended, lse, *tables)


MESH = pl.DeviceIdType.MESH
TILE = 256
HALF = 128
DEEP = 4
LAG = 1


def tile_at(i, size=TILE):
    return pl.ds(pl.multiple_of(i * size, size), size)


def vmem_whole():
    return pl.BlockSpec(memory_space=pltpu.VMEM)


def hbm_whole():
    return pl.BlockSpec(memory_space=pl.ANY)


def chip_away(chip, m):
    return 2 * ((chip // 2 + m // 2) % 2) + (chip + m) % 2


def inner_runs(shards, count, part):
    runs = []
    for block in range(shards * part // HALF):
        first = 0
        while first < HALF:
            shard, unit = divmod(block * HALF + first, part)
            last = min(HALF, first + part - unit)
            runs.append((block, first, last, shard * count * part + unit - first))
            first = last
    return runs


class Line:
    def __init__(self, own, whole, send, recv):
        self.own, self.whole, self.send, self.recv = own, whole, send, recv
        self.count = whole.shape[0]
        self.place, self.me = lax.axis_index("ctx"), lax.axis_index("fsdp")

    def copy(self, way, hop):
        ahead = 1 - 2 * way
        origin = self.place - (hop - 1) * ahead
        return pltpu.make_async_remote_copy(
            src_ref=self.own if hop == 1 else self.whole.at[origin],
            dst_ref=self.whole.at[origin],
            send_sem=self.send.at[way, hop - 1],
            recv_sem=self.recv.at[way, hop - 1],
            device_id=(self.place + ahead, self.me),
            device_id_type=MESH,
        )

    def sends(self, way, hop):
        if way == 0:
            return (self.place >= hop - 1) & (self.place <= self.count - 2)
        return (self.place <= self.count - hop) & (self.place >= 1)

    def lands(self, way, hop):
        return self.place >= hop if way == 0 else self.place <= self.count - 1 - hop

    def pass_on(self, hop):
        for way in range(2):
            if hop > 1:
                @pl.when(self.lands(way, hop - 1))
                def _(way=way):
                    self.copy(way, hop - 1).wait_recv()

            if hop < self.count:
                @pl.when(self.sends(way, hop))
                def _(way=way):
                    self.copy(way, hop).start()

    def finish(self):
        for way in range(2):
            for hop in range(1, self.count):
                @pl.when(self.sends(way, hop))
                def _(way=way, hop=hop):
                    self.copy(way, hop).wait_send()


class Plane:
    def __init__(self, mine, wholes, send, recv):
        self.mine, self.wholes, self.send, self.recv = mine, wholes, send, recv
        self.place, self.me = lax.axis_index("ctx"), lax.axis_index("fsdp")
        chip, core = self.me // 2, self.me % 2
        self.sibling = 2 * chip + 1 - core
        self.near = (2 * chip_away(chip, 1) + core, 2 * chip_away(chip, 2) + core)
        self.far = 2 * chip_away(chip, 3) + core

    def copy(self, which, kind, source, target, to):
        return pltpu.make_async_remote_copy(
            src_ref=source,
            dst_ref=target,
            send_sem=self.send.at[which, kind],
            recv_sem=self.recv.at[which, kind],
            device_id=(self.place, to),
            device_id_type=MESH,
        )

    def direct(self, which, a):
        return self.copy(which, a, self.mine[which], self.wholes[which].at[self.me], self.near[a])

    def across(self, which, a):
        half = self.wholes[which].shape[2] // 2
        piece = self.wholes[which].at[self.near[1 - a], :, a * half : (a + 1) * half]
        return self.copy(which, 2 + a, piece, piece, self.near[a])

    def beside(self, which, kind):
        source = (self.me, self.near[0], self.near[1], self.far)[kind]
        piece = self.wholes[which].at[source]
        return self.copy(which, 4 + kind, self.mine[which] if kind == 0 else piece, piece, self.sibling)

    def begin(self, which):
        for a in range(2):
            self.direct(which, a).start()
        self.beside(which, 0).start()

    def relay(self, which):
        for a in range(2):
            self.direct(which, a).wait_recv()
        for a in range(2):
            self.across(which, a).start()
            self.beside(which, 1 + a).start()

    def last(self, which):
        for a in range(2):
            self.across(which, a).wait_recv()
        self.beside(which, 3).start()

    def finish(self, which):
        for kind in range(4):
            self.beside(which, kind).wait()
        for a in range(2):
            self.direct(which, a).wait_send()
            self.across(which, a).wait_send()


class Own:
    def __init__(self, source, stage, target, sem, n):
        self.load = pltpu.make_async_copy(source, stage, sem.at[n, 0])
        self.store = pltpu.make_async_copy(stage, target, sem.at[n, 1])

    def turn(self):
        self.load.wait()
        self.store.start()


def greet(peers, meanwhile):
    barrier = pltpu.get_barrier_semaphore()
    for peer in peers:
        pl.semaphore_signal(barrier, inc=1, device_id=peer, device_id_type=MESH)
    meanwhile()
    pl.semaphore_wait(barrier, len(peers))


def forward_kernel(
    order, slots, cos, first, second, tokens, cot, vectors, w_gate, w_up, w_qkv, w_out, w_down,
    cot_all, rows_out, inner_out, heads_out, attn_out, down, normed_t, hat, both, hidden_t,
    q_out, k_out, v_out, att_out, low_t, lse_out, branch,
    raw, x_all, vectors_all, scales, inner, heads, attn,
    normed, hidden, low, hat_stage, turned_stage, both_stage, hidden_stage,
    q_buf, k_buf, v_buf, att_buf, low_stage, lse_buf, down_tile, term, branch_stage,
    load_sem, x_send, x_recv, line_send, line_recv, part_send, part_recv, vector_send, vector_recv,
    own_sem, out_sem, norm_sem, feed_sem, head_sem, tile_sem, branch_sem,
):
    count, rows = x_all.shape[0], x_all.shape[1]
    shards = inner.shape[0]
    place, me = lax.axis_index("ctx"), lax.axis_index("fsdp")
    width = w_gate.shape[1]
    my_attn = w_out.at[pl.ds(pl.multiple_of(place * attn.shape[1], 16), attn.shape[1])]
    my_down = w_down.at[pl.ds(pl.multiple_of(place * down.shape[1], 16), down.shape[1])]
    loads = [
        pltpu.make_async_copy(my_attn, attn.at[me], load_sem.at[0]),
        pltpu.make_async_copy(w_gate, raw.at[0, :, :width], load_sem.at[1]),
        pltpu.make_async_copy(w_up, raw.at[1, :, :width], load_sem.at[2]),
        pltpu.make_async_copy(tokens, x_all.at[place], load_sem.at[3]),
        pltpu.make_async_copy(vectors, vectors_all.at[me], load_sem.at[4]),
    ]
    owns = [
        Own(cot, hat_stage.at[0], cot_all.at[place], own_sem, 0),
        Own(my_down, hat_stage.at[1, : down.shape[1]], down.at[me], own_sem, 1),
    ]
    qkv_load = pltpu.make_async_copy(w_qkv, raw.at[0], load_sem.at[5])
    peers = [(place, (me + s) % shards) for s in range(1, shards)]
    peers += [((place + 1) % count, me), ((place + count - 1) % count, me)]

    def meanwhile():
        for c in loads + [own.load for own in owns]:
            c.start()

    greet(peers, meanwhile)
    x_line = Line(tokens, x_all, x_send, x_recv)
    line = Line(cot, cot_all, line_send, line_recv)
    plane = Plane(
        (inner.at[me], attn.at[me], heads.at[me], my_down), (inner, attn, heads, down), part_send, part_recv
    )
    x_line.pass_on(1)
    vector_copies = [
        pltpu.make_async_remote_copy(
            src_ref=vectors,
            dst_ref=vectors_all.at[me],
            send_sem=vector_send.at[s - 1],
            recv_sem=vector_recv.at[s - 1],
            device_id=(place, (me + s) % shards),
            device_id_type=MESH,
        )
        for s in range(1, shards)
    ]
    for c in vector_copies:
        c.start()
    loads[0].wait()
    plane.begin(1)

    row = lax.broadcasted_iota(jnp.int32, (TILE, HALF), 0)
    col = lax.broadcasted_iota(jnp.int32, (TILE, HALF), 1)

    def picked(sources, size, first, last, start):
        base = jnp.minimum((start + first) // HALF, size // HALF - TILE // HALF) * HALF
        choose = (row + base == col + start) & (col >= first) & (col < last)
        choose = choose.astype(F32).astype(BF)
        at = pl.ds(pl.multiple_of(base, HALF), TILE)
        return [contract(raw[source, :, at], choose, ((1,), (0,))) for source in sources]

    part = width // shards // count
    loads[1].wait()
    loads[2].wait()
    held = None
    for block, first_col, last_col, start in inner_runs(shards, count, part):
        values = picked((0, 1), width, first_col, last_col, start + place * part)
        held = values if first_col == 0 else [a + b for a, b in zip(held, values)]
        if last_col == HALF:
            for k in range(2):
                at = block * TILE + k * HALF
                inner[me, :, at : at + HALF] = held[k].astype(BF)
    plane.begin(0)
    qkv_load.start()
    qkv_load.wait()
    third = raw.shape[2] // 3
    for pair in range(shards // 2):
        for kind in range(3):
            value = 0.0
            for h in range(2):
                head = count * (2 * pair + h) + place
                start = kind * third + head * HD - h * HD
                value = value + picked((0,), raw.shape[2], h * HD, (h + 1) * HD, start)[0]
            at = (pair * 3 + kind) * HALF
            heads[me, :, at : at + HALF] = value.astype(BF)
    plane.begin(2)
    for own in owns:
        own.turn()
    plane.relay(1)
    x_line.pass_on(2)
    plane.relay(0)
    plane.last(1)
    x_line.pass_on(3)
    line.pass_on(1)
    plane.relay(2)
    plane.last(0)
    plane.finish(1)
    for c in loads[3:] + vector_copies:
        c.wait()
    scales[...] = jnp.concatenate([vectors_all[s] for s in range(shards)], axis=1)
    x_line.pass_on(4)
    plane.begin(3)
    outs = [
        pltpu.make_async_copy(attn, attn_out, out_sem.at[0]),
        pltpu.make_async_copy(scales, rows_out, out_sem.at[1]),
        pltpu.make_async_copy(inner, inner_out, out_sem.at[2]),
        pltpu.make_async_copy(heads, heads_out, out_sem.at[3]),
    ]
    outs[0].start()
    outs[1].start()

    def norm_copies(p):
        at = pl.ds(pl.multiple_of(p * rows, rows), rows)
        return (
            pltpu.make_async_copy(hat_stage.at[p % 2], hat.at[at], norm_sem.at[0, p % 2]),
            pltpu.make_async_copy(turned_stage.at[p % 2], normed_t.at[:, at], norm_sem.at[1, p % 2]),
        )

    def norm_step(p, carry):
        @pl.when(p >= 2)
        def _():
            for c in norm_copies(p - 2):
                c.wait()

        xf = x_all[slots[p]].astype(F32)
        mean = jnp.mean(xf, axis=1, keepdims=True)
        centered = xf - mean
        variance = jnp.mean(centered * centered, axis=1, keepdims=True)
        x_hat = centered * lax.rsqrt(variance + EPS)
        hat_stage[p % 2] = x_hat.astype(BF)
        value = x_hat * scales[0:1, :] + scales[1:2, :]
        normed[pl.ds(pl.multiple_of(p * rows, rows), rows), :] = value.astype(BF)
        turned_stage[p % 2] = value.T.astype(BF)
        for c in norm_copies(p):
            c.start()
        return carry

    for own in owns:
        own.store.wait()
    lax.fori_loop(0, count, norm_step, 0)
    plane.finish(0)
    outs[2].start()
    model = normed.shape[1]

    def feed_copies(i):
        wide = pl.ds(pl.multiple_of(i * TILE, TILE), TILE)
        slim = pl.ds(pl.multiple_of(i * HALF, HALF), HALF)
        return (
            pltpu.make_async_copy(both_stage.at[i % 2], both.at[:, wide], feed_sem.at[0, i % 2]),
            pltpu.make_async_copy(hidden_stage.at[i % 2], hidden_t.at[slim], feed_sem.at[1, i % 2]),
        )

    def feed_step(i, carry):
        @pl.when(i >= 2)
        def _():
            for c in feed_copies(i - 2):
                c.wait()

        value = contract(normed[...], inner[:, :, tile_at(i)].reshape(model, TILE), ((1,), (0,)))
        both_stage[i % 2] = value.astype(BF)
        gate, up = value[:, :HALF], value[:, HALF:]
        value = gate * jax.nn.sigmoid(gate) * up
        hidden[:, pl.ds(pl.multiple_of(i * HALF, HALF), HALF)] = value.astype(BF)
        hidden_stage[i % 2] = value.T.astype(BF)
        for c in feed_copies(i):
            c.start()
        return carry

    tiles = inner.shape[2] // TILE
    lax.fori_loop(0, tiles, feed_step, 0)
    line.pass_on(2)
    plane.relay(3)
    plane.last(2)
    plane.finish(2)
    outs[3].start()
    row = lax.broadcasted_iota(jnp.int32, (CHUNK, CHUNK), 0)
    col = lax.broadcasted_iota(jnp.int32, (CHUNK, CHUNK), 1)
    pairs = heads.shape[2] // (3 * HALF)

    def head_copies(h):
        at = pl.ds(pl.multiple_of(h * HALF, HALF), HALF)
        moves = ((q_buf, q_out), (k_buf, k_out), (v_buf, v_out), (att_buf, att_out), (lse_buf, lse_out))
        copies = [
            pltpu.make_async_copy(a.at[h % 2], b.at[:, at], head_sem.at[n, h % 2]) for n, (a, b) in enumerate(moves)
        ]
        return copies + [pltpu.make_async_copy(low_stage.at[h % 2], low_t.at[at], head_sem.at[5, h % 2])]

    def head_step(h, carry):
        @pl.when(h >= 2)
        def _():
            for c in head_copies(h - 2):
                c.wait()

        slot = h % 2
        w = heads[:, :, tile_at(h, 3 * HALF)].reshape(model, 3 * HALF)
        mixed = contract(normed[...], w, ((1,), (0,)))
        q = turn(mixed[:, :HALF], cos[...], first[...], second[...]).astype(BF).astype(F32)
        q_buf[slot] = (q * HD ** (-0.5)).astype(BF)
        k_buf[slot] = turn(mixed[:, HALF : 2 * HALF], cos[...], first[...], second[...]).astype(BF)
        v_buf[slot] = mixed[:, 2 * HALF :].astype(BF)
        for c in range(normed.shape[0] // CHUNK):
            lo, hi = c * CHUNK, (c + 1) * CHUNK
            for side in range(2):
                lanes = slice(side * HD, (side + 1) * HD)
                q = q_buf[slot, lo:hi, lanes]
                s = contract(q, k_buf[slot, lo:hi, lanes], ((1,), (1,)))
                s = jnp.where(col <= row, s, NEG)
                if c:
                    s = jnp.concatenate([contract(q, k_buf[slot, :lo, lanes], ((1,), (1,))), s], axis=1)
                top = jnp.max(s, axis=1, keepdims=True)
                p = jnp.exp(s - top)
                total = jnp.sum(p, axis=1, keepdims=True)
                o = contract(p.astype(BF), v_buf[slot, :hi, lanes], ((1,), (0,)))
                att_buf[slot, lo:hi, lanes] = o / total
                lse_buf[slot, lo:hi, lanes] = jnp.broadcast_to(top + jnp.log(total), (CHUNK, HD))
        att = att_buf[slot]
        low[:, pl.ds(pl.multiple_of(h * HALF, HALF), HALF)] = att.astype(BF)
        low_stage[slot] = att.T.astype(BF)
        for c in head_copies(h):
            c.start()
        return carry

    lax.fori_loop(0, pairs - 1, head_step, 0)
    plane.last(3)
    line.pass_on(3)
    lax.fori_loop(pairs - 1, pairs, head_step, 0)
    plane.finish(3)
    def tile_copies(i):
        at = pl.ds(pl.multiple_of(i * TILE, TILE), TILE)
        return [pltpu.make_async_copy(down.at[:, :, at], down_tile.at[i % 2], tile_sem.at[i % 2])]

    def branch_copy(i):
        at = pl.ds(pl.multiple_of(i * TILE, TILE), TILE)
        return pltpu.make_async_copy(branch_stage.at[i % 2], branch.at[:, :, at], branch_sem.at[i % 2])

    steps = branch.shape[2] // TILE
    for c in tile_copies(0):
        c.start()

    def branch_step(i, carry):
        @pl.when(i + 1 < steps)
        def _():
            for c in tile_copies(i + 1):
                c.start()

        for c in tile_copies(i):
            c.wait()

        @pl.when(i >= 2)
        def _():
            branch_copy(i - 2).wait()

        value = contract(hidden[...], down_tile[i % 2].reshape(hidden.shape[1], TILE), ((1,), (0,)))
        value = value + contract(low[...], attn[:, :, tile_at(i)].reshape(low.shape[1], TILE), ((1,), (0,)))
        term[...] = value.reshape(term.shape)
        for j in range(count):
            branch_stage[i % 2, j] = term[order[j]].astype(BF)
        branch_copy(i).start()
        return carry

    lax.fori_loop(0, steps, branch_step, 0)
    for hop in range(4, count + 1):
        line.pass_on(hop)
    line.finish()
    x_line.finish()
    for c in outs:
        c.wait()
    for back in range(2):
        for c in norm_copies(count - 1 - back) + feed_copies(tiles - 1 - back):
            c.wait()
        for c in head_copies(pairs - 1 - back):
            c.wait()
        branch_copy(steps - 1 - back).wait()


def forward(order, slots, tables, tokens, cot, vectors, w_gate, w_up, w_qkv, w_out, w_down, count, shards):
    rows, width = tokens.shape
    length = count * rows
    shard_rows = w_gate.shape[0]
    ff_part, attn_part = w_down.shape[0] // count, w_out.shape[0] // count
    ff, cols = shards * ff_part, shards * attn_part
    dma = pltpu.SemaphoreType.DMA
    smem = pl.BlockSpec(memory_space=pltpu.SMEM)
    bf = lambda *shape: jax.ShapeDtypeStruct(shape, BF)
    f32 = lambda *shape: jax.ShapeDtypeStruct(shape, F32)
    out_shape = [
        bf(count, rows, width),
        f32(vectors.shape[0], width),
        bf(shards, shard_rows, 2 * ff),
        bf(shards, shard_rows, 3 * cols),
        bf(shards, attn_part, width),
        bf(shards, ff_part, width),
        bf(width, length),
        bf(length, width),
        bf(length, 2 * ff),
        bf(ff, length),
        bf(length, cols),
        bf(length, cols),
        bf(length, cols),
        f32(length, cols),
        bf(cols, length),
        f32(length, cols),
        bf(count, rows, width),
    ]
    hops = (2, count - 1)
    return pl.pallas_call(
        forward_kernel,
        out_shape=out_shape,
        in_specs=[smem] * 2 + [vmem_whole()] * 3 + [hbm_whole()] * 8,
        out_specs=[hbm_whole()] * len(out_shape),
        scratch_shapes=[
            pltpu.VMEM((2,) + w_qkv.shape, BF),
            pltpu.VMEM((count, rows, width), BF),
            pltpu.VMEM((shards,) + vectors.shape, F32),
            pltpu.VMEM((vectors.shape[0], width), F32),
            pltpu.VMEM((shards, shard_rows, 2 * ff), BF),
            pltpu.VMEM((shards, shard_rows, 3 * cols), BF),
            pltpu.VMEM((shards, attn_part, width), BF),
            pltpu.VMEM((length, width), BF),
            pltpu.VMEM((length, ff), BF),
            pltpu.VMEM((length, cols), BF),
            pltpu.VMEM((2, rows, width), BF),
            pltpu.VMEM((2, width, rows), BF),
            pltpu.VMEM((2, length, TILE), BF),
            pltpu.VMEM((2, HALF, length), BF),
            pltpu.VMEM((2, length, HALF), BF),
            pltpu.VMEM((2, length, HALF), BF),
            pltpu.VMEM((2, length, HALF), BF),
            pltpu.VMEM((2, length, HALF), F32),
            pltpu.VMEM((2, HALF, length), BF),
            pltpu.VMEM((2, length, HALF), F32),
            pltpu.VMEM((2, shards, ff_part, TILE), BF),
            pltpu.VMEM((count, rows, TILE), F32),
            pltpu.VMEM((2, count, rows, TILE), BF),
            dma((6,)),
            dma(hops),
            dma(hops),
            dma(hops),
            dma(hops),
            dma((4, 8)),
            dma((4, 8)),
            dma((shards - 1,)),
            dma((shards - 1,)),
            dma((2, 2)),
            dma((4,)),
            dma((2, 2)),
            dma((2, 2)),
            dma((6, 2)),
            dma((2,)),
            dma((2,)),
        ],
        compiler_params=pltpu.CompilerParams(
            collective_id=3, has_side_effects=True, vmem_limit_bytes=62 * 2**20
        ),
        name="forward",
    )(order, slots, *tables, tokens, cot, vectors, w_gate, w_up, w_qkv, w_out, w_down)


def fixed_tables(length):
    half = ROT // 2
    inverse = np.float32(10000.0) ** (-np.arange(half, dtype=np.float32) / np.float32(half))
    grid = np.arange(length, dtype=np.float32)[:, None] * inverse.astype(np.float32)[None, :]
    cos, sin = np.cos(grid, dtype=np.float32), np.sin(grid, dtype=np.float32)
    zero, rest = np.zeros((length, half), np.float32), np.zeros((length, HD - ROT), np.float32)
    tables = ([cos, cos, rest + 1], [-sin, zero, rest], [zero, sin, rest])
    return [jnp.asarray(np.tile(np.concatenate(t, axis=1), (1, 2))) for t in tables]


def rows_of(shard, part):
    return slice(shard * part, (shard + 1) * part)


def heads_back_pair(q_in, k_in, v_in, do_in, att, lse, cos, first, second, out, dk, dv):
    length = q_in.shape[0]
    scale = HD ** (-0.5)
    row = lax.broadcasted_iota(jnp.int32, (CHUNK, CHUNK), 0)
    col = lax.broadcasted_iota(jnp.int32, (CHUNK, CHUNK), 1)
    dk[...] = jnp.zeros_like(dk)
    dv[...] = jnp.zeros_like(dv)
    for c in range(length // CHUNK):
        lo, hi = c * CHUNK, (c + 1) * CHUNK
        dqs = []
        for h in range(2):
            lanes = slice(h * HD, (h + 1) * HD)
            q, do = q_in[lo:hi, lanes], do_in[lo:hi, lanes]
            delta = jnp.sum(do.astype(F32) * att[lo:hi, lanes], axis=1, keepdims=True)
            s = contract(q, k_in[lo:hi, lanes], ((1,), (1,)))
            s = jnp.where(col <= row, s, NEG)
            if c:
                s = jnp.concatenate([contract(q, k_in[:lo, lanes], ((1,), (1,))), s], axis=1)
            p = jnp.exp(s - lse[lo:hi, h * HD : h * HD + 1])
            dp = contract(do, v_in[:hi, lanes], ((1,), (1,)))
            ds = (p * (dp - delta)).astype(BF)
            dqs.append(contract(ds, k_in[:hi, lanes], ((1,), (0,))) * scale)
            dk[:hi, lanes] += contract(ds, q, ((0,), (0,)))
            dv[:hi, lanes] += contract(p.astype(BF), do, ((0,), (0,)))
        dq = jnp.concatenate(dqs, axis=1)
        out[0, lo:hi, :] = turn(dq, cos[lo:hi, :], -first[lo:hi, :], -second[lo:hi, :]).astype(BF)
    out[1] = turn(dk[...], cos[...], -first[...], -second[...]).astype(BF)
    out[2] = dv[...].astype(BF)


def backward_kernel(
    order, slots, hid_t, att_t, cos, first, second,
    cot, norm_hbm, down, attn, both, branch, w_inner, w_heads, hat, q_in, k_in, v_in, att_in, lse_in,
    pieces, sums,
    cot_own, norm_t, d_inner, d_mixed, terms, term, small, w_tile, h_tile, hat_tile,
    attn_tile, q_tile, k_tile, v_tile, att_tile, lse_tile, d_att, turned, dk, dv, sums_stage,
    partial, theirs, pair, landed, total, sum_from, sum_land,
    core_send, core_recv, chip_send, chip_recv, line_send, line_recv, own_sem, sum_send, sum_recv,
    cot_sem, load_sem, feed_sem, back_sem, head_sem, sums_sem,
):
    count, chunks = pieces.shape[0], pieces.shape[1]
    shards = 2 * partial.shape[1]
    chips = shards // 2
    rows = terms.shape[1]
    place, me = lax.axis_index("ctx"), lax.axis_index("fsdp")
    chip, core = me // 2, me % 2
    ff_part, attn_part = hid_t.shape[0] // shards, att_t.shape[0] // shards
    sum_parts = terms.shape[2] // TILE
    early = cot_own.shape[1] // TILE - 1
    inner_end = early + d_inner.shape[1] // TILE

    def chunk_name(i):
        return jnp.where(i < early, i + chunks - 1 - early, jnp.where(i == chunks - 1, i, i - early))

    def core_copy(i):
        return pltpu.make_async_remote_copy(
            src_ref=partial.at[i % 2, :, 1 - core],
            dst_ref=theirs.at[i % DEEP],
            send_sem=core_send.at[i % 2],
            recv_sem=core_recv.at[i % DEEP],
            device_id=(place, me + 1 - 2 * core),
            device_id_type=MESH,
        )

    def chip_copy(j, m):
        return pltpu.make_async_remote_copy(
            src_ref=pair.at[j % 2, chip_away(chip, m)],
            dst_ref=landed.at[j % DEEP, m - 1],
            send_sem=chip_send.at[j % 2, m - 1],
            recv_sem=chip_recv.at[j % DEEP, m - 1],
            device_id=(place, 2 * chip_away(chip, m) + core),
            device_id_type=MESH,
        )

    def line_copy(way, hop, k, size):
        ahead = 1 - 2 * way
        origin = place - (hop - 1) * ahead
        target = pieces.at[origin, chunk_name(k), :size]
        return pltpu.make_async_remote_copy(
            src_ref=total.at[k % DEEP, :size] if hop == 1 else target,
            dst_ref=target,
            send_sem=line_send.at[way, hop - 1, k % DEEP],
            recv_sem=line_recv.at[way, k, hop - 1],
            device_id=(place + ahead, me),
            device_id_type=MESH,
        )

    def on_line(way, hop, k, act):
        @pl.when(k < early)
        def _():
            act(line_copy(way, hop, k, ff_part + attn_part))

        @pl.when(k >= early)
        def _():
            act(line_copy(way, hop, k, total.shape[1]))

    def sends(way, hop):
        if way == 0:
            return (place >= hop - 1) & (place <= count - 2)
        return (place <= count - hop) & (place >= 1)

    def lands(way, hop):
        return place >= hop if way == 0 else place <= count - 1 - hop

    def forward_chunk(hop, k):
        for way in range(2):
            if hop > 1:
                @pl.when(lands(way, hop - 1))
                def _(way=way):
                    on_line(way, hop - 1, k, lambda c: c.wait_recv())

            if hop < count:
                @pl.when(sends(way, hop))
                def _(way=way):
                    @pl.when(k >= DEEP)
                    def _():
                        on_line(way, hop, k - DEEP, lambda c: c.wait_send())

                    on_line(way, hop, k, lambda c: c.start())

    def own_copy(k):
        return pltpu.make_async_copy(total.at[k % DEEP], pieces.at[place, chunk_name(k)], own_sem.at[k % DEEP])

    def sum_copy(way, t, q):
        return pltpu.make_async_remote_copy(
            src_ref=sum_from.at[way, t - 1, q // sum_parts],
            dst_ref=sum_land.at[way, t - 1, q % sum_parts],
            send_sem=sum_send.at[way, t - 1, q // sum_parts],
            recv_sem=sum_recv.at[way, t - 1, q],
            device_id=(place + 1 - 2 * way, me),
            device_id_type=MESH,
        )

    def sum_sends(way, t):
        return place <= t - 1 if way == 0 else place >= count - t

    def sum_step(t, q):
        at = tile_at(q % sum_parts)
        for way in range(2):
            @pl.when(sum_sends(way, t))
            def _(way=way):
                to = count - t + place if way == 0 else t + place - count
                starts = place == 0 if way == 0 else place == count - 1

                @pl.when(q % sum_parts >= 1)
                def _():
                    sum_copy(way, t, q - 1).wait_send()

                @pl.when(starts)
                def _():
                    sum_from[way, t - 1, q // sum_parts] = terms[to, :, at]

                if t > 1:
                    @pl.when(jnp.logical_not(starts))
                    def _():
                        sum_copy(way, t - 1, q).wait_recv()
                        value = terms[to, :, at].astype(F32) + sum_land[way, t - 2, q % sum_parts].astype(F32)
                        sum_from[way, t - 1, q // sum_parts] = value.astype(BF)

                sum_copy(way, t, q).start()

    def sums_copy(q):
        return pltpu.make_async_copy(
            sums_stage.at[q // sum_parts],
            sums.at[q // sum_parts, :, tile_at(q % sum_parts)],
            sums_sem.at[q // sum_parts],
        )

    def sum_end(q):
        @pl.when(q % sum_parts >= 1)
        def _():
            sums_copy(q - 1).wait()

        sums_stage[q // sum_parts] = terms[place, :, tile_at(q % sum_parts)].astype(F32)
        for way in range(2):
            @pl.when(place >= 1 if way == 0 else place <= count - 2)
            def _(way=way):
                sum_copy(way, count - 1, q).wait_recv()
                sums_stage[q // sum_parts] += sum_land[way, count - 2, q % sum_parts].astype(F32)

        sums_copy(q).start()

    cot_load = pltpu.make_async_copy(cot, terms, cot_sem)

    def feed_load(b, size):
        at = pl.ds(pl.multiple_of(b * TILE, TILE), size)
        return pltpu.make_async_copy(
            down.at[at], w_tile.at[b % 2, :size, : cot_own.shape[1]], feed_sem.at[b % 2]
        )

    both_load = pltpu.make_async_copy(both, d_inner, load_sem.at[2])

    loads = [
        pltpu.make_async_copy(branch, terms, load_sem.at[0]),
        pltpu.make_async_copy(norm_hbm, norm_t, load_sem.at[1]),
    ]

    def back_loads(q):
        moves = (
            (w_inner.at[tile_at(q)], w_tile.at[q % 2]),
            (w_heads.at[tile_at(q)], h_tile.at[q % 2]),
            (hat.at[:, tile_at(q)], hat_tile.at[q % 2]),
        )
        return [pltpu.make_async_copy(a, b, back_sem.at[n, q % 2]) for n, (a, b) in enumerate(moves)]

    def head_loads(h):
        moves = ((q_in, q_tile), (k_in, k_tile), (v_in, v_tile), (att_in, att_tile), (lse_in, lse_tile))
        at = tile_at(h, HALF)
        copies = [
            pltpu.make_async_copy(a.at[:, at], b.at[h % 2], head_sem.at[n, h % 2]) for n, (a, b) in enumerate(moves)
        ]
        return copies

    def attn_load(h):
        return pltpu.make_async_copy(attn.at[tile_at(h // 2)], attn_tile, load_sem.at[3])

    pairs = q_in.shape[1] // HALF
    tiles = d_inner.shape[1] // TILE
    for c in [cot_load, both_load, feed_load(0, TILE), feed_load(1, TILE), attn_load(0)] + head_loads(0) + head_loads(1) + loads[1:]:
        c.start()
    peers = [(place, me + 1 - 2 * core)]
    peers += [(place, 2 * chip_away(chip, m) + core) for m in range(1, chips)]
    peers += [((place + 1) % count, me), ((place + count - 1) % count, me)]

    def meanwhile():
        cot_load.wait()
        for p in range(count):
            cot_own[p * rows : (p + 1) * rows, :] = terms[slots[p]]
        loads[0].start()
        loads[0].wait()

    greet(peers, meanwhile)
    ff = down.shape[0]
    whole_tiles = ff // TILE

    def feed_tile(b, size):
        feed_load(b, size).wait()
        d_hidden = contract(cot_own[...], w_tile[b % 2, :size, : cot_own.shape[1]], ((1,), (1,)))
        for n in range(size // HALF):
            d = d_hidden[:, n * HALF : (n + 1) * HALF]
            at = tile_at(2 * b + n)
            value = d_inner[:, at]
            gate = value[:, :HALF].astype(F32)
            up = value[:, HALF:].astype(F32)
            sig = jax.nn.sigmoid(gate)
            d_gate = d * up * sig * (1.0 + gate * (1.0 - sig))
            d_inner[:, at] = jnp.concatenate([d_gate, d * gate * sig], axis=1).astype(BF)

    def feed_step(b, carry):
        feed_tile(b, TILE)

        @pl.when(b + 2 < whole_tiles)
        def _():
            feed_load(b + 2, TILE).start()

        if ff % TILE:
            @pl.when(b + 2 == whole_tiles)
            def _():
                feed_load(whole_tiles, ff % TILE).start()

        return carry

    def store(i, shard, lo, value):
        partial[i % 2, shard // 2, shard % 2, lo : lo + value.shape[0], :] = value

    def from_norm(i, rhs):
        for s in range(0, shards, 2):
            part = norm_t.shape[0] // shards
            value = contract(norm_t[s * part : (s + 2) * part, :], rhs, ((1,), (0,))).astype(BF)
            store(i, s, 0, value[:part])
            store(i, s + 1, 0, value[part:])

    def step(i, carry):
        @pl.when((i < early) | (i == chunks - 1))
        def _():
            c = jnp.where(i < early, i, early)
            rhs = cot_own[:, tile_at(c)]
            for s in range(0, shards, 4):
                value = contract(hid_t[s * ff_part : (s + 4) * ff_part, :], rhs, ((1,), (0,))).astype(BF)
                for t in range(4):
                    store(i, s + t, 0, value[rows_of(t, ff_part)])
            value = contract(att_t[...], rhs, ((1,), (0,))).astype(BF)
            for s in range(shards):
                store(i, s, ff_part, value[rows_of(s, attn_part)])

        @pl.when(i == chunks - 1)
        def _():
            for s in range(shards):
                store(i, s, ff_part + attn_part, small[s])

        @pl.when(i == early)
        def _():
            loads[1].wait()

        @pl.when((i >= early) & (i < inner_end))
        def _():
            from_norm(i, d_inner[:, tile_at(i - early)])

        @pl.when((i >= inner_end) & (i < chunks - 1))
        def _():
            at = i - inner_end
            from_norm(i, d_mixed[:, tile_at(at)])

        @pl.when(i < chunks)
        def _():
            core_copy(i).start()

        @pl.when((i >= 1) & (i < chunks + 1))
        def _():
            j = i - 1
            core_copy(j).wait()
            for m in range(chips):
                a = partial[j % 2, m, core].astype(F32) + theirs[j % DEEP, m].astype(F32)
                pair[j % 2, m] = a.astype(BF)
            for m in range(1, chips):
                chip_copy(j, m).start()

        @pl.when((i >= 2) & (i < chunks + 2))
        def _():
            k = i - 2
            for m in range(1, chips):
                chip_copy(k, m).wait()

            a = pair[k % 2, chip].astype(F32)
            for m in range(1, chips):
                a = a + landed[k % DEEP, m - 1].astype(F32)
            for way in range(2):
                @pl.when(sends(way, 1) & (k >= DEEP))
                def _(way=way):
                    on_line(way, 1, k - DEEP, lambda c: c.wait_send())

            @pl.when(k >= DEEP)
            def _():
                own_copy(k - DEEP).wait()

            total[k % DEEP] = a.astype(BF)
            for way in range(2):
                @pl.when(sends(way, 1))
                def _(way=way):
                    on_line(way, 1, k, lambda c: c.start())

            own_copy(k).start()

        @pl.when((i >= 9) & (i < 9 + 2 * sum_parts) & (i % 2 == 1))
        def _():
            q = (i - 9) // 2
            for c in back_loads(q):
                c.wait()
            value = contract(d_inner[...], w_tile[q % 2], ((1,), (1,)))
            value = value + contract(d_mixed[...], h_tile[q % 2], ((1,), (1,)))
            term[...] = value.reshape(term.shape)
            gain = jnp.sum(value * hat_tile[q % 2].astype(F32), axis=0, keepdims=True)
            bias = jnp.sum(value, axis=0, keepdims=True)
            row = lax.broadcasted_iota(jnp.int32, small.shape[1:], 0)
            small[q] = jnp.where(row == 0, gain, jnp.where(row == 1, bias, 0.0)).astype(BF)
            for j in range(count):
                terms[j, :, tile_at(q)] = term[order[j]].astype(BF)

            @pl.when(q + 2 < sum_parts)
            def _():
                for c in back_loads(q + 2):
                    c.start()

        for t in range(1, count + 1):
            when = i - LAG * (t - 1)
            q = jnp.where(when % 2 == 0, when // 2, sum_parts + (when - 9) // 2)
            begins = jnp.where(when % 2 == 0, when, jnp.where(when >= 9, when - 9, -1))

            @pl.when((begins >= 0) & (begins < 2 * sum_parts))
            def _(q=q, t=t):
                if t < count:
                    sum_step(t, q)
                else:
                    sum_end(q)

        for hop in range(2, count + 1):
            k = i - 2 - LAG * (hop - 1)

            @pl.when((k >= 0) & (k < chunks))
            def _(k=k, hop=hop):
                forward_chunk(hop, k)

        @pl.when(i == 0)
        def _():
            both_load.wait()

        @pl.when((i == 0) | (i == 1) | (i == 4))
        def _():
            first_tile = jnp.where(i == 0, 0, jnp.where(i == 1, 1, 3))
            last_tile = jnp.where(i == 0, 1, jnp.where(i == 1, 3, whole_tiles))
            lax.fori_loop(first_tile, last_tile, feed_step, 0)

        if ff % TILE:
            @pl.when(i == 4)
            def _():
                feed_tile(whole_tiles, ff % TILE)

        @pl.when(i == 5)
        def _():
            for c in back_loads(0) + back_loads(1):
                c.start()

        @pl.when((i == 2) | (i == 3) | (i == 5) | (i == 6))
        def _():
            h = i - 2 - i // 5
            for c in head_loads(h):
                c.wait()
            slot = h % 2

            @pl.when(slot == 0)
            def _():
                attn_load(h).wait()
                value = contract(cot_own[...], attn_tile[...], ((1,), (1,)))
                for n in range(2):
                    d_att[n] = value[:, n * HALF : (n + 1) * HALF].astype(BF)

                @pl.when(h + 2 < pairs)
                def _():
                    attn_load(h + 2).start()

            heads_back_pair(
                q_tile.at[slot], k_tile.at[slot], v_tile.at[slot], d_att.at[slot], att_tile.at[slot],
                lse_tile.at[slot], cos, first, second, turned, dk, dv,
            )
            for n in range(3):
                d_mixed[:, tile_at(3 * h + n, HALF)] = turned[n]

            @pl.when(h + 2 < pairs)
            def _():
                for c in head_loads(h + 2):
                    c.start()

        return carry

    lax.fori_loop(0, chunks + 2 + LAG * (count - 1), step, 0)

    def drain(k, carry):
        own_copy(k).wait()
        for way in range(2):
            for hop in range(1, count):
                @pl.when(sends(way, hop))
                def _(way=way, hop=hop):
                    line_copy(way, hop, k, total.shape[1]).wait_send()
        return carry

    lax.fori_loop(chunks - DEEP, chunks, drain, 0)
    for kind in range(1, 3):
        sums_copy(kind * sum_parts - 1).wait()
    for way in range(2):
        for t in range(1, count):
            @pl.when(sum_sends(way, t))
            def _(way=way, t=t):
                for kind in range(1, 3):
                    sum_copy(way, t, kind * sum_parts - 1).wait_send()


def backward(
    order, slots, hid_t, att_t, tables, cot, norm_t, down, attn, both, branch, w_inner, w_heads, hat, heads, shards
):
    count, rows, width = cot.shape
    length = count * rows
    chips = shards // 2
    cols = heads[0].shape[1]
    inner = both.shape[1]
    chunks = (width + inner + 3 * cols) // TILE
    part = width // shards
    parts = width // TILE
    dma = pltpu.SemaphoreType.DMA
    smem = pl.BlockSpec(memory_space=pltpu.SMEM)
    return pl.pallas_call(
        backward_kernel,
        out_shape=[
            jax.ShapeDtypeStruct((count, chunks, part, TILE), BF),
            jax.ShapeDtypeStruct((2, rows, width), F32),
        ],
        in_specs=[smem] * 2 + [vmem_whole()] * 5 + [hbm_whole()] * 14,
        out_specs=[hbm_whole()] * 2,
        scratch_shapes=[
            pltpu.VMEM((length, width), BF),
            pltpu.VMEM((width, length), BF),
            pltpu.VMEM((length, inner), BF),
            pltpu.VMEM((length, 3 * cols), BF),
            pltpu.VMEM((count, rows, width), BF),
            pltpu.VMEM((count, rows, TILE), F32),
            pltpu.VMEM((parts, 16, TILE), BF),
            pltpu.VMEM((2, TILE, inner), BF),
            pltpu.VMEM((2, TILE, 3 * cols), BF),
            pltpu.VMEM((2, length, TILE), BF),
        ]
        + [pltpu.VMEM((TILE, width), BF)]
        + [pltpu.VMEM((2, length, HALF), BF)] * 3
        + [pltpu.VMEM((2, length, HALF), F32)] * 2
        + [pltpu.VMEM((2, length, HALF), BF)]
        + [pltpu.VMEM((3, length, HALF), BF)]
        + [pltpu.VMEM((length, HALF), F32)] * 2
        + [pltpu.VMEM((2, rows, TILE), F32)]
        + [
            pltpu.VMEM((2, chips, 2, part, TILE), BF),
            pltpu.VMEM((DEEP, chips, part, TILE), BF),
            pltpu.VMEM((2, chips, part, TILE), BF),
            pltpu.VMEM((DEEP, chips - 1, part, TILE), BF),
            pltpu.VMEM((DEEP, part, TILE), BF),
            pltpu.VMEM((2, count - 1, 2, rows, TILE), BF),
            pltpu.VMEM((2, count - 1, parts, rows, TILE), BF),
            dma((2,)),
            dma((DEEP,)),
            dma((2, chips - 1)),
            dma((DEEP, chips - 1)),
            dma((2, count - 1, DEEP)),
            dma((2, chunks, count - 1)),
            dma((DEEP,)),
            dma((2, count - 1, 2)),
            dma((2, count - 1, 2 * parts)),
            pltpu.SemaphoreType.DMA,
            dma((4,)),
            dma((2,)),
            dma((3, 2)),
            dma((5, 2)),
            dma((2,)),
        ],
        compiler_params=pltpu.CompilerParams(
            collective_id=1, has_side_effects=True, vmem_limit_bytes=62 * 2**20
        ),
        name="backward",
    )(order, slots, hid_t, att_t, *tables, cot, norm_t, down, attn, both, branch, w_inner, w_heads, hat, *heads)


def column_runs(columns, source):
    out = []
    for block in range(columns // HALF):
        first = 0
        while first < HALF:
            key, lane = source(block * HALF + first)
            last = first + 1
            while last < HALF and source(block * HALF + last) == (key, lane + last - first):
                last += 1
            out.append((block, first, last, key, (first - lane) % HALF))
            first = last
    return out


def assemble_kernel(rows_in, cols_in, sums, tokens, cot, gain, out, grad, qkv_out, gate_out, up_out, down_out, attn_out, gain_out, bias_out):
    count, chunks, rows, _ = rows_in.shape
    ff = gate_out.shape[1]
    width = qkv_out.shape[1]
    ff_part = down_out.shape[0] // count
    attn_part = attn_out.shape[0] // count
    shards = ff // (count * ff_part)
    inner_chunks = ff // count // HALF
    lane = lax.broadcasted_iota(jnp.int32, (rows, HALF), 1)
    own = tokens[...].astype(F32)
    out[...] = (own + sums[0]).astype(BF)
    own = own - jnp.mean(own, axis=1, keepdims=True)
    inv_std = lax.rsqrt(jnp.mean(own * own, axis=1, keepdims=True) + EPS)
    own = own * inv_std
    scaled = sums[1] * gain[0:1, :]
    scaled = scaled - jnp.mean(scaled, axis=1, keepdims=True) - own * jnp.mean(scaled * own, axis=1, keepdims=True)
    grad[...] = cot[...].astype(F32) + inv_std * scaled

    def gather(out, runs, load):
        for block, first, last, key, shift in runs:
            value = load(key).astype(F32)
            if shift:
                value = pltpu.roll(value, shift, 1)
            if first:
                value = jnp.where(lane >= first, value, held)
            held = value
            if last == HALF:
                out[:, block * HALF : (block + 1) * HALF] = value

    def inner_source(column):
        shard, rest = divmod(column, count * ff_part)
        unit = shard * ff_part + rest % ff_part
        return (rest // ff_part, unit // HALF), unit % HALF

    def head_source(column):
        part, rest = divmod(column, width // 3)
        head, dim = divmod(rest, HD)
        per = width // 3 // HD // shards // count
        shard, at = divmod(head, per * count)
        place, sub = divmod(at, per)
        pair, half = divmod(shard * per + sub, 2)
        return (place, 3 * pair + part), half * HD + dim

    runs = column_runs(ff, inner_source)
    gather(gate_out, runs, lambda key: rows_in[key[0], key[1], :, :HALF])
    gather(up_out, runs, lambda key: rows_in[key[0], key[1], :, HALF:])
    first_head = inner_chunks

    def head_load(key):
        at = key[1] % 2 * HALF
        return rows_in[key[0], first_head + key[1] // 2, :, at : at + HALF]

    gather(qkv_out, column_runs(width, head_source), head_load)
    for p in range(count):
        down_out[p * ff_part : (p + 1) * ff_part, :] = cols_in[p, 0, :ff_part, :].astype(F32)
        attn_out[p * attn_part : (p + 1) * attn_part, :] = cols_in[
            p, 0, ff_part : ff_part + attn_part, :
        ].astype(F32)
    small = [cols_in[p, 0, ff_part + attn_part :, :].astype(F32) for p in range(count)]
    small = functools.reduce(jnp.add, small)
    gain_out[...] = small[0:1]
    bias_out[...] = small[1:2]


def assemble_outputs(pieces, sums, tokens, cot, gain, qkv, attn, gate, down):
    count, chunks, rows, _ = pieces.shape
    steps = down[1] // TILE
    part = rows // steps
    width = tokens.shape[1]
    by_rows = lambda shape: pl.BlockSpec((part, shape[1]), lambda i: (i, 0))
    by_cols = lambda shape: pl.BlockSpec((shape[0], TILE), lambda i: (0, i))
    return pl.pallas_call(
        assemble_kernel,
        grid=(steps,),
        in_specs=[
            pl.BlockSpec((count, chunks - steps, part, TILE), lambda i: (0, 0, i, 0)),
            pl.BlockSpec((count, 1, rows, TILE), lambda i: (0, chunks - steps + i, 0, 0)),
            pl.BlockSpec((2, part, width), lambda i: (0, i, 0)),
            by_rows(tokens.shape),
            by_rows(tokens.shape),
            pl.BlockSpec(gain.shape, lambda i: (0, 0)),
        ],
        out_specs=[by_rows(tokens.shape)] * 2
        + [by_rows(qkv), by_rows(gate), by_rows(gate), by_cols(down), by_cols(attn)]
        + [pl.BlockSpec((1, TILE), lambda i: (0, 0))] * 2,
        out_shape=[jax.ShapeDtypeStruct(tokens.shape, BF), jax.ShapeDtypeStruct(tokens.shape, F32)]
        + [jax.ShapeDtypeStruct(s, F32) for s in (qkv, gate, gate, down, attn, (1, TILE), (1, TILE))],
        compiler_params=pltpu.CompilerParams(vmem_limit_bytes=60 * 2**20),
        name="assemble",
    )(pieces, pieces, sums, tokens, cot, gain)


def rotation_tables(length):
    half = ROT // 2
    inverse = 10000.0 ** (-jnp.arange(half, dtype=F32) / half)
    grid = jnp.arange(length, dtype=jnp.int32).astype(F32)[:, None] * inverse[None, :]
    cos, sin = jnp.cos(grid), jnp.sin(grid)
    zero = jnp.zeros((length, half), F32)
    rest = jnp.zeros((length, HD - ROT), F32)
    tables = (
        jnp.concatenate([cos, cos, rest + 1.0], axis=1),
        jnp.concatenate([-sin, zero, rest], axis=1),
        jnp.concatenate([zero, sin, rest], axis=1),
    )
    return tuple(jnp.tile(t, (1, 2)) for t in tables)


def body_general(tokens, block_order, ln_gain, ln_bias, w_qkv, w_out, w_gate, w_up, w_down, cotangent):
    rows, width = tokens.shape[1], tokens.shape[2]
    count = lax.axis_size("ctx")
    shards = lax.axis_size("fsdp")
    place = lax.axis_index("ctx")
    length = rows * count
    order = block_order[0]
    shard_rows = w_qkv.shape[0]
    ff_shard = w_down.shape[0]
    ff_part = ff_shard // count
    own_heads = H // count
    spread = (w_out.shape[0] // HD) % count == 0
    groups = shards if spread else 1
    head_cols = own_heads * HD // groups

    def my_cols(w, outer, group, part):
        w = w.reshape(w.shape[0], outer, group, count, part)
        return lax.dynamic_index_in_dim(w, place, 3, False).reshape(w.shape[0], outer * group * part)

    def all_cols(piece, outer, group, part):
        whole = gather_ctx(piece).reshape(count, piece.shape[0], outer, group, part)
        return whole.transpose(1, 2, 3, 0, 4).reshape(piece.shape[0], -1).astype(F32)

    def assemble(block, ready=None):
        whole = jnp.zeros((length, width), block.dtype)
        whole = lax.dynamic_update_slice_in_dim(whole, block, order[place] * rows, 0)
        last = None
        for k in range(1, count):
            last = ring_send(block, k)
            source = (place - k) % count
            whole = lax.dynamic_update_slice_in_dim(whole, last, order[source] * rows, 0)
        return whole, last

    gain = lax.all_gather(ln_gain, "fsdp", axis=0, tiled=True).astype(F32)
    bias = lax.all_gather(ln_bias, "fsdp", axis=0, tiled=True).astype(F32)
    tables = rotation_tables(length)

    block = tokens[0]
    x_all, arrived = assemble(block)
    grad_block = cotangent[0]
    cot_all, _ = assemble(after(grad_block, arrived))

    inner = jnp.concatenate(
        [my_cols(w_gate, 1, shards, ff_part), my_cols(w_up, 1, shards, ff_part)], axis=1
    )
    w_inner, sent = gather_rows(inner)
    w_heads, sent = gather_rows(after(my_cols(w_qkv, 3, groups, head_cols), sent))
    down = lax.dynamic_slice_in_dim(w_down, place * ff_part, ff_part, 0)
    w_hidden, sent = gather_rows(after(down, sent))
    if spread:
        part = w_out.shape[0] // count
        attn = lax.dynamic_slice_in_dim(w_out, place * part, part, 0)
        w_attn, sent = gather_rows(after(attn, sent))
    else:
        w_attn = lax.all_gather(after(w_out, sent), "fsdp", axis=0, tiled=True)
        w_attn = lax.dynamic_slice_in_dim(w_attn, place * own_heads * HD, own_heads * HD, 0)

    xf = x_all.astype(F32)
    average = jnp.mean(xf, axis=-1, keepdims=True)
    centered = xf - average
    variance = jnp.mean(centered * centered, axis=-1, keepdims=True)
    inv_std = lax.rsqrt(variance + EPS)
    x_hat = centered * inv_std
    normed = (x_hat * gain + bias).astype(BF)

    across = ((1,), (0,))
    over_tokens = ((0,), (0,))
    back = ((1,), (1,))
    ff_cols = shards * ff_part
    gate_value = dot(normed, w_inner[:, :ff_cols], across)
    up_value = dot(normed, w_inner[:, ff_cols:], across)
    sigmoid_gate = jax.nn.sigmoid(gate_value)
    hidden = (gate_value * sigmoid_gate * up_value).astype(BF)
    mixed = dot(normed, w_heads, across)
    q, k, v, attended, lse = attend(mixed, tables, own_heads)
    attended_low = attended.astype(BF)

    branch = dot(attended_low, w_attn, across) + dot(hidden, w_hidden, across)
    out = line_scatter(lambda j: lax.dynamic_slice_in_dim(branch, order[j] * rows, rows, 0))
    out = (block.astype(F32) + out).astype(BF)[None]

    d_hidden = dot(cot_all, w_hidden, back)
    grad_down = scatter_rows(dot(hidden, cot_all, over_tokens, BF))
    d_gate_act = (
        d_hidden * up_value * sigmoid_gate * (1.0 + gate_value * (1.0 - sigmoid_gate))
    ).astype(BF)
    d_up_act = (d_hidden * gate_value * sigmoid_gate).astype(BF)
    d_inner = jnp.concatenate([d_gate_act, d_up_act], axis=1)
    d_attended = dot(cot_all, w_attn, back, BF)
    d_mixed = attend_back(q, k, v, d_attended, attended, lse, tables, own_heads)
    d_mixed = jnp.concatenate(d_mixed, axis=1)
    grad_inner = scatter_rows(dot(normed, d_inner, over_tokens, BF))
    grad_attn = dot(attended_low, cot_all, over_tokens, BF)
    grad_heads = scatter_rows(dot(normed, d_mixed, over_tokens, BF))

    d_normed = dot(d_inner, w_inner, back) + dot(d_mixed, w_heads, back)
    small = jnp.stack([jnp.sum(d_normed * x_hat, axis=0), jnp.sum(d_normed, axis=0)])
    small = lax.psum(small, ("ctx", "fsdp"))
    small = lax.dynamic_slice_in_dim(small, lax.axis_index("fsdp") * shard_rows, shard_rows, 1)
    d_own = line_scatter(lambda j: lax.dynamic_slice_in_dim(d_normed, order[j] * rows, rows, 0))
    own = block.astype(F32)
    own_average = jnp.mean(own, axis=-1, keepdims=True)
    own = own - own_average
    own_std = lax.rsqrt(jnp.mean(own * own, axis=-1, keepdims=True) + EPS)
    own = own * own_std
    scaled = d_own * gain
    d_input = own_std * (
        scaled
        - jnp.mean(scaled, axis=-1, keepdims=True)
        - own * jnp.mean(scaled * own, axis=-1, keepdims=True)
    )
    grad_in = (grad_block.astype(F32) + d_input)[None]

    down_all = gather_ctx(grad_down).reshape(ff_shard, width).astype(F32)
    if spread:
        attn_all = gather_ctx(scatter_rows(grad_attn)).reshape(w_out.shape).astype(F32)
    else:
        full = jnp.zeros((H * HD, width), BF)
        full = lax.dynamic_update_slice_in_dim(full, grad_attn, place * own_heads * HD, 0)
        full = lax.psum_scatter(full, "fsdp", scatter_dimension=0, tiled=True)
        attn_all = lax.psum(full, "ctx").astype(F32)
    heads_all = all_cols(grad_heads, 3, groups, head_cols)
    inner_all = gather_ctx(grad_inner).reshape(count, shard_rows, 2, shards, ff_part)
    inner_all = inner_all.transpose(2, 1, 3, 0, 4).reshape(2, shard_rows, -1).astype(F32)
    return (
        out,
        grad_in,
        small[0],
        small[1],
        heads_all,
        attn_all,
        inner_all[0],
        inner_all[1],
        down_all,
    )


def body_fast(tokens, block_order, ln_gain, ln_bias, w_qkv, w_out, w_gate, w_up, w_down, cotangent):
    count, shards = lax.axis_size("ctx"), lax.axis_size("fsdp")
    place = lax.axis_index("ctx")
    block, grad_block = tokens[0], cotangent[0]
    rows, width = block.shape
    order = block_order[0]
    spots = jnp.arange(count, dtype=jnp.int32)
    slots = jnp.sum(jnp.where(order[None, :] == spots[:, None], spots[None, :], 0), axis=1)
    vectors = jnp.stack([ln_gain, ln_bias] + [jnp.zeros_like(ln_gain)] * 6).astype(F32)
    tables = fixed_tables(rows * count)
    (
        cot_all, scales, w_inner, w_heads, w_attn, w_hidden, normed_t, hat, both, hidden_t,
        q, k, v, attended, low_t, lse, branch,
    ) = forward(
        order, slots, tables, block, grad_block, vectors, w_gate, w_up, w_qkv, w_out, w_down, count, shards
    )
    w_inner = w_inner.reshape(width, -1)
    w_hidden, w_attn = w_hidden.reshape(-1, width), w_attn.reshape(-1, width)
    w_heads = w_heads.reshape(width, -1)
    pieces, sums = backward(
        order, slots, hidden_t, low_t, tables, cot_all, normed_t, w_hidden, w_attn, both, branch, w_inner,
        w_heads, hat, (q, k, v, attended, lse), shards,
    )
    out, grad_in, d_qkv, d_gate, d_up, d_down, d_attn, d_gain, d_bias = assemble_outputs(
        pieces, sums, block, grad_block, scales, w_qkv.shape, w_out.shape, w_gate.shape, w_down.shape
    )
    out, grad_in = out[None], grad_in[None]
    return out, grad_in, d_gain.reshape(-1), d_bias.reshape(-1), d_qkv, d_attn, d_gate, d_up, d_down


def solution(mesh):
    whole, once = P("fsdp", "ctx", None), P("fsdp", None)
    count, shards = mesh.shape["ctx"], mesh.shape["fsdp"]

    def body(*args):
        w_out, w_down = args[5], args[8]
        fits = shards == 8 and w_out.shape[0] == count * HD and w_out.shape[0] == TILE
        fits = fits and w_down.shape[0] % (16 * count) == 0 and w_down.shape[0] // count <= 176
        return (body_fast if fits else body_general)(*args)

    return jax.shard_map(
        body,
        mesh=mesh,
        in_specs=(whole, once, P("fsdp"), P("fsdp")) + (once,) * 5 + (whole,),
        out_specs=(whole, whole, P("fsdp"), P("fsdp")) + (once,) * 5,
        check_vma=False,
    )
```

```python
import functools

import jax
import jax.numpy as jnp
import numpy as np
from jax import lax
from jax.experimental import pallas as pl
from jax.experimental.pallas import tpu as pltpu
from jax.sharding import PartitionSpec as P

H = 32
HD = 64
ROT = 16
EPS = 1e-05
NEG = -1e30
CHUNK = 256

BF = jnp.bfloat16
F32 = jnp.float32


def xor_send(value, mask):
    count = lax.axis_size("fsdp")
    return lax.ppermute(value, "fsdp", [(i, i ^ mask) for i in range(count)])


def ring_send(value, steps):
    count = lax.axis_size("ctx")
    return lax.ppermute(value, "ctx", [(i, (i + steps) % count) for i in range(count)])


def after(value, *done):
    return lax.optimization_barrier((value,) + done)[0]


def dot(a, b, dims, out=F32):
    return lax.dot_general(a, b, (dims, ((), ())), preferred_element_type=F32).astype(out)


def gather_rows(piece):
    count = lax.axis_size("fsdp")
    chips = count // 2
    me = lax.axis_index("fsdp")
    chip, core = me // 2, me % 2
    parts = [piece] + [xor_send(piece, 2 * m) for m in range(1, chips)]
    others = [xor_send(p, 1) for p in parts]
    whole = jnp.zeros((count,) + piece.shape, piece.dtype)
    for m in range(chips):
        at = 2 * (chip ^ m)
        whole = lax.dynamic_update_index_in_dim(whole, parts[m], at + core, 0)
        whole = lax.dynamic_update_index_in_dim(whole, others[m], at + 1 - core, 0)
    return whole.reshape(count * piece.shape[0], piece.shape[1]), parts[-1]


def scatter_rows(grad):
    count = lax.axis_size("fsdp")
    chips = count // 2
    me = lax.axis_index("fsdp")
    chip, core = me // 2, me % 2
    rows = grad.shape[0] // count
    split = grad.reshape(chips, 2, rows, grad.shape[1])
    theirs = xor_send(lax.dynamic_index_in_dim(split, 1 - core, 1, False), 1)
    pair = lax.dynamic_index_in_dim(split, core, 1, False).astype(F32) + theirs.astype(F32)
    pair = pair.astype(BF)
    total = lax.dynamic_index_in_dim(pair, chip, 0, False).astype(F32)
    for m in range(1, chips):
        part = lax.dynamic_index_in_dim(pair, chip ^ m, 0, False)
        total = total + xor_send(part, 2 * m).astype(F32)
    return total.astype(BF)


def gather_ctx(piece):
    count = lax.axis_size("ctx")
    me = lax.axis_index("ctx")
    whole = jnp.zeros((count,) + piece.shape, piece.dtype)
    whole = lax.dynamic_update_index_in_dim(whole, piece, me, 0)
    for k in range(1, count):
        part = ring_send(piece, k)
        whole = lax.dynamic_update_index_in_dim(whole, part, (me - k) % count, 0)
    return whole


def line_scatter(blocks):
    count = lax.axis_size("ctx")
    me = lax.axis_index("ctx")
    down = up = None
    for t in range(1, count):
        to_down = blocks(jnp.clip(t + me - count, 0, count - 1))
        to_up = blocks(jnp.clip(count - 1 - (t + (count - 1 - me) - count), 0, count - 1))
        if down is not None:
            to_down = to_down + down.astype(F32)
            to_up = to_up + up.astype(F32)
        pairs = [(i, i - 1) for i in range(count - t, count)]
        down = lax.ppermute(to_down.astype(BF), "ctx", pairs)
        up = lax.ppermute(to_up.astype(BF), "ctx", [(count - 1 - i, count - 1 - j) for i, j in pairs])
    return blocks(me) + down.astype(F32) + up.astype(F32)


def turn(x, cos, first, second):
    width = x.shape[1]
    half = ROT // 2
    return x * cos + pltpu.roll(x, width - half, 1) * first + pltpu.roll(x, half, 1) * second


def contract(a, b, dims):
    return lax.dot_general(a, b, (dims, ((), ())), preferred_element_type=F32)


def attend_kernel(mq, mk, mv, cos, first, second, q_out, k_out, v_out, att_out, lse_out):
    length = mq.shape[0]
    scale = HD ** (-0.5)
    q_out[...] = (turn(mq[...], cos[...], first[...], second[...]).astype(BF).astype(F32) * scale).astype(BF)
    k_out[...] = turn(mk[...], cos[...], first[...], second[...]).astype(BF)
    v_out[...] = mv[...].astype(BF)
    row = lax.broadcasted_iota(jnp.int32, (CHUNK, CHUNK), 0)
    col = lax.broadcasted_iota(jnp.int32, (CHUNK, CHUNK), 1)
    for c in range(length // CHUNK):
        lo, hi = c * CHUNK, (c + 1) * CHUNK
        for h in range(2):
            lanes = slice(h * HD, (h + 1) * HD)
            q = q_out[lo:hi, lanes]
            s = contract(q, k_out[lo:hi, lanes], ((1,), (1,)))
            s = jnp.where(col <= row, s, NEG)
            if c:
                s = jnp.concatenate([contract(q, k_out[:lo, lanes], ((1,), (1,))), s], axis=1)
            top = jnp.max(s, axis=1, keepdims=True)
            p = jnp.exp(s - top)
            total = jnp.sum(p, axis=1, keepdims=True)
            o = contract(p.astype(BF), v_out[:hi, lanes], ((1,), (0,)))
            att_out[lo:hi, lanes] = o / total
            lse_out[lo:hi, lanes] = jnp.broadcast_to(top + jnp.log(total), (CHUNK, HD))


def attend(mixed, tables, heads):
    length = mixed.shape[0]
    pairs = heads // 2
    block = lambda at: pl.BlockSpec((length, 2 * HD), lambda h, at=at: (0, at + h))
    table = pl.BlockSpec((length, 2 * HD), lambda h: (0, 0))
    width = heads * HD
    return pl.pallas_call(
        attend_kernel,
        grid=(pairs,),
        in_specs=[block(0), block(pairs), block(2 * pairs), table, table, table],
        out_specs=[block(0)] * 5,
        out_shape=[jax.ShapeDtypeStruct((length, width), BF)] * 3
        + [jax.ShapeDtypeStruct((length, width), F32)] * 2,
        compiler_params=pltpu.CompilerParams(vmem_limit_bytes=40 * 2**20),
        cost_estimate=pl.CostEstimate(
            flops=16 * heads * length * length * HD // 2,
            bytes_accessed=26 * length * width,
            transcendentals=heads * length * length // 2,
        ),
        name="attend",
    )(mixed, mixed, mixed, *tables)


def attend_back_kernel(q_in, k_in, v_in, do_in, att, lse, cos, first, second, dq_out, dk_out, dv_out, dk, dv):
    length = q_in.shape[0]
    scale = HD ** (-0.5)
    row = lax.broadcasted_iota(jnp.int32, (CHUNK, CHUNK), 0)
    col = lax.broadcasted_iota(jnp.int32, (CHUNK, CHUNK), 1)
    dk[...] = jnp.zeros_like(dk)
    dv[...] = jnp.zeros_like(dv)
    for c in range(length // CHUNK):
        lo, hi = c * CHUNK, (c + 1) * CHUNK
        dqs = []
        for h in range(2):
            lanes = slice(h * HD, (h + 1) * HD)
            q, do = q_in[lo:hi, lanes], do_in[lo:hi, lanes]
            delta = jnp.sum(do.astype(F32) * att[lo:hi, lanes], axis=1, keepdims=True)
            s = contract(q, k_in[lo:hi, lanes], ((1,), (1,)))
            s = jnp.where(col <= row, s, NEG)
            if c:
                s = jnp.concatenate([contract(q, k_in[:lo, lanes], ((1,), (1,))), s], axis=1)
            p = jnp.exp(s - lse[lo:hi, h * HD : h * HD + 1])
            dp = contract(do, v_in[:hi, lanes], ((1,), (1,)))
            ds = (p * (dp - delta)).astype(BF)
            dqs.append(contract(ds, k_in[:hi, lanes], ((1,), (0,))) * scale)
            dk[:hi, lanes] += contract(ds, q, ((0,), (0,)))
            dv[:hi, lanes] += contract(p.astype(BF), do, ((0,), (0,)))
        dq = jnp.concatenate(dqs, axis=1)
        dq_out[lo:hi, :] = turn(dq, cos[lo:hi, :], -first[lo:hi, :], -second[lo:hi, :]).astype(BF)
    dk_out[...] = turn(dk[...], cos[...], -first[...], -second[...]).astype(BF)
    dv_out[...] = dv[...].astype(BF)


def attend_back(q, k, v, d_attended, attended, lse, tables, heads):
    length, width = q.shape
    block = pl.BlockSpec((length, 2 * HD), lambda h: (0, h))
    table = pl.BlockSpec((length, 2 * HD), lambda h: (0, 0))
    return pl.pallas_call(
        attend_back_kernel,
        grid=(heads // 2,),
        in_specs=[block] * 6 + [table] * 3,
        out_specs=[block] * 3,
        out_shape=[jax.ShapeDtypeStruct((length, width), BF)] * 3,
        scratch_shapes=[pltpu.VMEM((length, 2 * HD), F32)] * 2,
        compiler_params=pltpu.CompilerParams(vmem_limit_bytes=40 * 2**20),
        cost_estimate=pl.CostEstimate(
            flops=40 * heads * length * length * HD // 2,
            bytes_accessed=22 * length * width,
            transcendentals=heads * length * length // 2,
        ),
        name="attend_back",
    )(q, k, v, d_attended, attended, lse, *tables)


MESH = pl.DeviceIdType.MESH
TILE = 256
HALF = 128
DEEP = 4
LAG = 1


def tile_at(i, size=TILE):
    return pl.ds(pl.multiple_of(i * size, size), size)


def vmem_whole():
    return pl.BlockSpec(memory_space=pltpu.VMEM)


def hbm_whole():
    return pl.BlockSpec(memory_space=pl.ANY)


def chip_away(chip, m):
    return 2 * ((chip // 2 + m // 2) % 2) + (chip + m) % 2


def inner_runs(shards, count, part):
    runs = []
    for block in range(shards * part // HALF):
        first = 0
        while first < HALF:
            shard, unit = divmod(block * HALF + first, part)
            last = min(HALF, first + part - unit)
            runs.append((block, first, last, shard * count * part + unit - first))
            first = last
    return runs


class Line:
    def __init__(self, own, whole, send, recv):
        self.own, self.whole, self.send, self.recv = own, whole, send, recv
        self.count = whole.shape[0]
        self.place, self.me = lax.axis_index("ctx"), lax.axis_index("fsdp")

    def copy(self, way, hop):
        ahead = 1 - 2 * way
        origin = self.place - (hop - 1) * ahead
        return pltpu.make_async_remote_copy(
            src_ref=self.own if hop == 1 else self.whole.at[origin],
            dst_ref=self.whole.at[origin],
            send_sem=self.send.at[way, hop - 1],
            recv_sem=self.recv.at[way, hop - 1],
            device_id=(self.place + ahead, self.me),
            device_id_type=MESH,
        )

    def sends(self, way, hop):
        if way == 0:
            return (self.place >= hop - 1) & (self.place <= self.count - 2)
        return (self.place <= self.count - hop) & (self.place >= 1)

    def lands(self, way, hop):
        return self.place >= hop if way == 0 else self.place <= self.count - 1 - hop

    def pass_on(self, hop):
        for way in range(2):
            @pl.when(self.sends(way, hop))
            def _(way=way):
                if hop > 1:
                    self.copy(way, hop - 1).wait_recv()
                self.copy(way, hop).start()

    def land(self):
        for way in range(2):
            @pl.when(self.place == (self.count - 1 if way == 0 else 0))
            def _(way=way):
                for hop in range(1, self.count):
                    self.copy(way, hop).wait_recv()

    def finish(self):
        for way in range(2):
            for hop in range(1, self.count):
                @pl.when(self.sends(way, hop))
                def _(way=way, hop=hop):
                    self.copy(way, hop).wait_send()


class Plane:
    def __init__(self, mine, wholes, send, recv):
        self.mine, self.wholes, self.send, self.recv = mine, wholes, send, recv
        self.place, self.me = lax.axis_index("ctx"), lax.axis_index("fsdp")
        chip, core = self.me // 2, self.me % 2
        self.sibling = 2 * chip + 1 - core
        self.near = (2 * chip_away(chip, 1) + core, 2 * chip_away(chip, 2) + core)
        self.far = 2 * chip_away(chip, 3) + core

    def copy(self, which, kind, source, target, to):
        return pltpu.make_async_remote_copy(
            src_ref=source,
            dst_ref=target,
            send_sem=self.send.at[which, kind],
            recv_sem=self.recv.at[which, kind],
            device_id=(self.place, to),
            device_id_type=MESH,
        )

    def direct(self, which, a):
        return self.copy(which, a, self.mine[which], self.wholes[which].at[self.me], self.near[a])

    def across(self, which, a):
        half = self.wholes[which].shape[2] // 2
        piece = self.wholes[which].at[self.near[1 - a], :, a * half : (a + 1) * half]
        return self.copy(which, 2 + a, piece, piece, self.near[a])

    def beside(self, which, kind):
        source = (self.me, self.near[0], self.near[1], self.far)[kind]
        piece = self.wholes[which].at[source]
        return self.copy(which, 4 + kind, self.mine[which] if kind == 0 else piece, piece, self.sibling)

    def begin(self, which):
        for a in range(2):
            self.direct(which, a).start()
        self.beside(which, 0).start()

    def relay(self, which):
        for a in range(2):
            self.direct(which, a).wait_recv()
        for a in range(2):
            self.across(which, a).start()
            self.beside(which, 1 + a).start()

    def last(self, which):
        for a in range(2):
            self.across(which, a).wait_recv()
        self.beside(which, 3).start()

    def finish(self, which):
        for kind in range(4):
            self.beside(which, kind).wait()
        for a in range(2):
            self.direct(which, a).wait_send()
            self.across(which, a).wait_send()


class Own:
    def __init__(self, source, stage, target, sem, n):
        self.load = pltpu.make_async_copy(source, stage, sem.at[n, 0])
        self.store = pltpu.make_async_copy(stage, target, sem.at[n, 1])

    def turn(self):
        self.load.wait()
        self.store.start()


def greet(peers, meanwhile):
    barrier = pltpu.get_barrier_semaphore()
    for peer in peers:
        pl.semaphore_signal(barrier, inc=1, device_id=peer, device_id_type=MESH)
    meanwhile()
    pl.semaphore_wait(barrier, len(peers))


def forward_kernel(
    order, slots, cos, first, second, tokens, cot, vectors, w_gate, w_up, w_qkv, w_out, w_down,
    cot_all, rows_out, inner_out, heads_out, attn_out, down, normed_t, hat, both, hidden_t,
    q_out, k_out, v_out, att_out, low_t, lse_out, branch,
    raw, x_all, vectors_all, scales, inner, heads, attn,
    normed, hidden, low, hat_stage, turned_stage, both_stage, hidden_stage,
    q_buf, k_buf, v_buf, att_buf, low_stage, lse_buf, down_tile, term, branch_stage,
    load_sem, x_send, x_recv, line_send, line_recv, part_send, part_recv, vector_send, vector_recv,
    own_sem, out_sem, norm_sem, feed_sem, head_sem, tile_sem, branch_sem,
):
    count, rows = x_all.shape[0], x_all.shape[1]
    shards = inner.shape[0]
    place, me = lax.axis_index("ctx"), lax.axis_index("fsdp")
    width = w_gate.shape[1]
    my_attn = w_out.at[pl.ds(pl.multiple_of(place * attn.shape[1], 16), attn.shape[1])]
    my_down = w_down.at[pl.ds(pl.multiple_of(place * down.shape[1], 16), down.shape[1])]
    loads = [
        pltpu.make_async_copy(my_attn, attn.at[me], load_sem.at[0]),
        pltpu.make_async_copy(w_gate, raw.at[0, :, :width], load_sem.at[1]),
        pltpu.make_async_copy(w_up, raw.at[1, :, :width], load_sem.at[2]),
        pltpu.make_async_copy(tokens, x_all.at[place], load_sem.at[3]),
        pltpu.make_async_copy(vectors, vectors_all.at[me], load_sem.at[4]),
    ]
    owns = [
        Own(cot, hat_stage.at[0], cot_all.at[place], own_sem, 0),
        Own(my_down, hat_stage.at[1, : down.shape[1]], down.at[me], own_sem, 1),
    ]
    qkv_load = pltpu.make_async_copy(w_qkv, raw.at[0], load_sem.at[5])
    peers = [(place, (me + s) % shards) for s in range(1, shards)]
    peers += [((place + 1) % count, me), ((place + count - 1) % count, me)]

    def meanwhile():
        for c in loads + [own.load for own in owns]:
            c.start()

    greet(peers, meanwhile)
    x_line = Line(tokens, x_all, x_send, x_recv)
    line = Line(cot, cot_all, line_send, line_recv)
    plane = Plane(
        (inner.at[me], attn.at[me], heads.at[me], my_down), (inner, attn, heads, down), part_send, part_recv
    )
    x_line.pass_on(1)
    vector_copies = [
        pltpu.make_async_remote_copy(
            src_ref=vectors,
            dst_ref=vectors_all.at[me],
            send_sem=vector_send.at[s - 1],
            recv_sem=vector_recv.at[s - 1],
            device_id=(place, (me + s) % shards),
            device_id_type=MESH,
        )
        for s in range(1, shards)
    ]
    for c in vector_copies:
        c.start()
    loads[0].wait()
    plane.begin(1)

    row = lax.broadcasted_iota(jnp.int32, (TILE, HALF), 0)
    col = lax.broadcasted_iota(jnp.int32, (TILE, HALF), 1)

    def picked(sources, size, first, last, start):
        base = jnp.minimum((start + first) // HALF, size // HALF - TILE // HALF) * HALF
        choose = (row + base == col + start) & (col >= first) & (col < last)
        choose = choose.astype(F32).astype(BF)
        at = pl.ds(pl.multiple_of(base, HALF), TILE)
        return [contract(raw[source, :, at], choose, ((1,), (0,))) for source in sources]

    part = width // shards // count
    loads[1].wait()
    loads[2].wait()
    held = None
    for block, first_col, last_col, start in inner_runs(shards, count, part):
        values = picked((0, 1), width, first_col, last_col, start + place * part)
        held = values if first_col == 0 else [a + b for a, b in zip(held, values)]
        if last_col == HALF:
            for k in range(2):
                at = block * TILE + k * HALF
                inner[me, :, at : at + HALF] = held[k].astype(BF)
    plane.begin(0)
    qkv_load.start()
    qkv_load.wait()
    third = raw.shape[2] // 3
    for pair in range(shards // 2):
        for kind in range(3):
            value = 0.0
            for h in range(2):
                head = count * (2 * pair + h) + place
                start = kind * third + head * HD - h * HD
                value = value + picked((0,), raw.shape[2], h * HD, (h + 1) * HD, start)[0]
            at = (pair * 3 + kind) * HALF
            heads[me, :, at : at + HALF] = value.astype(BF)
    plane.begin(2)
    for own in owns:
        own.turn()
    plane.relay(1)
    x_line.pass_on(2)
    plane.relay(0)
    plane.last(1)
    x_line.pass_on(3)
    line.pass_on(1)
    plane.relay(2)
    plane.last(0)
    plane.finish(1)
    for c in loads[3:] + vector_copies:
        c.wait()
    scales[...] = jnp.concatenate([vectors_all[s] for s in range(shards)], axis=1)
    x_line.land()
    plane.begin(3)
    outs = [
        pltpu.make_async_copy(attn, attn_out, out_sem.at[0]),
        pltpu.make_async_copy(scales, rows_out, out_sem.at[1]),
        pltpu.make_async_copy(inner, inner_out, out_sem.at[2]),
        pltpu.make_async_copy(heads, heads_out, out_sem.at[3]),
    ]
    outs[0].start()
    outs[1].start()

    def norm_copies(p):
        at = pl.ds(pl.multiple_of(p * rows, rows), rows)
        return (
            pltpu.make_async_copy(hat_stage.at[p % 2], hat.at[at], norm_sem.at[0, p % 2]),
            pltpu.make_async_copy(turned_stage.at[p % 2], normed_t.at[:, at], norm_sem.at[1, p % 2]),
        )

    def norm_step(p, carry):
        @pl.when(p >= 2)
        def _():
            for c in norm_copies(p - 2):
                c.wait()

        xf = x_all[slots[p]].astype(F32)
        mean = jnp.mean(xf, axis=1, keepdims=True)
        centered = xf - mean
        variance = jnp.mean(centered * centered, axis=1, keepdims=True)
        x_hat = centered * lax.rsqrt(variance + EPS)
        hat_stage[p % 2] = x_hat.astype(BF)
        value = x_hat * scales[0:1, :] + scales[1:2, :]
        normed[pl.ds(pl.multiple_of(p * rows, rows), rows), :] = value.astype(BF)
        turned_stage[p % 2] = value.T.astype(BF)
        for c in norm_copies(p):
            c.start()
        return carry

    for own in owns:
        own.store.wait()
    line.pass_on(2)
    lax.fori_loop(0, count, norm_step, 0)
    plane.finish(0)
    outs[2].start()
    model = normed.shape[1]

    def feed_copies(i):
        wide = pl.ds(pl.multiple_of(i * TILE, TILE), TILE)
        slim = pl.ds(pl.multiple_of(i * HALF, HALF), HALF)
        return (
            pltpu.make_async_copy(both_stage.at[i % 2], both.at[:, wide], feed_sem.at[0, i % 2]),
            pltpu.make_async_copy(hidden_stage.at[i % 2], hidden_t.at[slim], feed_sem.at[1, i % 2]),
        )

    def feed_step(i, carry):
        @pl.when(i >= 2)
        def _():
            for c in feed_copies(i - 2):
                c.wait()

        value = contract(normed[...], inner[:, :, tile_at(i)].reshape(model, TILE), ((1,), (0,)))
        both_stage[i % 2] = value.astype(BF)
        gate, up = value[:, :HALF], value[:, HALF:]
        value = gate * jax.nn.sigmoid(gate) * up
        hidden[:, pl.ds(pl.multiple_of(i * HALF, HALF), HALF)] = value.astype(BF)
        hidden_stage[i % 2] = value.T.astype(BF)
        for c in feed_copies(i):
            c.start()
        return carry

    tiles = inner.shape[2] // TILE
    lax.fori_loop(0, tiles, feed_step, 0)
    line.pass_on(3)
    plane.relay(3)
    plane.last(2)
    plane.finish(2)
    outs[3].start()
    row = lax.broadcasted_iota(jnp.int32, (CHUNK, CHUNK), 0)
    col = lax.broadcasted_iota(jnp.int32, (CHUNK, CHUNK), 1)
    pairs = heads.shape[2] // (3 * HALF)

    def head_copies(h):
        at = pl.ds(pl.multiple_of(h * HALF, HALF), HALF)
        moves = ((q_buf, q_out), (k_buf, k_out), (v_buf, v_out), (att_buf, att_out), (lse_buf, lse_out))
        copies = [
            pltpu.make_async_copy(a.at[h % 2], b.at[:, at], head_sem.at[n, h % 2]) for n, (a, b) in enumerate(moves)
        ]
        return copies + [pltpu.make_async_copy(low_stage.at[h % 2], low_t.at[at], head_sem.at[5, h % 2])]

    def head_step(h, carry):
        @pl.when(h >= 2)
        def _():
            for c in head_copies(h - 2):
                c.wait()

        slot = h % 2
        w = heads[:, :, tile_at(h, 3 * HALF)].reshape(model, 3 * HALF)
        mixed = contract(normed[...], w, ((1,), (0,)))
        q = turn(mixed[:, :HALF], cos[...], first[...], second[...]).astype(BF).astype(F32)
        q_buf[slot] = (q * HD ** (-0.5)).astype(BF)
        k_buf[slot] = turn(mixed[:, HALF : 2 * HALF], cos[...], first[...], second[...]).astype(BF)
        v_buf[slot] = mixed[:, 2 * HALF :].astype(BF)
        for c in range(normed.shape[0] // CHUNK):
            lo, hi = c * CHUNK, (c + 1) * CHUNK
            for side in range(2):
                lanes = slice(side * HD, (side + 1) * HD)
                q = q_buf[slot, lo:hi, lanes]
                s = contract(q, k_buf[slot, lo:hi, lanes], ((1,), (1,)))
                s = jnp.where(col <= row, s, NEG)
                if c:
                    s = jnp.concatenate([contract(q, k_buf[slot, :lo, lanes], ((1,), (1,))), s], axis=1)
                top = jnp.max(s, axis=1, keepdims=True)
                p = jnp.exp(s - top)
                total = jnp.sum(p, axis=1, keepdims=True)
                o = contract(p.astype(BF), v_buf[slot, :hi, lanes], ((1,), (0,)))
                att_buf[slot, lo:hi, lanes] = o / total
                lse_buf[slot, lo:hi, lanes] = jnp.broadcast_to(top + jnp.log(total), (CHUNK, HD))
        att = att_buf[slot]
        low[:, pl.ds(pl.multiple_of(h * HALF, HALF), HALF)] = att.astype(BF)
        low_stage[slot] = att.T.astype(BF)
        for c in head_copies(h):
            c.start()
        return carry

    lax.fori_loop(0, pairs - 1, head_step, 0)
    plane.last(3)
    lax.fori_loop(pairs - 1, pairs, head_step, 0)
    plane.finish(3)
    def tile_copies(i):
        at = pl.ds(pl.multiple_of(i * TILE, TILE), TILE)
        return [pltpu.make_async_copy(down.at[:, :, at], down_tile.at[i % 2], tile_sem.at[i % 2])]

    def branch_copy(i):
        at = pl.ds(pl.multiple_of(i * TILE, TILE), TILE)
        return pltpu.make_async_copy(branch_stage.at[i % 2], branch.at[:, :, at], branch_sem.at[i % 2])

    steps = branch.shape[2] // TILE
    for c in tile_copies(0):
        c.start()

    def branch_step(i, carry):
        @pl.when(i + 1 < steps)
        def _():
            for c in tile_copies(i + 1):
                c.start()

        for c in tile_copies(i):
            c.wait()

        @pl.when(i >= 2)
        def _():
            branch_copy(i - 2).wait()

        value = contract(hidden[...], down_tile[i % 2].reshape(hidden.shape[1], TILE), ((1,), (0,)))
        value = value + contract(low[...], attn[:, :, tile_at(i)].reshape(low.shape[1], TILE), ((1,), (0,)))
        term[...] = value.reshape(term.shape)
        for j in range(count):
            branch_stage[i % 2, j] = term[order[j]].astype(BF)
        branch_copy(i).start()
        return carry

    lax.fori_loop(0, steps, branch_step, 0)
    line.land()
    line.finish()
    x_line.finish()
    for c in outs:
        c.wait()
    for back in range(2):
        for c in norm_copies(count - 1 - back) + feed_copies(tiles - 1 - back):
            c.wait()
        for c in head_copies(pairs - 1 - back):
            c.wait()
        branch_copy(steps - 1 - back).wait()


def forward(order, slots, tables, tokens, cot, vectors, w_gate, w_up, w_qkv, w_out, w_down, count, shards):
    rows, width = tokens.shape
    length = count * rows
    shard_rows = w_gate.shape[0]
    ff_part, attn_part = w_down.shape[0] // count, w_out.shape[0] // count
    ff, cols = shards * ff_part, shards * attn_part
    dma = pltpu.SemaphoreType.DMA
    smem = pl.BlockSpec(memory_space=pltpu.SMEM)
    bf = lambda *shape: jax.ShapeDtypeStruct(shape, BF)
    f32 = lambda *shape: jax.ShapeDtypeStruct(shape, F32)
    out_shape = [
        bf(count, rows, width),
        f32(vectors.shape[0], width),
        bf(shards, shard_rows, 2 * ff),
        bf(shards, shard_rows, 3 * cols),
        bf(shards, attn_part, width),
        bf(shards, ff_part, width),
        bf(width, length),
        bf(length, width),
        bf(length, 2 * ff),
        bf(ff, length),
        bf(length, cols),
        bf(length, cols),
        bf(length, cols),
        f32(length, cols),
        bf(cols, length),
        f32(length, cols),
        bf(count, rows, width),
    ]
    hops = (2, count - 1)
    return pl.pallas_call(
        forward_kernel,
        out_shape=out_shape,
        in_specs=[smem] * 2 + [vmem_whole()] * 3 + [hbm_whole()] * 8,
        out_specs=[hbm_whole()] * len(out_shape),
        scratch_shapes=[
            pltpu.VMEM((2,) + w_qkv.shape, BF),
            pltpu.VMEM((count, rows, width), BF),
            pltpu.VMEM((shards,) + vectors.shape, F32),
            pltpu.VMEM((vectors.shape[0], width), F32),
            pltpu.VMEM((shards, shard_rows, 2 * ff), BF),
            pltpu.VMEM((shards, shard_rows, 3 * cols), BF),
            pltpu.VMEM((shards, attn_part, width), BF),
            pltpu.VMEM((length, width), BF),
            pltpu.VMEM((length, ff), BF),
            pltpu.VMEM((length, cols), BF),
            pltpu.VMEM((2, rows, width), BF),
            pltpu.VMEM((2, width, rows), BF),
            pltpu.VMEM((2, length, TILE), BF),
            pltpu.VMEM((2, HALF, length), BF),
            pltpu.VMEM((2, length, HALF), BF),
            pltpu.VMEM((2, length, HALF), BF),
            pltpu.VMEM((2, length, HALF), BF),
            pltpu.VMEM((2, length, HALF), F32),
            pltpu.VMEM((2, HALF, length), BF),
            pltpu.VMEM((2, length, HALF), F32),
            pltpu.VMEM((2, shards, ff_part, TILE), BF),
            pltpu.VMEM((count, rows, TILE), F32),
            pltpu.VMEM((2, count, rows, TILE), BF),
            dma((6,)),
            dma(hops),
            dma(hops),
            dma(hops),
            dma(hops),
            dma((4, 8)),
            dma((4, 8)),
            dma((shards - 1,)),
            dma((shards - 1,)),
            dma((2, 2)),
            dma((4,)),
            dma((2, 2)),
            dma((2, 2)),
            dma((6, 2)),
            dma((2,)),
            dma((2,)),
        ],
        compiler_params=pltpu.CompilerParams(
            collective_id=3, has_side_effects=True, vmem_limit_bytes=62 * 2**20
        ),
        name="forward",
    )(order, slots, *tables, tokens, cot, vectors, w_gate, w_up, w_qkv, w_out, w_down)


def fixed_tables(length):
    half = ROT // 2
    inverse = np.float32(10000.0) ** (-np.arange(half, dtype=np.float32) / np.float32(half))
    grid = np.arange(length, dtype=np.float32)[:, None] * inverse.astype(np.float32)[None, :]
    cos, sin = np.cos(grid, dtype=np.float32), np.sin(grid, dtype=np.float32)
    zero, rest = np.zeros((length, half), np.float32), np.zeros((length, HD - ROT), np.float32)
    tables = ([cos, cos, rest + 1], [-sin, zero, rest], [zero, sin, rest])
    return [jnp.asarray(np.tile(np.concatenate(t, axis=1), (1, 2))) for t in tables]


def rows_of(shard, part):
    return slice(shard * part, (shard + 1) * part)


def heads_back_pair(q_in, k_in, v_in, do_in, att, lse, cos, first, second, out, dk, dv):
    length = q_in.shape[0]
    scale = HD ** (-0.5)
    row = lax.broadcasted_iota(jnp.int32, (CHUNK, CHUNK), 0)
    col = lax.broadcasted_iota(jnp.int32, (CHUNK, CHUNK), 1)
    dk[...] = jnp.zeros_like(dk)
    dv[...] = jnp.zeros_like(dv)
    for c in range(length // CHUNK):
        lo, hi = c * CHUNK, (c + 1) * CHUNK
        dqs = []
        for h in range(2):
            lanes = slice(h * HD, (h + 1) * HD)
            q, do = q_in[lo:hi, lanes], do_in[lo:hi, lanes]
            delta = jnp.sum(do.astype(F32) * att[lo:hi, lanes], axis=1, keepdims=True)
            s = contract(q, k_in[lo:hi, lanes], ((1,), (1,)))
            s = jnp.where(col <= row, s, NEG)
            if c:
                s = jnp.concatenate([contract(q, k_in[:lo, lanes], ((1,), (1,))), s], axis=1)
            p = jnp.exp(s - lse[lo:hi, h * HD : h * HD + 1])
            dp = contract(do, v_in[:hi, lanes], ((1,), (1,)))
            ds = (p * (dp - delta)).astype(BF)
            dqs.append(contract(ds, k_in[:hi, lanes], ((1,), (0,))) * scale)
            dk[:hi, lanes] += contract(ds, q, ((0,), (0,)))
            dv[:hi, lanes] += contract(p.astype(BF), do, ((0,), (0,)))
        dq = jnp.concatenate(dqs, axis=1)
        out[0, lo:hi, :] = turn(dq, cos[lo:hi, :], -first[lo:hi, :], -second[lo:hi, :]).astype(BF)
    out[1] = turn(dk[...], cos[...], -first[...], -second[...]).astype(BF)
    out[2] = dv[...].astype(BF)


def backward_kernel(
    order, slots, hid_t, att_t, cos, first, second,
    cot, norm_hbm, down, attn, both, branch, w_inner, w_heads, hat, q_in, k_in, v_in, att_in, lse_in,
    pieces, sums,
    cot_own, norm_t, d_inner, d_mixed, terms, term, small, w_tile, h_tile, hat_tile,
    attn_tile, q_tile, k_tile, v_tile, att_tile, lse_tile, d_att, turned, dk, dv, sums_stage,
    partial, theirs, pair, landed, total, sum_from, sum_land,
    core_send, core_recv, chip_send, chip_recv, line_send, line_recv, own_sem, sum_send, sum_recv,
    cot_sem, load_sem, feed_sem, back_sem, head_sem, sums_sem,
):
    count, chunks = pieces.shape[0], pieces.shape[1]
    shards = 2 * partial.shape[1]
    chips = shards // 2
    rows = terms.shape[1]
    place, me = lax.axis_index("ctx"), lax.axis_index("fsdp")
    chip, core = me // 2, me % 2
    ff_part, attn_part = hid_t.shape[0] // shards, att_t.shape[0] // shards
    sum_parts = terms.shape[2] // TILE
    early = cot_own.shape[1] // TILE - 1
    inner_end = early + d_inner.shape[1] // TILE

    def chunk_name(i):
        return jnp.where(i < early, i + chunks - 1 - early, jnp.where(i == chunks - 1, i, i - early))

    def core_copy(i):
        return pltpu.make_async_remote_copy(
            src_ref=partial.at[i % 2, :, 1 - core],
            dst_ref=theirs.at[i % DEEP],
            send_sem=core_send.at[i % 2],
            recv_sem=core_recv.at[i % DEEP],
            device_id=(place, me + 1 - 2 * core),
            device_id_type=MESH,
        )

    def chip_copy(j, m):
        return pltpu.make_async_remote_copy(
            src_ref=pair.at[j % 2, chip_away(chip, m)],
            dst_ref=landed.at[j % DEEP, m - 1],
            send_sem=chip_send.at[j % 2, m - 1],
            recv_sem=chip_recv.at[j % DEEP, m - 1],
            device_id=(place, 2 * chip_away(chip, m) + core),
            device_id_type=MESH,
        )

    def line_copy(way, hop, k, size):
        ahead = 1 - 2 * way
        origin = place - (hop - 1) * ahead
        target = pieces.at[origin, chunk_name(k), :size]
        return pltpu.make_async_remote_copy(
            src_ref=total.at[k % DEEP, :size] if hop == 1 else target,
            dst_ref=target,
            send_sem=line_send.at[way, hop - 1, k % DEEP],
            recv_sem=line_recv.at[way, k, hop - 1],
            device_id=(place + ahead, me),
            device_id_type=MESH,
        )

    def on_line(way, hop, k, act):
        @pl.when(k < early)
        def _():
            act(line_copy(way, hop, k, ff_part + attn_part))

        @pl.when(k >= early)
        def _():
            act(line_copy(way, hop, k, total.shape[1]))

    def sends(way, hop):
        if way == 0:
            return (place >= hop - 1) & (place <= count - 2)
        return (place <= count - hop) & (place >= 1)

    def lands(way, hop):
        return place >= hop if way == 0 else place <= count - 1 - hop

    def forward_chunk(hop, k):
        for way in range(2):
            if hop > 1:
                @pl.when(lands(way, hop - 1))
                def _(way=way):
                    on_line(way, hop - 1, k, lambda c: c.wait_recv())

            if hop < count:
                @pl.when(sends(way, hop))
                def _(way=way):
                    @pl.when(k >= DEEP)
                    def _():
                        on_line(way, hop, k - DEEP, lambda c: c.wait_send())

                    on_line(way, hop, k, lambda c: c.start())

    def own_copy(k):
        return pltpu.make_async_copy(total.at[k % DEEP], pieces.at[place, chunk_name(k)], own_sem.at[k % DEEP])

    def sum_copy(way, t, q):
        return pltpu.make_async_remote_copy(
            src_ref=sum_from.at[way, t - 1, q // sum_parts],
            dst_ref=sum_land.at[way, t - 1, q % sum_parts],
            send_sem=sum_send.at[way, t - 1, q // sum_parts],
            recv_sem=sum_recv.at[way, t - 1, q],
            device_id=(place + 1 - 2 * way, me),
            device_id_type=MESH,
        )

    def sum_sends(way, t):
        return place <= t - 1 if way == 0 else place >= count - t

    def sum_step(t, q):
        at = tile_at(q % sum_parts)
        for way in range(2):
            @pl.when(sum_sends(way, t))
            def _(way=way):
                to = count - t + place if way == 0 else t + place - count
                starts = place == 0 if way == 0 else place == count - 1

                @pl.when(q % sum_parts >= 1)
                def _():
                    sum_copy(way, t, q - 1).wait_send()

                @pl.when(starts)
                def _():
                    sum_from[way, t - 1, q // sum_parts] = terms[to, :, at]

                if t > 1:
                    @pl.when(jnp.logical_not(starts))
                    def _():
                        sum_copy(way, t - 1, q).wait_recv()
                        value = terms[to, :, at].astype(F32) + sum_land[way, t - 2, q % sum_parts].astype(F32)
                        sum_from[way, t - 1, q // sum_parts] = value.astype(BF)

                sum_copy(way, t, q).start()

    def sums_copy(q):
        return pltpu.make_async_copy(
            sums_stage.at[q // sum_parts],
            sums.at[q // sum_parts, :, tile_at(q % sum_parts)],
            sums_sem.at[q // sum_parts],
        )

    def sum_end(q):
        @pl.when(q % sum_parts >= 1)
        def _():
            sums_copy(q - 1).wait()

        sums_stage[q // sum_parts] = terms[place, :, tile_at(q % sum_parts)].astype(F32)
        for way in range(2):
            @pl.when(place >= 1 if way == 0 else place <= count - 2)
            def _(way=way):
                sum_copy(way, count - 1, q).wait_recv()
                sums_stage[q // sum_parts] += sum_land[way, count - 2, q % sum_parts].astype(F32)

        sums_copy(q).start()

    cot_load = pltpu.make_async_copy(cot, terms, cot_sem)

    def feed_load(b, size):
        at = pl.ds(pl.multiple_of(b * TILE, TILE), size)
        return pltpu.make_async_copy(
            down.at[at], w_tile.at[b % 2, :size, : cot_own.shape[1]], feed_sem.at[b % 2]
        )

    both_load = pltpu.make_async_copy(both, d_inner, load_sem.at[2])

    loads = [
        pltpu.make_async_copy(branch, terms, load_sem.at[0]),
        pltpu.make_async_copy(norm_hbm, norm_t, load_sem.at[1]),
    ]

    def back_loads(q):
        moves = (
            (w_inner.at[tile_at(q)], w_tile.at[q % 2]),
            (w_heads.at[tile_at(q)], h_tile.at[q % 2]),
            (hat.at[:, tile_at(q)], hat_tile.at[q % 2]),
        )
        return [pltpu.make_async_copy(a, b, back_sem.at[n, q % 2]) for n, (a, b) in enumerate(moves)]

    def head_loads(h):
        moves = ((q_in, q_tile), (k_in, k_tile), (v_in, v_tile), (att_in, att_tile), (lse_in, lse_tile))
        at = tile_at(h, HALF)
        copies = [
            pltpu.make_async_copy(a.at[:, at], b.at[h % 2], head_sem.at[n, h % 2]) for n, (a, b) in enumerate(moves)
        ]
        return copies

    def attn_load(h):
        return pltpu.make_async_copy(attn.at[tile_at(h // 2)], attn_tile, load_sem.at[3])

    pairs = q_in.shape[1] // HALF
    tiles = d_inner.shape[1] // TILE
    for c in [cot_load, both_load, feed_load(0, TILE), feed_load(1, TILE), attn_load(0)] + head_loads(0) + head_loads(1) + loads[1:]:
        c.start()
    peers = [(place, me + 1 - 2 * core)]
    peers += [(place, 2 * chip_away(chip, m) + core) for m in range(1, chips)]
    peers += [((place + 1) % count, me), ((place + count - 1) % count, me)]

    def meanwhile():
        cot_load.wait()
        for p in range(count):
            cot_own[p * rows : (p + 1) * rows, :] = terms[slots[p]]
        loads[0].start()
        loads[0].wait()

    greet(peers, meanwhile)
    ff = down.shape[0]
    whole_tiles = ff // TILE

    def feed_tile(b, size):
        feed_load(b, size).wait()
        d_hidden = contract(cot_own[...], w_tile[b % 2, :size, : cot_own.shape[1]], ((1,), (1,)))
        for n in range(size // HALF):
            d = d_hidden[:, n * HALF : (n + 1) * HALF]
            at = tile_at(2 * b + n)
            value = d_inner[:, at]
            gate = value[:, :HALF].astype(F32)
            up = value[:, HALF:].astype(F32)
            sig = jax.nn.sigmoid(gate)
            d_gate = d * up * sig * (1.0 + gate * (1.0 - sig))
            d_inner[:, at] = jnp.concatenate([d_gate, d * gate * sig], axis=1).astype(BF)

    def feed_step(b, carry):
        feed_tile(b, TILE)

        @pl.when(b + 2 < whole_tiles)
        def _():
            feed_load(b + 2, TILE).start()

        if ff % TILE:
            @pl.when(b + 2 == whole_tiles)
            def _():
                feed_load(whole_tiles, ff % TILE).start()

        return carry

    def store(i, shard, lo, value):
        partial[i % 2, shard // 2, shard % 2, lo : lo + value.shape[0], :] = value

    def from_norm(i, rhs):
        for s in range(0, shards, 2):
            part = norm_t.shape[0] // shards
            value = contract(norm_t[s * part : (s + 2) * part, :], rhs, ((1,), (0,))).astype(BF)
            store(i, s, 0, value[:part])
            store(i, s + 1, 0, value[part:])

    def step(i, carry):
        @pl.when((i < early) | (i == chunks - 1))
        def _():
            c = jnp.where(i < early, i, early)
            rhs = cot_own[:, tile_at(c)]
            for s in range(0, shards, 4):
                value = contract(hid_t[s * ff_part : (s + 4) * ff_part, :], rhs, ((1,), (0,))).astype(BF)
                for t in range(4):
                    store(i, s + t, 0, value[rows_of(t, ff_part)])
            value = contract(att_t[...], rhs, ((1,), (0,))).astype(BF)
            for s in range(shards):
                store(i, s, ff_part, value[rows_of(s, attn_part)])

        @pl.when(i == chunks - 1)
        def _():
            for s in range(shards):
                store(i, s, ff_part + attn_part, small[s])

        @pl.when(i == early)
        def _():
            loads[1].wait()

        @pl.when((i >= early) & (i < inner_end))
        def _():
            from_norm(i, d_inner[:, tile_at(i - early)])

        @pl.when((i >= inner_end) & (i < chunks - 1))
        def _():
            at = i - inner_end
            from_norm(i, d_mixed[:, tile_at(at)])

        @pl.when(i < chunks)
        def _():
            core_copy(i).start()

        @pl.when((i >= 1) & (i < chunks + 1))
        def _():
            j = i - 1
            core_copy(j).wait()
            for m in range(chips):
                a = partial[j % 2, m, core].astype(F32) + theirs[j % DEEP, m].astype(F32)
                pair[j % 2, m] = a.astype(BF)
            for m in range(1, chips):
                chip_copy(j, m).start()

        @pl.when((i >= 2) & (i < chunks + 2))
        def _():
            k = i - 2
            for m in range(1, chips):
                chip_copy(k, m).wait()

            a = pair[k % 2, chip].astype(F32)
            for m in range(1, chips):
                a = a + landed[k % DEEP, m - 1].astype(F32)
            for way in range(2):
                @pl.when(sends(way, 1) & (k >= DEEP))
                def _(way=way):
                    on_line(way, 1, k - DEEP, lambda c: c.wait_send())

            @pl.when(k >= DEEP)
            def _():
                own_copy(k - DEEP).wait()

            total[k % DEEP] = a.astype(BF)
            for way in range(2):
                @pl.when(sends(way, 1))
                def _(way=way):
                    on_line(way, 1, k, lambda c: c.start())

            own_copy(k).start()

        @pl.when((i >= 9) & (i < 9 + 2 * sum_parts) & (i % 2 == 1))
        def _():
            q = (i - 9) // 2
            for c in back_loads(q):
                c.wait()
            value = contract(d_inner[...], w_tile[q % 2], ((1,), (1,)))
            value = value + contract(d_mixed[...], h_tile[q % 2], ((1,), (1,)))
            term[...] = value.reshape(term.shape)
            gain = jnp.sum(value * hat_tile[q % 2].astype(F32), axis=0, keepdims=True)
            bias = jnp.sum(value, axis=0, keepdims=True)
            row = lax.broadcasted_iota(jnp.int32, small.shape[1:], 0)
            small[q] = jnp.where(row == 0, gain, jnp.where(row == 1, bias, 0.0)).astype(BF)
            for j in range(count):
                terms[j, :, tile_at(q)] = term[order[j]].astype(BF)

            @pl.when(q + 2 < sum_parts)
            def _():
                for c in back_loads(q + 2):
                    c.start()

        for t in range(1, count + 1):
            when = i - LAG * (t - 1)
            q = jnp.where(when % 2 == 0, when // 2, sum_parts + (when - 9) // 2)
            begins = jnp.where(when % 2 == 0, when, jnp.where(when >= 9, when - 9, -1))

            @pl.when((begins >= 0) & (begins < 2 * sum_parts))
            def _(q=q, t=t):
                if t < count:
                    sum_step(t, q)
                else:
                    sum_end(q)

        for hop in range(2, count + 1):
            k = i - 2 - LAG * (hop - 1)

            @pl.when((k >= 0) & (k < chunks))
            def _(k=k, hop=hop):
                forward_chunk(hop, k)

        @pl.when(i == 0)
        def _():
            both_load.wait()

        @pl.when((i == 0) | (i == 1) | (i == 4))
        def _():
            first_tile = jnp.where(i == 0, 0, jnp.where(i == 1, 1, 3))
            last_tile = jnp.where(i == 0, 1, jnp.where(i == 1, 3, whole_tiles))
            lax.fori_loop(first_tile, last_tile, feed_step, 0)

        if ff % TILE:
            @pl.when(i == 4)
            def _():
                feed_tile(whole_tiles, ff % TILE)

        @pl.when(i == 5)
        def _():
            for c in back_loads(0) + back_loads(1):
                c.start()

        @pl.when((i == 2) | (i == 3) | (i == 5) | (i == 6))
        def _():
            h = i - 2 - i // 5
            for c in head_loads(h):
                c.wait()
            slot = h % 2

            @pl.when(slot == 0)
            def _():
                attn_load(h).wait()
                value = contract(cot_own[...], attn_tile[...], ((1,), (1,)))
                for n in range(2):
                    d_att[n] = value[:, n * HALF : (n + 1) * HALF].astype(BF)

                @pl.when(h + 2 < pairs)
                def _():
                    attn_load(h + 2).start()

            heads_back_pair(
                q_tile.at[slot], k_tile.at[slot], v_tile.at[slot], d_att.at[slot], att_tile.at[slot],
                lse_tile.at[slot], cos, first, second, turned, dk, dv,
            )
            for n in range(3):
                d_mixed[:, tile_at(3 * h + n, HALF)] = turned[n]

            @pl.when(h + 2 < pairs)
            def _():
                for c in head_loads(h + 2):
                    c.start()

        return carry

    lax.fori_loop(0, chunks + 2 + LAG * (count - 1), step, 0)

    def drain(k, carry):
        own_copy(k).wait()
        for way in range(2):
            for hop in range(1, count):
                @pl.when(sends(way, hop))
                def _(way=way, hop=hop):
                    line_copy(way, hop, k, total.shape[1]).wait_send()
        return carry

    lax.fori_loop(chunks - DEEP, chunks, drain, 0)
    for kind in range(1, 3):
        sums_copy(kind * sum_parts - 1).wait()
    for way in range(2):
        for t in range(1, count):
            @pl.when(sum_sends(way, t))
            def _(way=way, t=t):
                for kind in range(1, 3):
                    sum_copy(way, t, kind * sum_parts - 1).wait_send()


def backward(
    order, slots, hid_t, att_t, tables, cot, norm_t, down, attn, both, branch, w_inner, w_heads, hat, heads, shards
):
    count, rows, width = cot.shape
    length = count * rows
    chips = shards // 2
    cols = heads[0].shape[1]
    inner = both.shape[1]
    chunks = (width + inner + 3 * cols) // TILE
    part = width // shards
    parts = width // TILE
    dma = pltpu.SemaphoreType.DMA
    smem = pl.BlockSpec(memory_space=pltpu.SMEM)
    return pl.pallas_call(
        backward_kernel,
        out_shape=[
            jax.ShapeDtypeStruct((count, chunks, part, TILE), BF),
            jax.ShapeDtypeStruct((2, rows, width), F32),
        ],
        in_specs=[smem] * 2 + [vmem_whole()] * 5 + [hbm_whole()] * 14,
        out_specs=[hbm_whole()] * 2,
        scratch_shapes=[
            pltpu.VMEM((length, width), BF),
            pltpu.VMEM((width, length), BF),
            pltpu.VMEM((length, inner), BF),
            pltpu.VMEM((length, 3 * cols), BF),
            pltpu.VMEM((count, rows, width), BF),
            pltpu.VMEM((count, rows, TILE), F32),
            pltpu.VMEM((parts, 16, TILE), BF),
            pltpu.VMEM((2, TILE, inner), BF),
            pltpu.VMEM((2, TILE, 3 * cols), BF),
            pltpu.VMEM((2, length, TILE), BF),
        ]
        + [pltpu.VMEM((TILE, width), BF)]
        + [pltpu.VMEM((2, length, HALF), BF)] * 3
        + [pltpu.VMEM((2, length, HALF), F32)] * 2
        + [pltpu.VMEM((2, length, HALF), BF)]
        + [pltpu.VMEM((3, length, HALF), BF)]
        + [pltpu.VMEM((length, HALF), F32)] * 2
        + [pltpu.VMEM((2, rows, TILE), F32)]
        + [
            pltpu.VMEM((2, chips, 2, part, TILE), BF),
            pltpu.VMEM((DEEP, chips, part, TILE), BF),
            pltpu.VMEM((2, chips, part, TILE), BF),
            pltpu.VMEM((DEEP, chips - 1, part, TILE), BF),
            pltpu.VMEM((DEEP, part, TILE), BF),
            pltpu.VMEM((2, count - 1, 2, rows, TILE), BF),
            pltpu.VMEM((2, count - 1, parts, rows, TILE), BF),
            dma((2,)),
            dma((DEEP,)),
            dma((2, chips - 1)),
            dma((DEEP, chips - 1)),
            dma((2, count - 1, DEEP)),
            dma((2, chunks, count - 1)),
            dma((DEEP,)),
            dma((2, count - 1, 2)),
            dma((2, count - 1, 2 * parts)),
            pltpu.SemaphoreType.DMA,
            dma((4,)),
            dma((2,)),
            dma((3, 2)),
            dma((5, 2)),
            dma((2,)),
        ],
        compiler_params=pltpu.CompilerParams(
            collective_id=1, has_side_effects=True, vmem_limit_bytes=62 * 2**20
        ),
        name="backward",
    )(order, slots, hid_t, att_t, *tables, cot, norm_t, down, attn, both, branch, w_inner, w_heads, hat, *heads)


def column_runs(columns, source):
    out = []
    for block in range(columns // HALF):
        first = 0
        while first < HALF:
            key, lane = source(block * HALF + first)
            last = first + 1
            while last < HALF and source(block * HALF + last) == (key, lane + last - first):
                last += 1
            out.append((block, first, last, key, (first - lane) % HALF))
            first = last
    return out


def assemble_kernel(rows_in, cols_in, sums, tokens, cot, gain, out, grad, qkv_out, gate_out, up_out, down_out, attn_out, gain_out, bias_out):
    count, chunks, rows, _ = rows_in.shape
    ff = gate_out.shape[1]
    width = qkv_out.shape[1]
    ff_part = down_out.shape[0] // count
    attn_part = attn_out.shape[0] // count
    shards = ff // (count * ff_part)
    inner_chunks = ff // count // HALF
    lane = lax.broadcasted_iota(jnp.int32, (rows, HALF), 1)
    own = tokens[...].astype(F32)
    out[...] = (own + sums[0]).astype(BF)
    own = own - jnp.mean(own, axis=1, keepdims=True)
    inv_std = lax.rsqrt(jnp.mean(own * own, axis=1, keepdims=True) + EPS)
    own = own * inv_std
    scaled = sums[1] * gain[0:1, :]
    scaled = scaled - jnp.mean(scaled, axis=1, keepdims=True) - own * jnp.mean(scaled * own, axis=1, keepdims=True)
    grad[...] = cot[...].astype(F32) + inv_std * scaled

    def gather(out, runs, load):
        for block, first, last, key, shift in runs:
            value = load(key).astype(F32)
            if shift:
                value = pltpu.roll(value, shift, 1)
            if first:
                value = jnp.where(lane >= first, value, held)
            held = value
            if last == HALF:
                out[:, block * HALF : (block + 1) * HALF] = value

    def inner_source(column):
        shard, rest = divmod(column, count * ff_part)
        unit = shard * ff_part + rest % ff_part
        return (rest // ff_part, unit // HALF), unit % HALF

    def head_source(column):
        part, rest = divmod(column, width // 3)
        head, dim = divmod(rest, HD)
        per = width // 3 // HD // shards // count
        shard, at = divmod(head, per * count)
        place, sub = divmod(at, per)
        pair, half = divmod(shard * per + sub, 2)
        return (place, 3 * pair + part), half * HD + dim

    runs = column_runs(ff, inner_source)
    gather(gate_out, runs, lambda key: rows_in[key[0], key[1], :, :HALF])
    gather(up_out, runs, lambda key: rows_in[key[0], key[1], :, HALF:])
    first_head = inner_chunks

    def head_load(key):
        at = key[1] % 2 * HALF
        return rows_in[key[0], first_head + key[1] // 2, :, at : at + HALF]

    gather(qkv_out, column_runs(width, head_source), head_load)
    for p in range(count):
        down_out[p * ff_part : (p + 1) * ff_part, :] = cols_in[p, 0, :ff_part, :].astype(F32)
        attn_out[p * attn_part : (p + 1) * attn_part, :] = cols_in[
            p, 0, ff_part : ff_part + attn_part, :
        ].astype(F32)
    small = [cols_in[p, 0, ff_part + attn_part :, :].astype(F32) for p in range(count)]
    small = functools.reduce(jnp.add, small)
    gain_out[...] = small[0:1]
    bias_out[...] = small[1:2]


def assemble_outputs(pieces, sums, tokens, cot, gain, qkv, attn, gate, down):
    count, chunks, rows, _ = pieces.shape
    steps = down[1] // TILE
    part = rows // steps
    width = tokens.shape[1]
    by_rows = lambda shape: pl.BlockSpec((part, shape[1]), lambda i: (i, 0))
    by_cols = lambda shape: pl.BlockSpec((shape[0], TILE), lambda i: (0, i))
    return pl.pallas_call(
        assemble_kernel,
        grid=(steps,),
        in_specs=[
            pl.BlockSpec((count, chunks - steps, part, TILE), lambda i: (0, 0, i, 0)),
            pl.BlockSpec((count, 1, rows, TILE), lambda i: (0, chunks - steps + i, 0, 0)),
            pl.BlockSpec((2, part, width), lambda i: (0, i, 0)),
            by_rows(tokens.shape),
            by_rows(tokens.shape),
            pl.BlockSpec(gain.shape, lambda i: (0, 0)),
        ],
        out_specs=[by_rows(tokens.shape)] * 2
        + [by_rows(qkv), by_rows(gate), by_rows(gate), by_cols(down), by_cols(attn)]
        + [pl.BlockSpec((1, TILE), lambda i: (0, 0))] * 2,
        out_shape=[jax.ShapeDtypeStruct(tokens.shape, BF), jax.ShapeDtypeStruct(tokens.shape, F32)]
        + [jax.ShapeDtypeStruct(s, F32) for s in (qkv, gate, gate, down, attn, (1, TILE), (1, TILE))],
        compiler_params=pltpu.CompilerParams(vmem_limit_bytes=60 * 2**20),
        name="assemble",
    )(pieces, pieces, sums, tokens, cot, gain)


def rotation_tables(length):
    half = ROT // 2
    inverse = 10000.0 ** (-jnp.arange(half, dtype=F32) / half)
    grid = jnp.arange(length, dtype=jnp.int32).astype(F32)[:, None] * inverse[None, :]
    cos, sin = jnp.cos(grid), jnp.sin(grid)
    zero = jnp.zeros((length, half), F32)
    rest = jnp.zeros((length, HD - ROT), F32)
    tables = (
        jnp.concatenate([cos, cos, rest + 1.0], axis=1),
        jnp.concatenate([-sin, zero, rest], axis=1),
        jnp.concatenate([zero, sin, rest], axis=1),
    )
    return tuple(jnp.tile(t, (1, 2)) for t in tables)


def body_general(tokens, block_order, ln_gain, ln_bias, w_qkv, w_out, w_gate, w_up, w_down, cotangent):
    rows, width = tokens.shape[1], tokens.shape[2]
    count = lax.axis_size("ctx")
    shards = lax.axis_size("fsdp")
    place = lax.axis_index("ctx")
    length = rows * count
    order = block_order[0]
    shard_rows = w_qkv.shape[0]
    ff_shard = w_down.shape[0]
    ff_part = ff_shard // count
    own_heads = H // count
    spread = (w_out.shape[0] // HD) % count == 0
    groups = shards if spread else 1
    head_cols = own_heads * HD // groups

    def my_cols(w, outer, group, part):
        w = w.reshape(w.shape[0], outer, group, count, part)
        return lax.dynamic_index_in_dim(w, place, 3, False).reshape(w.shape[0], outer * group * part)

    def all_cols(piece, outer, group, part):
        whole = gather_ctx(piece).reshape(count, piece.shape[0], outer, group, part)
        return whole.transpose(1, 2, 3, 0, 4).reshape(piece.shape[0], -1).astype(F32)

    def assemble(block, ready=None):
        whole = jnp.zeros((length, width), block.dtype)
        whole = lax.dynamic_update_slice_in_dim(whole, block, order[place] * rows, 0)
        last = None
        for k in range(1, count):
            last = ring_send(block, k)
            source = (place - k) % count
            whole = lax.dynamic_update_slice_in_dim(whole, last, order[source] * rows, 0)
        return whole, last

    gain = lax.all_gather(ln_gain, "fsdp", axis=0, tiled=True).astype(F32)
    bias = lax.all_gather(ln_bias, "fsdp", axis=0, tiled=True).astype(F32)
    tables = rotation_tables(length)

    block = tokens[0]
    x_all, arrived = assemble(block)
    grad_block = cotangent[0]
    cot_all, _ = assemble(after(grad_block, arrived))

    inner = jnp.concatenate(
        [my_cols(w_gate, 1, shards, ff_part), my_cols(w_up, 1, shards, ff_part)], axis=1
    )
    w_inner, sent = gather_rows(inner)
    w_heads, sent = gather_rows(after(my_cols(w_qkv, 3, groups, head_cols), sent))
    down = lax.dynamic_slice_in_dim(w_down, place * ff_part, ff_part, 0)
    w_hidden, sent = gather_rows(after(down, sent))
    if spread:
        part = w_out.shape[0] // count
        attn = lax.dynamic_slice_in_dim(w_out, place * part, part, 0)
        w_attn, sent = gather_rows(after(attn, sent))
    else:
        w_attn = lax.all_gather(after(w_out, sent), "fsdp", axis=0, tiled=True)
        w_attn = lax.dynamic_slice_in_dim(w_attn, place * own_heads * HD, own_heads * HD, 0)

    xf = x_all.astype(F32)
    average = jnp.mean(xf, axis=-1, keepdims=True)
    centered = xf - average
    variance = jnp.mean(centered * centered, axis=-1, keepdims=True)
    inv_std = lax.rsqrt(variance + EPS)
    x_hat = centered * inv_std
    normed = (x_hat * gain + bias).astype(BF)

    across = ((1,), (0,))
    over_tokens = ((0,), (0,))
    back = ((1,), (1,))
    ff_cols = shards * ff_part
    gate_value = dot(normed, w_inner[:, :ff_cols], across)
    up_value = dot(normed, w_inner[:, ff_cols:], across)
    sigmoid_gate = jax.nn.sigmoid(gate_value)
    hidden = (gate_value * sigmoid_gate * up_value).astype(BF)
    mixed = dot(normed, w_heads, across)
    q, k, v, attended, lse = attend(mixed, tables, own_heads)
    attended_low = attended.astype(BF)

    branch = dot(attended_low, w_attn, across) + dot(hidden, w_hidden, across)
    out = line_scatter(lambda j: lax.dynamic_slice_in_dim(branch, order[j] * rows, rows, 0))
    out = (block.astype(F32) + out).astype(BF)[None]

    d_hidden = dot(cot_all, w_hidden, back)
    grad_down = scatter_rows(dot(hidden, cot_all, over_tokens, BF))
    d_gate_act = (
        d_hidden * up_value * sigmoid_gate * (1.0 + gate_value * (1.0 - sigmoid_gate))
    ).astype(BF)
    d_up_act = (d_hidden * gate_value * sigmoid_gate).astype(BF)
    d_inner = jnp.concatenate([d_gate_act, d_up_act], axis=1)
    d_attended = dot(cot_all, w_attn, back, BF)
    d_mixed = attend_back(q, k, v, d_attended, attended, lse, tables, own_heads)
    d_mixed = jnp.concatenate(d_mixed, axis=1)
    grad_inner = scatter_rows(dot(normed, d_inner, over_tokens, BF))
    grad_attn = dot(attended_low, cot_all, over_tokens, BF)
    grad_heads = scatter_rows(dot(normed, d_mixed, over_tokens, BF))

    d_normed = dot(d_inner, w_inner, back) + dot(d_mixed, w_heads, back)
    small = jnp.stack([jnp.sum(d_normed * x_hat, axis=0), jnp.sum(d_normed, axis=0)])
    small = lax.psum(small, ("ctx", "fsdp"))
    small = lax.dynamic_slice_in_dim(small, lax.axis_index("fsdp") * shard_rows, shard_rows, 1)
    d_own = line_scatter(lambda j: lax.dynamic_slice_in_dim(d_normed, order[j] * rows, rows, 0))
    own = block.astype(F32)
    own_average = jnp.mean(own, axis=-1, keepdims=True)
    own = own - own_average
    own_std = lax.rsqrt(jnp.mean(own * own, axis=-1, keepdims=True) + EPS)
    own = own * own_std
    scaled = d_own * gain
    d_input = own_std * (
        scaled
        - jnp.mean(scaled, axis=-1, keepdims=True)
        - own * jnp.mean(scaled * own, axis=-1, keepdims=True)
    )
    grad_in = (grad_block.astype(F32) + d_input)[None]

    down_all = gather_ctx(grad_down).reshape(ff_shard, width).astype(F32)
    if spread:
        attn_all = gather_ctx(scatter_rows(grad_attn)).reshape(w_out.shape).astype(F32)
    else:
        full = jnp.zeros((H * HD, width), BF)
        full = lax.dynamic_update_slice_in_dim(full, grad_attn, place * own_heads * HD, 0)
        full = lax.psum_scatter(full, "fsdp", scatter_dimension=0, tiled=True)
        attn_all = lax.psum(full, "ctx").astype(F32)
    heads_all = all_cols(grad_heads, 3, groups, head_cols)
    inner_all = gather_ctx(grad_inner).reshape(count, shard_rows, 2, shards, ff_part)
    inner_all = inner_all.transpose(2, 1, 3, 0, 4).reshape(2, shard_rows, -1).astype(F32)
    return (
        out,
        grad_in,
        small[0],
        small[1],
        heads_all,
        attn_all,
        inner_all[0],
        inner_all[1],
        down_all,
    )


def body_fast(tokens, block_order, ln_gain, ln_bias, w_qkv, w_out, w_gate, w_up, w_down, cotangent):
    count, shards = lax.axis_size("ctx"), lax.axis_size("fsdp")
    place = lax.axis_index("ctx")
    block, grad_block = tokens[0], cotangent[0]
    rows, width = block.shape
    order = block_order[0]
    spots = jnp.arange(count, dtype=jnp.int32)
    slots = jnp.sum(jnp.where(order[None, :] == spots[:, None], spots[None, :], 0), axis=1)
    vectors = jnp.stack([ln_gain, ln_bias] + [jnp.zeros_like(ln_gain)] * 6).astype(F32)
    tables = fixed_tables(rows * count)
    (
        cot_all, scales, w_inner, w_heads, w_attn, w_hidden, normed_t, hat, both, hidden_t,
        q, k, v, attended, low_t, lse, branch,
    ) = forward(
        order, slots, tables, block, grad_block, vectors, w_gate, w_up, w_qkv, w_out, w_down, count, shards
    )
    w_inner = w_inner.reshape(width, -1)
    w_hidden, w_attn = w_hidden.reshape(-1, width), w_attn.reshape(-1, width)
    w_heads = w_heads.reshape(width, -1)
    pieces, sums = backward(
        order, slots, hidden_t, low_t, tables, cot_all, normed_t, w_hidden, w_attn, both, branch, w_inner,
        w_heads, hat, (q, k, v, attended, lse), shards,
    )
    out, grad_in, d_qkv, d_gate, d_up, d_down, d_attn, d_gain, d_bias = assemble_outputs(
        pieces, sums, block, grad_block, scales, w_qkv.shape, w_out.shape, w_gate.shape, w_down.shape
    )
    out, grad_in = out[None], grad_in[None]
    return out, grad_in, d_gain.reshape(-1), d_bias.reshape(-1), d_qkv, d_attn, d_gate, d_up, d_down


def solution(mesh):
    whole, once = P("fsdp", "ctx", None), P("fsdp", None)
    count, shards = mesh.shape["ctx"], mesh.shape["fsdp"]

    def body(*args):
        w_out, w_down = args[5], args[8]
        fits = shards == 8 and w_out.shape[0] == count * HD and w_out.shape[0] == TILE
        fits = fits and w_down.shape[0] % (16 * count) == 0 and w_down.shape[0] // count <= 176
        return (body_fast if fits else body_general)(*args)

    return jax.shard_map(
        body,
        mesh=mesh,
        in_specs=(whole, once, P("fsdp"), P("fsdp")) + (once,) * 5 + (whole,),
        out_specs=(whole, whole, P("fsdp"), P("fsdp")) + (once,) * 5,
        check_vma=False,
    )
```
